32 devices in a mesh: ctx: 4 (over y, x), seq: 8 (over z, core).
Axes of the slice: x: 2, y: 2, z: 4, core: 2. Of those that a mesh axis runs over, the one named last changes fastest.
Arguments:
- hidden_in: bfloat16 [8192, 1024], P(('ctx', 'seq')), may hold values from -6 to 6
- cotangent: bfloat16 [8192, 1024], P(('ctx', 'seq')), may hold values from -6 to 6
- norm_gain: bfloat16 [2, 1024], P(None, ('ctx', 'seq')), may hold values from 0.5 to 1.5
- in_weight: bfloat16 [2, 1024, 4096], P(None, None, ('ctx', 'seq')), may hold values from -0.1875 to 0.1875
- conv_weight: bfloat16 [2, 4, 2048], P(None, None, ('ctx', 'seq')), may hold values from -3 to 3
- conv_bias: bfloat16 [2, 2048], P(None, ('ctx', 'seq')), may hold values from -3 to 3
- x_weight: bfloat16 [2, 2048, 96], P(None, ('ctx', 'seq')), may hold values from -0.125 to 0.125
- dt_weight: bfloat16 [2, 64, 2048], P(None, None, ('ctx', 'seq')), may hold values from -0.75 to 0.75
- dt_bias: bfloat16 [2, 2048], P(None, ('ctx', 'seq')), may hold values from -4.5 to -1
- a_log: bfloat16 [2, 2048, 16], P(None, ('ctx', 'seq')), may hold values from -8 to 1
- skip_gain: bfloat16 [2, 2048], P(None, ('ctx', 'seq')), may hold values from 0.5 to 1.5
- out_weight: bfloat16 [2, 2048, 1024], P(None, None, ('ctx', 'seq')), may hold values from -0.125 to 0.125
Outputs:
- out_stream: bfloat16 [8192, 1024], P(('ctx', 'seq'))
- hidden_grad: float32 [8192, 1024], P(('ctx', 'seq'))
- norm_gain_grad: float32 [2, 1024], P(None, ('ctx', 'seq'))
- in_weight_grad: float32 [2, 1024, 4096], P(None, None, ('ctx', 'seq'))
- conv_weight_grad: float32 [2, 4, 2048], P(None, None, ('ctx', 'seq'))
- conv_bias_grad: float32 [2, 2048], P(None, ('ctx', 'seq'))
- x_weight_grad: float32 [2, 2048, 96], P(None, ('ctx', 'seq'))
- dt_weight_grad: float32 [2, 64, 2048], P(None, None, ('ctx', 'seq'))
- dt_bias_grad: float32 [2, 2048], P(None, ('ctx', 'seq'))
- a_log_grad: float32 [2, 2048, 16], P(None, ('ctx', 'seq'))
- skip_gain_grad: float32 [2, 2048], P(None, ('ctx', 'seq'))
- out_weight_grad: float32 [2, 2048, 1024], P(None, None, ('ctx', 'seq'))
The draws below stay inside these ranges and needn't reach their ends.
All inputs are finite; a program needn't handle non-finite values.
Results may differ from the reference program's by a relative error of at most 0.015.
Values may be sent and summed in bfloat16 or wider, within the bound.
A program may use at most 640 MiB of HBM per device.

```python
import math
import jax
import jax.numpy as jnp
from jax import lax

D = 1024
DI = 2048
NS = 16
RANK = 64
CONV = 4
LAYERS = 2
SEQ_LEN = 2048
TOKENS = 8192
N_CTX = 4


def steps_of(rng, extent, cuts, smallest, high):
    gain, own = 1.0, jax.random.fold_in(rng, 6)
    for axis_at, parts in cuts:
        steps = jnp.exp(jax.random.uniform(jax.random.fold_in(own, axis_at), (parts,), jnp.float32, smallest / len(cuts), high / len(cuts)))
        gain = gain * jnp.repeat(steps, extent[axis_at] // parts).reshape([-1 if axis == axis_at else 1 for axis in range(len(extent))])
    return gain


def bell_draw(own_key, shape, scale, bound, split=(), dtype=jnp.bfloat16):
    values = jax.random.normal(own_key, shape, jnp.float32) * scale
    if len(split) > 0:
        values = steps_of(own_key, shape, split, -0.22, 0.18) * values
    return jnp.clip(values, min=-bound, max=bound).astype(dtype)


def setup_inputs(seed: int = 0) -> dict:
    splits = jax.random.split(jax.random.key(seed), 13)
    hidden_in = bell_draw(splits[0], (TOKENS, D), 1.0, 6.0, ((0, 32),))
    cotangent = bell_draw(splits[1], (TOKENS, D), 1.0, 6.0, ((0, 32),))
    norm_gain = jnp.clip(1.0 + 0.1 * jax.random.normal(splits[2], (LAYERS, D), jnp.float32), 0.5, 1.5).astype(jnp.bfloat16)
    in_weight = bell_draw(splits[3], (LAYERS, D, 2 * DI), D ** -0.5, 0.1875, ((2, 32),))
    conv_weight = bell_draw(splits[4], (LAYERS, CONV, DI), CONV ** -0.5, 3.0, ((2, 32),))
    conv_bias = bell_draw(splits[5], (LAYERS, DI), 0.5, 3.0, ((1, 32),))
    x_weight = bell_draw(splits[6], (LAYERS, DI, RANK + 2 * NS), DI ** -0.5, 0.125, ((1, 32),))
    dt_weight = bell_draw(splits[7], (LAYERS, RANK, DI), RANK ** -0.5, 0.75, ((2, 32),))
    dt_bias = jnp.clip(-4.5 + 3.5 * jax.random.uniform(splits[8], (LAYERS, DI), jnp.float32) ** steps_of(splits[8], (LAYERS, DI), ((1, 32),), -0.2, 0.2), -4.5, -1.0).astype(jnp.bfloat16)
    a_log = jnp.clip(-8.0 + 9.0 * jax.random.uniform(splits[9], (LAYERS, DI, NS), jnp.float32) ** steps_of(splits[9], (LAYERS, DI, NS), ((1, 32),), -0.2, 0.2), -8.0, 1.0).astype(jnp.bfloat16)
    skip_gain = jnp.clip(0.5 + 1.0 * jax.random.uniform(splits[10], (LAYERS, DI), jnp.float32) ** steps_of(splits[10], (LAYERS, DI), ((1, 32),), -0.2, 0.2), 0.5, 1.5).astype(jnp.bfloat16)
    out_weight = bell_draw(splits[11], (LAYERS, DI, D), DI ** -0.5, 0.125, ((2, 32),))
    return {"hidden_in": hidden_in, "cotangent": cotangent, "norm_gain": norm_gain, "in_weight": in_weight, "conv_weight": conv_weight, "conv_bias": conv_bias, "x_weight": x_weight, "dt_weight": dt_weight, "dt_bias": dt_bias, "a_log": a_log, "skip_gain": skip_gain, "out_weight": out_weight}


EPS = 1e-05
HIGH = lax.Precision.HIGHEST

@jax.custom_vjp
def low(v):
    return lax.optimization_barrier(v.astype(jnp.bfloat16)).astype(jnp.float32)

@jax.custom_vjp
def low_back(v):
    return v

def low_keep(v):
    return (low(v), None)

def low_pass(kept, grad):
    return (grad,)

def back_keep(v):
    return (v, None)

def back_low(kept, grad):
    return (low(grad),)
low.defvjp(low_keep, low_pass)
low_back.defvjp(back_keep, back_low)

def combine(earlier, later):
    return (earlier[0] * later[0], later[0] * earlier[1] + later[1])

def rms_norm(stream, gain_vec):
    return stream * lax.rsqrt(lax.optimization_barrier(jnp.mean(stream * stream, axis=1, keepdims=True)) + EPS) * gain_vec

def causal_conv(padded, conv_w, conv_b):
    length = padded.shape[0] - conv_w.shape[0] + 1
    summed = conv_b[None, :] + conv_w[0][None, :] * padded[0:length]
    for offset in range(1, conv_w.shape[0]):
        summed = summed + conv_w[offset][None, :] * padded[offset:offset + length]
    return jax.nn.silu(summed)

def scan_states(conv_act, step_size, in_coeff, out_coeff, a_log32, start):
    decay_rate = -jnp.exp(a_log32)
    length = conv_act.shape[0]
    blk_rows = math.gcd(length, 128)

    def block_step(carried, pieces):
        act_rows, step_rows, in_rows, out_rows = pieces
        decays = jnp.exp(step_rows[:, :, None] * decay_rate[None])
        driven = (step_rows * act_rows)[:, :, None] * in_rows[:, None, :]
        products, states = lax.associative_scan(combine, (decays, driven), axis=0)
        states = states + products * carried[None]
        outputs = jnp.einsum('tin,tn->ti', states, out_rows, precision=HIGH)
        return (states[-1], outputs)
    shaped = tuple((member.reshape(length // blk_rows, blk_rows, member.shape[1]) for member in (conv_act, step_size, in_coeff, out_coeff)))
    final_state, outputs = lax.scan(jax.checkpoint(block_step), start, shaped)
    return (outputs.reshape(length, -1), final_state)

def mixer(stream, weights):
    gain_vec, w_in, conv_w, conv_b, w_x, w_dt, b_dt, a_lg, skip_vec, w_out = weights
    inner_width = w_dt.shape[1]
    rank_width = w_dt.shape[0]
    state_width = a_lg.shape[1]
    rim_width = conv_w.shape[0] - 1
    normed = rms_norm(stream, gain_vec)
    projected = low_back(jnp.dot(low(normed), w_in, precision=HIGH))
    conv_input = low(projected[:, :inner_width])
    gate_branch = projected[:, inner_width:]
    padded = jnp.concatenate([jnp.zeros((rim_width, inner_width), jnp.float32), conv_input], 0)
    conv_act = low(causal_conv(padded, conv_w, conv_b))
    small_proj = low_back(jnp.dot(conv_act, w_x, precision=HIGH))
    step_low = low(small_proj[:, :rank_width])
    in_coeff = small_proj[:, rank_width:rank_width + state_width]
    out_coeff = small_proj[:, rank_width + state_width:]
    step_size = jax.nn.softplus(low_back(jnp.dot(step_low, w_dt, precision=HIGH)) + b_dt)
    scan_out, _ = scan_states(conv_act, step_size, in_coeff, out_coeff, a_lg, jnp.zeros((inner_width, state_width), jnp.float32))
    mixed = low((scan_out + skip_vec * conv_act) * jax.nn.silu(gate_branch))
    return stream + low_back(jnp.dot(mixed, w_out, precision=HIGH))

def reference(hidden_in, cotangent, norm_gain, in_weight, conv_weight, conv_bias, x_weight, dt_weight, dt_bias, a_log, skip_gain, out_weight):
    params = tuple((member.astype(jnp.float32) for member in (norm_gain, in_weight, conv_weight, conv_bias, x_weight, dt_weight, dt_bias, a_log, skip_gain, out_weight)))
    inputs = hidden_in.astype(jnp.float32).reshape(N_CTX, SEQ_LEN, D)

    def network(streams, weights):

        def context(stream):
            for layer_idx in range(LAYERS):
                stream = mixer(stream, tuple((member[layer_idx] for member in weights)))
            return stream
        return lax.map(jax.checkpoint(context), streams)
    result, pullback = jax.vjp(network, inputs, params)
    input_grad, param_grads = pullback(cotangent.astype(jnp.float32).reshape(N_CTX, SEQ_LEN, D))
    return (result.reshape(TOKENS, D).astype(jnp.bfloat16), input_grad.reshape(TOKENS, D), param_grads[0], param_grads[1], param_grads[2], param_grads[3], param_grads[4], param_grads[5], param_grads[6], param_grads[7], param_grads[8], param_grads[9])
```

```python
import functools

import jax
import jax.numpy as jnp
from jax import lax
from jax.experimental import pallas as pl
from jax.experimental.pallas import tpu as pltpu
from jax.sharding import PartitionSpec as P

EPS = 1e-05
LOG2E = 1.4426950408889634
MESH = pl.DeviceIdType.MESH
F32, BF16 = jnp.float32, jnp.bfloat16
NT = (((1,), (1,)), ((), ()))
TN = (((0,), (0,)), ((), ()))
VMEM_BYTES = 63 * 2**20
CHUNK = 16
GROUP = 512
HALO = 16


def dot(a, b, dims=None):
    if dims is None:
        dims = (((1,), (0,)), ((), ()))
    return lax.dot_general(a, b, dims, preferred_element_type=F32)


def lanes(index, width):
    return pl.ds(pl.multiple_of(index * width, width), width)


def widen(tile, width):
    times = width // tile.shape[1]
    return jnp.concatenate([tile] * times, axis=1) if times > 1 else tile


def softplus(v):
    return jnp.maximum(v, 0.0) + jnp.log1p(jnp.exp(-jnp.abs(v)))


def sigmoid(v):
    return 1.0 / (1.0 + jnp.exp(-v))


def keep_sum(own_sum, i, step):
    total = jnp.sum(step, axis=0, keepdims=True)
    fold = own_sum.shape[1]
    for part in range(GROUP // fold):
        row = i * (GROUP // fold) + part
        own_sum[pl.ds(row, 1), :] = total[:, part * fold : (part + 1) * fold]


def sum_of(sum_s, j, g):
    fold = sum_s.shape[2]
    each = GROUP // fold
    return jnp.concatenate(
        [sum_s[j, pl.ds(g * each + part, 1), :] for part in range(each)], 1
    )


def chunk_mask(rows, states):
    wide = CHUNK * states
    token = lax.rem(lax.broadcasted_iota(jnp.int32, (rows, wide), 0), CHUNK)
    owner = lax.broadcasted_iota(jnp.int32, (rows, wide), 1) // states
    return token == owner


def spread(small_low, first, states):
    wide = CHUNK * states
    row = lax.broadcasted_iota(jnp.int32, (small_low.shape[1], wide), 0)
    col = lax.broadcasted_iota(jnp.int32, (small_low.shape[1], wide), 1)
    pick = (row == first + lax.rem(col, states)).astype(F32).astype(BF16)
    tiled = dot(small_low, pick)
    return jnp.where(chunk_mask(small_low.shape[0], states), tiled, 0.0).astype(BF16)


def gather_back(partial, first, states, width):
    wide = CHUNK * states
    row = lax.broadcasted_iota(jnp.int32, (wide, width), 0)
    col = lax.broadcasted_iota(jnp.int32, (wide, width), 1)
    pick = (col == first + lax.rem(row, states)).astype(F32).astype(BF16)
    kept = jnp.where(chunk_mask(partial.shape[0], states), partial, 0.0)
    return dot(kept.astype(BF16), pick)


class Names:
    def __init__(self, states, taps):
        self.conv = states
        self.conv_b = states + taps
        self.dt_b = states + taps + 1
        self.skip = states + taps + 2
        self.count = states + taps + 3
        self.padded = -(-self.count // 8) * 8


def forward_kernel(
    cfg,
    stream_ref,
    gain_ref,
    win_ref,
    xw_ref,
    dtw_ref,
    vec_ref,
    wout_ref,
    new_ref,
    pad_ref,
    gate_ref,
    act_ref,
    sp_ref,
    pre_ref,
    h_hbm,
    y_ref,
    mixed_ref,
    normed_s,
    padf_s,
    halo_s,
    dt_s,
    dx_s,
    bb_s,
    cd_s,
    hs,
    own_sum,
    sum_s,
    own_end,
    end_s,
    halo_sem,
    sum_send,
    sum_recv,
    end_send,
    end_recv,
    h_sem,
):
    rows, inner, states, taps, rank, count = cfg
    at = Names(states, taps)
    ctx, me = lax.axis_index("ctx"), lax.axis_index("seq")
    groups, steps = inner // GROUP, rows // CHUNK
    barrier = pltpu.get_barrier_semaphore()

    def greet(j, _):
        pl.semaphore_signal(barrier, inc=1, device_id=(ctx, j), device_id_type=MESH)
        return 0

    lax.fori_loop(0, me, greet, 0)
    stream = stream_ref[...]
    scale = lax.rsqrt(jnp.mean(stream * stream, axis=1, keepdims=True) + EPS)
    normed_s[...] = (stream * scale * gain_ref[...]).astype(BF16)

    @pl.loop(0, inner // GROUP)
    def _(i):
        low = dot(normed_s[...], win_ref[lanes(i, GROUP), :], NT).astype(BF16)
        pad_ref[pl.ds(HALO, rows), lanes(i, GROUP)] = low
        padf_s[pl.ds(HALO, rows), lanes(i, GROUP)] = low.astype(F32)

    @pl.when(me < count - 1)
    def _():
        pl.semaphore_wait(barrier, count - 1 - me)

    def edge():
        return pltpu.make_async_remote_copy(
            pad_ref.at[pl.ds(rows, HALO)],
            halo_s,
            halo_sem.at[0],
            halo_sem.at[1],
            device_id=(ctx, jnp.minimum(me + 1, count - 1)),
            device_id_type=MESH,
        )

    @pl.when(me < count - 1)
    def _():
        edge().start()

    @pl.loop(0, inner // GROUP)
    def _(i):
        gate_ref[:, lanes(i, GROUP)] = dot(
            normed_s[...], win_ref[lanes(i + inner // GROUP, GROUP), :], NT
        )

    @pl.when(me > 0)
    def _():
        edge().wait_recv()

    @pl.when(me == 0)
    def _():
        halo_s[...] = jnp.zeros_like(halo_s)

    pad_ref[pl.ds(0, HALO), :] = halo_s[...]
    padf_s[pl.ds(0, HALO), :] = halo_s[...].astype(F32)

    @pl.loop(0, inner // GROUP)
    def _(i):
        here = lanes(i, GROUP)
        total = vec_ref[pl.ds(at.conv_b, 1), here]
        for k in range(taps):
            total = (
                total
                + vec_ref[pl.ds(at.conv + k, 1), here]
                * padf_s[pl.ds(HALO - taps + 1 + k, rows), here]
            )
        act_ref[:, here] = (total * sigmoid(total)).astype(BF16)

    small = dot(act_ref[...], xw_ref[...], NT)
    sp_ref[...] = small
    small_low = small.astype(BF16)

    @pl.loop(0, inner // GROUP)
    def _(i):
        here = lanes(i, GROUP)
        before = dot(small_low, dtw_ref[:, here]) + vec_ref[pl.ds(at.dt_b, 1), here]
        step = softplus(before)
        pre_ref[:, here] = before
        dt_s[:, here] = step
        dx_s[:, here] = step * act_ref[:, here].astype(F32)
        keep_sum(own_sum, i, step)

    def sums(j):
        return pltpu.make_async_remote_copy(
            own_sum,
            sum_s.at[me],
            sum_send.at[j],
            sum_recv.at[me],
            device_id=(ctx, j),
            device_id_type=MESH,
        )

    def sums_from(j):
        return pltpu.make_async_remote_copy(
            own_sum,
            sum_s.at[j],
            sum_send.at[j],
            sum_recv.at[j],
            device_id=(ctx, j),
            device_id_type=MESH,
        )

    def ends(g, j, slot):
        return pltpu.make_async_remote_copy(
            own_end.at[:, pl.ds(g * GROUP, GROUP)],
            end_s.at[slot, :, pl.ds(g * GROUP, GROUP)],
            end_send.at[g, j],
            end_recv.at[g, slot],
            device_id=(ctx, j),
            device_id_type=MESH,
        )

    def each(first, last, act):
        def body(j, _):
            act(j)
            return 0

        lax.fori_loop(first, last, body, 0)

    each(me + 1, count, lambda j: sums(j).start())
    for n in range(states):
        bb_s[:, n, :] = jnp.broadcast_to(
            small[:, rank + n : rank + n + 1], (rows, 128)
        )
    cd_s[...] = spread(small_low, rank + states, states)

    def advance(t, state, rate2, here):
        return (
            jnp.exp2(dt_s[pl.ds(t, 1), here] * rate2) * state
            + dx_s[pl.ds(t, 1), here] * widen(bb_s[t], GROUP)
        )

    for g in range(groups):
        here = pl.ds(g * GROUP, GROUP)
        rate2 = vec_ref[pl.ds(0, states), here] * LOG2E

        def first_pass(step, state):
            for i in range(CHUNK):
                state = advance(step * CHUNK + i, state, rate2, here)
            return state

        own_end[:, here] = lax.fori_loop(
            0, steps, first_pass, jnp.zeros((states, GROUP), F32)
        ).astype(BF16)
        each(me + 1, count, lambda j: ends(g, j, me).start())

    for g in range(groups):
        here = pl.ds(g * GROUP, GROUP)
        rate2 = vec_ref[pl.ds(0, states), here] * LOG2E

        def carry(j, state):
            if g == 0:
                sums_from(j).wait_recv()
            ends(g, j, j).wait_recv()
            return (
                jnp.exp2(rate2 * sum_of(sum_s, j, g)) * state
                + end_s[j, :, here].astype(F32)
            )

        start = lax.fori_loop(0, me, carry, jnp.zeros((states, GROUP), F32))
        hs[pl.ds(0, states), here] = start.astype(BF16)

        def second_pass(step, state):
            base = pl.multiple_of(step * CHUNK * states + states, states)
            for i in range(CHUNK):
                state = advance(step * CHUNK + i, state, rate2, here)
                hs[pl.ds(base + i * states, states), here] = state.astype(BF16)
            tokens = pl.ds(pl.multiple_of(step * CHUNK, CHUNK), CHUNK)
            y_ref[tokens, here] = dot(
                cd_s[tokens, :], hs[pl.ds(base, CHUNK * states), here]
            )
            return state

        lax.fori_loop(0, steps, second_pass, start)
        pltpu.make_async_copy(hs.at[:, here], h_hbm.at[:, here], h_sem.at[g]).start()
        y_value = (
            y_ref[:, here]
            + vec_ref[pl.ds(at.skip, 1), here] * act_ref[:, here].astype(F32)
        )
        gate = gate_ref[:, here]
        y_ref[:, here] = y_value
        mixed_ref[:, here] = (y_value * gate * sigmoid(gate)).astype(BF16)

    width = stream_ref.shape[1]
    for i in range(width // 256):
        here = pl.ds(i * 256, 256)
        new_ref[:, here] = stream_ref[:, here] + dot(
            mixed_ref[...], wout_ref[here, :], NT
        )

    @pl.when(me < count - 1)
    def _():
        edge().wait_send()

    each(me + 1, count, lambda j: sums(j).wait_send())
    for g in range(groups):
        here = pl.ds(g * GROUP, GROUP)
        each(me + 1, count, lambda j: ends(g, j, me).wait_send())
        pltpu.make_async_copy(hs.at[:, here], h_hbm.at[:, here], h_sem.at[g]).wait()


def backward_kernel(
    cfg,
    sgrad_ref,
    stream_ref,
    gain_ref,
    win_ref,
    xw_ref,
    dtw_ref,
    vec_ref,
    wout_ref,
    pad_ref,
    gate_ref,
    act_ref,
    sp_ref,
    pre_ref,
    h_hbm,
    y_ref,
    mixed_ref,
    nsg_ref,
    gin_hbm,
    gout_hbm,
    gx_ref,
    gdt_ref,
    gvec_ref,
    ggain_ref,
    hb,
    normed_s,
    low_s,
    sg_s,
    dt_s,
    dx_s,
    stepg_s,
    pb_s,
    cb_s,
    bd_s,
    ab_s,
    rb_s,
    pin_s,
    pout_s,
    prelow_s,
    stage_in,
    stage_out,
    halo_s,
    own_sum,
    sum_s,
    own_end,
    end_s,
    halo_sem,
    sum_send,
    sum_recv,
    end_send,
    end_recv,
    h_sem,
    in_sem,
    out_sem,
):
    rows, inner, states, taps, rank, count = cfg
    at = Names(states, taps)
    ctx, me = lax.axis_index("ctx"), lax.axis_index("seq")
    groups, steps = inner // GROUP, rows // CHUNK
    width = stream_ref.shape[1]
    barrier = pltpu.get_barrier_semaphore()

    def each(first, last, act):
        def body(j, _):
            act(j)
            return 0

        lax.fori_loop(first, last, body, 0)

    each(
        me + 1,
        count,
        lambda j: pl.semaphore_signal(
            barrier, inc=1, device_id=(ctx, j), device_id_type=MESH
        ),
    )

    def states_in(g):
        return pltpu.make_async_copy(
            h_hbm.at[:, pl.ds(g * GROUP, GROUP)], hb.at[g % 2], h_sem.at[g % 2]
        )

    states_in(0).start()
    low_s[...] = sgrad_ref[...].astype(BF16)
    stream = stream_ref[...]
    scale = lax.rsqrt(jnp.mean(stream * stream, axis=1, keepdims=True) + EPS)
    normed_s[...] = (stream * scale * gain_ref[...]).astype(BF16)
    small_low = sp_ref[...].astype(BF16)

    @pl.loop(0, inner // GROUP)
    def _(i):
        here = lanes(i, GROUP)
        mixed_grad = dot(low_s[...], wout_ref[:, here])
        gate = gate_ref[:, here]
        sig = sigmoid(gate)
        act = act_ref[:, here].astype(F32)
        scan_grad = mixed_grad * gate * sig
        sg_s[:, here] = scan_grad
        pb_s[:, lanes(i + inner // GROUP, GROUP)] = (
            mixed_grad * y_ref[:, here] * sig * (1.0 + gate * (1.0 - sig))
        ).astype(BF16)
        gvec_ref[pl.ds(at.skip, 1), here] = jnp.sum(
            scan_grad * act, axis=0, keepdims=True
        )
        step = softplus(pre_ref[:, here])
        dt_s[:, here] = step
        dx_s[pl.ds(0, rows), here] = step * act
        keep_sum(own_sum, i, step)

    def sums(j, slot):
        return pltpu.make_async_remote_copy(
            own_sum,
            sum_s.at[slot],
            sum_send.at[j],
            sum_recv.at[slot],
            device_id=(ctx, j),
            device_id_type=MESH,
        )

    def ends(g, j, slot):
        return pltpu.make_async_remote_copy(
            own_end.at[:, pl.ds(g * GROUP, GROUP)],
            end_s.at[slot, :, pl.ds(g * GROUP, GROUP)],
            end_send.at[g, j],
            end_recv.at[g, slot],
            device_id=(ctx, j),
            device_id_type=MESH,
        )

    @pl.when(me > 0)
    def _():
        pl.semaphore_wait(barrier, me)

    each(0, me, lambda j: sums(j, me).start())
    for n in range(states):
        first = rank + states + n
        cb_s[:, n, :] = jnp.broadcast_to(
            sp_ref[:, first : first + 1], (rows, 128)
        )
    bd_s[...] = spread(small_low, rank, states)
    ones = jnp.where(chunk_mask(CHUNK, states), 1.0, 0.0).astype(BF16)

    for g in range(groups):
        here = pl.ds(g * GROUP, GROUP)
        rate2 = vec_ref[pl.ds(0, states), here] * LOG2E

        def first_pass(k, state):
            step = steps - 1 - k
            for i in reversed(range(CHUNK)):
                t = step * CHUNK + i
                state = jnp.exp2(dt_s[pl.ds(t, 1), here] * rate2) * (
                    state + sg_s[pl.ds(t, 1), here] * widen(cb_s[t], GROUP)
                )
            return state

        own_end[:, here] = lax.fori_loop(
            0, steps, first_pass, jnp.zeros((states, GROUP), F32)
        ).astype(BF16)
        each(0, me, lambda j: ends(g, j, me).start())

    for g in range(groups):
        here = pl.ds(g * GROUP, GROUP)
        rate = vec_ref[pl.ds(0, states), here]
        rate2 = rate * LOG2E
        if g + 1 < groups:
            states_in(g + 1).start()

        def carry(k, state):
            j = count - 1 - k
            if g == 0:
                sums(j, j).wait_recv()
            ends(g, j, j).wait_recv()
            return (
                jnp.exp2(rate2 * sum_of(sum_s, j, g)) * state
                + end_s[j, :, here].astype(F32)
            )

        begin = lax.fori_loop(
            0, count - 1 - me, carry, jnp.zeros((states, GROUP), F32)
        )
        states_in(g).wait()

        def second_pass(k, both):
            state, total = both
            step = steps - 1 - k
            base = pl.multiple_of(step * CHUNK * states, states)
            for i in reversed(range(CHUNK)):
                t = step * CHUNK + i
                dt = dt_s[pl.ds(t, 1), here]
                adjoint = state + sg_s[pl.ds(t, 1), here] * widen(cb_s[t], GROUP)
                state = jnp.exp2(dt * rate2) * adjoint
                held = hb[g % 2, pl.ds(base + i * states, states), :].astype(F32)
                rated = state * held * rate
                total = total + dt * rated
                ab_s[pl.ds(i * states, states), :] = adjoint.astype(BF16)
                rb_s[pl.ds(i * states, states), :] = rated.astype(BF16)
            tokens = pl.ds(pl.multiple_of(step * CHUNK, CHUNK), CHUNK)
            from_in = dot(bd_s[tokens, :], ab_s[...])
            from_rate = dot(ones, rb_s[...])
            scan_grad = sg_s[tokens, here]
            into_in = dot(dx_s[tokens, here].astype(BF16), ab_s[...], NT)
            into_out = dot(
                scan_grad.astype(BF16),
                hb[g % 2, pl.ds(base + states, CHUNK * states), :],
                NT,
            )
            if g == 0:
                pin_s[tokens, :] = into_in
                pout_s[tokens, :] = into_out
            else:
                pin_s[tokens, :] += into_in
                pout_s[tokens, :] += into_out
            stepg_s[tokens, here] = (
                act_ref[tokens, here].astype(F32) * from_in + from_rate
            )
            sg_s[tokens, here] = (
                dt_s[tokens, here] * from_in
                + vec_ref[pl.ds(at.skip, 1), here] * scan_grad
            )
            return state, total

        _, total = lax.fori_loop(
            0, steps, second_pass, (begin, jnp.zeros((states, GROUP), F32))
        )
        gvec_ref[pl.ds(0, states), here] = total

    @pl.loop(0, inner // GROUP)
    def _(i):
        here = lanes(i, GROUP)
        pre_grad = stepg_s[pl.ds(0, rows), here] * sigmoid(pre_ref[:, here])
        gvec_ref[pl.ds(at.dt_b, 1), here] = jnp.sum(pre_grad, axis=0, keepdims=True)
        prelow_s[:, here] = pre_grad.astype(BF16)
        dx_s[:, here] = pad_ref[:, here].astype(F32)

    small_grad = (
        dot(prelow_s[...], dtw_ref[...], NT)
        + gather_back(pin_s[...], rank, states, sp_ref.shape[1])
        + gather_back(pout_s[...], rank + states, states, sp_ref.shape[1])
    ).astype(BF16)

    @pl.loop(0, inner // GROUP)
    def _(i):
        here = lanes(i, GROUP)
        gdt_ref[:, here] = dot(small_low, prelow_s[:, here], TN)
        gx_ref[:, here] = dot(small_grad, act_ref[:, here], TN)
        act_grad = sg_s[:, here] + dot(small_grad, xw_ref[:, here])
        total = vec_ref[pl.ds(at.conv_b, 1), here]
        for k in range(taps):
            total = (
                total
                + vec_ref[pl.ds(at.conv + k, 1), here]
                * dx_s[pl.ds(HALO - taps + 1 + k, rows), here]
            )
        sig = sigmoid(total)
        conv_grad = act_grad * sig * (1.0 + total * (1.0 - sig))
        stepg_s[pl.ds(0, rows), here] = conv_grad
        gvec_ref[pl.ds(at.conv_b, 1), here] = jnp.sum(conv_grad, axis=0, keepdims=True)
        for k in range(taps):
            gvec_ref[pl.ds(at.conv + k, 1), here] = jnp.sum(
                conv_grad * dx_s[pl.ds(HALO - taps + 1 + k, rows), here],
                axis=0,
                keepdims=True,
            )

    def edge():
        return pltpu.make_async_remote_copy(
            stepg_s.at[pl.ds(0, 8)],
            halo_s,
            halo_sem.at[0],
            halo_sem.at[1],
            device_id=(ctx, jnp.maximum(me - 1, 0)),
            device_id_type=MESH,
        )

    @pl.when(me > 0)
    def _():
        edge().start()

    tiles = inner // GROUP

    def project(i, first):
        here = lanes(i, GROUP)
        slot = lax.rem(i, 2)
        copy = pltpu.make_async_copy(
            stage_in.at[slot], gin_hbm.at[here], in_sem.at[slot]
        )

        @pl.when(first >= 2)
        def _():
            copy.wait()

        stage_in[slot] = dot(pb_s[:, here], normed_s[...], TN).astype(BF16)
        copy.start()
        part = dot(pb_s[:, here], win_ref[here, :])

        @pl.when(first == 0)
        def _():
            nsg_ref[...] = part

        @pl.when(first > 0)
        def _():
            nsg_ref[...] += part

    @pl.loop(0, tiles)
    def _(i):
        project(i + tiles, i)

    out_rows = stage_out.shape[1]
    for r in range(width // out_rows):
        slot = r % 2
        copy = pltpu.make_async_copy(
            stage_out.at[slot],
            gout_hbm.at[pl.ds(r * out_rows, out_rows)],
            out_sem.at[slot],
        )
        if r >= 2:
            copy.wait()

        @pl.loop(0, tiles)
        def _(i):
            here = lanes(i, GROUP)
            stage_out[slot, :, here] = dot(
                low_s[:, pl.ds(r * out_rows, out_rows)], mixed_ref[:, here], TN
            ).astype(BF16)

        copy.start()

    @pl.when(me < count - 1)
    def _():
        edge().wait_recv()

    @pl.when(me == count - 1)
    def _():
        halo_s[...] = jnp.zeros_like(halo_s)

    @pl.when(me > 0)
    def _():
        edge().wait_send()

    stepg_s[pl.ds(rows, 8), :] = halo_s[...]

    @pl.loop(0, tiles)
    def _(i):
        here = lanes(i, GROUP)
        total = jnp.zeros((rows, GROUP), F32)
        for k in range(taps):
            total = (
                total
                + vec_ref[pl.ds(at.conv + k, 1), here]
                * stepg_s[pl.ds(taps - 1 - k, rows), here]
            )
        pb_s[:, here] = total.astype(BF16)
        project(i, i + tiles)

    stream = stream_ref[...]
    scale = lax.rsqrt(jnp.mean(stream * stream, axis=1, keepdims=True) + EPS)
    normed_grad = nsg_ref[...]
    ggain_ref[...] = jnp.broadcast_to(
        jnp.sum(normed_grad * stream * scale, axis=0, keepdims=True), (8, width)
    )
    scaled = normed_grad * gain_ref[...]
    inner_sum = jnp.mean(scaled * stream, axis=1, keepdims=True)
    nsg_ref[...] = (
        sgrad_ref[...] + scale * scaled - stream * (scale * scale * scale) * inner_sum
    )
    for slot in range(2):
        pltpu.make_async_copy(
            stage_in.at[slot], gin_hbm.at[pl.ds(0, GROUP)], in_sem.at[slot]
        ).wait()
        pltpu.make_async_copy(
            stage_out.at[slot], gout_hbm.at[pl.ds(0, out_rows)], out_sem.at[slot]
        ).wait()
    each(0, me, lambda j: sums(j, me).wait_send())
    for g in range(groups):
        each(0, me, lambda j: ends(g, j, me).wait_send())


def in_vmem(count):
    return [pl.BlockSpec(memory_space=pltpu.VMEM)] * count


def in_any(count):
    return [pl.BlockSpec(memory_space=pl.ANY)] * count


def forward_call(cfg, stream, gain, win, xw, dtw, vec, wout):
    rows, inner, states, taps, rank, count = cfg
    small = rank + 2 * states
    groups = inner // GROUP
    shape = jax.ShapeDtypeStruct
    dma = pltpu.SemaphoreType.DMA
    return pl.pallas_call(
        functools.partial(forward_kernel, cfg),
        out_shape=(
            shape(stream.shape, F32),
            shape((rows + HALO, inner), BF16),
            shape((rows, inner), F32),
            shape((rows, inner), BF16),
            shape((rows, small), F32),
            shape((rows, inner), F32),
            shape(((rows + 1) * states, inner), BF16),
            shape((rows, inner), F32),
            shape((rows, inner), BF16),
        ),
        in_specs=in_vmem(7),
        out_specs=tuple(in_vmem(6) + in_any(1) + in_vmem(2)),
        scratch_shapes=[
            pltpu.VMEM(stream.shape, BF16),
            pltpu.VMEM((rows + HALO, inner), F32),
            pltpu.VMEM((HALO, inner), BF16),
            pltpu.VMEM((rows, inner), F32),
            pltpu.VMEM((rows, inner), F32),
            pltpu.VMEM((rows, states, 128), F32),
            pltpu.VMEM((rows, CHUNK * states), BF16),
            pltpu.VMEM(((rows + 1) * states, inner), BF16),
            pltpu.VMEM((8, inner // 8), F32),
            pltpu.VMEM((count, 8, inner // 8), F32),
            pltpu.VMEM((states, inner), BF16),
            pltpu.VMEM((count, states, inner), BF16),
            dma((2,)),
            dma((count,)),
            dma((count,)),
            dma((groups, count)),
            dma((groups, count)),
            dma((groups,)),
        ],
        compiler_params=pltpu.CompilerParams(
            collective_id=0, has_side_effects=True, vmem_limit_bytes=VMEM_BYTES
        ),
        name="forward_layer",
    )(stream, gain, win, xw, dtw, vec, wout)


def backward_call(cfg, sgrad, stream, gain, win, xw, dtw, vec, wout, saved):
    rows, inner, states, taps, rank, count = cfg
    width = stream.shape[1]
    small = rank + 2 * states
    groups = inner // GROUP
    wide = CHUNK * states
    shape = jax.ShapeDtypeStruct
    dma = pltpu.SemaphoreType.DMA
    return pl.pallas_call(
        functools.partial(backward_kernel, cfg),
        out_shape=(
            shape((rows, width), F32),
            shape((2 * inner, width), BF16),
            shape((width, inner), BF16),
            shape((small, inner), F32),
            shape((small, inner), F32),
            shape((Names(states, taps).padded, inner), F32),
            shape((8, width), F32),
        ),
        in_specs=in_vmem(13) + in_any(1) + in_vmem(2),
        out_specs=tuple(in_vmem(1) + in_any(2) + in_vmem(4)),
        scratch_shapes=[
            pltpu.VMEM((2, (rows + 1) * states, GROUP), BF16),
            pltpu.VMEM((rows, width), BF16),
            pltpu.VMEM((rows, width), BF16),
            pltpu.VMEM((rows, inner), F32),
            pltpu.VMEM((rows, inner), F32),
            pltpu.VMEM((rows + HALO, inner), F32),
            pltpu.VMEM((rows + 8, inner), F32),
            pltpu.VMEM((rows, 2 * inner), BF16),
            pltpu.VMEM((rows, states, 128), F32),
            pltpu.VMEM((rows, wide), BF16),
            pltpu.VMEM((wide, GROUP), BF16),
            pltpu.VMEM((wide, GROUP), BF16),
            pltpu.VMEM((rows, wide), F32),
            pltpu.VMEM((rows, wide), F32),
            pltpu.VMEM((rows, inner), BF16),
            pltpu.VMEM((2, GROUP, width), BF16),
            pltpu.VMEM((2, width // 4, inner), BF16),
            pltpu.VMEM((8, inner), F32),
            pltpu.VMEM((8, inner // 8), F32),
            pltpu.VMEM((count, 8, inner // 8), F32),
            pltpu.VMEM((states, inner), BF16),
            pltpu.VMEM((count, states, inner), BF16),
            dma((2,)),
            dma((count,)),
            dma((count,)),
            dma((groups, count)),
            dma((groups, count)),
            dma((2,)),
            dma((2,)),
            dma((2,)),
        ],
        compiler_params=pltpu.CompilerParams(
            collective_id=1, has_side_effects=True, vmem_limit_bytes=VMEM_BYTES
        ),
        name="backward_layer",
    )(sgrad, stream, gain, win, xw, dtw, vec, wout, *saved)


def parts_of(in_rows, out_rows, small_rows):
    cut = in_rows * 3 // 4 // 16 * 16
    return (
        (0, 0, cut, 1),
        (2, 0, small_rows, 1),
        (0, cut, in_rows - cut, 0),
        (1, 0, out_rows, 0),
    )


def places():
    ctx, seq = lax.axis_index("ctx"), lax.axis_index("seq")
    return lax.div(ctx, 2), lax.rem(ctx, 2), lax.div(seq, 2), lax.rem(seq, 2)


def device(y, x, z, core):
    return (2 * y + x, 2 * z + core)


def greet_square(depth):
    y, x, z, core = places()
    barrier = pltpu.get_barrier_semaphore()
    partners = [device(y, x, z, 1 - core), device(y, 1 - x, z, core)]
    partners.append(device(1 - y, x, z, core))
    for step in range(1, depth):
        partners.append(device(y, x, lax.rem(z + step, depth), core))
    for partner in partners:
        pl.semaphore_signal(barrier, inc=1, device_id=partner, device_id_type=MESH)
    pl.semaphore_wait(barrier, len(partners))


def gather_kernel(layers, depth, parts, *refs):
    local, whole = refs[: 3 * layers], refs[3 * layers : 6 * layers]
    own_sem, send_sem, recv_sem = refs[6 * layers :]
    y, x, z, core = places()
    greet_square(depth)
    own_copies = []
    for layer in range(layers):
        for array in range(3):
            copy = pltpu.make_async_copy(
                local[3 * layer + array],
                whole[3 * layer + array].at[y, x, z, core],
                own_sem.at[layer, array],
            )
            copy.start()
            own_copies.append(copy)
    sent = []
    used = [0] * layers

    def span(layer, part, block):
        array, first, rows, _ = parts[part]
        return whole[3 * layer + array].at[(*block, pl.ds(first, rows))]

    def send(layer, part, block, to, own=False):
        array, first, rows, _ = parts[part]
        source = (
            local[3 * layer + array].at[pl.ds(first, rows)]
            if own
            else span(layer, part, block)
        )
        copy = pltpu.make_async_remote_copy(
            source,
            span(layer, part, block),
            send_sem.at[layer, used[layer]],
            recv_sem.at[(layer, *block[:2], block[2], block[3], part)],
            device_id=to,
            device_id_type=MESH,
        )
        used[layer] += 1
        copy.start()
        sent.append(copy)

    def arrive(layer, part, block):
        pltpu.make_async_remote_copy(
            span(layer, part, block),
            span(layer, part, block),
            send_sem.at[layer, 0],
            recv_sem.at[(layer, *block[:2], block[2], block[3], part)],
            device_id=device(y, x, z, 1 - core),
            device_id_type=MESH,
        ).wait_recv()

    x_side, y_side = device(y, 1 - x, z, core), device(1 - y, x, z, core)
    sibling = device(y, x, z, 1 - core)
    everything = range(len(parts))
    line = [lax.rem(z + step, depth) for step in range(depth)]

    def begin(layer):
        block = (y, x, z, core)
        for part in everything:
            for to in (x_side, y_side):
                send(layer, part, block, to, own=True)
            for step in range(1, depth):
                to = device(y, x, line[step], core)
                send(layer, part, block, to, own=True)
            send(layer, part, block, sibling, own=True)

    def along(layer):
        for step in range(depth):
            for part in everything:
                block = (y, x, line[step], core)
                if step > 0:
                    arrive(layer, part, block)
                    for to in (x_side, y_side, sibling):
                        send(layer, part, block, to)
                if parts[part][3] == 1:
                    block, to = (y, 1 - x, line[step], core), y_side
                else:
                    block, to = (1 - y, x, line[step], core), x_side
                arrive(layer, part, block)
                send(layer, part, block, to)
                send(layer, part, block, sibling)

    def rest(layer):
        for step in range(depth):
            for part in everything:
                for other in (0, 1):
                    if parts[part][3] == 1:
                        block = (1 - y, x if other == 0 else 1 - x, line[step], core)
                    else:
                        block = (y if other == 0 else 1 - y, 1 - x, line[step], core)
                    arrive(layer, part, block)
                    send(layer, part, block, sibling)

    def finish(layer):
        for step in range(depth):
            for part in everything:
                for far_y in (y, 1 - y):
                    for far_x in (x, 1 - x):
                        arrive(layer, part, (far_y, far_x, line[step], 1 - core))

    for layer in range(layers):
        begin(layer)
        along(layer)
        rest(layer)
    for layer in range(layers):
        finish(layer)
    for copy in own_copies:
        copy.wait()
    for copy in sent:
        copy.wait_send()


def gather_call(depth, local):
    layers = len(local)
    flat = [array for layer in local for array in layer]
    parts = parts_of(*(array.shape[0] for array in local[0]))
    outs = [
        jax.ShapeDtypeStruct((2, 2, depth, 2) + array.shape, array.dtype)
        for array in flat
    ]
    sends = len(parts) * (2 + depth + 3 * (depth - 1) + 2 * depth + 2 * depth)
    dma = pltpu.SemaphoreType.DMA
    gathered = pl.pallas_call(
        functools.partial(gather_kernel, layers, depth, parts),
        out_shape=tuple(outs),
        in_specs=in_any(len(flat)),
        out_specs=tuple(in_any(len(flat))),
        scratch_shapes=[
            dma((layers, 3)),
            dma((layers, sends)),
            dma((layers, 2, 2, depth, 2, len(parts))),
        ],
        compiler_params=pltpu.CompilerParams(collective_id=2, has_side_effects=True),
        name="gather_weights",
    )(*flat)
    joined = [
        array.reshape((-1,) + piece.shape[1:]) for array, piece in zip(gathered, flat)
    ]
    return [joined[3 * layer : 3 * layer + 3] for layer in range(layers)]


def reduce_kernel(depth, parts, *refs):
    whole, outs = refs[:3], refs[3:6]
    pieces = len(parts)
    own = refs[6 : 6 + pieces]
    core_in = refs[6 + pieces : 6 + 2 * pieces]
    first_in = refs[6 + 2 * pieces : 6 + 3 * pieces]
    second_in = refs[6 + 3 * pieces : 6 + 4 * pieces]
    line_in = refs[6 + 4 * pieces : 6 + 5 * pieces]
    own_sem, send_sem, recv_sem = refs[6 + 5 * pieces :]
    y, x, z, core = places()
    greet_square(depth)
    line = [lax.rem(z + step + 1, depth) for step in range(depth)]
    x_side, y_side = device(y, 1 - x, z, core), device(1 - y, x, z, core)
    sibling = device(y, x, z, 1 - core)

    def part_of(part, step, side):
        array, first, rows, _ = parts[part]
        return whole[array].at[:, :, line[step], side, pl.ds(first, rows)]

    def local(part, step):
        return pltpu.make_async_copy(
            part_of(part, step, core), own[part].at[step], own_sem.at[step, part]
        )

    def remote(stage, part, step, source, target, to):
        return pltpu.make_async_remote_copy(
            source,
            target,
            send_sem.at[stage, step, part],
            recv_sem.at[stage, step, part],
            device_id=to,
            device_id_type=MESH,
        )

    def hop(stage, part, step):
        crosses_y = parts[part][3] == 1
        if stage == 0:
            return remote(
                0,
                part,
                step,
                part_of(part, step, 1 - core),
                core_in[part].at[step],
                sibling,
            )
        if stage == 1:
            source = (
                core_in[part].at[step, 1 - y]
                if crosses_y
                else core_in[part].at[step, :, 1 - x]
            )
            to = y_side if crosses_y else x_side
            return remote(1, part, step, source, first_in[part].at[step], to)
        if stage == 2:
            source = first_in[part].at[step, 1 - x if crosses_y else 1 - y]
            to = x_side if crosses_y else y_side
            return remote(2, part, step, source, second_in[part].at[step], to)
        to = device(y, x, line[step], core)
        return remote(
            3, part, step, second_in[part].at[step], line_in[part].at[step], to
        )

    def add(target, other, rows):
        @pl.loop(0, rows // 16)
        def _(r):
            here = pl.ds(pl.multiple_of(r * 16, 16), 16)
            target[here] = (
                target[here].astype(F32) + other[here].astype(F32)
            ).astype(BF16)

    def settle(stage, part, step):
        rows = parts[part][2]
        crosses_y = parts[part][3] == 1
        hop(stage, part, step).wait_recv()
        if stage == 0:
            local(part, step).wait()
            for far_y in (0, 1):
                for far_x in (0, 1):
                    add(
                        core_in[part].at[step, far_y, far_x],
                        own[part].at[step, far_y, far_x],
                        rows,
                    )
        elif stage == 1:
            for far in (0, 1):
                kept = (
                    core_in[part].at[step, y, far]
                    if crosses_y
                    else core_in[part].at[step, far, x]
                )
                add(first_in[part].at[step, far], kept, rows)
        elif stage == 2:
            add(
                second_in[part].at[step],
                first_in[part].at[step, x if crosses_y else y],
                rows,
            )

    everything = range(pieces)
    for step in range(depth):
        for part in everything:
            hop(0, part, step).start()
            local(part, step).start()
    for turn in range(depth + 2):
        for stage in range(3):
            step = turn - stage
            if 0 <= step < depth:
                for part in everything:
                    settle(stage, part, step)
                    if stage < 2 or step < depth - 1:
                        hop(stage + 1, part, step).start()
    for step in range(depth - 1):
        for part in everything:
            hop(3, part, step).wait_recv()
    for part in everything:
        array, first, rows, _ = parts[part]

        @pl.loop(0, rows // 16)
        def _(r):
            here = pl.ds(pl.multiple_of(r * 16, 16), 16)
            total = second_in[part][depth - 1, here].astype(F32)
            for step in range(depth - 1):
                total = total + line_in[part][step, here].astype(F32)
            there = pl.ds(pl.multiple_of(first + r * 16, 16), 16)
            outs[array][there] = total

    for step in range(depth):
        for part in everything:
            for stage in range(4):
                if stage < 3 or step < depth - 1:
                    hop(stage, part, step).wait_send()


def reduce_call(depth, whole):
    count = 8 * depth
    sizes = [array.shape[0] // count for array in whole]
    widths = [array.shape[1] for array in whole]
    parts = parts_of(*sizes)
    shaped = [
        array.reshape(2, 2, depth, 2, size, wide)
        for array, size, wide in zip(whole, sizes, widths)
    ]

    def buffers(lead):
        return [
            pltpu.VMEM(lead + (rows, widths[array]), BF16)
            for array, _, rows, _ in parts
        ]

    dma = pltpu.SemaphoreType.DMA
    return pl.pallas_call(
        functools.partial(reduce_kernel, depth, parts),
        out_shape=tuple(
            jax.ShapeDtypeStruct((size, wide), F32) for size, wide in zip(sizes, widths)
        ),
        in_specs=in_any(3),
        out_specs=tuple(in_vmem(3)),
        scratch_shapes=buffers((depth, 2, 2))
        + buffers((depth, 2, 2))
        + buffers((depth, 2))
        + buffers((depth,))
        + buffers((depth,))
        + [
            dma((depth, len(parts))),
            dma((4, depth, len(parts))),
            dma((4, depth, len(parts))),
        ],
        compiler_params=pltpu.CompilerParams(
            collective_id=3, has_side_effects=True, vmem_limit_bytes=VMEM_BYTES
        ),
        name="reduce_gradients",
    )(*shaped)


def round_up(value, step):
    return -(-value // step) * step


def on_device(
    mesh,
    hidden_in,
    cotangent,
    norm_gain,
    in_weight,
    conv_weight,
    conv_bias,
    x_weight,
    dt_weight,
    dt_bias,
    a_log,
    skip_gain,
    out_weight,
):
    layers = norm_gain.shape[0]
    rows, width = hidden_in.shape
    taps, channels = conv_weight.shape[1:]
    states = a_log.shape[2]
    rank = dt_weight.shape[1]
    small = rank + 2 * states
    devices, count = mesh.shape["ctx"] * mesh.shape["seq"], mesh.shape["seq"]
    inner = channels * devices
    gains = norm_gain.shape[1]
    at = Names(states, taps)
    cfg = (rows, inner, states, taps, rank, count)
    per_channel = small + rank + at.count
    packed = per_channel * channels + gains
    small_rows = round_up(packed, 16 * 1024) // 1024
    depth = count // 2
    by_kernel = (
        mesh.shape["ctx"] == 4
        and count % 2 == 0
        and in_weight.shape[2] % 64 == 0
        and out_weight.shape[2] % 16 == 0
    )

    def pack(layer):
        by_row = jnp.concatenate(
            [
                x_weight[layer].T,
                dt_weight[layer],
                a_log[layer].T,
                conv_weight[layer],
                conv_bias[layer][None],
                dt_bias[layer][None],
                skip_gain[layer][None],
            ],
            0,
        )
        flat = jnp.concatenate([by_row.reshape(-1), norm_gain[layer]])
        flat = jnp.pad(flat, (0, small_rows * 1024 - packed))
        return flat.reshape(small_rows, 1024)

    local = [
        (in_weight[layer].T, out_weight[layer].T, pack(layer))
        for layer in range(layers)
    ]
    if by_kernel:
        gathered = gather_call(depth, local)
    else:
        gathered = [
            [lax.all_gather(array, ("ctx", "seq"), axis=0, tiled=True) for array in layer]
            for layer in local
        ]

    weights = []
    for win, wout, pack_all in gathered:
        flat = pack_all.reshape(devices, small_rows * 1024)
        by_row = flat[:, : per_channel * channels].reshape(
            devices, per_channel, channels
        )
        by_row = by_row.transpose(1, 0, 2).reshape(per_channel, inner)
        gain = flat[:, per_channel * channels : packed].reshape(1, width).astype(F32)
        xw = by_row[:small]
        dtw = jnp.pad(by_row[small : small + rank], ((0, small - rank), (0, 0)))
        vec = by_row[small + rank :].astype(F32)
        vec = jnp.concatenate([-jnp.exp(vec[:states]), vec[states:]], 0)
        vec = jnp.pad(vec, ((0, at.padded - at.count), (0, 0)))
        weights.append((gain, win, xw, dtw, vec, wout))

    stream = hidden_in.astype(F32)
    streams, saved = [], []
    for layer in range(layers):
        streams.append(stream)
        stream, *kept = forward_call(cfg, stream, *weights[layer])
        saved.append(kept)
    stream_grad = cotangent.astype(F32)
    grads = [None] * layers
    for layer in reversed(range(layers)):
        stream_grad, g_in, g_out, g_x, g_dt, g_vec, g_gain = backward_call(
            cfg, stream_grad, streams[layer], *weights[layer], saved[layer]
        )
        by_row = jnp.concatenate([g_x, g_dt[:rank], g_vec[: at.count]], 0)
        by_row = by_row.reshape(per_channel, devices, channels).transpose(1, 0, 2)
        flat = jnp.concatenate(
            [
                by_row.reshape(devices, per_channel * channels),
                g_gain[0].reshape(devices, gains),
            ],
            1,
        )
        flat = jnp.pad(flat, ((0, 0), (0, small_rows * 1024 - packed)))
        g_small = flat.astype(BF16).reshape(devices * small_rows, 1024)
        if by_kernel:
            summed = reduce_call(depth, (g_in, g_out, g_small))
        else:
            summed = [
                lax.psum_scatter(
                    array.astype(F32), ("ctx", "seq"), scatter_dimension=0, tiled=True
                )
                for array in (g_in, g_out, g_small)
            ]
        s_in, s_out, s_small = summed
        flat = s_small.reshape(-1)
        by_row = flat[: per_channel * channels].reshape(per_channel, channels)
        s_x, s_dt, s_vec = (
            by_row[:small],
            by_row[small : small + rank],
            by_row[small + rank :],
        )
        grads[layer] = (
            flat[per_channel * channels : packed],
            s_in.T,
            s_vec[at.conv : at.conv + taps],
            s_vec[at.conv_b],
            s_x.T,
            s_dt,
            s_vec[at.dt_b],
            s_vec[:states].T,
            s_vec[at.skip],
            s_out.T,
        )
    stacked = tuple(
        jnp.stack([grads[layer][member] for layer in range(layers)], 0)
        for member in range(10)
    )
    return (stream.astype(BF16), stream_grad) + stacked


def solution(mesh):
    split = ("ctx", "seq")
    tokens, last = P(split, None), P(None, split)
    middle, third = P(None, split, None), P(None, None, split)
    weights = (last, third, third, last, middle, third, last, middle, last, third)
    return jax.shard_map(
        functools.partial(on_device, mesh),
        mesh=mesh,
        in_specs=(tokens, tokens) + weights,
        out_specs=(tokens, tokens) + weights,
        check_vma=False,
    )
```

```python
import collections
import functools
import types

import jax
import jax.numpy as jnp
from jax import lax
from jax.experimental import pallas as pl
from jax.experimental.pallas import tpu as pltpu
from jax.sharding import PartitionSpec as P

EPS = 1e-05
LOG2E = 1.4426950408889634
MESH = pl.DeviceIdType.MESH
F32, BF16 = jnp.float32, jnp.bfloat16
NT = (((1,), (1,)), ((), ()))
TN = (((0,), (0,)), ((), ()))
VMEM_BYTES = 63 * 2**20
CHUNK = 16
GROUP = 512
HALO = 16


def dot(a, b, dims=None):
    if dims is None:
        dims = (((1,), (0,)), ((), ()))
    return lax.dot_general(a, b, dims, preferred_element_type=F32)


def lanes(index, width):
    return pl.ds(pl.multiple_of(index * width, width), width)


def widen(tile, width):
    times = width // tile.shape[1]
    return jnp.concatenate([tile] * times, axis=1) if times > 1 else tile


def softplus(v):
    return jnp.maximum(v, 0.0) + jnp.log1p(jnp.exp(-jnp.abs(v)))


def sigmoid(v):
    return 1.0 / (1.0 + jnp.exp(-v))


def keep_sum(own_sum, i, step):
    total = jnp.sum(step, axis=0, keepdims=True)
    fold = own_sum.shape[1]
    for part in range(GROUP // fold):
        row = i * (GROUP // fold) + part
        own_sum[pl.ds(row, 1), :] = total[:, part * fold : (part + 1) * fold]


def sum_of(sum_s, j, g):
    fold = sum_s.shape[2]
    each = GROUP // fold
    return jnp.concatenate(
        [sum_s[j, pl.ds(g * each + part, 1), :] for part in range(each)], 1
    )


def chunk_mask(rows, states):
    wide = CHUNK * states
    token = lax.rem(lax.broadcasted_iota(jnp.int32, (rows, wide), 0), CHUNK)
    owner = lax.broadcasted_iota(jnp.int32, (rows, wide), 1) // states
    return token == owner


def spread(small_low, first, states):
    wide = CHUNK * states
    row = lax.broadcasted_iota(jnp.int32, (small_low.shape[1], wide), 0)
    col = lax.broadcasted_iota(jnp.int32, (small_low.shape[1], wide), 1)
    pick = (row == first + lax.rem(col, states)).astype(F32).astype(BF16)
    tiled = dot(small_low, pick)
    return jnp.where(chunk_mask(small_low.shape[0], states), tiled, 0.0).astype(BF16)


def gather_back(partial, first, states, width):
    wide = CHUNK * states
    row = lax.broadcasted_iota(jnp.int32, (wide, width), 0)
    col = lax.broadcasted_iota(jnp.int32, (wide, width), 1)
    pick = (col == first + lax.rem(row, states)).astype(F32).astype(BF16)
    kept = jnp.where(chunk_mask(partial.shape[0], states), partial, 0.0)
    return dot(kept.astype(BF16), pick)


class Names:
    def __init__(self, states, taps, rank):
        self.small = rank + 2 * states
        self.dt = self.small
        self.vec = self.small + rank
        self.count = self.vec + states + taps + 4
        self.rows = -(-self.count // 16) * 16
        self.conv = states
        self.conv_b = states + taps
        self.dt_b = states + taps + 1
        self.skip = states + taps + 2
        self.gain = states + taps + 3


def load_small(at, sw_ref, vec_s, dtw_s):
    states, rank = at.conv, at.vec - at.dt
    vec_s[...] = sw_ref[pl.ds(at.vec, at.rows - at.vec), :].astype(F32)
    vec_s[pl.ds(0, states), :] = -jnp.exp(vec_s[pl.ds(0, states), :])
    dtw_s[pl.ds(0, rank), :] = sw_ref[pl.ds(at.dt, rank), :]
    dtw_s[pl.ds(rank, at.small - rank), :] = jnp.zeros(
        (at.small - rank, dtw_s.shape[1]), BF16
    )


def gain_pick(channels):
    gains = channels // 2
    row = lax.broadcasted_iota(jnp.int32, (256, 128), 0)
    col = lax.broadcasted_iota(jnp.int32, (256, 128), 1)
    place = lax.div(col, gains) * channels + lax.rem(col, gains)
    return (row == place).astype(F32).astype(BF16)


def gain_row(at, channels, vec_s):
    pick = gain_pick(channels)
    row = vec_s[pl.ds(at.gain // 8 * 8, 8), :].astype(BF16)
    tiles = [
        dot(row[:, 256 * i : 256 * i + 256], pick) for i in range(row.shape[1] // 256)
    ]
    gain = jnp.concatenate(tiles, 1)
    return gain[at.gain % 8 : at.gain % 8 + 1]


def merge_small(channels, blocks, sw_ref):
    each = 128 // channels
    rows = blocks.shape[1]
    owner = lax.div(lax.broadcasted_iota(jnp.int32, (rows, 128), 1), channels)

    @pl.loop(0, sw_ref.shape[1] // 128)
    def _(j):
        held = [blocks[j * each + part].astype(F32) for part in range(each)]
        for fold in range(each):
            tile = None
            for part in range(each):
                shift = (part - fold) * channels % 128
                moved = pltpu.roll(held[part], shift, 1) if shift else held[part]
                tile = moved if tile is None else jnp.where(owner == part, moved, tile)
            sw_ref[pl.ds(fold * rows, rows), lanes(j, 128)] = tile.astype(BF16)


def split_small(channels, full_ref, blocks):
    each = 128 // channels
    rows = blocks.shape[1]
    owner = lax.div(lax.broadcasted_iota(jnp.int32, (rows, 128), 1), channels)

    @pl.loop(0, full_ref.shape[1] // 128)
    def _(j):
        held = [
            full_ref[pl.ds(fold * rows, rows), lanes(j, 128)] for fold in range(each)
        ]
        for part in range(each):
            tile = None
            for fold in range(each):
                shift = (fold - part) * channels % 128
                moved = pltpu.roll(held[fold], shift, 1) if shift else held[fold]
                tile = moved if tile is None else jnp.where(owner == fold, moved, tile)
            blocks[j * each + part] = tile.astype(BF16)


def places():
    ctx, seq = lax.axis_index("ctx"), lax.axis_index("seq")
    return lax.div(ctx, 2), lax.rem(ctx, 2), lax.div(seq, 2), lax.rem(seq, 2)


def device(y, x, z, core):
    return (2 * y + x, 2 * z + core)


def square_partners(depth):
    y, x, z, core = places()
    partners = [device(y, x, z, 1 - core), device(y, 1 - x, z, core)]
    partners.append(device(1 - y, x, z, core))
    for step in range(1, depth):
        partners.append(device(y, x, lax.rem(z + step, depth), core))
    return partners


def greet_square(depth):
    barrier = pltpu.get_barrier_semaphore()
    partners = square_partners(depth)
    for partner in partners:
        pl.semaphore_signal(barrier, inc=1, device_id=partner, device_id_type=MESH)
    pl.semaphore_wait(barrier, len(partners))


class Gather:
    def __init__(self, depth, pieces, own_sem, send_sem, recv_sem):
        self.depth, self.pieces = depth, pieces
        self.own_sem, self.send_sem, self.recv_sem = own_sem, send_sem, recv_sem
        self.y, self.x, self.z, self.core = places()
        self.used = [0] * len(pieces)
        self.sent = []
        turn = 1 - 2 * lax.div(self.z, max(depth // 2, 1))
        self.line = [
            lax.rem(self.z + turn * step + depth, depth) for step in range(depth)
        ]
        y, x, z, core = self.y, self.x, self.z, self.core
        self.x_side, self.y_side = device(y, 1 - x, z, core), device(1 - y, x, z, core)
        self.sibling = device(y, x, z, 1 - core)

    @staticmethod
    def sends(depth):
        return 3 + depth - 1 + 3 * (depth - 1) + 2 * depth + 2 * depth

    def slot(self, y, x, z, core):
        return ((2 * y + x) * self.depth + z) * 2 + core

    def span(self, item, slot):
        _, whole, first, rows, _ = self.pieces[item]
        return whole.at[slot, pl.ds(first, rows)]

    def send(self, item, slot, to, own=False):
        local, _, first, rows, _ = self.pieces[item]
        copy = pltpu.make_async_remote_copy(
            local.at[pl.ds(first, rows)] if own else self.span(item, slot),
            self.span(item, slot),
            self.send_sem.at[item, self.used[item]],
            self.recv_sem.at[item, slot],
            device_id=to,
            device_id_type=MESH,
        )
        self.used[item] += 1
        copy.start()
        self.sent.append(copy)

    def arrive(self, item, slot):
        pltpu.make_async_remote_copy(
            self.span(item, slot),
            self.span(item, slot),
            self.send_sem.at[item, 0],
            self.recv_sem.at[item, slot],
            device_id=self.sibling,
            device_id_type=MESH,
        ).wait_recv()

    def own_copy(self, item):
        local, _, first, rows, _ = self.pieces[item]
        mine = self.slot(self.y, self.x, self.z, self.core)
        return pltpu.make_async_copy(
            local.at[pl.ds(first, rows)], self.span(item, mine), self.own_sem.at[item]
        )

    def begin(self, item):
        mine = self.slot(self.y, self.x, self.z, self.core)
        self.own_copy(item).start()
        for to in (self.x_side, self.y_side):
            self.send(item, mine, to, own=True)
        for step in range(1, self.depth):
            to = device(self.y, self.x, self.line[step], self.core)
            self.send(item, mine, to, own=True)
        self.send(item, mine, self.sibling, own=True)

    def along(self, item, step):
        slot = self.slot(self.y, self.x, self.line[step], self.core)
        self.arrive(item, slot)
        for to in (self.x_side, self.y_side, self.sibling):
            self.send(item, slot, to)

    def near(self, item, step):
        if self.pieces[item][4]:
            slot = self.slot(self.y, 1 - self.x, self.line[step], self.core)
            to = self.y_side
        else:
            slot = self.slot(1 - self.y, self.x, self.line[step], self.core)
            to = self.x_side
        self.arrive(item, slot)
        self.send(item, slot, to)
        self.send(item, slot, self.sibling)

    def far(self, item, step, other):
        y, x = 1 - self.y, 1 - self.x
        if self.pieces[item][4]:
            x = x if other else self.x
        else:
            y = y if other else self.y
        slot = self.slot(y, x, self.line[step], self.core)
        self.arrive(item, slot)
        self.send(item, slot, self.sibling)

    def settle(self, item):
        self.own_copy(item).wait()
        for step in range(self.depth):
            for y in (self.y, 1 - self.y):
                for x in (self.x, 1 - self.x):
                    self.arrive(item, self.slot(y, x, self.line[step], 1 - self.core))

    def turns(self, items):
        order = [("near", 0)]
        for step in range(1, self.depth):
            order.append(("along", step))
            order.append(("near", step))
            if step >= 2:
                order.append(("far", step - 2, 1))
            order.append(("far", step - 1, 0))
        for step in range(max(self.depth - 2, 0), self.depth):
            if step == self.depth - 1:
                order.append(("far", step, 0))
            order.append(("far", step, 1))
        actions = []
        for name, *rest in order:
            for item in items:
                actions.append(functools.partial(getattr(self, name), item, *rest))
        return actions

    def finish(self):
        for copy in self.sent:
            copy.wait_send()


def chain(count, me, ctx, own_sum, sum_s, own_end, end_s, sems):
    sum_send, sum_recv, end_send, end_recv = sems

    def sums(j, slot):
        return pltpu.make_async_remote_copy(
            own_sum,
            sum_s.at[slot],
            sum_send.at[j],
            sum_recv.at[slot],
            device_id=(ctx, j),
            device_id_type=MESH,
        )

    def ends(g, j, slot):
        return pltpu.make_async_remote_copy(
            own_end.at[:, pl.ds(g * GROUP, GROUP)],
            end_s.at[slot, :, pl.ds(g * GROUP, GROUP)],
            end_send.at[g, j],
            end_recv.at[g, slot],
            device_id=(ctx, j),
            device_id_type=MESH,
        )

    return sums, ends


def each(first, last, act):
    def body(j, _):
        act(j)
        return 0

    lax.fori_loop(first, last, body, 0)


def forward_kernel(cfg, mode, names, *refs):
    r = types.SimpleNamespace(**dict(zip(names, refs)))
    rows, inner, states, taps, rank, count, channels = cfg
    at = Names(states, taps, rank)
    ctx, me = lax.axis_index("ctx"), lax.axis_index("seq")
    groups, steps, tiles = inner // GROUP, rows // CHUNK, inner // GROUP
    depth = count // 2
    width = r.stream.shape[1]
    barrier = pltpu.get_barrier_semaphore()

    def greet(to):
        pl.semaphore_signal(barrier, inc=1, device_id=to, device_id_type=MESH)

    queue = collections.deque()

    def weave(times):
        for _ in range(min(times, len(queue))):
            queue.popleft()()

    if mode == "given":
        each(0, me, lambda j: greet((ctx, j)))
    else:
        each(0, me, lambda j: greet((ctx, j)))
        each(me + 1, count, lambda j: greet((ctx, j)))
        y, x, z, core = places()
        greet(device(y, 1 - x, z, core))
        greet(device(1 - y, x, z, core))

    if mode != "first":
        half = r.win_hbm.shape[0] // 2
        halves = [
            pltpu.make_async_copy(
                r.win_hbm.at[pl.ds(k * half, half)],
                r.win_s.at[pl.ds(k * half, half)],
                r.load_sem.at[k],
            )
            for k in range(2)
        ]
        if mode == "later":
            small_copy = pltpu.make_async_copy(r.gsm_hbm, r.gsm_s, r.load_sem.at[2])
            small_copy.start()
        for copy in halves:
            copy.start()
    if mode == "given":
        out_copy = pltpu.make_async_copy(r.wout_hbm, r.wout_s, r.load_sem.at[2])
        out_copy.start()

    stream = r.stream[...]
    scale = lax.rsqrt(jnp.mean(stream * stream, axis=1, keepdims=True) + EPS)
    stores = []

    if mode == "given":

        @pl.when(me < count - 1)
        def _():
            pl.semaphore_wait(barrier, count - 1 - me)

    else:
        pl.semaphore_wait(barrier, count + 1)
        pieces = []

        def add_piece(local, whole, cuts):
            start = len(pieces)
            total = local.shape[0]
            for k, last_y in enumerate(cuts):
                piece = total // len(cuts)
                pieces.append((local, whole, k * piece, piece, last_y))
            return list(range(start, len(pieces)))

        first_items, next_items = [], []
        if mode == "first":
            first_items = add_piece(r.own_in, r.win_s, (1, 0))
            first_items += add_piece(r.own_small, r.gsm_s, (1,))
        out_items = add_piece(r.own_out, r.wout_s, (1, 0))
        if mode == "first":
            next_items = add_piece(r.next_in, r.win2_all, (1, 0))
            next_items += add_piece(r.next_small, r.gsm2_all, (0,))
        gather = Gather(depth, pieces, r.own_sem, r.send_sem, r.recv_sem)

        def begin(items):
            for item in items:
                gather.begin(item)

        def settle(items):
            for item in items:
                gather.settle(item)

        def keep(source, target, slot):
            copy = pltpu.make_async_copy(source, target, r.store_sem.at[slot])
            copy.start()
            stores.append(copy)

        if mode == "first":
            begin(first_items)
            turns = gather.turns(first_items)
            for k, turn in enumerate(turns):
                if k == len(turns) // 2:
                    begin(out_items + next_items)
                turn()
            settle(first_items)
            keep(r.win_s, r.win_all, 1)
            turns = gather.turns(out_items)
            queue.extend(gather.turns(out_items + next_items))
        else:
            begin(out_items)
            queue.extend(gather.turns(out_items))
        queue.append(lambda: settle(out_items))
        queue.append(lambda: keep(r.wout_s, r.wout_all, 0))
        if mode == "first":
            queue.append(lambda: settle(next_items))
        if mode == "later":
            small_copy.wait()
        merge_small(channels, r.gsm_s, r.sw)
    pace = -(-len(queue) // 21)

    load_small(at, r.sw, r.vec_s, r.dtw_s)
    r.normed_s[...] = (stream * scale * gain_row(at, channels, r.vec_s)).astype(BF16)
    per_tile = GROUP // r.win_s.shape[1]

    def win_tile(i):
        return r.win_s[pl.ds(i * per_tile, per_tile)].reshape(GROUP, width)

    if mode != "first":
        halves[0].wait()

    @pl.loop(0, tiles)
    def _(i):
        low = dot(r.normed_s[...], win_tile(i), NT).astype(BF16)
        r.pad[pl.ds(HALO, rows), lanes(i, GROUP)] = low
        r.padf_s[pl.ds(HALO, rows), lanes(i, GROUP)] = low.astype(F32)

    def edge():
        return pltpu.make_async_remote_copy(
            r.pad.at[pl.ds(rows, HALO)],
            r.halo_s,
            r.halo_sem.at[0],
            r.halo_sem.at[1],
            device_id=(ctx, jnp.minimum(me + 1, count - 1)),
            device_id_type=MESH,
        )

    @pl.when(me < count - 1)
    def _():
        edge().start()

    weave(pace)
    if mode != "first":
        halves[1].wait()

    @pl.loop(0, tiles)
    def _(i):
        r.gate[:, lanes(i, GROUP)] = dot(r.normed_s[...], win_tile(i + tiles), NT)

    weave(pace)

    @pl.when(me > 0)
    def _():
        edge().wait_recv()

    @pl.when(me == 0)
    def _():
        r.halo_s[...] = jnp.zeros_like(r.halo_s)

    r.pad[pl.ds(0, HALO), :] = r.halo_s[...]
    r.padf_s[pl.ds(0, HALO), :] = r.halo_s[...].astype(F32)

    @pl.loop(0, tiles)
    def _(i):
        here = lanes(i, GROUP)
        total = r.vec_s[pl.ds(at.conv_b, 1), here]
        for k in range(taps):
            total = (
                total
                + r.vec_s[pl.ds(at.conv + k, 1), here]
                * r.padf_s[pl.ds(HALO - taps + 1 + k, rows), here]
            )
        r.act[:, here] = (total * sigmoid(total)).astype(BF16)

    weave(pace)
    small = dot(r.act[...], r.sw[pl.ds(0, at.small), :], NT)
    r.sp[...] = small
    small_low = small.astype(BF16)

    @pl.loop(0, tiles)
    def _(i):
        here = lanes(i, GROUP)
        before = dot(small_low, r.dtw_s[:, here]) + r.vec_s[pl.ds(at.dt_b, 1), here]
        step = softplus(before)
        r.pre[:, here] = before
        r.dt_s[:, here] = step
        r.dx_s[:, here] = step * r.act[:, here].astype(F32)
        keep_sum(r.own_sum, i, step)

    sums, ends = chain(
        count, me, ctx, r.own_sum, r.sum_s, r.own_end, r.end_s,
        (r.sum_send, r.sum_recv, r.end_send, r.end_recv),
    )
    each(me + 1, count, lambda j: sums(j, me).start())
    weave(pace)
    for n in range(states):
        r.bb_s[:, n, :] = jnp.broadcast_to(
            small[:, rank + n : rank + n + 1], (rows, 128)
        )
    r.cd_s[...] = spread(small_low, rank + states, states)

    def advance(t, state, rate2, here):
        return (
            jnp.exp2(r.dt_s[pl.ds(t, 1), here] * rate2) * state
            + r.dx_s[pl.ds(t, 1), here] * widen(r.bb_s[t], GROUP)
        )

    for g in range(groups):
        here = pl.ds(g * GROUP, GROUP)
        rate2 = r.vec_s[pl.ds(0, states), here] * LOG2E

        def first_pass(step, state):
            for i in range(CHUNK):
                state = advance(step * CHUNK + i, state, rate2, here)
            return state

        r.own_end[:, here] = lax.fori_loop(
            0, steps, first_pass, jnp.zeros((states, GROUP), F32)
        ).astype(BF16)
        each(me + 1, count, lambda j: ends(g, j, me).start())
        weave(pace)

    def h_copy(g):
        here = pl.ds(g * GROUP, GROUP)
        return pltpu.make_async_copy(
            r.hs.at[:, here], r.h_hbm.at[:, here], r.h_sem.at[g]
        )

    for g in range(groups):
        here = pl.ds(g * GROUP, GROUP)
        rate2 = r.vec_s[pl.ds(0, states), here] * LOG2E

        def carry(j, state):
            if g == 0:
                sums(j, j).wait_recv()
            ends(g, j, j).wait_recv()
            return (
                jnp.exp2(rate2 * sum_of(r.sum_s, j, g)) * state
                + r.end_s[j, :, here].astype(F32)
            )

        state = lax.fori_loop(0, me, carry, jnp.zeros((states, GROUP), F32))
        r.hs[pl.ds(0, states), here] = state.astype(BF16)

        def second_pass(step, state):
            base = pl.multiple_of(step * CHUNK * states + states, states)
            for i in range(CHUNK):
                state = advance(step * CHUNK + i, state, rate2, here)
                r.hs[pl.ds(base + i * states, states), here] = state.astype(BF16)
            tokens = pl.ds(pl.multiple_of(step * CHUNK, CHUNK), CHUNK)
            r.y[tokens, here] = dot(
                r.cd_s[tokens, :], r.hs[pl.ds(base, CHUNK * states), here]
            )
            return state

        thirds = 1 if mode == "given" else 3
        for part in range(thirds):
            state = lax.fori_loop(
                steps * part // thirds,
                steps * (part + 1) // thirds,
                second_pass,
                state,
            )
            weave(pace)
        h_copy(g).start()
        y_value = (
            r.y[:, here]
            + r.vec_s[pl.ds(at.skip, 1), here] * r.act[:, here].astype(F32)
        )
        gate = r.gate[:, here]
        r.y[:, here] = y_value
        r.mixed[:, here] = (y_value * gate * sigmoid(gate)).astype(BF16)

    if mode == "given":
        out_copy.wait()
    else:
        while queue and not stores_hold_out(mode, stores):
            weave(1)
    out_tile = 256 // r.wout_s.shape[1]
    for i in range(width // 256):
        here = pl.ds(i * 256, 256)
        wout = r.wout_s[pl.ds(i * out_tile, out_tile)].reshape(256, inner)
        r.new[:, here] = r.stream[:, here] + dot(r.mixed[...], wout, NT)

    weave(len(queue))
    if mode != "given":
        gather.finish()

    @pl.when(me < count - 1)
    def _():
        edge().wait_send()

    each(me + 1, count, lambda j: sums(j, me).wait_send())
    for g in range(groups):
        each(me + 1, count, lambda j: ends(g, j, me).wait_send())
        h_copy(g).wait()
    for copy in stores:
        copy.wait()


def stores_hold_out(mode, stores):
    return len(stores) == (2 if mode == "first" else 1)


def backward_kernel(
    cfg,
    sgrad_ref,
    stream_ref,
    sw_ref,
    win_ref,
    wout_ref,
    pad_ref,
    gate_ref,
    act_ref,
    sp_ref,
    pre_ref,
    h_hbm,
    y_ref,
    mixed_ref,
    nsg_ref,
    gin_hbm,
    gout_hbm,
    gsmall_ref,
    full_s,
    vec_ref,
    dtw_ref,
    hb,
    normed_s,
    low_s,
    sg_s,
    dt_s,
    dx_s,
    stepg_s,
    pb_s,
    cb_s,
    bd_s,
    ab_s,
    rb_s,
    pin_s,
    pout_s,
    prelow_s,
    stage_in,
    stage_out,
    halo_s,
    own_sum,
    sum_s,
    own_end,
    end_s,
    halo_sem,
    sum_send,
    sum_recv,
    end_send,
    end_recv,
    h_sem,
    in_sem,
    out_sem,
):
    rows, inner, states, taps, rank, count, channels = cfg
    at = Names(states, taps, rank)
    ctx, me = lax.axis_index("ctx"), lax.axis_index("seq")
    groups, steps = inner // GROUP, rows // CHUNK
    width = stream_ref.shape[1]
    barrier = pltpu.get_barrier_semaphore()
    gvec_ref = full_s.at[pl.ds(at.vec, at.rows - at.vec)]

    each(
        me + 1,
        count,
        lambda j: pl.semaphore_signal(
            barrier, inc=1, device_id=(ctx, j), device_id_type=MESH
        ),
    )

    def states_in(g):
        return pltpu.make_async_copy(
            h_hbm.at[:, pl.ds(g * GROUP, GROUP)], hb.at[g % 2], h_sem.at[g % 2]
        )

    states_in(0).start()
    load_small(at, sw_ref, vec_ref, dtw_ref)
    gain = gain_row(at, channels, vec_ref)
    low_s[...] = sgrad_ref[...].astype(BF16)
    stream = stream_ref[...]
    scale = lax.rsqrt(jnp.mean(stream * stream, axis=1, keepdims=True) + EPS)
    normed_s[...] = (stream * scale * gain).astype(BF16)
    small_low = sp_ref[...].astype(BF16)

    @pl.loop(0, inner // GROUP)
    def _(i):
        here = lanes(i, GROUP)
        mixed_grad = dot(low_s[...], wout_ref[:, here])
        gate = gate_ref[:, here]
        sig = sigmoid(gate)
        act = act_ref[:, here].astype(F32)
        scan_grad = mixed_grad * gate * sig
        sg_s[:, here] = scan_grad
        pb_s[:, lanes(i + inner // GROUP, GROUP)] = (
            mixed_grad * y_ref[:, here] * sig * (1.0 + gate * (1.0 - sig))
        ).astype(BF16)
        gvec_ref[pl.ds(at.skip, 1), here] = jnp.sum(
            scan_grad * act, axis=0, keepdims=True
        )
        step = softplus(pre_ref[:, here])
        dt_s[:, here] = step
        dx_s[pl.ds(0, rows), here] = step * act
        keep_sum(own_sum, i, step)

    sums, ends = chain(
        count, me, ctx, own_sum, sum_s, own_end, end_s,
        (sum_send, sum_recv, end_send, end_recv),
    )

    @pl.when(me > 0)
    def _():
        pl.semaphore_wait(barrier, me)

    each(0, me, lambda j: sums(j, me).start())
    for n in range(states):
        first = rank + states + n
        cb_s[:, n, :] = jnp.broadcast_to(
            sp_ref[:, first : first + 1], (rows, 128)
        )
    bd_s[...] = spread(small_low, rank, states)
    ones = jnp.where(chunk_mask(CHUNK, states), 1.0, 0.0).astype(BF16)

    for g in range(groups):
        here = pl.ds(g * GROUP, GROUP)
        rate2 = vec_ref[pl.ds(0, states), here] * LOG2E

        def first_pass(k, state):
            step = steps - 1 - k
            for i in reversed(range(CHUNK)):
                t = step * CHUNK + i
                state = jnp.exp2(dt_s[pl.ds(t, 1), here] * rate2) * (
                    state + sg_s[pl.ds(t, 1), here] * widen(cb_s[t], GROUP)
                )
            return state

        own_end[:, here] = lax.fori_loop(
            0, steps, first_pass, jnp.zeros((states, GROUP), F32)
        ).astype(BF16)
        each(0, me, lambda j: ends(g, j, me).start())

    for g in range(groups):
        here = pl.ds(g * GROUP, GROUP)
        rate = vec_ref[pl.ds(0, states), here]
        rate2 = rate * LOG2E
        if g + 1 < groups:
            states_in(g + 1).start()

        def carry(k, state):
            j = count - 1 - k
            if g == 0:
                sums(j, j).wait_recv()
            ends(g, j, j).wait_recv()
            return (
                jnp.exp2(rate2 * sum_of(sum_s, j, g)) * state
                + end_s[j, :, here].astype(F32)
            )

        begin = lax.fori_loop(
            0, count - 1 - me, carry, jnp.zeros((states, GROUP), F32)
        )
        states_in(g).wait()

        def second_pass(k, both):
            state, total = both
            step = steps - 1 - k
            base = pl.multiple_of(step * CHUNK * states, states)
            for i in reversed(range(CHUNK)):
                t = step * CHUNK + i
                dt = dt_s[pl.ds(t, 1), here]
                adjoint = state + sg_s[pl.ds(t, 1), here] * widen(cb_s[t], GROUP)
                state = jnp.exp2(dt * rate2) * adjoint
                held = hb[g % 2, pl.ds(base + i * states, states), :].astype(F32)
                rated = state * held * rate
                total = total + dt * rated
                ab_s[pl.ds(i * states, states), :] = adjoint.astype(BF16)
                rb_s[pl.ds(i * states, states), :] = rated.astype(BF16)
            tokens = pl.ds(pl.multiple_of(step * CHUNK, CHUNK), CHUNK)
            from_in = dot(bd_s[tokens, :], ab_s[...])
            from_rate = dot(ones, rb_s[...])
            scan_grad = sg_s[tokens, here]
            into_in = dot(dx_s[tokens, here].astype(BF16), ab_s[...], NT)
            into_out = dot(
                scan_grad.astype(BF16),
                hb[g % 2, pl.ds(base + states, CHUNK * states), :],
                NT,
            )
            if g == 0:
                pin_s[tokens, :] = into_in
                pout_s[tokens, :] = into_out
            else:
                pin_s[tokens, :] += into_in
                pout_s[tokens, :] += into_out
            stepg_s[tokens, here] = (
                act_ref[tokens, here].astype(F32) * from_in + from_rate
            )
            sg_s[tokens, here] = (
                dt_s[tokens, here] * from_in
                + vec_ref[pl.ds(at.skip, 1), here] * scan_grad
            )
            return state, total

        _, total = lax.fori_loop(
            0, steps, second_pass, (begin, jnp.zeros((states, GROUP), F32))
        )
        gvec_ref[pl.ds(0, states), here] = total

    @pl.loop(0, inner // GROUP)
    def _(i):
        here = lanes(i, GROUP)
        pre_grad = stepg_s[pl.ds(0, rows), here] * sigmoid(pre_ref[:, here])
        gvec_ref[pl.ds(at.dt_b, 1), here] = jnp.sum(pre_grad, axis=0, keepdims=True)
        prelow_s[:, here] = pre_grad.astype(BF16)
        dx_s[:, here] = pad_ref[:, here].astype(F32)

    small_grad = (
        dot(prelow_s[...], dtw_ref[...], NT)
        + gather_back(pin_s[...], rank, states, sp_ref.shape[1])
        + gather_back(pout_s[...], rank + states, states, sp_ref.shape[1])
    ).astype(BF16)

    @pl.loop(0, inner // GROUP)
    def _(i):
        here = lanes(i, GROUP)
        full_s[pl.ds(at.dt, rank), here] = dot(
            small_low, prelow_s[:, here], TN
        )[:rank]
        full_s[pl.ds(0, at.small), here] = dot(small_grad, act_ref[:, here], TN)
        act_grad = sg_s[:, here] + dot(
            small_grad, sw_ref[pl.ds(0, at.small), here]
        )
        total = vec_ref[pl.ds(at.conv_b, 1), here]
        for k in range(taps):
            total = (
                total
                + vec_ref[pl.ds(at.conv + k, 1), here]
                * dx_s[pl.ds(HALO - taps + 1 + k, rows), here]
            )
        sig = sigmoid(total)
        conv_grad = act_grad * sig * (1.0 + total * (1.0 - sig))
        stepg_s[pl.ds(0, rows), here] = conv_grad
        gvec_ref[pl.ds(at.conv_b, 1), here] = jnp.sum(conv_grad, axis=0, keepdims=True)
        for k in range(taps):
            gvec_ref[pl.ds(at.conv + k, 1), here] = jnp.sum(
                conv_grad * dx_s[pl.ds(HALO - taps + 1 + k, rows), here],
                axis=0,
                keepdims=True,
            )

    def edge():
        return pltpu.make_async_remote_copy(
            stepg_s.at[pl.ds(0, 8)],
            halo_s,
            halo_sem.at[0],
            halo_sem.at[1],
            device_id=(ctx, jnp.maximum(me - 1, 0)),
            device_id_type=MESH,
        )

    @pl.when(me > 0)
    def _():
        edge().start()

    tiles = inner // GROUP

    def project(i, first):
        here = lanes(i, GROUP)
        slot = lax.rem(i, 2)
        copy = pltpu.make_async_copy(
            stage_in.at[slot], gin_hbm.at[here], in_sem.at[slot]
        )

        @pl.when(first >= 2)
        def _():
            copy.wait()

        stage_in[slot] = dot(pb_s[:, here], normed_s[...], TN).astype(BF16)
        copy.start()
        part = dot(pb_s[:, here], win_ref[here, :])

        @pl.when(first == 0)
        def _():
            nsg_ref[...] = part

        @pl.when(first > 0)
        def _():
            nsg_ref[...] += part

    @pl.loop(0, tiles)
    def _(i):
        project(i + tiles, i)

    out_rows = stage_out.shape[1]
    for r in range(width // out_rows):
        slot = r % 2
        copy = pltpu.make_async_copy(
            stage_out.at[slot],
            gout_hbm.at[pl.ds(r * out_rows, out_rows)],
            out_sem.at[slot],
        )
        if r >= 2:
            copy.wait()

        @pl.loop(0, tiles)
        def _(i):
            here = lanes(i, GROUP)
            stage_out[slot, :, here] = dot(
                low_s[:, pl.ds(r * out_rows, out_rows)], mixed_ref[:, here], TN
            ).astype(BF16)

        copy.start()

    @pl.when(me < count - 1)
    def _():
        edge().wait_recv()

    @pl.when(me == count - 1)
    def _():
        halo_s[...] = jnp.zeros_like(halo_s)

    @pl.when(me > 0)
    def _():
        edge().wait_send()

    stepg_s[pl.ds(rows, 8), :] = halo_s[...]

    @pl.loop(0, tiles)
    def _(i):
        here = lanes(i, GROUP)
        total = jnp.zeros((rows, GROUP), F32)
        for k in range(taps):
            total = (
                total
                + vec_ref[pl.ds(at.conv + k, 1), here]
                * stepg_s[pl.ds(taps - 1 - k, rows), here]
            )
        pb_s[:, here] = total.astype(BF16)
        project(i, i + tiles)

    stream = stream_ref[...]
    scale = lax.rsqrt(jnp.mean(stream * stream, axis=1, keepdims=True) + EPS)
    normed_grad = nsg_ref[...]
    gain_grad = jnp.sum(normed_grad * stream * scale, axis=0, keepdims=True)
    gain_grad = jnp.broadcast_to(gain_grad, (8, width)).astype(BF16)
    pick = gain_pick(channels)
    for i in range(inner // 256):
        wide = dot(gain_grad[:, 128 * i : 128 * i + 128], pick, NT)
        gvec_ref[pl.ds(at.gain, 1), pl.ds(256 * i, 256)] = wide[:1]
    for k in range(at.count, at.rows):
        full_s[pl.ds(k, 1), :] = jnp.zeros((1, inner), F32)
    if len(gsmall_ref.shape) == 3:
        split_small(channels, full_s, gsmall_ref)
    else:
        gsmall_ref[...] = full_s[...]
    scaled = normed_grad * gain
    inner_sum = jnp.mean(scaled * stream, axis=1, keepdims=True)
    nsg_ref[...] = (
        sgrad_ref[...] + scale * scaled - stream * (scale * scale * scale) * inner_sum
    )
    for slot in range(2):
        pltpu.make_async_copy(
            stage_in.at[slot], gin_hbm.at[pl.ds(0, GROUP)], in_sem.at[slot]
        ).wait()
        pltpu.make_async_copy(
            stage_out.at[slot], gout_hbm.at[pl.ds(0, out_rows)], out_sem.at[slot]
        ).wait()
    each(0, me, lambda j: sums(j, me).wait_send())
    for g in range(groups):
        each(0, me, lambda j: ends(g, j, me).wait_send())


def in_vmem(count):
    return [pl.BlockSpec(memory_space=pltpu.VMEM)] * count


def in_any(count):
    return [pl.BlockSpec(memory_space=pl.ANY)] * count


def forward_call(cfg, mode, stream, operands):
    rows, inner, states, taps, rank, count, channels = cfg
    at = Names(states, taps, rank)
    width = stream.shape[1]
    groups = inner // GROUP
    devices = inner // channels
    shape = jax.ShapeDtypeStruct
    dma = pltpu.SemaphoreType.DMA
    vmem, any_space = in_vmem(1)[0], in_any(1)[0]
    inputs = [("stream", stream, vmem)]
    for name, array in operands:
        inputs.append((name, array, vmem if name == "sw" else any_space))
    outputs = [
        ("new", shape(stream.shape, F32), vmem),
        ("pad", shape((rows + HALO, inner), BF16), vmem),
        ("gate", shape((rows, inner), F32), vmem),
        ("act", shape((rows, inner), BF16), vmem),
        ("sp", shape((rows, at.small), F32), vmem),
        ("pre", shape((rows, inner), F32), vmem),
        ("h_hbm", shape(((rows + 1) * states, inner), BF16), any_space),
        ("y", shape((rows, inner), F32), vmem),
        ("mixed", shape((rows, inner), BF16), vmem),
    ]
    if mode == "given":
        given = dict(operands)
        in_shape, out_shape = given["win_hbm"].shape, given["wout_hbm"].shape
    else:
        in_shape = (devices, 2 * inner // devices, width)
        out_shape = (devices, width // devices, inner)
        small_shape = (devices, at.rows * channels // 128, 128)
        outputs.append(("sw", shape((at.rows, inner), BF16), vmem))
        outputs.append(("wout_all", shape(out_shape, BF16), any_space))
    if mode == "first":
        outputs.append(("win_all", shape(in_shape, BF16), any_space))
        outputs.append(("win2_all", shape(in_shape, BF16), any_space))
        outputs.append(("gsm2_all", shape(small_shape, BF16), any_space))
    scratch = [
        ("win_s", pltpu.VMEM(in_shape, BF16)),
        ("wout_s", pltpu.VMEM(out_shape, BF16)),
        ("vec_s", pltpu.VMEM((at.rows - at.vec, inner), F32)),
        ("dtw_s", pltpu.VMEM((at.small, inner), BF16)),
        ("normed_s", pltpu.VMEM(stream.shape, BF16)),
        ("padf_s", pltpu.VMEM((rows + HALO, inner), F32)),
        ("halo_s", pltpu.VMEM((HALO, inner), BF16)),
        ("dt_s", pltpu.VMEM((rows, inner), F32)),
        ("dx_s", pltpu.VMEM((rows, inner), F32)),
        ("bb_s", pltpu.VMEM((rows, states, 128), F32)),
        ("cd_s", pltpu.VMEM((rows, CHUNK * states), BF16)),
        ("hs", pltpu.VMEM(((rows + 1) * states, inner), BF16)),
        ("own_sum", pltpu.VMEM((8, inner // 8), F32)),
        ("sum_s", pltpu.VMEM((count, 8, inner // 8), F32)),
        ("own_end", pltpu.VMEM((states, inner), BF16)),
        ("end_s", pltpu.VMEM((count, states, inner), BF16)),
        ("halo_sem", dma((2,))),
        ("sum_send", dma((count,))),
        ("sum_recv", dma((count,))),
        ("end_send", dma((groups, count))),
        ("end_recv", dma((groups, count))),
        ("h_sem", dma((groups,))),
        ("load_sem", dma((3,))),
    ]
    if mode != "given":
        pieces = 8 if mode == "first" else 2
        scratch += [
            ("gsm_s", pltpu.VMEM(small_shape, BF16)),
            ("own_sem", dma((pieces,))),
            ("send_sem", dma((pieces, Gather.sends(count // 2)))),
            ("recv_sem", dma((pieces, devices))),
            ("store_sem", dma((2,))),
        ]
    names = [entry[0] for entry in inputs + outputs + scratch]
    results = pl.pallas_call(
        functools.partial(forward_kernel, cfg, mode, names),
        out_shape=tuple(entry[1] for entry in outputs),
        in_specs=[entry[2] for entry in inputs],
        out_specs=tuple(entry[2] for entry in outputs),
        scratch_shapes=[entry[1] for entry in scratch],
        compiler_params=pltpu.CompilerParams(
            collective_id={"given": 0, "first": 4, "later": 5}[mode],
            has_side_effects=True,
            vmem_limit_bytes=VMEM_BYTES,
        ),
        name="forward_" + mode,
    )(*[entry[1] for entry in inputs])
    return {entry[0]: result for entry, result in zip(outputs, results)}


def backward_call(cfg, in_blocks, sgrad, stream, sw, win, wout, saved):
    rows, inner, states, taps, rank, count, channels = cfg
    at = Names(states, taps, rank)
    width = stream.shape[1]
    small = rank + 2 * states
    groups = inner // GROUP
    wide = CHUNK * states
    shape = jax.ShapeDtypeStruct
    dma = pltpu.SemaphoreType.DMA
    return pl.pallas_call(
        functools.partial(backward_kernel, cfg),
        out_shape=(
            shape((rows, width), F32),
            shape((2 * inner, width), BF16),
            shape((width, inner), BF16),
            shape((inner // channels, at.rows * channels // 128, 128), BF16)
            if in_blocks
            else shape((at.rows, inner), F32),
        ),
        in_specs=in_vmem(10) + in_any(1) + in_vmem(2),
        out_specs=tuple(in_vmem(1) + in_any(2) + in_vmem(1)),
        scratch_shapes=[
            pltpu.VMEM((at.rows, inner), F32),
            pltpu.VMEM((at.rows - at.vec, inner), F32),
            pltpu.VMEM((small, inner), BF16),
            pltpu.VMEM((2, (rows + 1) * states, GROUP), BF16),
            pltpu.VMEM((rows, width), BF16),
            pltpu.VMEM((rows, width), BF16),
            pltpu.VMEM((rows, inner), F32),
            pltpu.VMEM((rows, inner), F32),
            pltpu.VMEM((rows + HALO, inner), F32),
            pltpu.VMEM((rows + 8, inner), F32),
            pltpu.VMEM((rows, 2 * inner), BF16),
            pltpu.VMEM((rows, states, 128), F32),
            pltpu.VMEM((rows, wide), BF16),
            pltpu.VMEM((wide, GROUP), BF16),
            pltpu.VMEM((wide, GROUP), BF16),
            pltpu.VMEM((rows, wide), F32),
            pltpu.VMEM((rows, wide), F32),
            pltpu.VMEM((rows, inner), BF16),
            pltpu.VMEM((2, GROUP, width), BF16),
            pltpu.VMEM((2, width // 8, inner), BF16),
            pltpu.VMEM((8, inner), F32),
            pltpu.VMEM((8, inner // 8), F32),
            pltpu.VMEM((count, 8, inner // 8), F32),
            pltpu.VMEM((states, inner), BF16),
            pltpu.VMEM((count, states, inner), BF16),
            dma((2,)),
            dma((count,)),
            dma((count,)),
            dma((groups, count)),
            dma((groups, count)),
            dma((2,)),
            dma((2,)),
            dma((2,)),
        ],
        compiler_params=pltpu.CompilerParams(
            collective_id=1, has_side_effects=True, vmem_limit_bytes=VMEM_BYTES
        ),
        name="backward_layer",
    )(sgrad, stream, sw, win, wout, *saved)


def parts_of(in_rows, out_rows, small_rows):
    cut = in_rows * 3 // 4 // 16 * 16
    return (
        (0, 0, cut, 1),
        (2, 0, small_rows, 1),
        (0, cut, in_rows - cut, 0),
        (1, 0, out_rows, 0),
    )


def reduce_kernel(depth, parts, *refs):
    whole, outs = refs[:3], refs[3:6]
    pieces = len(parts)
    own = refs[6 : 6 + pieces]
    core_in = refs[6 + pieces : 6 + 2 * pieces]
    first_in = refs[6 + 2 * pieces : 6 + 3 * pieces]
    second_in = refs[6 + 3 * pieces : 6 + 4 * pieces]
    line_in = refs[6 + 4 * pieces : 6 + 5 * pieces]
    own_sem, send_sem, recv_sem = refs[6 + 5 * pieces :]
    y, x, z, core = places()
    greet_square(depth)
    line = [lax.rem(z + step + 1, depth) for step in range(depth)]
    x_side, y_side = device(y, 1 - x, z, core), device(1 - y, x, z, core)
    sibling = device(y, x, z, 1 - core)

    def part_of(part, step, side):
        array, first, rows, _ = parts[part]
        return whole[array].at[:, :, line[step], side, pl.ds(first, rows)]

    def local(part, step):
        return pltpu.make_async_copy(
            part_of(part, step, core), own[part].at[step], own_sem.at[step, part]
        )

    def remote(stage, part, step, source, target, to):
        return pltpu.make_async_remote_copy(
            source,
            target,
            send_sem.at[stage, step, part],
            recv_sem.at[stage, step, part],
            device_id=to,
            device_id_type=MESH,
        )

    def hop(stage, part, step):
        crosses_y = parts[part][3] == 1
        if stage == 0:
            return remote(
                0,
                part,
                step,
                part_of(part, step, 1 - core),
                core_in[part].at[step],
                sibling,
            )
        if stage == 1:
            source = (
                core_in[part].at[step, 1 - y]
                if crosses_y
                else core_in[part].at[step, :, 1 - x]
            )
            to = y_side if crosses_y else x_side
            return remote(1, part, step, source, first_in[part].at[step], to)
        if stage == 2:
            source = first_in[part].at[step, 1 - x if crosses_y else 1 - y]
            to = x_side if crosses_y else y_side
            return remote(2, part, step, source, second_in[part].at[step], to)
        to = device(y, x, line[step], core)
        return remote(
            3, part, step, second_in[part].at[step], line_in[part].at[step], to
        )

    def add(target, other, rows):
        @pl.loop(0, rows // 16)
        def _(r):
            here = pl.ds(pl.multiple_of(r * 16, 16), 16)
            target[here] = (
                target[here].astype(F32) + other[here].astype(F32)
            ).astype(BF16)

    def settle(stage, part, step):
        rows = parts[part][2]
        crosses_y = parts[part][3] == 1
        hop(stage, part, step).wait_recv()
        if stage == 0:
            local(part, step).wait()
            for far_y in (0, 1):
                for far_x in (0, 1):
                    add(
                        core_in[part].at[step, far_y, far_x],
                        own[part].at[step, far_y, far_x],
                        rows,
                    )
        elif stage == 1:
            for far in (0, 1):
                kept = (
                    core_in[part].at[step, y, far]
                    if crosses_y
                    else core_in[part].at[step, far, x]
                )
                add(first_in[part].at[step, far], kept, rows)
        elif stage == 2:
            add(
                second_in[part].at[step],
                first_in[part].at[step, x if crosses_y else y],
                rows,
            )

    everything = range(pieces)
    for step in range(depth):
        for part in everything:
            hop(0, part, step).start()
            local(part, step).start()
    for turn in range(depth + 2):
        for stage in range(3):
            step = turn - stage
            if 0 <= step < depth:
                for part in everything:
                    settle(stage, part, step)
                    if stage < 2 or step < depth - 1:
                        hop(stage + 1, part, step).start()
    for step in range(depth - 1):
        for part in everything:
            hop(3, part, step).wait_recv()
    for part in everything:
        array, first, rows, _ = parts[part]

        @pl.loop(0, rows // 16)
        def _(r):
            here = pl.ds(pl.multiple_of(r * 16, 16), 16)
            total = second_in[part][depth - 1, here].astype(F32)
            for step in range(depth - 1):
                total = total + line_in[part][step, here].astype(F32)
            there = pl.ds(pl.multiple_of(first + r * 16, 16), 16)
            outs[array][there] = total

    for step in range(depth):
        for part in everything:
            for stage in range(4):
                if stage < 3 or step < depth - 1:
                    hop(stage, part, step).wait_send()


def reduce_call(depth, whole):
    count = 8 * depth
    sizes = [array.shape[0] // count for array in whole]
    widths = [array.shape[1] for array in whole]
    parts = parts_of(*sizes)
    shaped = [
        array.reshape(2, 2, depth, 2, size, wide)
        for array, size, wide in zip(whole, sizes, widths)
    ]

    def buffers(lead):
        return [
            pltpu.VMEM(lead + (rows, widths[array]), BF16)
            for array, _, rows, _ in parts
        ]

    dma = pltpu.SemaphoreType.DMA
    return pl.pallas_call(
        functools.partial(reduce_kernel, depth, parts),
        out_shape=tuple(
            jax.ShapeDtypeStruct((size, wide), F32) for size, wide in zip(sizes, widths)
        ),
        in_specs=in_any(3),
        out_specs=tuple(in_vmem(3)),
        scratch_shapes=buffers((depth, 2, 2))
        + buffers((depth, 2, 2))
        + buffers((depth, 2))
        + buffers((depth,))
        + buffers((depth,))
        + [
            dma((depth, len(parts))),
            dma((4, depth, len(parts))),
            dma((4, depth, len(parts))),
        ],
        compiler_params=pltpu.CompilerParams(
            collective_id=3, has_side_effects=True, vmem_limit_bytes=VMEM_BYTES
        ),
        name="reduce_gradients",
    )(*shaped)


def on_device(
    mesh,
    hidden_in,
    cotangent,
    norm_gain,
    in_weight,
    conv_weight,
    conv_bias,
    x_weight,
    dt_weight,
    dt_bias,
    a_log,
    skip_gain,
    out_weight,
):
    layers = norm_gain.shape[0]
    rows, width = hidden_in.shape
    taps, channels = conv_weight.shape[1:]
    states = a_log.shape[2]
    rank = dt_weight.shape[1]
    devices, count = mesh.shape["ctx"] * mesh.shape["seq"], mesh.shape["seq"]
    inner = channels * devices
    gains = norm_gain.shape[1]
    at = Names(states, taps, rank)
    cfg = (rows, inner, states, taps, rank, count, channels)
    depth = count // 2
    by_kernel = (
        mesh.shape["ctx"] == 4
        and depth % 2 == 0
        and layers == 2
        and in_weight.shape[2] % 32 == 0
        and out_weight.shape[2] % 32 == 0
        and 128 % channels == 0
        and at.rows * channels // 128 % 16 == 0
    )

    def pack(layer):
        by_row = jnp.concatenate(
            [
                x_weight[layer].T,
                dt_weight[layer],
                a_log[layer].T,
                conv_weight[layer],
                conv_bias[layer][None],
                dt_bias[layer][None],
                skip_gain[layer][None],
                jnp.pad(norm_gain[layer], (0, channels - gains))[None],
            ],
            0,
        )
        by_row = jnp.pad(by_row, ((0, at.rows - at.count), (0, 0)))
        if by_kernel:
            folds = by_row.reshape(128 // channels, -1, channels)
            by_row = jnp.concatenate(list(folds), 1)
        return by_row

    local = [
        (in_weight[layer].T, out_weight[layer].T, pack(layer))
        for layer in range(layers)
    ]
    kept = ("pad", "gate", "act", "sp", "pre", "h_hbm", "y", "mixed")
    stream = hidden_in.astype(F32)
    streams, runs, weights = [], [], []
    if by_kernel:
        (in0, out0, small0), (in1, out1, small1) = local
        operands = [
            ("own_in", in0),
            ("own_small", small0),
            ("own_out", out0),
            ("next_in", in1),
            ("next_small", small1),
        ]
        first = forward_call(cfg, "first", stream, operands)
        operands = [
            ("win_hbm", first["win2_all"]),
            ("gsm_hbm", first["gsm2_all"]),
            ("own_out", out1),
        ]
        second = forward_call(cfg, "later", first["new"], operands)
        runs = [first, second]
        wins = [first["win_all"], first["win2_all"]]
        weights = [
            (
                run["sw"],
                win.reshape(2 * inner, width),
                run["wout_all"].reshape(width, inner),
            )
            for run, win in zip(runs, wins)
        ]
        streams = [stream, first["new"]]
        stream = second["new"]
    else:
        for w_in, w_out, w_small in local:
            w_in = lax.all_gather(w_in, ("ctx", "seq"), axis=0, tiled=True)
            w_out = lax.all_gather(w_out, ("ctx", "seq"), axis=0, tiled=True)
            sw = lax.all_gather(w_small, ("ctx", "seq"), axis=1, tiled=True)
            operands = [
                ("win_hbm", w_in.reshape(-1, 128, width)),
                ("sw", sw),
                ("wout_hbm", w_out.reshape(-1, 32, inner)),
            ]
            run = forward_call(cfg, "given", stream, operands)
            runs.append(run)
            weights.append((sw, w_in, w_out))
            streams.append(stream)
            stream = run["new"]
    stream_grad = cotangent.astype(F32)
    grads = [None] * layers
    for layer in reversed(range(layers)):
        stream_grad, g_in, g_out, g_small = backward_call(
            cfg,
            by_kernel,
            stream_grad,
            streams[layer],
            *weights[layer],
            [runs[layer][name] for name in kept],
        )
        if by_kernel:
            s_in, s_out, s_small = reduce_call(
                depth, (g_in, g_out, g_small.reshape(-1, 128))
            )
            s_small = s_small.reshape(-1, 128 // channels, channels)
            s_small = s_small.transpose(1, 0, 2).reshape(at.rows, channels)
        else:
            s_in, s_out, s_small = [
                lax.psum_scatter(
                    array.astype(F32),
                    ("ctx", "seq"),
                    scatter_dimension=dim,
                    tiled=True,
                )
                for array, dim in ((g_in, 0), (g_out, 0), (g_small, 1))
            ]
        s_x = s_small[: at.small, :channels]
        s_dt = s_small[at.dt : at.dt + rank, :channels]
        s_vec = s_small[at.vec : at.count, :channels]
        grads[layer] = (
            s_vec[at.gain, :gains],
            s_in.T,
            s_vec[at.conv : at.conv + taps],
            s_vec[at.conv_b],
            s_x.T,
            s_dt,
            s_vec[at.dt_b],
            s_vec[:states].T,
            s_vec[at.skip],
            s_out.T,
        )
    stacked = tuple(
        jnp.stack([grads[layer][member] for layer in range(layers)], 0)
        for member in range(10)
    )
    return (stream.astype(BF16), stream_grad) + stacked


def solution(mesh):
    split = ("ctx", "seq")
    tokens, last = P(split, None), P(None, split)
    middle, third = P(None, split, None), P(None, None, split)
    weights = (last, third, third, last, middle, third, last, middle, last, third)
    return jax.shard_map(
        functools.partial(on_device, mesh),
        mesh=mesh,
        in_specs=(tokens, tokens) + weights,
        out_specs=(tokens, tokens) + weights,
        check_vma=False,
    )
```

```python
import collections
import functools
import types

import jax
import jax.numpy as jnp
from jax import lax
from jax.experimental import pallas as pl
from jax.experimental.pallas import tpu as pltpu
from jax.sharding import PartitionSpec as P

EPS = 1e-05
LOG2E = 1.4426950408889634
MESH = pl.DeviceIdType.MESH
F32, BF16 = jnp.float32, jnp.bfloat16
NT = (((1,), (1,)), ((), ()))
TN = (((0,), (0,)), ((), ()))
VMEM_BYTES = 63 * 2**20
CHUNK = 16
GROUP = 512
HALO = 16


def dot(a, b, dims=None):
    if dims is None:
        dims = (((1,), (0,)), ((), ()))
    return lax.dot_general(a, b, dims, preferred_element_type=F32)


def lanes(index, width):
    return pl.ds(pl.multiple_of(index * width, width), width)


def widen(tile, width):
    times = width // tile.shape[1]
    return jnp.concatenate([tile] * times, axis=1) if times > 1 else tile


def softplus(v):
    return jnp.maximum(v, 0.0) + jnp.log1p(jnp.exp(-jnp.abs(v)))


def sigmoid(v):
    return 1.0 / (1.0 + jnp.exp(-v))


def keep_sum(own_sum, i, step):
    total = jnp.sum(step, axis=0, keepdims=True)
    fold = own_sum.shape[1]
    for part in range(GROUP // fold):
        row = i * (GROUP // fold) + part
        own_sum[pl.ds(row, 1), :] = total[:, part * fold : (part + 1) * fold]


def sum_of(sum_s, j, g):
    fold = sum_s.shape[2]
    each = GROUP // fold
    return jnp.concatenate(
        [sum_s[j, pl.ds(g * each + part, 1), :] for part in range(each)], 1
    )


def chunk_mask(rows, states):
    wide = CHUNK * states
    token = lax.rem(lax.broadcasted_iota(jnp.int32, (rows, wide), 0), CHUNK)
    owner = lax.broadcasted_iota(jnp.int32, (rows, wide), 1) // states
    return token == owner


def spread(small_low, first, states):
    wide = CHUNK * states
    row = lax.broadcasted_iota(jnp.int32, (small_low.shape[1], wide), 0)
    col = lax.broadcasted_iota(jnp.int32, (small_low.shape[1], wide), 1)
    pick = (row == first + lax.rem(col, states)).astype(F32).astype(BF16)
    tiled = dot(small_low, pick)
    return jnp.where(chunk_mask(small_low.shape[0], states), tiled, 0.0).astype(BF16)


def gather_back(partial, first, states, width):
    wide = CHUNK * states
    row = lax.broadcasted_iota(jnp.int32, (wide, width), 0)
    col = lax.broadcasted_iota(jnp.int32, (wide, width), 1)
    pick = (col == first + lax.rem(row, states)).astype(F32).astype(BF16)
    kept = jnp.where(chunk_mask(partial.shape[0], states), partial, 0.0)
    return dot(kept.astype(BF16), pick)


class Names:
    def __init__(self, states, taps, rank):
        self.small = rank + 2 * states
        self.dt = self.small
        self.vec = self.small + rank
        self.count = self.vec + states + taps + 4
        self.rows = -(-self.count // 16) * 16
        self.conv = states
        self.conv_b = states + taps
        self.dt_b = states + taps + 1
        self.skip = states + taps + 2
        self.gain = states + taps + 3


def load_small(at, sw_ref, vec_s, dtw_s):
    states, rank = at.conv, at.vec - at.dt
    vec_s[...] = sw_ref[pl.ds(at.vec, at.rows - at.vec), :].astype(F32)
    vec_s[pl.ds(0, states), :] = -jnp.exp(vec_s[pl.ds(0, states), :])
    dtw_s[pl.ds(0, rank), :] = sw_ref[pl.ds(at.dt, rank), :]
    dtw_s[pl.ds(rank, at.small - rank), :] = jnp.zeros(
        (at.small - rank, dtw_s.shape[1]), BF16
    )


def gain_pick(channels):
    gains = channels // 2
    row = lax.broadcasted_iota(jnp.int32, (256, 128), 0)
    col = lax.broadcasted_iota(jnp.int32, (256, 128), 1)
    place = lax.div(col, gains) * channels + lax.rem(col, gains)
    return (row == place).astype(F32).astype(BF16)


def gain_row(at, channels, vec_s):
    pick = gain_pick(channels)
    row = vec_s[pl.ds(at.gain // 8 * 8, 8), :].astype(BF16)
    tiles = [
        dot(row[:, 256 * i : 256 * i + 256], pick) for i in range(row.shape[1] // 256)
    ]
    gain = jnp.concatenate(tiles, 1)
    return gain[at.gain % 8 : at.gain % 8 + 1]


def merge_small(channels, blocks, sw_ref):
    each = 128 // channels
    rows = blocks.shape[1]
    owner = lax.div(lax.broadcasted_iota(jnp.int32, (rows, 128), 1), channels)

    @pl.loop(0, sw_ref.shape[1] // 128)
    def _(j):
        held = [blocks[j * each + part].astype(F32) for part in range(each)]
        for fold in range(each):
            tile = None
            for part in range(each):
                shift = (part - fold) * channels % 128
                moved = pltpu.roll(held[part], shift, 1) if shift else held[part]
                tile = moved if tile is None else jnp.where(owner == part, moved, tile)
            sw_ref[pl.ds(fold * rows, rows), lanes(j, 128)] = tile.astype(BF16)


def split(number, by):
    if isinstance(number, int):
        return divmod(number, by)
    return lax.div(number, by), lax.rem(number, by)


class Folded:
    def __init__(self, ref):
        self.ref, self.shape = ref, ref.shape[3:]

    def __setitem__(self, block, value):
        _, x, z, core = self.ref.shape[:4]
        row = lax.div(block, z * core)
        self.ref[
            lax.div(row, x), lax.rem(row, x), lax.rem(lax.div(block, core), z), lax.rem(block, core)
        ] = value


def split_small(channels, full_ref, blocks):
    each = 128 // channels
    rows = blocks.shape[1]
    owner = lax.div(lax.broadcasted_iota(jnp.int32, (rows, 128), 1), channels)

    @pl.loop(0, full_ref.shape[1] // 128)
    def _(j):
        held = [
            full_ref[pl.ds(fold * rows, rows), lanes(j, 128)] for fold in range(each)
        ]
        for part in range(each):
            tile = None
            for fold in range(each):
                shift = (fold - part) * channels % 128
                moved = pltpu.roll(held[fold], shift, 1) if shift else held[fold]
                tile = moved if tile is None else jnp.where(owner == fold, moved, tile)
            blocks[j * each + part] = tile.astype(BF16)


def places():
    ctx, seq = lax.axis_index("ctx"), lax.axis_index("seq")
    return lax.div(ctx, 2), lax.rem(ctx, 2), lax.div(seq, 2), lax.rem(seq, 2)


def device(y, x, z, core):
    return (2 * y + x, 2 * z + core)


def square_partners(depth):
    y, x, z, core = places()
    partners = [device(y, x, z, 1 - core), device(y, 1 - x, z, core)]
    partners.append(device(1 - y, x, z, core))
    for step in range(1, depth):
        partners.append(device(y, x, lax.rem(z + step, depth), core))
    return partners


def greet_square(depth):
    barrier = pltpu.get_barrier_semaphore()
    partners = square_partners(depth)
    for partner in partners:
        pl.semaphore_signal(barrier, inc=1, device_id=partner, device_id_type=MESH)
    pl.semaphore_wait(barrier, len(partners))


class Gather:
    def __init__(self, depth, pieces, own_sem, send_sem, recv_sem):
        self.depth, self.pieces = depth, pieces
        self.own_sem, self.send_sem, self.recv_sem = own_sem, send_sem, recv_sem
        self.y, self.x, self.z, self.core = places()
        self.used = [0] * len(pieces)
        self.sent = []
        turn = 1 - 2 * lax.div(self.z, max(depth // 2, 1))
        self.line = [
            lax.rem(self.z + turn * step + depth, depth) for step in range(depth)
        ]
        y, x, z, core = self.y, self.x, self.z, self.core
        self.x_side, self.y_side = device(y, 1 - x, z, core), device(1 - y, x, z, core)
        self.sibling = device(y, x, z, 1 - core)

    @staticmethod
    def sends(depth):
        return 3 + depth - 1 + 3 * (depth - 1) + 2 * depth + 2 * depth

    def slot(self, y, x, z, core):
        return ((2 * y + x) * self.depth + z) * 2 + core

    def span(self, item, slot):
        _, whole, first, rows, _ = self.pieces[item]
        return whole.at[slot, pl.ds(first, rows)]

    def send(self, item, slot, to, own=False):
        local, _, first, rows, _ = self.pieces[item]
        copy = pltpu.make_async_remote_copy(
            local.at[pl.ds(first, rows)] if own else self.span(item, slot),
            self.span(item, slot),
            self.send_sem.at[item, self.used[item]],
            self.recv_sem.at[item, slot],
            device_id=to,
            device_id_type=MESH,
        )
        self.used[item] += 1
        copy.start()
        self.sent.append(copy)

    def arrive(self, item, slot):
        pltpu.make_async_remote_copy(
            self.span(item, slot),
            self.span(item, slot),
            self.send_sem.at[item, 0],
            self.recv_sem.at[item, slot],
            device_id=self.sibling,
            device_id_type=MESH,
        ).wait_recv()

    def own_copy(self, item):
        local, _, first, rows, _ = self.pieces[item]
        mine = self.slot(self.y, self.x, self.z, self.core)
        return pltpu.make_async_copy(
            local.at[pl.ds(first, rows)], self.span(item, mine), self.own_sem.at[item]
        )

    def begin(self, item):
        mine = self.slot(self.y, self.x, self.z, self.core)
        self.own_copy(item).start()
        for to in (self.x_side, self.y_side):
            self.send(item, mine, to, own=True)
        for step in range(1, self.depth):
            to = device(self.y, self.x, self.line[step], self.core)
            self.send(item, mine, to, own=True)
        self.send(item, mine, self.sibling, own=True)

    def along(self, item, step):
        slot = self.slot(self.y, self.x, self.line[step], self.core)
        self.arrive(item, slot)
        for to in (self.x_side, self.y_side, self.sibling):
            self.send(item, slot, to)

    def near(self, item, step):
        if self.pieces[item][4]:
            slot = self.slot(self.y, 1 - self.x, self.line[step], self.core)
            to = self.y_side
        else:
            slot = self.slot(1 - self.y, self.x, self.line[step], self.core)
            to = self.x_side
        self.arrive(item, slot)
        self.send(item, slot, to)
        self.send(item, slot, self.sibling)

    def far(self, item, step, other):
        y, x = 1 - self.y, 1 - self.x
        if self.pieces[item][4]:
            x = x if other else self.x
        else:
            y = y if other else self.y
        slot = self.slot(y, x, self.line[step], self.core)
        self.arrive(item, slot)
        self.send(item, slot, self.sibling)

    def settle(self, item):
        self.own_copy(item).wait()
        for step in range(self.depth):
            for y in (self.y, 1 - self.y):
                for x in (self.x, 1 - self.x):
                    self.arrive(item, self.slot(y, x, self.line[step], 1 - self.core))

    def turns(self, items):
        order = [("near", 0)]
        for step in range(1, self.depth):
            order.append(("along", step))
            order.append(("near", step))
            if step >= 2:
                order.append(("far", step - 2, 1))
            order.append(("far", step - 1, 0))
        for step in range(max(self.depth - 2, 0), self.depth):
            if step == self.depth - 1:
                order.append(("far", step, 0))
            order.append(("far", step, 1))
        actions = []
        for name, *rest in order:
            for item in items:
                actions.append(functools.partial(getattr(self, name), item, *rest))
        return actions

    def finish(self):
        for copy in self.sent:
            copy.wait_send()


class Reduce:
    def __init__(self, depth, pieces, buffers, own_sem, send_sem, recv_sem):
        self.depth, self.pieces, self.buffers = depth, pieces, buffers
        self.own_sem, self.send_sem, self.recv_sem = own_sem, send_sem, recv_sem
        y, x, z, core = places()
        self.y, self.x, self.core = y, x, core
        self.line = [lax.rem(z + step + 1, depth) for step in range(depth)]
        self.x_side, self.y_side = device(y, 1 - x, z, core), device(1 - y, x, z, core)
        self.sibling = device(y, x, z, 1 - core)
        self.along = [device(y, x, there, core) for there in self.line]
        self.sent = []

    @staticmethod
    def buffers_of(depth, rows, width):
        return [
            pltpu.VMEM(lead + (rows, width), BF16)
            for lead in ((2, 2, 2), (depth, 2, 2), (depth, 2), (depth,), (depth - 1,))
        ]

    def part_of(self, item, step, side):
        whole, _, first, rows, _ = self.pieces[item]
        return whole.at[:, :, self.line[step], side, pl.ds(first, rows)]

    def local(self, item, step):
        return pltpu.make_async_copy(
            self.part_of(item, step, self.core),
            self.buffers[item][0].at[step % 2],
            self.own_sem.at[item, step % 2],
        )

    def hop(self, stage, item, step):
        _, core_in, first_in, second_in, line_in = self.buffers[item]
        crosses_y = self.pieces[item][4]
        y, x = self.y, self.x
        if stage == 0:
            source = self.part_of(item, step, 1 - self.core)
            target, to = core_in.at[step], self.sibling
        elif stage == 1:
            source = core_in.at[step, 1 - y] if crosses_y else core_in.at[step, :, 1 - x]
            target, to = first_in.at[step], self.y_side if crosses_y else self.x_side
        elif stage == 2:
            source = first_in.at[step, 1 - x if crosses_y else 1 - y]
            target, to = second_in.at[step], self.x_side if crosses_y else self.y_side
        else:
            source, target, to = second_in.at[step], line_in.at[step], self.along[step]
        return pltpu.make_async_remote_copy(
            source,
            target,
            self.send_sem.at[item, stage, step],
            self.recv_sem.at[item, stage, step],
            device_id=to,
            device_id_type=MESH,
        )

    def send(self, stage, item, step):
        copy = self.hop(stage, item, step)
        copy.start()
        self.sent.append(copy)

    @staticmethod
    def add(target, other, rows):
        @pl.loop(0, rows // 16)
        def _(k):
            here = pl.ds(pl.multiple_of(k * 16, 16), 16)
            target[here] = (
                target[here].astype(F32) + other[here].astype(F32)
            ).astype(BF16)

    def begin(self, item):
        for step in range(self.depth):
            self.send(0, item, step)
            if step < 2:
                self.local(item, step).start()

    def settle(self, stage, item, step):
        own, core_in, first_in, second_in, _ = self.buffers[item]
        rows, crosses_y = self.pieces[item][3:]
        self.hop(stage, item, step).wait_recv()
        if stage == 0:
            self.local(item, step).wait()
            for y in (0, 1):
                for x in (0, 1):
                    self.add(core_in.at[step, y, x], own.at[step % 2, y, x], rows)
            if step + 2 < self.depth:
                self.local(item, step + 2).start()
        elif stage == 1:
            for far in (0, 1):
                kept = (
                    core_in.at[step, self.y, far]
                    if crosses_y
                    else core_in.at[step, far, self.x]
                )
                self.add(first_in.at[step, far], kept, rows)
        else:
            kept = first_in.at[step, self.x if crosses_y else self.y]
            self.add(second_in.at[step], kept, rows)
        if stage < 2 or step < self.depth - 1:
            self.send(stage + 1, item, step)

    def last(self, item):
        _, out, first, rows, _ = self.pieces[item]
        second_in, line_in = self.buffers[item][3:]
        for step in range(self.depth - 1):
            self.hop(3, item, step).wait_recv()

        @pl.loop(0, rows // 16)
        def _(k):
            here = pl.ds(pl.multiple_of(k * 16, 16), 16)
            total = second_in[self.depth - 1, here].astype(F32)
            for step in range(self.depth - 1):
                total = total + line_in[step, here].astype(F32)
            out[pl.ds(pl.multiple_of(first + k * 16, 16), 16)] = total

    def turns(self, items):
        actions = []
        for turn in range(self.depth + 2):
            for stage in range(3):
                step = turn - stage
                if 0 <= step < self.depth:
                    for item in items:
                        actions.append(
                            functools.partial(self.settle, stage, item, step)
                        )
        for item in items:
            actions.append(functools.partial(self.last, item))
        return actions

    def finish(self):
        for copy in self.sent:
            copy.wait_send()
        self.sent = []


def chain(count, me, ctx, own_sum, sum_s, own_end, end_s, sems):
    sum_send, sum_recv, end_send, end_recv = sems

    def sums(j, slot):
        return pltpu.make_async_remote_copy(
            own_sum,
            sum_s.at[slot],
            sum_send.at[j],
            sum_recv.at[slot],
            device_id=(ctx, j),
            device_id_type=MESH,
        )

    def ends(g, j, slot):
        return pltpu.make_async_remote_copy(
            own_end.at[:, pl.ds(g * GROUP, GROUP)],
            end_s.at[slot, :, pl.ds(g * GROUP, GROUP)],
            end_send.at[g, j],
            end_recv.at[g, slot],
            device_id=(ctx, j),
            device_id_type=MESH,
        )

    return sums, ends


def each(first, last, act):
    def body(j, _):
        act(j)
        return 0

    lax.fori_loop(first, last, body, 0)


def forward_kernel(cfg, mode, names, *refs):
    r = types.SimpleNamespace(**dict(zip(names, refs)))
    rows, inner, states, taps, rank, count, channels = cfg
    at = Names(states, taps, rank)
    ctx, me = lax.axis_index("ctx"), lax.axis_index("seq")
    groups, steps, tiles = inner // GROUP, rows // CHUNK, inner // GROUP
    depth = count // 2
    width = r.stream.shape[1]
    barrier = pltpu.get_barrier_semaphore()

    def greet(to):
        pl.semaphore_signal(barrier, inc=1, device_id=to, device_id_type=MESH)

    queue = collections.deque()

    def weave(times):
        for _ in range(min(times, len(queue))):
            queue.popleft()()

    if mode == "given":
        each(0, me, lambda j: greet((ctx, j)))
    else:
        each(0, me, lambda j: greet((ctx, j)))
        each(me + 1, count, lambda j: greet((ctx, j)))
        y, x, z, core = places()
        greet(device(y, 1 - x, z, core))
        greet(device(1 - y, x, z, core))

    if mode != "first":
        half = r.win_hbm.shape[0] // 2
        halves = [
            pltpu.make_async_copy(
                r.win_hbm.at[pl.ds(k * half, half)],
                r.win_s.at[pl.ds(k * half, half)],
                r.load_sem.at[k],
            )
            for k in range(2)
        ]
        if mode == "later":
            small_copy = pltpu.make_async_copy(r.gsm_hbm, r.gsm_s, r.load_sem.at[2])
            small_copy.start()
        for copy in halves:
            copy.start()
    if mode == "given":
        out_copy = pltpu.make_async_copy(r.wout_hbm, r.wout_s, r.load_sem.at[2])
        out_copy.start()

    stream = r.stream[...]
    scale = lax.rsqrt(jnp.mean(stream * stream, axis=1, keepdims=True) + EPS)
    stores = []

    if mode == "given":

        @pl.when(me < count - 1)
        def _():
            pl.semaphore_wait(barrier, count - 1 - me)

    else:
        pl.semaphore_wait(barrier, count + 1)
        pieces = []

        def add_piece(local, whole, cuts):
            start = len(pieces)
            total = local.shape[0]
            for k, last_y in enumerate(cuts):
                piece = total // len(cuts)
                pieces.append((local, whole, k * piece, piece, last_y))
            return list(range(start, len(pieces)))

        first_items, next_items = [], []
        if mode == "first":
            first_items = add_piece(r.own_in, r.win_s, (1, 0))
            first_items += add_piece(r.own_small, r.gsm_s, (1,))
        out_items = add_piece(r.own_out, r.wout_s, (1, 0))
        if mode == "first":
            next_items = add_piece(r.next_in, r.win2_all, (1, 0))
            next_items += add_piece(r.next_small, r.gsm2_all, (0,))
        gather = Gather(depth, pieces, r.own_sem, r.send_sem, r.recv_sem)

        def begin(items):
            for item in items:
                gather.begin(item)

        def settle(items):
            for item in items:
                gather.settle(item)

        def keep(source, target, slot):
            copy = pltpu.make_async_copy(source, target, r.store_sem.at[slot])
            copy.start()
            stores.append(copy)

        if mode == "first":
            begin(first_items)
            turns = gather.turns(first_items)
            for k, turn in enumerate(turns):
                if k == len(turns) // 2:
                    begin(out_items + next_items)
                turn()
            settle(first_items)
            keep(r.win_s, r.win_all, 1)
            turns = gather.turns(out_items)
            queue.extend(gather.turns(out_items + next_items))
        else:
            begin(out_items)
            queue.extend(gather.turns(out_items))
        queue.append(lambda: settle(out_items))
        queue.append(lambda: keep(r.wout_s, r.wout_all, 0))
        if mode == "first":
            queue.append(lambda: settle(next_items))
        if mode == "later":
            small_copy.wait()
        merge_small(channels, r.gsm_s, r.sw)
    pace = -(-len(queue) // 21)

    load_small(at, r.sw, r.vec_s, r.dtw_s)
    r.normed_s[...] = (stream * scale * gain_row(at, channels, r.vec_s)).astype(BF16)
    per_tile = GROUP // r.win_s.shape[1]

    def win_tile(i):
        return r.win_s[pl.ds(i * per_tile, per_tile)].reshape(GROUP, width)

    if mode != "first":
        halves[0].wait()

    @pl.loop(0, tiles)
    def _(i):
        low = dot(r.normed_s[...], win_tile(i), NT).astype(BF16)
        r.pad[pl.ds(HALO, rows), lanes(i, GROUP)] = low
        r.padf_s[pl.ds(HALO, rows), lanes(i, GROUP)] = low.astype(F32)

    def edge():
        return pltpu.make_async_remote_copy(
            r.pad.at[pl.ds(rows, HALO)],
            r.halo_s,
            r.halo_sem.at[0],
            r.halo_sem.at[1],
            device_id=(ctx, jnp.minimum(me + 1, count - 1)),
            device_id_type=MESH,
        )

    @pl.when(me < count - 1)
    def _():
        edge().start()

    weave(pace)
    if mode != "first":
        halves[1].wait()

    @pl.loop(0, tiles)
    def _(i):
        r.gate[:, lanes(i, GROUP)] = dot(r.normed_s[...], win_tile(i + tiles), NT)

    weave(pace)

    @pl.when(me > 0)
    def _():
        edge().wait_recv()

    @pl.when(me == 0)
    def _():
        r.halo_s[...] = jnp.zeros_like(r.halo_s)

    r.pad[pl.ds(0, HALO), :] = r.halo_s[...]
    r.padf_s[pl.ds(0, HALO), :] = r.halo_s[...].astype(F32)

    @pl.loop(0, tiles)
    def _(i):
        here = lanes(i, GROUP)
        total = r.vec_s[pl.ds(at.conv_b, 1), here]
        for k in range(taps):
            total = (
                total
                + r.vec_s[pl.ds(at.conv + k, 1), here]
                * r.padf_s[pl.ds(HALO - taps + 1 + k, rows), here]
            )
        r.act[:, here] = (total * sigmoid(total)).astype(BF16)

    weave(pace)
    small = dot(r.act[...], r.sw[pl.ds(0, at.small), :], NT)
    r.sp[...] = small
    small_low = small.astype(BF16)

    @pl.loop(0, tiles)
    def _(i):
        here = lanes(i, GROUP)
        before = dot(small_low, r.dtw_s[:, here]) + r.vec_s[pl.ds(at.dt_b, 1), here]
        step = softplus(before)
        r.pre[:, here] = before
        r.dt_s[:, here] = step
        r.dx_s[:, here] = step * r.act[:, here].astype(F32)
        keep_sum(r.own_sum, i, step)

    sums, ends = chain(
        count, me, ctx, r.own_sum, r.sum_s, r.own_end, r.end_s,
        (r.sum_send, r.sum_recv, r.end_send, r.end_recv),
    )
    each(me + 1, count, lambda j: sums(j, me).start())
    weave(pace)
    for n in range(states):
        r.bb_s[:, n, :] = jnp.broadcast_to(
            small[:, rank + n : rank + n + 1], (rows, 128)
        )
    r.cd_s[...] = spread(small_low, rank + states, states)

    def advance(t, state, rate2, here):
        return (
            jnp.exp2(r.dt_s[pl.ds(t, 1), here] * rate2) * state
            + r.dx_s[pl.ds(t, 1), here] * widen(r.bb_s[t], GROUP)
        )

    for g in range(groups):
        here = pl.ds(g * GROUP, GROUP)
        rate2 = r.vec_s[pl.ds(0, states), here] * LOG2E

        def first_pass(step, state):
            for i in range(CHUNK):
                state = advance(step * CHUNK + i, state, rate2, here)
            return state

        r.own_end[:, here] = lax.fori_loop(
            0, steps, first_pass, jnp.zeros((states, GROUP), F32)
        ).astype(BF16)
        each(me + 1, count, lambda j: ends(g, j, me).start())
        weave(pace)

    def h_copy(g):
        here = pl.ds(g * GROUP, GROUP)
        return pltpu.make_async_copy(
            r.hs.at[:, here], r.h_hbm.at[:, here], r.h_sem.at[g]
        )

    for g in range(groups):
        here = pl.ds(g * GROUP, GROUP)
        rate2 = r.vec_s[pl.ds(0, states), here] * LOG2E

        def carry(j, state):
            if g == 0:
                sums(j, j).wait_recv()
            ends(g, j, j).wait_recv()
            return (
                jnp.exp2(rate2 * sum_of(r.sum_s, j, g)) * state
                + r.end_s[j, :, here].astype(F32)
            )

        state = lax.fori_loop(0, me, carry, jnp.zeros((states, GROUP), F32))
        r.hs[pl.ds(0, states), here] = state.astype(BF16)

        def second_pass(step, state):
            base = pl.multiple_of(step * CHUNK * states + states, states)
            for i in range(CHUNK):
                state = advance(step * CHUNK + i, state, rate2, here)
                r.hs[pl.ds(base + i * states, states), here] = state.astype(BF16)
            tokens = pl.ds(pl.multiple_of(step * CHUNK, CHUNK), CHUNK)
            r.y[tokens, here] = dot(
                r.cd_s[tokens, :], r.hs[pl.ds(base, CHUNK * states), here]
            )
            return state

        thirds = 1 if mode == "given" else 3
        for part in range(thirds):
            state = lax.fori_loop(
                steps * part // thirds,
                steps * (part + 1) // thirds,
                second_pass,
                state,
            )
            weave(pace)
        h_copy(g).start()
        y_value = (
            r.y[:, here]
            + r.vec_s[pl.ds(at.skip, 1), here] * r.act[:, here].astype(F32)
        )
        gate = r.gate[:, here]
        r.y[:, here] = y_value
        r.mixed[:, here] = (y_value * gate * sigmoid(gate)).astype(BF16)

    if mode == "given":
        out_copy.wait()
    else:
        while queue and not stores_hold_out(mode, stores):
            weave(1)
    out_tile = 256 // r.wout_s.shape[1]
    for i in range(width // 256):
        here = pl.ds(i * 256, 256)
        wout = r.wout_s[pl.ds(i * out_tile, out_tile)].reshape(256, inner)
        r.new[:, here] = r.stream[:, here] + dot(r.mixed[...], wout, NT)

    weave(len(queue))
    if mode != "given":
        gather.finish()

    @pl.when(me < count - 1)
    def _():
        edge().wait_send()

    each(me + 1, count, lambda j: sums(j, me).wait_send())
    for g in range(groups):
        each(me + 1, count, lambda j: ends(g, j, me).wait_send())
        h_copy(g).wait()
    for copy in stores:
        copy.wait()


def stores_hold_out(mode, stores):
    return len(stores) == (2 if mode == "first" else 1)


def backward_kernel(cfg, mode, names, *refs):
    r = types.SimpleNamespace(**dict(zip(names, refs)))
    rows, inner, states, taps, rank, count, channels = cfg
    at = Names(states, taps, rank)
    ctx, me = lax.axis_index("ctx"), lax.axis_index("seq")
    groups, steps, tiles = inner // GROUP, rows // CHUNK, inner // GROUP
    depth = count // 2
    width = r.stream.shape[1]
    barrier = pltpu.get_barrier_semaphore()
    gvec = r.full_s.at[pl.ds(at.vec, at.rows - at.vec)]

    def signal(semaphore, to):
        pl.semaphore_signal(semaphore, inc=1, device_id=to, device_id_type=MESH)

    queue = collections.deque()

    def weave(times):
        for _ in range(min(times, len(queue))):
            queue.popleft()()

    each(me + 1, count, lambda j: signal(barrier, (ctx, j)))
    if mode != "given":
        each(0, me, lambda j: signal(barrier, (ctx, j)))
        y, x, z, core = places()
        signal(barrier, device(y, 1 - x, z, core))
        signal(barrier, device(1 - y, x, z, core))

    def wout_copy(i):
        slot = lax.rem(i, 2)
        return pltpu.make_async_copy(
            r.wout.at[:, :, lanes(i, GROUP)], r.wout_s.at[slot], r.wout_sem.at[slot]
        )

    def gate_copies(i):
        slot = lax.rem(i, 2)
        return [
            pltpu.make_async_copy(
                array.at[:, lanes(i, GROUP)], r.gate_s.at[slot, k], r.gate_sem.at[slot, k]
            )
            for k, array in enumerate((r.gate, r.y))
        ]

    win_rows = r.win_s.shape[1]

    def win_copy(i, slot):
        return pltpu.make_async_copy(
            r.win.at[pl.ds(i * win_rows, win_rows)], r.win_s.at[slot], r.win_sem.at[slot]
        )

    span = rows // 2 * states

    def states_in(k):
        g, half = k // 2, 1 - k % 2
        return pltpu.make_async_copy(
            r.h_hbm.at[pl.ds(half * span, span + states), pl.ds(g * GROUP, GROUP)],
            r.hb.at[k % 2],
            r.h_sem.at[k % 2],
        )

    wout_copy(0).start()
    for copy in gate_copies(0):
        copy.start()
    load_small(at, r.sw, r.vec_s, r.dtw_s)
    gain = gain_row(at, channels, r.vec_s)
    r.low_s[...] = r.sgrad[...].astype(BF16)
    stream = r.stream[...]
    scale = lax.rsqrt(jnp.mean(stream * stream, axis=1, keepdims=True) + EPS)
    r.normed_s[...] = (stream * scale * gain).astype(BF16)
    small_low = r.sp[...].astype(BF16)

    in_items, out_items, own_items = [], [], []
    if mode == "given":

        @pl.when(me > 0)
        def _():
            pl.semaphore_wait(barrier, me)

    else:
        pl.semaphore_wait(barrier, count + 1)
        pieces, buffers = [], []

        def add_piece(whole, out, cuts, held):
            start = len(pieces)
            total = whole.shape[4]
            for k, first_y in enumerate(cuts):
                piece = total // len(cuts)
                pieces.append((whole, out, k * piece, piece, first_y))
                buffers.append(held[k])
            return list(range(start, len(pieces)))

        def held_by(name):
            found = []
            while hasattr(r, f"{name}{len(found)}_0"):
                k = len(found)
                found.append([getattr(r, f"{name}{k}_{part}") for part in range(5)])
            return found

        held_in, held_small, held_out = (
            held_by("rin"),
            held_by("rsmall"),
            held_by("rout"),
        )
        out_items = add_piece(r.gout, r.sum_out, (1, 0), held_out)
        if mode == "first":
            in_items = add_piece(r.next_gin, r.sum_next_in, (1, 0), held_in)
            in_items += add_piece(r.next_gsmall, r.sum_next_small, (1,), held_small)
            own_items = add_piece(r.gin, r.sum_in, (1, 0), held_in)
            own_items += add_piece(r.gsmall_hbm, r.sum_small, (0,), held_small)
        reduce = Reduce(depth, pieces, buffers, r.own_sem, r.send_sem, r.recv_sem)
        for item in in_items:
            reduce.begin(item)

    out_shape = r.stage_out.shape[1:]
    out_rows = out_shape[0] * out_shape[1] * out_shape[2]
    line = r.gout.shape[2]

    def block_of(whole, i):
        row, z = split(2 * i, line)
        y, x = split(row, 2)
        return whole.at[y, x, pl.ds(z, 2)]

    for k in range(width // out_rows):
        slot = k % 2
        copy = pltpu.make_async_copy(
            r.stage_out.at[slot], block_of(r.gout, k), r.out_sem.at[slot]
        )
        if k >= 2:
            copy.wait()

        @pl.loop(0, tiles)
        def _(i):
            here = lanes(i, GROUP)
            r.stage_out[slot, :, :, :, here] = (
                dot(r.low_s[:, pl.ds(k * out_rows, out_rows)], r.mixed[:, here], TN)
                .astype(BF16)
                .reshape(out_shape[:-1] + (GROUP,))
            )

        copy.start()
    for slot in range(2):
        pltpu.make_async_copy(
            r.stage_out.at[slot], block_of(r.gout, 0), r.out_sem.at[slot]
        ).wait()
    if mode != "given":
        for item in out_items:
            reduce.begin(item)
        queue.extend(reduce.turns(in_items + out_items))
    pace = -(-len(queue) // (24 if mode == "first" else 16))
    weave(pace)

    @pl.loop(0, tiles)
    def _(i):
        here = lanes(i, GROUP)
        slot = lax.rem(i, 2)

        @pl.when(i + 1 < tiles)
        def _():
            wout_copy(i + 1).start()
            for copy in gate_copies(i + 1):
                copy.start()

        wout_copy(i).wait()
        for copy in gate_copies(i):
            copy.wait()
        mixed_grad = dot(r.low_s[...], r.wout_s[slot].reshape(width, GROUP))
        gate = r.gate_s[slot, 0]
        sig = sigmoid(gate)
        act = r.act[:, here].astype(F32)
        scan_grad = mixed_grad * gate * sig
        r.sg_s[:, here] = scan_grad
        r.pb_s[:, lanes(i + tiles, GROUP)] = (
            mixed_grad * r.gate_s[slot, 1] * sig * (1.0 + gate * (1.0 - sig))
        ).astype(BF16)
        gvec[pl.ds(at.skip, 1), here] = jnp.sum(scan_grad * act, axis=0, keepdims=True)
        step = softplus(r.pre[:, here])
        r.dt_s[:, here] = step
        r.dx_s[pl.ds(0, rows), here] = step * act
        keep_sum(r.own_sum, i, step)

    sums, ends = chain(
        count, me, ctx, r.own_sum, r.sum_s, r.own_end, r.end_s,
        (r.sum_send, r.sum_recv, r.end_send, r.end_recv),
    )
    each(0, me, lambda j: sums(j, me).start())
    weave(pace)
    for n in range(states):
        first = rank + states + n
        r.cb_s[:, n, :] = jnp.broadcast_to(r.sp[:, first : first + 1], (rows, 128))
    r.bd_s[...] = spread(small_low, rank, states)
    ones = jnp.where(chunk_mask(CHUNK, states), 1.0, 0.0).astype(BF16)
    states_in(0).start()

    for g in range(groups):
        here = pl.ds(g * GROUP, GROUP)
        rate2 = r.vec_s[pl.ds(0, states), here] * LOG2E

        def first_pass(k, state):
            step = steps - 1 - k
            for i in reversed(range(CHUNK)):
                t = step * CHUNK + i
                state = jnp.exp2(r.dt_s[pl.ds(t, 1), here] * rate2) * (
                    state + r.sg_s[pl.ds(t, 1), here] * widen(r.cb_s[t], GROUP)
                )
            return state

        r.own_end[:, here] = lax.fori_loop(
            0, steps, first_pass, jnp.zeros((states, GROUP), F32)
        ).astype(BF16)
        each(0, me, lambda j: ends(g, j, me).start())
        weave(pace)

    for g in range(groups):
        here = pl.ds(g * GROUP, GROUP)
        rate = r.vec_s[pl.ds(0, states), here]
        rate2 = rate * LOG2E

        def carry(k, state):
            j = count - 1 - k
            if g == 0:
                sums(j, j).wait_recv()
            ends(g, j, j).wait_recv()
            return (
                jnp.exp2(rate2 * sum_of(r.sum_s, j, g)) * state
                + r.end_s[j, :, here].astype(F32)
            )

        begin = lax.fori_loop(
            0, count - 1 - me, carry, jnp.zeros((states, GROUP), F32)
        )
        both = (begin, jnp.zeros((states, GROUP), F32))
        for part in range(2):
            k = 2 * g + part
            half = 1 - part
            held_states = r.hb.at[k % 2]
            if k + 1 < 2 * groups:
                states_in(k + 1).start()
            states_in(k).wait()

            def second_pass(turn, both):
                state, total = both
                step = steps - 1 - turn
                base = pl.multiple_of(step * CHUNK * states - half * span, states)
                for i in reversed(range(CHUNK)):
                    t = step * CHUNK + i
                    dt = r.dt_s[pl.ds(t, 1), here]
                    adjoint = state + r.sg_s[pl.ds(t, 1), here] * widen(
                        r.cb_s[t], GROUP
                    )
                    state = jnp.exp2(dt * rate2) * adjoint
                    held = held_states[pl.ds(base + i * states, states), :]
                    rated = state * held.astype(F32) * rate
                    total = total + dt * rated
                    r.ab_s[pl.ds(i * states, states), :] = adjoint.astype(BF16)
                    r.rb_s[pl.ds(i * states, states), :] = rated.astype(BF16)
                tokens = pl.ds(pl.multiple_of(step * CHUNK, CHUNK), CHUNK)
                from_in = dot(r.bd_s[tokens, :], r.ab_s[...])
                from_rate = dot(ones, r.rb_s[...])
                scan_grad = r.sg_s[tokens, here]
                into_in = dot(r.dx_s[tokens, here].astype(BF16), r.ab_s[...], NT)
                into_out = dot(
                    scan_grad.astype(BF16),
                    held_states[pl.ds(base + states, CHUNK * states), :],
                    NT,
                )
                if g == 0:
                    r.pin_s[tokens, :] = into_in
                    r.pout_s[tokens, :] = into_out
                else:
                    r.pin_s[tokens, :] += into_in
                    r.pout_s[tokens, :] += into_out
                r.stepg_s[tokens, here] = (
                    r.act[tokens, here].astype(F32) * from_in + from_rate
                )
                r.sg_s[tokens, here] = (
                    r.dt_s[tokens, here] * from_in
                    + r.vec_s[pl.ds(at.skip, 1), here] * scan_grad
                )
                return state, total

            for quarter in range(2):
                low = (2 * part + quarter) * steps // 4
                high = (2 * part + quarter + 1) * steps // 4
                both = lax.fori_loop(low, high, second_pass, both)
                weave(pace)
        gvec[pl.ds(0, states), here] = both[1]

    win_copy(tiles, 0).start()

    @pl.loop(0, tiles)
    def _(i):
        here = lanes(i, GROUP)
        pre_grad = r.stepg_s[pl.ds(0, rows), here] * sigmoid(r.pre[:, here])
        gvec[pl.ds(at.dt_b, 1), here] = jnp.sum(pre_grad, axis=0, keepdims=True)
        r.prelow_s[:, here] = pre_grad.astype(BF16)
        r.dx_s[:, here] = r.pad[:, here].astype(F32)

    small_grad = (
        dot(r.prelow_s[...], r.dtw_s[...], NT)
        + gather_back(r.pin_s[...], rank, states, at.small)
        + gather_back(r.pout_s[...], rank + states, states, at.small)
    ).astype(BF16)

    @pl.loop(0, tiles)
    def _(i):
        here = lanes(i, GROUP)
        r.full_s[pl.ds(at.dt, rank), here] = dot(
            small_low, r.prelow_s[:, here], TN
        )[:rank]
        r.full_s[pl.ds(0, at.small), here] = dot(small_grad, r.act[:, here], TN)
        act_grad = r.sg_s[:, here] + dot(small_grad, r.sw[pl.ds(0, at.small), here])
        total = r.vec_s[pl.ds(at.conv_b, 1), here]
        for k in range(taps):
            total = (
                total
                + r.vec_s[pl.ds(at.conv + k, 1), here]
                * r.dx_s[pl.ds(HALO - taps + 1 + k, rows), here]
            )
        sig = sigmoid(total)
        conv_grad = act_grad * sig * (1.0 + total * (1.0 - sig))
        r.stepg_s[pl.ds(0, rows), here] = conv_grad
        gvec[pl.ds(at.conv_b, 1), here] = jnp.sum(conv_grad, axis=0, keepdims=True)
        for k in range(taps):
            gvec[pl.ds(at.conv + k, 1), here] = jnp.sum(
                conv_grad * r.dx_s[pl.ds(HALO - taps + 1 + k, rows), here],
                axis=0,
                keepdims=True,
            )

    def edge():
        return pltpu.make_async_remote_copy(
            r.stepg_s.at[pl.ds(0, 8)],
            r.halo_s,
            r.halo_sem.at[0],
            r.halo_sem.at[1],
            device_id=(ctx, jnp.maximum(me - 1, 0)),
            device_id_type=MESH,
        )

    @pl.when(me > 0)
    def _():
        edge().start()

    weave(pace)
    in_shape = r.stage_in.shape[1:]

    def project(i, turn):
        here = lanes(i, GROUP)
        slot = lax.rem(turn, 2)
        copy = pltpu.make_async_copy(
            r.stage_in.at[slot], block_of(r.gin, i), r.in_sem.at[slot]
        )
        following = lax.rem(i + 1, 2 * tiles)

        @pl.when(turn + 1 < 2 * tiles)
        def _():
            win_copy(following, 1 - slot).start()

        @pl.when(turn >= 2)
        def _():
            copy.wait()

        r.stage_in[slot] = (
            dot(r.pb_s[:, here], r.normed_s[...], TN).astype(BF16).reshape(in_shape)
        )
        copy.start()
        win_copy(i, slot).wait()
        part = dot(r.pb_s[:, here], r.win_s[slot].reshape(GROUP, width))

        @pl.when(turn == 0)
        def _():
            r.nsg[...] = part

        @pl.when(turn > 0)
        def _():
            r.nsg[...] += part

    @pl.loop(0, tiles)
    def _(i):
        project(i + tiles, i)

    weave(pace)

    @pl.when(me < count - 1)
    def _():
        edge().wait_recv()

    @pl.when(me == count - 1)
    def _():
        r.halo_s[...] = jnp.zeros_like(r.halo_s)

    @pl.when(me > 0)
    def _():
        edge().wait_send()

    r.stepg_s[pl.ds(rows, 8), :] = r.halo_s[...]

    @pl.loop(0, tiles)
    def _(i):
        here = lanes(i, GROUP)
        total = jnp.zeros((rows, GROUP), F32)
        for k in range(taps):
            total = (
                total
                + r.vec_s[pl.ds(at.conv + k, 1), here]
                * r.stepg_s[pl.ds(taps - 1 - k, rows), here]
            )
        r.pb_s[:, here] = total.astype(BF16)
        project(i, i + tiles)

    stream = r.stream[...]
    scale = lax.rsqrt(jnp.mean(stream * stream, axis=1, keepdims=True) + EPS)
    normed_grad = r.nsg[...]
    gain_grad = jnp.sum(normed_grad * stream * scale, axis=0, keepdims=True)
    gain_grad = jnp.broadcast_to(gain_grad, (8, width)).astype(BF16)
    pick = gain_pick(channels)
    for i in range(inner // 256):
        wide = dot(gain_grad[:, 128 * i : 128 * i + 128], pick, NT)
        gvec[pl.ds(at.gain, 1), pl.ds(256 * i, 256)] = wide[:1]
    for k in range(at.count, at.rows):
        r.full_s[pl.ds(k, 1), :] = jnp.zeros((1, inner), F32)
    if mode == "given":
        r.gsmall[...] = r.full_s[...]
    elif mode == "last":
        split_small(channels, r.full_s, r.gsmall)
    else:
        split_small(channels, r.full_s, Folded(r.gsmall_s))
        small_copy = pltpu.make_async_copy(r.gsmall_s, r.gsmall_hbm, r.small_sem.at[0])
        small_copy.start()
    scaled = normed_grad * gain
    inner_sum = jnp.mean(scaled * stream, axis=1, keepdims=True)
    r.nsg[...] = (
        r.sgrad[...] + scale * scaled - stream * (scale * scale * scale) * inner_sum
    )
    for slot in range(2):
        pltpu.make_async_copy(
            r.stage_in.at[slot], block_of(r.gin, 0), r.in_sem.at[slot]
        ).wait()
    weave(len(queue))
    if mode == "first":
        small_copy.wait()
        reduce.finish()
        for partner in square_partners(depth):
            signal(r.ready_sem, partner)
        pl.semaphore_wait(r.ready_sem, len(square_partners(depth)))
        for item in own_items:
            reduce.begin(item)
        for turn in reduce.turns(own_items):
            turn()
    if mode != "given":
        reduce.finish()
    each(0, me, lambda j: sums(j, me).wait_send())
    for g in range(groups):
        each(0, me, lambda j: ends(g, j, me).wait_send())


def in_vmem(count):
    return [pl.BlockSpec(memory_space=pltpu.VMEM)] * count


def in_any(count):
    return [pl.BlockSpec(memory_space=pl.ANY)] * count


def forward_call(cfg, mode, stream, operands):
    rows, inner, states, taps, rank, count, channels = cfg
    at = Names(states, taps, rank)
    width = stream.shape[1]
    groups = inner // GROUP
    devices = inner // channels
    shape = jax.ShapeDtypeStruct
    dma = pltpu.SemaphoreType.DMA
    vmem, any_space = in_vmem(1)[0], in_any(1)[0]
    inputs = [("stream", stream, vmem)]
    for name, array in operands:
        inputs.append((name, array, vmem if name == "sw" else any_space))
    outputs = [
        ("new", shape(stream.shape, F32), vmem),
        ("pad", shape((rows + HALO, inner), BF16), vmem),
        ("gate", shape((rows, inner), F32), vmem),
        ("act", shape((rows, inner), BF16), vmem),
        ("sp", shape((rows, at.small), F32), vmem),
        ("pre", shape((rows, inner), F32), vmem),
        ("h_hbm", shape(((rows + 1) * states, inner), BF16), any_space),
        ("y", shape((rows, inner), F32), vmem),
        ("mixed", shape((rows, inner), BF16), vmem),
    ]
    if mode == "given":
        given = dict(operands)
        in_shape, out_shape = given["win_hbm"].shape, given["wout_hbm"].shape
    else:
        in_shape = (devices, 2 * inner // devices, width)
        out_shape = (devices, width // devices, inner)
        small_shape = (devices, at.rows * channels // 128, 128)
        outputs.append(("sw", shape((at.rows, inner), BF16), vmem))
        outputs.append(("wout_all", shape(out_shape, BF16), any_space))
    if mode == "first":
        outputs.append(("win_all", shape(in_shape, BF16), any_space))
        outputs.append(("win2_all", shape(in_shape, BF16), any_space))
        outputs.append(("gsm2_all", shape(small_shape, BF16), any_space))
    scratch = [
        ("win_s", pltpu.VMEM(in_shape, BF16)),
        ("wout_s", pltpu.VMEM(out_shape, BF16)),
        ("vec_s", pltpu.VMEM((at.rows - at.vec, inner), F32)),
        ("dtw_s", pltpu.VMEM((at.small, inner), BF16)),
        ("normed_s", pltpu.VMEM(stream.shape, BF16)),
        ("padf_s", pltpu.VMEM((rows + HALO, inner), F32)),
        ("halo_s", pltpu.VMEM((HALO, inner), BF16)),
        ("dt_s", pltpu.VMEM((rows, inner), F32)),
        ("dx_s", pltpu.VMEM((rows, inner), F32)),
        ("bb_s", pltpu.VMEM((rows, states, 128), F32)),
        ("cd_s", pltpu.VMEM((rows, CHUNK * states), BF16)),
        ("hs", pltpu.VMEM(((rows + 1) * states, inner), BF16)),
        ("own_sum", pltpu.VMEM((8, inner // 8), F32)),
        ("sum_s", pltpu.VMEM((count, 8, inner // 8), F32)),
        ("own_end", pltpu.VMEM((states, inner), BF16)),
        ("end_s", pltpu.VMEM((count, states, inner), BF16)),
        ("halo_sem", dma((2,))),
        ("sum_send", dma((count,))),
        ("sum_recv", dma((count,))),
        ("end_send", dma((groups, count))),
        ("end_recv", dma((groups, count))),
        ("h_sem", dma((groups,))),
        ("load_sem", dma((3,))),
    ]
    if mode != "given":
        pieces = 8 if mode == "first" else 2
        scratch += [
            ("gsm_s", pltpu.VMEM(small_shape, BF16)),
            ("own_sem", dma((pieces,))),
            ("send_sem", dma((pieces, Gather.sends(count // 2)))),
            ("recv_sem", dma((pieces, devices))),
            ("store_sem", dma((2,))),
        ]
    names = [entry[0] for entry in inputs + outputs + scratch]
    results = pl.pallas_call(
        functools.partial(forward_kernel, cfg, mode, names),
        out_shape=tuple(entry[1] for entry in outputs),
        in_specs=[entry[2] for entry in inputs],
        out_specs=tuple(entry[2] for entry in outputs),
        scratch_shapes=[entry[1] for entry in scratch],
        compiler_params=pltpu.CompilerParams(
            collective_id={"given": 0, "first": 4, "later": 5}[mode],
            has_side_effects=True,
            vmem_limit_bytes=VMEM_BYTES,
        ),
        name="forward_" + mode,
    )(*[entry[1] for entry in inputs])
    return {entry[0]: result for entry, result in zip(outputs, results)}


def backward_call(cfg, mode, sgrad, stream, weights, saved, later):
    rows, inner, states, taps, rank, count, channels = cfg
    at = Names(states, taps, rank)
    width = stream.shape[1]
    groups = inner // GROUP
    wide = CHUNK * states
    depth = count // 2
    sw, win, wout = weights
    shape = jax.ShapeDtypeStruct
    dma = pltpu.SemaphoreType.DMA
    vmem, any_space = in_vmem(1)[0], in_any(1)[0]
    in_rows, out_rows = win.shape[1], wout.shape[1]
    lead = (1, 1, win.shape[0] // 2, 2) if mode == "given" else (2, 2, depth, 2)
    small_rows = at.rows * channels // 128
    inputs = [
        ("sgrad", sgrad, vmem),
        ("stream", stream, vmem),
        ("sw", sw, vmem),
        ("win", win, any_space),
        ("wout", wout, any_space),
    ]
    for name in ("pad", "act", "sp", "pre", "mixed"):
        inputs.append((name, saved[name], vmem))
    for name in ("gate", "y", "h_hbm"):
        inputs.append((name, saved[name], any_space))
    outputs = [
        ("nsg", shape((rows, width), F32), vmem),
        ("gin", shape(lead + (in_rows, width), BF16), any_space),
        ("gout", shape(lead + (out_rows, inner), BF16), any_space),
    ]
    scratch = [
        ("full_s", pltpu.VMEM((at.rows, inner), F32)),
        ("vec_s", pltpu.VMEM((at.rows - at.vec, inner), F32)),
        ("dtw_s", pltpu.VMEM((at.small, inner), BF16)),
        ("hb", pltpu.VMEM((2, (rows // 2 + 1) * states, GROUP), BF16)),
        ("normed_s", pltpu.VMEM((rows, width), BF16)),
        ("low_s", pltpu.VMEM((rows, width), BF16)),
        ("sg_s", pltpu.VMEM((rows, inner), F32)),
        ("dt_s", pltpu.VMEM((rows, inner), F32)),
        ("dx_s", pltpu.VMEM((rows + HALO, inner), F32)),
        ("stepg_s", pltpu.VMEM((rows + 8, inner), F32)),
        ("pb_s", pltpu.VMEM((rows, 2 * inner), BF16)),
        ("cb_s", pltpu.VMEM((rows, states, 128), F32)),
        ("bd_s", pltpu.VMEM((rows, wide), BF16)),
        ("ab_s", pltpu.VMEM((wide, GROUP), BF16)),
        ("rb_s", pltpu.VMEM((wide, GROUP), BF16)),
        ("pin_s", pltpu.VMEM((rows, wide), F32)),
        ("pout_s", pltpu.VMEM((rows, wide), F32)),
        ("prelow_s", pltpu.VMEM((rows, inner), BF16)),
        ("stage_in", pltpu.VMEM((2, 2, 2, in_rows, width), BF16)),
        ("stage_out", pltpu.VMEM((2, 2, 2, out_rows, inner), BF16)),
        ("win_s", pltpu.VMEM((2, GROUP // in_rows, in_rows, width), BF16)),
        ("wout_s", pltpu.VMEM((2,) + wout.shape[:2] + (GROUP,), BF16)),
        ("gate_s", pltpu.VMEM((2, 2, rows, GROUP), F32)),
        ("halo_s", pltpu.VMEM((8, inner), F32)),
        ("own_sum", pltpu.VMEM((8, inner // 8), F32)),
        ("sum_s", pltpu.VMEM((count, 8, inner // 8), F32)),
        ("own_end", pltpu.VMEM((states, inner), BF16)),
        ("end_s", pltpu.VMEM((count, states, inner), BF16)),
        ("halo_sem", dma((2,))),
        ("sum_send", dma((count,))),
        ("sum_recv", dma((count,))),
        ("end_send", dma((groups, count))),
        ("end_recv", dma((groups, count))),
        ("h_sem", dma((2,))),
        ("in_sem", dma((2,))),
        ("out_sem", dma((2,))),
        ("win_sem", dma((2,))),
        ("wout_sem", dma((2,))),
        ("gate_sem", dma((2, 2))),
    ]
    if mode == "given":
        outputs.append(("gsmall", shape((at.rows, inner), F32), vmem))
    else:
        outputs.append(("sum_out", shape((out_rows, inner), F32), vmem))
        held = [("rout", out_rows // 2, inner, 2)]
        pieces = 2
        if mode == "last":
            small_shape = (inner // channels, small_rows, 128)
            outputs.append(("gsmall", shape(small_shape, BF16), vmem))
        else:
            inputs.append(("next_gin", later["gin"], any_space))
            small = later["gsmall"].reshape(lead + (small_rows, 128))
            inputs.append(("next_gsmall", small, any_space))
            outputs.append(("gsmall_hbm", shape(small.shape, BF16), any_space))
            scratch.append(("gsmall_s", pltpu.VMEM(small.shape, BF16)))
            for name in ("sum_in", "sum_next_in"):
                outputs.append((name, shape((in_rows, width), F32), vmem))
            for name in ("sum_small", "sum_next_small"):
                outputs.append((name, shape((small_rows, 128), F32), vmem))
            held.append(("rin", in_rows // 2, width, 2))
            held.append(("rsmall", small_rows, 128, 1))
            scratch.append(("small_sem", dma((1,))))
            scratch.append(("ready_sem", pltpu.SemaphoreType.REGULAR))
            pieces = 8
        for name, piece, wide_by, cuts in held:
            for k in range(cuts):
                for part, buffer in enumerate(Reduce.buffers_of(depth, piece, wide_by)):
                    scratch.append((f"{name}{k}_{part}", buffer))
        scratch += [
            ("own_sem", dma((pieces, 2))),
            ("send_sem", dma((pieces, 4, depth))),
            ("recv_sem", dma((pieces, 4, depth))),
        ]
    names = [entry[0] for entry in inputs + outputs + scratch]
    results = pl.pallas_call(
        functools.partial(backward_kernel, cfg, mode, names),
        out_shape=tuple(entry[1] for entry in outputs),
        in_specs=[entry[2] for entry in inputs],
        out_specs=tuple(entry[2] for entry in outputs),
        scratch_shapes=[entry[1] for entry in scratch],
        compiler_params=pltpu.CompilerParams(
            collective_id={"given": 1, "last": 6, "first": 7}[mode],
            has_side_effects=True,
            vmem_limit_bytes=VMEM_BYTES,
        ),
        name="backward_" + mode,
    )(*[entry[1] for entry in inputs])
    return {entry[0]: result for entry, result in zip(outputs, results)}


def on_device(
    mesh,
    hidden_in,
    cotangent,
    norm_gain,
    in_weight,
    conv_weight,
    conv_bias,
    x_weight,
    dt_weight,
    dt_bias,
    a_log,
    skip_gain,
    out_weight,
):
    layers = norm_gain.shape[0]
    rows, width = hidden_in.shape
    taps, channels = conv_weight.shape[1:]
    states = a_log.shape[2]
    rank = dt_weight.shape[1]
    devices, count = mesh.shape["ctx"] * mesh.shape["seq"], mesh.shape["seq"]
    inner = channels * devices
    gains = norm_gain.shape[1]
    at = Names(states, taps, rank)
    cfg = (rows, inner, states, taps, rank, count, channels)
    depth = count // 2
    by_kernel = (
        mesh.shape["ctx"] == 4
        and depth % 2 == 0
        and layers == 2
        and in_weight.shape[2] % 32 == 0
        and out_weight.shape[2] % 32 == 0
        and 128 % channels == 0
        and at.rows * channels // 128 % 16 == 0
    )

    def pack(layer):
        by_row = jnp.concatenate(
            [
                x_weight[layer].T,
                dt_weight[layer],
                a_log[layer].T,
                conv_weight[layer],
                conv_bias[layer][None],
                dt_bias[layer][None],
                skip_gain[layer][None],
                jnp.pad(norm_gain[layer], (0, channels - gains))[None],
            ],
            0,
        )
        by_row = jnp.pad(by_row, ((0, at.rows - at.count), (0, 0)))
        if by_kernel:
            folds = by_row.reshape(128 // channels, -1, channels)
            by_row = jnp.concatenate(list(folds), 1)
        return by_row

    local = [
        (in_weight[layer].T, out_weight[layer].T, pack(layer))
        for layer in range(layers)
    ]
    stream = hidden_in.astype(F32)
    streams, runs, weights = [], [], []
    if by_kernel:
        (in0, out0, small0), (in1, out1, small1) = local
        operands = [
            ("own_in", in0),
            ("own_small", small0),
            ("own_out", out0),
            ("next_in", in1),
            ("next_small", small1),
        ]
        first = forward_call(cfg, "first", stream, operands)
        operands = [
            ("win_hbm", first["win2_all"]),
            ("gsm_hbm", first["gsm2_all"]),
            ("own_out", out1),
        ]
        second = forward_call(cfg, "later", first["new"], operands)
        runs = [first, second]
        wins = [first["win_all"], first["win2_all"]]
        weights = [
            (run["sw"], win, run["wout_all"]) for run, win in zip(runs, wins)
        ]
        streams = [stream, first["new"]]
        stream = second["new"]
    else:
        for w_in, w_out, w_small in local:
            w_in = lax.all_gather(w_in, ("ctx", "seq"), axis=0, tiled=True)
            w_out = lax.all_gather(w_out, ("ctx", "seq"), axis=0, tiled=True)
            sw = lax.all_gather(w_small, ("ctx", "seq"), axis=1, tiled=True)
            w_in = w_in.reshape(-1, 128, width)
            w_out = w_out.reshape(-1, 32, inner)
            operands = [("win_hbm", w_in), ("sw", sw), ("wout_hbm", w_out)]
            run = forward_call(cfg, "given", stream, operands)
            runs.append(run)
            weights.append((sw, w_in, w_out))
            streams.append(stream)
            stream = run["new"]
    stream_grad = cotangent.astype(F32)
    summed = [None] * layers
    if by_kernel:
        last = backward_call(
            cfg, "last", stream_grad, streams[1], weights[1], runs[1], None
        )
        head = backward_call(
            cfg, "first", last["nsg"], streams[0], weights[0], runs[0], last
        )
        stream_grad = head["nsg"]

        def unfold(small):
            small = small.reshape(-1, 128 // channels, channels)
            return small.transpose(1, 0, 2).reshape(at.rows, channels)

        summed = [
            (head["sum_in"], head["sum_out"], unfold(head["sum_small"])),
            (head["sum_next_in"], last["sum_out"], unfold(head["sum_next_small"])),
        ]
    else:
        for layer in reversed(range(layers)):
            run = backward_call(
                cfg,
                "given",
                stream_grad,
                streams[layer],
                weights[layer],
                runs[layer],
                None,
            )
            stream_grad = run["nsg"]
            summed[layer] = [
                lax.psum_scatter(
                    array.astype(F32),
                    ("ctx", "seq"),
                    scatter_dimension=dim,
                    tiled=True,
                )
                for array, dim in (
                    (run["gin"].reshape(-1, width), 0),
                    (run["gout"].reshape(-1, inner), 0),
                    (run["gsmall"], 1),
                )
            ]
    grads = [None] * layers
    for layer in range(layers):
        s_in, s_out, s_small = summed[layer]
        s_x = s_small[: at.small, :channels]
        s_dt = s_small[at.dt : at.dt + rank, :channels]
        s_vec = s_small[at.vec : at.count, :channels]
        grads[layer] = (
            s_vec[at.gain, :gains],
            s_in.T,
            s_vec[at.conv : at.conv + taps],
            s_vec[at.conv_b],
            s_x.T,
            s_dt,
            s_vec[at.dt_b],
            s_vec[:states].T,
            s_vec[at.skip],
            s_out.T,
        )
    stacked = tuple(
        jnp.stack([grads[layer][member] for layer in range(layers)], 0)
        for member in range(10)
    )
    return (stream.astype(BF16), stream_grad) + stacked


def solution(mesh):
    split = ("ctx", "seq")
    tokens, last = P(split, None), P(None, split)
    middle, third = P(None, split, None), P(None, None, split)
    weights = (last, third, third, last, middle, third, last, middle, last, third)
    return jax.shard_map(
        functools.partial(on_device, mesh),
        mesh=mesh,
        in_specs=(tokens, tokens) + weights,
        out_specs=(tokens, tokens) + weights,
        check_vma=False,
    )
```

```python
import collections
import functools
import types

import jax
import jax.numpy as jnp
from jax import lax
from jax.experimental import pallas as pl
from jax.experimental.pallas import tpu as pltpu
from jax.sharding import PartitionSpec as P

EPS = 1e-05
LOG2E = 1.4426950408889634
MESH = pl.DeviceIdType.MESH
F32, BF16 = jnp.float32, jnp.bfloat16
NT = (((1,), (1,)), ((), ()))
TN = (((0,), (0,)), ((), ()))
VMEM_BYTES = 63 * 2**20
CHUNK = 16
GROUP = 512
HALO = 16


def dot(a, b, dims=None):
    if dims is None:
        dims = (((1,), (0,)), ((), ()))
    return lax.dot_general(a, b, dims, preferred_element_type=F32)


def lanes(index, width):
    return pl.ds(pl.multiple_of(index * width, width), width)


def widen(tile, width):
    times = width // tile.shape[1]
    return jnp.concatenate([tile] * times, axis=1) if times > 1 else tile


def softplus(v):
    return jnp.maximum(v, 0.0) + jnp.log1p(jnp.exp(-jnp.abs(v)))


def sigmoid(v):
    return 1.0 / (1.0 + jnp.exp(-v))


def keep_sum(own_sum, i, step):
    total = jnp.sum(step, axis=0, keepdims=True)
    fold = own_sum.shape[1]
    for part in range(GROUP // fold):
        row = i * (GROUP // fold) + part
        own_sum[pl.ds(row, 1), :] = total[:, part * fold : (part + 1) * fold]


def sum_of(sum_s, j, g):
    fold = sum_s.shape[2]
    each = GROUP // fold
    return jnp.concatenate(
        [sum_s[j, pl.ds(g * each + part, 1), :] for part in range(each)], 1
    )


def chunk_mask(rows, states):
    wide = CHUNK * states
    token = lax.rem(lax.broadcasted_iota(jnp.int32, (rows, wide), 0), CHUNK)
    owner = lax.broadcasted_iota(jnp.int32, (rows, wide), 1) // states
    return token == owner


def spread(small_low, first, states):
    wide = CHUNK * states
    row = lax.broadcasted_iota(jnp.int32, (small_low.shape[1], wide), 0)
    col = lax.broadcasted_iota(jnp.int32, (small_low.shape[1], wide), 1)
    pick = (row == first + lax.rem(col, states)).astype(F32).astype(BF16)
    tiled = dot(small_low, pick)
    return jnp.where(chunk_mask(small_low.shape[0], states), tiled, 0.0).astype(BF16)


def gather_back(partial, first, states, width):
    wide = CHUNK * states
    row = lax.broadcasted_iota(jnp.int32, (wide, width), 0)
    col = lax.broadcasted_iota(jnp.int32, (wide, width), 1)
    pick = (col == first + lax.rem(row, states)).astype(F32).astype(BF16)
    kept = jnp.where(chunk_mask(partial.shape[0], states), partial, 0.0)
    return dot(kept.astype(BF16), pick)


class Names:
    def __init__(self, states, taps, rank):
        self.small = rank + 2 * states
        self.dt = self.small
        self.vec = self.small + rank
        self.count = self.vec + states + taps + 4
        self.rows = -(-self.count // 16) * 16
        self.conv = states
        self.conv_b = states + taps
        self.dt_b = states + taps + 1
        self.skip = states + taps + 2
        self.gain = states + taps + 3


def load_small(at, sw_ref, vec_s, dtw_s):
    states, rank = at.conv, at.vec - at.dt
    vec_s[...] = sw_ref[pl.ds(at.vec, at.rows - at.vec), :].astype(F32)
    vec_s[pl.ds(0, states), :] = -jnp.exp(vec_s[pl.ds(0, states), :])
    dtw_s[pl.ds(0, rank), :] = sw_ref[pl.ds(at.dt, rank), :]
    dtw_s[pl.ds(rank, at.small - rank), :] = jnp.zeros(
        (at.small - rank, dtw_s.shape[1]), BF16
    )


def gain_pick(channels):
    gains = channels // 2
    row = lax.broadcasted_iota(jnp.int32, (256, 128), 0)
    col = lax.broadcasted_iota(jnp.int32, (256, 128), 1)
    place = lax.div(col, gains) * channels + lax.rem(col, gains)
    return (row == place).astype(F32).astype(BF16)


def gain_row(at, channels, vec_s):
    pick = gain_pick(channels)
    row = vec_s[pl.ds(at.gain // 8 * 8, 8), :].astype(BF16)
    tiles = [
        dot(row[:, 256 * i : 256 * i + 256], pick) for i in range(row.shape[1] // 256)
    ]
    gain = jnp.concatenate(tiles, 1)
    return gain[at.gain % 8 : at.gain % 8 + 1]


def merge_small(channels, blocks, sw_ref):
    each = 128 // channels
    rows = blocks.shape[1]
    owner = lax.div(lax.broadcasted_iota(jnp.int32, (rows, 128), 1), channels)

    @pl.loop(0, sw_ref.shape[1] // 128)
    def _(j):
        held = [blocks[j * each + part].astype(F32) for part in range(each)]
        for fold in range(each):
            tile = None
            for part in range(each):
                shift = (part - fold) * channels % 128
                moved = pltpu.roll(held[part], shift, 1) if shift else held[part]
                tile = moved if tile is None else jnp.where(owner == part, moved, tile)
            sw_ref[pl.ds(fold * rows, rows), lanes(j, 128)] = tile.astype(BF16)


def split(number, by):
    if isinstance(number, int):
        return divmod(number, by)
    return lax.div(number, by), lax.rem(number, by)


class Folded:
    def __init__(self, ref):
        self.ref, self.shape = ref, ref.shape[3:]

    def __setitem__(self, block, value):
        _, x, z, core = self.ref.shape[:4]
        row = lax.div(block, z * core)
        self.ref[
            lax.div(row, x), lax.rem(row, x), lax.rem(lax.div(block, core), z), lax.rem(block, core)
        ] = value


def split_small(channels, full_ref, blocks):
    each = 128 // channels
    rows = blocks.shape[1]
    owner = lax.div(lax.broadcasted_iota(jnp.int32, (rows, 128), 1), channels)

    @pl.loop(0, full_ref.shape[1] // 128)
    def _(j):
        held = [
            full_ref[pl.ds(fold * rows, rows), lanes(j, 128)] for fold in range(each)
        ]
        for part in range(each):
            tile = None
            for fold in range(each):
                shift = (fold - part) * channels % 128
                moved = pltpu.roll(held[fold], shift, 1) if shift else held[fold]
                tile = moved if tile is None else jnp.where(owner == fold, moved, tile)
            blocks[j * each + part] = tile.astype(BF16)


def places():
    ctx, seq = lax.axis_index("ctx"), lax.axis_index("seq")
    return lax.div(ctx, 2), lax.rem(ctx, 2), lax.div(seq, 2), lax.rem(seq, 2)


def device(y, x, z, core):
    return (2 * y + x, 2 * z + core)


def square_partners(depth):
    y, x, z, core = places()
    partners = [device(y, x, z, 1 - core), device(y, 1 - x, z, core)]
    partners.append(device(1 - y, x, z, core))
    for step in range(1, depth):
        partners.append(device(y, x, lax.rem(z + step, depth), core))
    return partners


def greet_square(depth):
    barrier = pltpu.get_barrier_semaphore()
    partners = square_partners(depth)
    for partner in partners:
        pl.semaphore_signal(barrier, inc=1, device_id=partner, device_id_type=MESH)
    pl.semaphore_wait(barrier, len(partners))


class Gather:
    def __init__(self, depth, pieces, own_sem, send_sem, recv_sem):
        self.depth, self.pieces = depth, pieces
        self.own_sem, self.send_sem, self.recv_sem = own_sem, send_sem, recv_sem
        self.y, self.x, self.z, self.core = places()
        self.used = [0] * len(pieces)
        self.sent = []
        turn = 1 - 2 * lax.div(self.z, max(depth // 2, 1))
        self.line = [
            lax.rem(self.z + turn * step + depth, depth) for step in range(depth)
        ]
        y, x, z, core = self.y, self.x, self.z, self.core
        self.x_side, self.y_side = device(y, 1 - x, z, core), device(1 - y, x, z, core)
        self.sibling = device(y, x, z, 1 - core)

    @staticmethod
    def sends(depth):
        return 3 + depth - 1 + 3 * (depth - 1) + 2 * depth + 2 * depth

    def slot(self, y, x, z, core):
        return ((2 * y + x) * self.depth + z) * 2 + core

    def span(self, item, slot):
        _, whole, first, rows, _ = self.pieces[item]
        return whole.at[slot, pl.ds(first, rows)]

    def send(self, item, slot, to, own=False):
        local, _, first, rows, _ = self.pieces[item]
        copy = pltpu.make_async_remote_copy(
            local.at[pl.ds(first, rows)] if own else self.span(item, slot),
            self.span(item, slot),
            self.send_sem.at[item, self.used[item]],
            self.recv_sem.at[item, slot],
            device_id=to,
            device_id_type=MESH,
        )
        self.used[item] += 1
        copy.start()
        self.sent.append(copy)

    def arrive(self, item, slot):
        pltpu.make_async_remote_copy(
            self.span(item, slot),
            self.span(item, slot),
            self.send_sem.at[item, 0],
            self.recv_sem.at[item, slot],
            device_id=self.sibling,
            device_id_type=MESH,
        ).wait_recv()

    def own_copy(self, item):
        local, _, first, rows, _ = self.pieces[item]
        mine = self.slot(self.y, self.x, self.z, self.core)
        return pltpu.make_async_copy(
            local.at[pl.ds(first, rows)], self.span(item, mine), self.own_sem.at[item]
        )

    def begin(self, item):
        mine = self.slot(self.y, self.x, self.z, self.core)
        self.own_copy(item).start()
        for to in (self.x_side, self.y_side):
            self.send(item, mine, to, own=True)
        for step in range(1, self.depth):
            to = device(self.y, self.x, self.line[step], self.core)
            self.send(item, mine, to, own=True)
        self.send(item, mine, self.sibling, own=True)

    def along(self, item, step):
        slot = self.slot(self.y, self.x, self.line[step], self.core)
        self.arrive(item, slot)
        for to in (self.x_side, self.y_side, self.sibling):
            self.send(item, slot, to)

    def near(self, item, step):
        if self.pieces[item][4]:
            slot = self.slot(self.y, 1 - self.x, self.line[step], self.core)
            to = self.y_side
        else:
            slot = self.slot(1 - self.y, self.x, self.line[step], self.core)
            to = self.x_side
        self.arrive(item, slot)
        self.send(item, slot, to)
        self.send(item, slot, self.sibling)

    def far(self, item, step, other):
        y, x = 1 - self.y, 1 - self.x
        if self.pieces[item][4]:
            x = x if other else self.x
        else:
            y = y if other else self.y
        slot = self.slot(y, x, self.line[step], self.core)
        self.arrive(item, slot)
        self.send(item, slot, self.sibling)

    def settle(self, item):
        self.own_copy(item).wait()
        for step in range(self.depth):
            for y in (self.y, 1 - self.y):
                for x in (self.x, 1 - self.x):
                    self.arrive(item, self.slot(y, x, self.line[step], 1 - self.core))

    def turns(self, items):
        order = [("near", 0)]
        for step in range(1, self.depth):
            order.append(("along", step))
            order.append(("near", step))
            if step >= 2:
                order.append(("far", step - 2, 1))
            order.append(("far", step - 1, 0))
        for step in range(max(self.depth - 2, 0), self.depth):
            if step == self.depth - 1:
                order.append(("far", step, 0))
            order.append(("far", step, 1))
        actions = []
        for name, *rest in order:
            for item in items:
                actions.append(functools.partial(getattr(self, name), item, *rest))
        return actions

    def finish(self):
        for copy in self.sent:
            copy.wait_send()


class Reduce:
    def __init__(self, depth, pieces, buffers, own_sem, send_sem, recv_sem):
        self.depth, self.pieces, self.buffers = depth, pieces, buffers
        self.own_sem, self.send_sem, self.recv_sem = own_sem, send_sem, recv_sem
        y, x, z, core = places()
        self.y, self.x, self.core = y, x, core
        self.line = [lax.rem(z + step + 1, depth) for step in range(depth)]
        self.x_side, self.y_side = device(y, 1 - x, z, core), device(1 - y, x, z, core)
        self.sibling = device(y, x, z, 1 - core)
        self.along = [device(y, x, there, core) for there in self.line]
        self.sent = []

    @staticmethod
    def buffers_of(depth, rows, width, sided=False):
        square, row = ((2,), ()) if sided else ((2, 2), (2,))
        leads = ((2,) + square, (depth,) + square, (depth,) + row, (depth,), (depth - 1,))
        return [pltpu.VMEM(lead + (rows, width), BF16) for lead in leads]

    def part_of(self, item, step, core):
        whole, _, first, rows, _, side = self.pieces[item]
        y = slice(None) if side is None else side
        return whole.at[y, :, self.line[step], core, pl.ds(first, rows)]

    def local(self, item, step):
        return pltpu.make_async_copy(
            self.part_of(item, step, self.core),
            self.buffers[item][0].at[step % 2],
            self.own_sem.at[item, step % 2],
        )

    def hop(self, stage, item, step):
        _, core_in, first_in, second_in, line_in = self.buffers[item]
        crosses_y, side = self.pieces[item][4:]
        y, x = self.y, self.x
        if stage == 0:
            source = self.part_of(item, step, 1 - self.core)
            target, to = core_in.at[step], self.sibling
        elif stage == 1:
            if side is not None:
                source = core_in.at[step, 1 - x]
            elif crosses_y:
                source = core_in.at[step, 1 - y]
            else:
                source = core_in.at[step, :, 1 - x]
            target, to = first_in.at[step], self.y_side if crosses_y else self.x_side
        elif stage == 2:
            if side is not None:
                source = first_in.at[step]
            else:
                source = first_in.at[step, 1 - x if crosses_y else 1 - y]
            target, to = second_in.at[step], self.x_side if crosses_y else self.y_side
        else:
            source, target, to = second_in.at[step], line_in.at[step], self.along[step]
        return pltpu.make_async_remote_copy(
            source,
            target,
            self.send_sem.at[item, stage, step],
            self.recv_sem.at[item, stage, step],
            device_id=to,
            device_id_type=MESH,
        )

    def when(self, stage, item, receives, act):
        side = self.pieces[item][5]
        if side is None or stage < 2:
            act()
        elif stage == 2 and not receives:
            pl.when(self.y != side)(act)
        else:
            pl.when(self.y == side)(act)

    def send(self, stage, item, step):
        copy = self.hop(stage, item, step)
        self.when(stage, item, False, copy.start)
        self.sent.append((stage, item, copy))

    @staticmethod
    def add(target, other, rows):
        @pl.loop(0, rows // 16)
        def _(k):
            here = pl.ds(pl.multiple_of(k * 16, 16), 16)
            target[here] = (
                target[here].astype(F32) + other[here].astype(F32)
            ).astype(BF16)

    def begin(self, item):
        for step in range(self.depth):
            self.send(0, item, step)
            if step < 2:
                self.local(item, step).start()

    def settle(self, stage, item, step):
        self.when(
            stage, item, True, functools.partial(self.receive, stage, item, step)
        )
        if stage < 2 or step < self.depth - 1:
            self.send(stage + 1, item, step)

    def receive(self, stage, item, step):
        own, core_in, first_in, second_in, _ = self.buffers[item]
        rows, crosses_y, side = self.pieces[item][3:]
        self.hop(stage, item, step).wait_recv()
        if stage == 0:
            self.local(item, step).wait()
            for x in (0, 1):
                if side is not None:
                    self.add(core_in.at[step, x], own.at[step % 2, x], rows)
                    continue
                for y in (0, 1):
                    self.add(core_in.at[step, y, x], own.at[step % 2, y, x], rows)
            if step + 2 < self.depth:
                self.local(item, step + 2).start()
        elif stage == 1:
            if side is not None:
                self.add(first_in.at[step], core_in.at[step, self.x], rows)
                return
            for far in (0, 1):
                kept = (
                    core_in.at[step, self.y, far]
                    if crosses_y
                    else core_in.at[step, far, self.x]
                )
                self.add(first_in.at[step, far], kept, rows)
        elif side is not None:
            self.add(second_in.at[step], first_in.at[step], rows)
        else:
            kept = first_in.at[step, self.x if crosses_y else self.y]
            self.add(second_in.at[step], kept, rows)

    def last(self, item):
        self.when(3, item, True, functools.partial(self.total, item))

    def total(self, item):
        _, out, first, rows, _, _ = self.pieces[item]
        second_in, line_in = self.buffers[item][3:]
        for step in range(self.depth - 1):
            self.hop(3, item, step).wait_recv()

        @pl.loop(0, rows // 16)
        def _(k):
            here = pl.ds(pl.multiple_of(k * 16, 16), 16)
            total = second_in[self.depth - 1, here].astype(F32)
            for step in range(self.depth - 1):
                total = total + line_in[step, here].astype(F32)
            out[pl.ds(pl.multiple_of(first + k * 16, 16), 16)] = total

    def turns(self, items):
        actions = []
        for turn in range(self.depth + 2):
            for stage in range(3):
                step = turn - stage
                if 0 <= step < self.depth:
                    for item in items:
                        actions.append(
                            functools.partial(self.settle, stage, item, step)
                        )
        for item in items:
            actions.append(functools.partial(self.last, item))
        return actions

    def finish(self):
        for stage, item, copy in self.sent:
            self.when(stage, item, False, copy.wait_send)
        self.sent = []


def chain(count, me, ctx, own_sum, sum_s, own_end, end_s, sems):
    sum_send, sum_recv, end_send, end_recv = sems

    def sums(j, slot):
        return pltpu.make_async_remote_copy(
            own_sum,
            sum_s.at[slot],
            sum_send.at[j],
            sum_recv.at[slot],
            device_id=(ctx, j),
            device_id_type=MESH,
        )

    def ends(g, j, slot):
        return pltpu.make_async_remote_copy(
            own_end.at[:, pl.ds(g * GROUP, GROUP)],
            end_s.at[slot, :, pl.ds(g * GROUP, GROUP)],
            end_send.at[g, j],
            end_recv.at[g, slot],
            device_id=(ctx, j),
            device_id_type=MESH,
        )

    return sums, ends


def each(first, last, act):
    def body(j, _):
        act(j)
        return 0

    lax.fori_loop(first, last, body, 0)


def forward_kernel(cfg, mode, names, *refs):
    r = types.SimpleNamespace(**dict(zip(names, refs)))
    rows, inner, states, taps, rank, count, channels = cfg
    at = Names(states, taps, rank)
    ctx, me = lax.axis_index("ctx"), lax.axis_index("seq")
    groups, steps, tiles = inner // GROUP, rows // CHUNK, inner // GROUP
    depth = count // 2
    width = r.stream.shape[1]
    barrier = pltpu.get_barrier_semaphore()

    def greet(to):
        pl.semaphore_signal(barrier, inc=1, device_id=to, device_id_type=MESH)

    queue = collections.deque()

    def weave(times):
        for _ in range(min(times, len(queue))):
            queue.popleft()()

    if mode == "given":
        each(0, me, lambda j: greet((ctx, j)))
    else:
        each(0, me, lambda j: greet((ctx, j)))
        each(me + 1, count, lambda j: greet((ctx, j)))
        y, x, z, core = places()
        greet(device(y, 1 - x, z, core))
        greet(device(1 - y, x, z, core))

    if mode != "first":
        half = r.win_hbm.shape[0] // 2
        halves = [
            pltpu.make_async_copy(
                r.win_hbm.at[pl.ds(k * half, half)],
                r.win_s.at[pl.ds(k * half, half)],
                r.load_sem.at[k],
            )
            for k in range(2)
        ]
        if mode == "later":
            small_copy = pltpu.make_async_copy(r.gsm_hbm, r.gsm_s, r.load_sem.at[2])
            small_copy.start()
        for copy in halves:
            copy.start()
    if mode == "given":
        out_copy = pltpu.make_async_copy(r.wout_hbm, r.wout_s, r.load_sem.at[2])
        out_copy.start()

    stream = r.stream[...].astype(F32)
    scale = lax.rsqrt(jnp.mean(stream * stream, axis=1, keepdims=True) + EPS)
    stores = []

    if mode == "given":

        @pl.when(me < count - 1)
        def _():
            pl.semaphore_wait(barrier, count - 1 - me)

    else:
        pl.semaphore_wait(barrier, count + 1)
        pieces = []

        def add_piece(local, whole, cuts):
            start = len(pieces)
            total = local.shape[0]
            for k, last_y in enumerate(cuts):
                piece = total // len(cuts)
                pieces.append((local, whole, k * piece, piece, last_y))
            return list(range(start, len(pieces)))

        first_items, next_items = [], []
        if mode == "first":
            first_items = add_piece(r.all_in.at[0], r.win_s, (1, 0))
            first_items += add_piece(r.all_small.at[0], r.gsm_s, (1,))
        out_items = add_piece(
            r.all_out.at[0 if mode == "first" else 1], r.wout_s, (1, 0)
        )
        if mode == "first":
            next_items = add_piece(r.all_in.at[1], r.win2_all, (1, 0))
            next_items += add_piece(r.all_small.at[1], r.gsm2_all, (0,))
        gather = Gather(depth, pieces, r.own_sem, r.send_sem, r.recv_sem)

        def begin(items):
            for item in items:
                gather.begin(item)

        def settle(items):
            for item in items:
                gather.settle(item)

        def keep(source, target, slot):
            copy = pltpu.make_async_copy(source, target, r.store_sem.at[slot])
            copy.start()
            stores.append(copy)

        if mode == "first":
            begin(first_items)
            turns = gather.turns(first_items)
            for k, turn in enumerate(turns):
                if k == len(turns) // 2:
                    begin(out_items + next_items)
                turn()
            settle(first_items)
            keep(r.win_s, r.win_all, 1)
            turns = gather.turns(out_items)
            queue.extend(gather.turns(out_items + next_items))
        else:
            begin(out_items)
            queue.extend(gather.turns(out_items))
        queue.append(lambda: settle(out_items))
        queue.append(lambda: keep(r.wout_s, r.wout_all, 0))
        if mode == "first":
            queue.append(lambda: settle(next_items))
        if mode == "later":
            small_copy.wait()
        merge_small(channels, r.gsm_s, r.sw)
    pace = -(-len(queue) // 33)

    load_small(at, r.sw, r.vec_s, r.dtw_s)
    r.normed_s[...] = (stream * scale * gain_row(at, channels, r.vec_s)).astype(BF16)
    per_tile = GROUP // r.win_s.shape[1]

    def win_tile(i):
        return r.win_s[pl.ds(i * per_tile, per_tile)].reshape(GROUP, width)

    if mode != "first":
        halves[0].wait()

    @pl.loop(0, tiles)
    def _(i):
        low = dot(r.normed_s[...], win_tile(i), NT).astype(BF16)
        r.pad[pl.ds(HALO, rows), lanes(i, GROUP)] = low
        r.padf_s[pl.ds(HALO, rows), lanes(i, GROUP)] = low.astype(F32)

    def edge():
        return pltpu.make_async_remote_copy(
            r.pad.at[pl.ds(rows, HALO)],
            r.halo_s,
            r.halo_sem.at[0],
            r.halo_sem.at[1],
            device_id=(ctx, jnp.minimum(me + 1, count - 1)),
            device_id_type=MESH,
        )

    @pl.when(me < count - 1)
    def _():
        edge().start()

    weave(pace)
    if mode != "first":
        halves[1].wait()

    @pl.loop(0, tiles)
    def _(i):
        r.gate[:, lanes(i, GROUP)] = dot(r.normed_s[...], win_tile(i + tiles), NT)

    weave(pace)

    @pl.when(me > 0)
    def _():
        edge().wait_recv()

    @pl.when(me == 0)
    def _():
        r.halo_s[...] = jnp.zeros_like(r.halo_s)

    r.pad[pl.ds(0, HALO), :] = r.halo_s[...]
    r.padf_s[pl.ds(0, HALO), :] = r.halo_s[...].astype(F32)

    @pl.loop(0, tiles)
    def _(i):
        here = lanes(i, GROUP)
        total = r.vec_s[pl.ds(at.conv_b, 1), here]
        for k in range(taps):
            total = (
                total
                + r.vec_s[pl.ds(at.conv + k, 1), here]
                * r.padf_s[pl.ds(HALO - taps + 1 + k, rows), here]
            )
        r.act[:, here] = (total * sigmoid(total)).astype(BF16)

    weave(pace)
    small = dot(r.act[...], r.sw[pl.ds(0, at.small), :], NT)
    r.sp[...] = small
    small_low = small.astype(BF16)

    @pl.loop(0, tiles)
    def _(i):
        here = lanes(i, GROUP)
        before = dot(small_low, r.dtw_s[:, here]) + r.vec_s[pl.ds(at.dt_b, 1), here]
        step = softplus(before)
        r.pre[:, here] = before
        r.dt_s[:, here] = step
        r.dx_s[:, here] = step * r.act[:, here].astype(F32)
        keep_sum(r.own_sum, i, step)

    sums, ends = chain(
        count, me, ctx, r.own_sum, r.sum_s, r.own_end, r.end_s,
        (r.sum_send, r.sum_recv, r.end_send, r.end_recv),
    )
    each(me + 1, count, lambda j: sums(j, me).start())
    weave(pace)
    for n in range(states):
        r.bb_s[:, n, :] = jnp.broadcast_to(
            small[:, rank + n : rank + n + 1], (rows, 128)
        )
    r.cd_s[...] = spread(small_low, rank + states, states)

    def advance(t, state, rate2, here):
        return (
            jnp.exp2(r.dt_s[pl.ds(t, 1), here] * rate2) * state
            + r.dx_s[pl.ds(t, 1), here] * widen(r.bb_s[t], GROUP)
        )

    for g in range(groups):
        here = pl.ds(g * GROUP, GROUP)
        rate2 = r.vec_s[pl.ds(0, states), here] * LOG2E

        def first_pass(step, state):
            for i in range(CHUNK):
                state = advance(step * CHUNK + i, state, rate2, here)
            return state

        state = jnp.zeros((states, GROUP), F32)
        for part in range(2):
            state = lax.fori_loop(
                steps * part // 2, steps * (part + 1) // 2, first_pass, state
            )
            weave(pace)
        r.own_end[:, here] = state.astype(BF16)
        each(me + 1, count, lambda j: ends(g, j, me).start())

    def h_copy(g):
        here = pl.ds(g * GROUP, GROUP)
        return pltpu.make_async_copy(
            r.hs.at[:, here], r.h_hbm.at[:, here], r.h_sem.at[g]
        )

    for g in range(groups):
        here = pl.ds(g * GROUP, GROUP)
        rate2 = r.vec_s[pl.ds(0, states), here] * LOG2E

        def carry(j, state):
            if g == 0:
                sums(j, j).wait_recv()
            ends(g, j, j).wait_recv()
            return (
                jnp.exp2(rate2 * sum_of(r.sum_s, j, g)) * state
                + r.end_s[j, :, here].astype(F32)
            )

        state = lax.fori_loop(0, me, carry, jnp.zeros((states, GROUP), F32))
        r.hs[pl.ds(0, states), here] = state.astype(BF16)

        def second_pass(step, state):
            base = pl.multiple_of(step * CHUNK * states + states, states)
            for i in range(CHUNK):
                state = advance(step * CHUNK + i, state, rate2, here)
                r.hs[pl.ds(base + i * states, states), here] = state.astype(BF16)
            tokens = pl.ds(pl.multiple_of(step * CHUNK, CHUNK), CHUNK)
            r.y[tokens, here] = dot(
                r.cd_s[tokens, :], r.hs[pl.ds(base, CHUNK * states), here]
            )
            return state

        thirds = 1 if mode == "given" else 5
        for part in range(thirds):
            state = lax.fori_loop(
                steps * part // thirds,
                steps * (part + 1) // thirds,
                second_pass,
                state,
            )
            weave(pace)
        h_copy(g).start()
        y_value = (
            r.y[:, here]
            + r.vec_s[pl.ds(at.skip, 1), here] * r.act[:, here].astype(F32)
        )
        gate = r.gate[:, here]
        r.y[:, here] = y_value
        r.mixed[:, here] = (y_value * gate * sigmoid(gate)).astype(BF16)

    if mode == "given":
        out_copy.wait()
    else:
        while queue and not stores_hold_out(mode, stores):
            weave(1)
    out_tile = 256 // r.wout_s.shape[1]
    for i in range(width // 256):
        here = pl.ds(i * 256, 256)
        wout = r.wout_s[pl.ds(i * out_tile, out_tile)].reshape(256, inner)
        r.new[:, here] = (
            r.stream[:, here].astype(F32) + dot(r.mixed[...], wout, NT)
        ).astype(r.new.dtype)

    weave(len(queue))
    if mode != "given":
        gather.finish()

    @pl.when(me < count - 1)
    def _():
        edge().wait_send()

    each(me + 1, count, lambda j: sums(j, me).wait_send())
    for g in range(groups):
        each(me + 1, count, lambda j: ends(g, j, me).wait_send())
        h_copy(g).wait()
    for copy in stores:
        copy.wait()


def stores_hold_out(mode, stores):
    return len(stores) == (2 if mode == "first" else 1)


def backward_kernel(cfg, mode, names, *refs):
    r = types.SimpleNamespace(**dict(zip(names, refs)))
    rows, inner, states, taps, rank, count, channels = cfg
    at = Names(states, taps, rank)
    ctx, me = lax.axis_index("ctx"), lax.axis_index("seq")
    groups, steps, tiles = inner // GROUP, rows // CHUNK, inner // GROUP
    depth = count // 2
    width = r.stream.shape[1]
    barrier = pltpu.get_barrier_semaphore()
    gvec = r.full_s.at[pl.ds(at.vec, at.rows - at.vec)]

    def signal(semaphore, to):
        pl.semaphore_signal(semaphore, inc=1, device_id=to, device_id_type=MESH)

    queue = collections.deque()

    def weave(times):
        for _ in range(min(times, len(queue))):
            queue.popleft()()

    each(me + 1, count, lambda j: signal(barrier, (ctx, j)))
    if mode != "given":
        each(0, me, lambda j: signal(barrier, (ctx, j)))
        y, x, z, core = places()
        signal(barrier, device(y, 1 - x, z, core))
        signal(barrier, device(1 - y, x, z, core))

    def wout_copy(i):
        slot = lax.rem(i, 2)
        return pltpu.make_async_copy(
            r.wout.at[:, :, lanes(i, GROUP)], r.wout_s.at[slot], r.wout_sem.at[slot]
        )

    def gate_copies(i):
        slot = lax.rem(i, 2)
        return [
            pltpu.make_async_copy(
                array.at[:, lanes(i, GROUP)], r.gate_s.at[slot, k], r.gate_sem.at[slot, k]
            )
            for k, array in enumerate((r.gate, r.y))
        ]

    win_rows = r.win_s.shape[1]

    def win_copy(i, slot):
        return pltpu.make_async_copy(
            r.win.at[pl.ds(i * win_rows, win_rows)], r.win_s.at[slot], r.win_sem.at[slot]
        )

    span = rows // 2 * states

    def states_in(k):
        g, half = k // 2, 1 - k % 2
        return pltpu.make_async_copy(
            r.h_hbm.at[pl.ds(half * span, span + states), pl.ds(g * GROUP, GROUP)],
            r.hb.at[k % 2],
            r.h_sem.at[k % 2],
        )

    wout_copy(0).start()
    win_copy(tiles, 0).start()
    for copy in gate_copies(0):
        copy.start()
    load_small(at, r.sw, r.vec_s, r.dtw_s)
    gain = gain_row(at, channels, r.vec_s)
    r.low_s[...] = r.sgrad[...].astype(BF16)
    stream = r.stream[...].astype(F32)
    scale = lax.rsqrt(jnp.mean(stream * stream, axis=1, keepdims=True) + EPS)
    r.normed_s[...] = (stream * scale * gain).astype(BF16)
    small_low = r.sp[...].astype(BF16)

    in_items, out_items, own_items = [], [], []
    if mode == "given":

        @pl.when(me > 0)
        def _():
            pl.semaphore_wait(barrier, me)

    else:
        pl.semaphore_wait(barrier, count + 1)
        pieces, buffers = [], []

        def add_piece(whole, out, cuts, held, side=None):
            start = len(pieces)
            total = whole.shape[4]
            for k, first_y in enumerate(cuts):
                piece = total // len(cuts)
                pieces.append((whole, out, k * piece, piece, first_y, side))
                buffers.append(held[k])
            return list(range(start, len(pieces)))

        def held_by(name):
            found = []
            while hasattr(r, f"{name}{len(found)}_0"):
                k = len(found)
                found.append([getattr(r, f"{name}{k}_{part}") for part in range(5)])
            return found

        held_in, held_small, held_out = (
            held_by("rin"),
            held_by("rsmall"),
            held_by("rout"),
        )
        out_items = add_piece(r.gout, r.sum_out, (1, 0), held_out)
        if mode == "first":
            in_items = add_piece(r.next_gin, r.sum_next_in, (1, 0, 1, 0), held_in)
            in_items += add_piece(r.next_gsmall, r.sum_next_small, (1,), held_small)
            own_items = add_piece(r.gin, r.sum_in, (1, 0, 1, 0), held_in)
            own_items += add_piece(r.gsmall_hbm, r.sum_small, (1,), held_small)
        reduce = Reduce(depth, pieces, buffers, r.own_sem, r.send_sem, r.recv_sem)
        for item in in_items:
            reduce.begin(item)

    r.lowt_s[...] = r.sgrad[...].astype(F32).T.astype(BF16)
    out_shape = r.stage_out.shape[1:]
    out_rows = out_shape[0] * out_shape[1] * out_shape[2]
    line = r.gout.shape[2]

    def block_of(whole, i):
        row, z = split(2 * i, line)
        y, x = split(row, 2)
        return whole.at[y, x, pl.ds(z, 2)]

    for k in range(width // out_rows):
        slot = k % 2
        copy = pltpu.make_async_copy(
            r.stage_out.at[slot], block_of(r.gout, k), r.out_sem.at[slot]
        )
        if k >= 2:
            copy.wait()

        @pl.loop(0, tiles)
        def _(i):
            here = lanes(i, GROUP)
            r.stage_out[slot, :, :, :, here] = (
                dot(r.lowt_s[pl.ds(k * out_rows, out_rows), :], r.mixed[:, here])
                .astype(BF16)
                .reshape(out_shape[:-1] + (GROUP,))
            )

        copy.start()
    for slot in range(2):
        pltpu.make_async_copy(
            r.stage_out.at[slot], block_of(r.gout, 0), r.out_sem.at[slot]
        ).wait()
    if mode != "given":
        for item in out_items:
            reduce.begin(item)
        queue.extend(reduce.turns(in_items + out_items))
    pace = -(-len(queue) // (24 if mode == "first" else 26))

    @pl.loop(0, tiles)
    def _(i):
        here = lanes(i, GROUP)
        slot = lax.rem(i, 2)

        @pl.when(i + 1 < tiles)
        def _():
            wout_copy(i + 1).start()
            for copy in gate_copies(i + 1):
                copy.start()

        wout_copy(i).wait()
        for copy in gate_copies(i):
            copy.wait()
        mixed_grad = dot(r.low_s[...], r.wout_s[slot].reshape(width, GROUP))
        gate = r.gate_s[slot, 0]
        sig = sigmoid(gate)
        act = r.act[:, here].astype(F32)
        scan_grad = mixed_grad * gate * sig
        r.sg_s[:, here] = scan_grad
        r.pb_s[:, lanes(i + tiles, GROUP)] = (
            mixed_grad * r.gate_s[slot, 1] * sig * (1.0 + gate * (1.0 - sig))
        ).astype(BF16)
        gvec[pl.ds(at.skip, 1), here] = jnp.sum(scan_grad * act, axis=0, keepdims=True)
        step = softplus(r.pre[:, here])
        r.dt_s[:, here] = step
        r.dx_s[pl.ds(0, rows), here] = step * act
        keep_sum(r.own_sum, i, step)

    sums, ends = chain(
        count, me, ctx, r.own_sum, r.sum_s, r.own_end, r.end_s,
        (r.sum_send, r.sum_recv, r.end_send, r.end_recv),
    )
    each(0, me, lambda j: sums(j, me).start())
    weave(pace)
    in_shape = r.stage_in.shape[1:]

    def in_copy(i, slot):
        return pltpu.make_async_copy(
            r.stage_in.at[slot], block_of(r.gin, i), r.in_sem.at[slot]
        )

    def project(i, turn):
        here = lanes(i, GROUP)
        slot = lax.rem(turn, 2)
        copy = in_copy(i, slot)
        following = lax.rem(i + 1, 2 * tiles)

        @pl.when(turn + 1 < 2 * tiles)
        def _():
            win_copy(following, 1 - slot).start()

        @pl.when(turn >= 2)
        def _():
            copy.wait()

        r.stage_in[slot] = (
            dot(r.pb_s[:, here], r.normed_s[...], TN).astype(BF16).reshape(in_shape)
        )
        copy.start()
        win_copy(i, slot).wait()
        part = dot(r.pb_s[:, here], r.win_s[slot].reshape(GROUP, width))

        @pl.when(turn == 0)
        def _():
            r.nsg[...] = part

        @pl.when(turn > 0)
        def _():
            r.nsg[...] += part

    @pl.loop(0, tiles)
    def _(i):
        project(i + tiles, i)

    weave(pace)
    for n in range(states):
        first = rank + states + n
        r.cb_s[:, n, :] = jnp.broadcast_to(r.sp[:, first : first + 1], (rows, 128))
    r.bd_s[...] = spread(small_low, rank, states)
    ones = jnp.where(chunk_mask(CHUNK, states), 1.0, 0.0).astype(BF16)
    states_in(0).start()

    for g in range(groups):
        here = pl.ds(g * GROUP, GROUP)
        rate2 = r.vec_s[pl.ds(0, states), here] * LOG2E

        def first_pass(k, state):
            step = steps - 1 - k
            for i in reversed(range(CHUNK)):
                t = step * CHUNK + i
                state = jnp.exp2(r.dt_s[pl.ds(t, 1), here] * rate2) * (
                    state + r.sg_s[pl.ds(t, 1), here] * widen(r.cb_s[t], GROUP)
                )
            return state

        r.own_end[:, here] = lax.fori_loop(
            0, steps, first_pass, jnp.zeros((states, GROUP), F32)
        ).astype(BF16)
        each(0, me, lambda j: ends(g, j, me).start())
        weave(pace)

    for g in range(groups):
        here = pl.ds(g * GROUP, GROUP)
        rate = r.vec_s[pl.ds(0, states), here]
        rate2 = rate * LOG2E

        def carry(k, state):
            j = count - 1 - k
            if g == 0:
                sums(j, j).wait_recv()
            ends(g, j, j).wait_recv()
            return (
                jnp.exp2(rate2 * sum_of(r.sum_s, j, g)) * state
                + r.end_s[j, :, here].astype(F32)
            )

        begin = lax.fori_loop(
            0, count - 1 - me, carry, jnp.zeros((states, GROUP), F32)
        )
        both = (begin, jnp.zeros((states, GROUP), F32))
        for part in range(2):
            k = 2 * g + part
            half = 1 - part
            held_states = r.hb.at[k % 2]
            if k + 1 < 2 * groups:
                states_in(k + 1).start()
            states_in(k).wait()

            def second_pass(turn, both):
                state, total = both
                step = steps - 1 - turn
                base = pl.multiple_of(step * CHUNK * states - half * span, states)
                for i in reversed(range(CHUNK)):
                    t = step * CHUNK + i
                    dt = r.dt_s[pl.ds(t, 1), here]
                    adjoint = state + r.sg_s[pl.ds(t, 1), here] * widen(
                        r.cb_s[t], GROUP
                    )
                    state = jnp.exp2(dt * rate2) * adjoint
                    held = held_states[pl.ds(base + i * states, states), :]
                    rated = state * held.astype(F32) * rate
                    total = total + dt * rated
                    r.ab_s[pl.ds(i * states, states), :] = adjoint.astype(BF16)
                    r.rb_s[pl.ds(i * states, states), :] = rated.astype(BF16)
                tokens = pl.ds(pl.multiple_of(step * CHUNK, CHUNK), CHUNK)
                from_in = dot(r.bd_s[tokens, :], r.ab_s[...])
                from_rate = dot(ones, r.rb_s[...])
                scan_grad = r.sg_s[tokens, here]
                into_in = dot(r.dx_s[tokens, here].astype(BF16), r.ab_s[...], NT)
                into_out = dot(
                    scan_grad.astype(BF16),
                    held_states[pl.ds(base + states, CHUNK * states), :],
                    NT,
                )
                if g == 0:
                    r.pin_s[tokens, :] = into_in
                    r.pout_s[tokens, :] = into_out
                else:
                    r.pin_s[tokens, :] += into_in
                    r.pout_s[tokens, :] += into_out
                r.stepg_s[tokens, here] = (
                    r.act[tokens, here].astype(F32) * from_in + from_rate
                )
                r.sg_s[tokens, here] = (
                    r.dt_s[tokens, here] * from_in
                    + r.vec_s[pl.ds(at.skip, 1), here] * scan_grad
                )
                return state, total

            for quarter in range(2):
                low = (2 * part + quarter) * steps // 4
                high = (2 * part + quarter + 1) * steps // 4
                both = lax.fori_loop(low, high, second_pass, both)
                weave(pace)
        gvec[pl.ds(0, states), here] = both[1]

    @pl.loop(0, tiles)
    def _(i):
        here = lanes(i, GROUP)
        pre_grad = r.stepg_s[pl.ds(0, rows), here] * sigmoid(r.pre[:, here])
        gvec[pl.ds(at.dt_b, 1), here] = jnp.sum(pre_grad, axis=0, keepdims=True)
        r.prelow_s[:, here] = pre_grad.astype(BF16)
        r.dx_s[:, here] = r.pad[:, here].astype(F32)

    small_grad = (
        dot(r.prelow_s[...], r.dtw_s[...], NT)
        + gather_back(r.pin_s[...], rank, states, at.small)
        + gather_back(r.pout_s[...], rank + states, states, at.small)
    ).astype(BF16)

    @pl.loop(0, tiles)
    def _(i):
        here = lanes(i, GROUP)
        r.full_s[pl.ds(at.dt, rank), here] = dot(
            small_low, r.prelow_s[:, here], TN
        )[:rank]
        r.full_s[pl.ds(0, at.small), here] = dot(small_grad, r.act[:, here], TN)
        act_grad = r.sg_s[:, here] + dot(small_grad, r.sw[pl.ds(0, at.small), here])
        total = r.vec_s[pl.ds(at.conv_b, 1), here]
        for k in range(taps):
            total = (
                total
                + r.vec_s[pl.ds(at.conv + k, 1), here]
                * r.dx_s[pl.ds(HALO - taps + 1 + k, rows), here]
            )
        sig = sigmoid(total)
        conv_grad = act_grad * sig * (1.0 + total * (1.0 - sig))
        r.stepg_s[pl.ds(0, rows), here] = conv_grad
        gvec[pl.ds(at.conv_b, 1), here] = jnp.sum(conv_grad, axis=0, keepdims=True)
        for k in range(taps):
            gvec[pl.ds(at.conv + k, 1), here] = jnp.sum(
                conv_grad * r.dx_s[pl.ds(HALO - taps + 1 + k, rows), here],
                axis=0,
                keepdims=True,
            )

    def edge():
        return pltpu.make_async_remote_copy(
            r.stepg_s.at[pl.ds(0, 8)],
            r.halo_s,
            r.halo_sem.at[0],
            r.halo_sem.at[1],
            device_id=(ctx, jnp.maximum(me - 1, 0)),
            device_id_type=MESH,
        )

    @pl.when(me > 0)
    def _():
        edge().start()

    weave(pace)
    @pl.when(me < count - 1)
    def _():
        edge().wait_recv()

    @pl.when(me == count - 1)
    def _():
        r.halo_s[...] = jnp.zeros_like(r.halo_s)

    @pl.when(me > 0)
    def _():
        edge().wait_send()

    r.stepg_s[pl.ds(rows, 8), :] = r.halo_s[...]

    @pl.loop(0, tiles)
    def _(i):
        here = lanes(i, GROUP)
        total = jnp.zeros((rows, GROUP), F32)
        for k in range(taps):
            total = (
                total
                + r.vec_s[pl.ds(at.conv + k, 1), here]
                * r.stepg_s[pl.ds(taps - 1 - k, rows), here]
            )
        r.pb_s[:, here] = total.astype(BF16)
        project(i, i + tiles)

    stream = r.stream[...].astype(F32)
    scale = lax.rsqrt(jnp.mean(stream * stream, axis=1, keepdims=True) + EPS)
    normed_grad = r.nsg[...]
    gain_grad = jnp.sum(normed_grad * stream * scale, axis=0, keepdims=True)
    gain_grad = jnp.broadcast_to(gain_grad, (8, width)).astype(BF16)
    pick = gain_pick(channels)
    for i in range(inner // 256):
        wide = dot(gain_grad[:, 128 * i : 128 * i + 128], pick, NT)
        gvec[pl.ds(at.gain, 1), pl.ds(256 * i, 256)] = wide[:1]
    for k in range(at.count, at.rows):
        r.full_s[pl.ds(k, 1), :] = jnp.zeros((1, inner), F32)
    if mode == "given":
        r.gsmall[...] = r.full_s[...]
    elif mode == "last":
        split_small(channels, r.full_s, r.gsmall)
    else:
        split_small(channels, r.full_s, Folded(r.gsmall_s))
        small_copy = pltpu.make_async_copy(r.gsmall_s, r.gsmall_hbm, r.small_sem.at[0])
        small_copy.start()
    scaled = normed_grad * gain
    inner_sum = jnp.mean(scaled * stream, axis=1, keepdims=True)
    r.nsg[...] = (
        r.sgrad[...].astype(F32) + scale * scaled - stream * (scale * scale * scale) * inner_sum
    )
    for slot in range(2):
        in_copy(0, slot).wait()
    weave(len(queue))
    if mode == "first":
        small_copy.wait()
        reduce.finish()
        for partner in square_partners(depth):
            signal(r.ready_sem, partner)
        pl.semaphore_wait(r.ready_sem, len(square_partners(depth)))
        for item in own_items:
            reduce.begin(item)
        for turn in reduce.turns(own_items):
            turn()
    if mode != "given":
        reduce.finish()
    each(0, me, lambda j: sums(j, me).wait_send())
    for g in range(groups):
        each(0, me, lambda j: ends(g, j, me).wait_send())


def in_vmem(count):
    return [pl.BlockSpec(memory_space=pltpu.VMEM)] * count


def in_any(count):
    return [pl.BlockSpec(memory_space=pl.ANY)] * count


def forward_call(cfg, mode, stream, operands):
    rows, inner, states, taps, rank, count, channels = cfg
    at = Names(states, taps, rank)
    width = stream.shape[1]
    groups = inner // GROUP
    devices = inner // channels
    shape = jax.ShapeDtypeStruct
    dma = pltpu.SemaphoreType.DMA
    vmem, any_space = in_vmem(1)[0], in_any(1)[0]
    inputs = [("stream", stream, vmem)]
    for name, array in operands:
        inputs.append((name, array, vmem if name == "sw" else any_space))
    outputs = [
        ("new", shape(stream.shape, BF16 if mode == "later" else F32), vmem),
        ("pad", shape((rows + HALO, inner), BF16), vmem),
        ("gate", shape((rows, inner), F32), vmem),
        ("act", shape((rows, inner), BF16), vmem),
        ("sp", shape((rows, at.small), F32), vmem),
        ("pre", shape((rows, inner), F32), vmem),
        ("h_hbm", shape(((rows + 1) * states, inner), BF16), any_space),
        ("y", shape((rows, inner), F32), vmem),
        ("mixed", shape((rows, inner), BF16), vmem),
    ]
    if mode == "given":
        given = dict(operands)
        in_shape, out_shape = given["win_hbm"].shape, given["wout_hbm"].shape
    else:
        in_shape = (devices, 2 * inner // devices, width)
        out_shape = (devices, width // devices, inner)
        small_shape = (devices, at.rows * channels // 128, 128)
        outputs.append(("sw", shape((at.rows, inner), BF16), vmem))
        outputs.append(("wout_all", shape(out_shape, BF16), any_space))
    if mode == "first":
        outputs.append(("win_all", shape(in_shape, BF16), any_space))
        outputs.append(("win2_all", shape(in_shape, BF16), any_space))
        outputs.append(("gsm2_all", shape(small_shape, BF16), any_space))
    scratch = [
        ("win_s", pltpu.VMEM(in_shape, BF16)),
        ("wout_s", pltpu.VMEM(out_shape, BF16)),
        ("vec_s", pltpu.VMEM((at.rows - at.vec, inner), F32)),
        ("dtw_s", pltpu.VMEM((at.small, inner), BF16)),
        ("normed_s", pltpu.VMEM(stream.shape, BF16)),
        ("padf_s", pltpu.VMEM((rows + HALO, inner), F32)),
        ("halo_s", pltpu.VMEM((HALO, inner), BF16)),
        ("dt_s", pltpu.VMEM((rows, inner), F32)),
        ("dx_s", pltpu.VMEM((rows, inner), F32)),
        ("bb_s", pltpu.VMEM((rows, states, 128), F32)),
        ("cd_s", pltpu.VMEM((rows, CHUNK * states), BF16)),
        ("hs", pltpu.VMEM(((rows + 1) * states, inner), BF16)),
        ("own_sum", pltpu.VMEM((8, inner // 8), F32)),
        ("sum_s", pltpu.VMEM((count, 8, inner // 8), F32)),
        ("own_end", pltpu.VMEM((states, inner), BF16)),
        ("end_s", pltpu.VMEM((count, states, inner), BF16)),
        ("halo_sem", dma((2,))),
        ("sum_send", dma((count,))),
        ("sum_recv", dma((count,))),
        ("end_send", dma((groups, count))),
        ("end_recv", dma((groups, count))),
        ("h_sem", dma((groups,))),
        ("load_sem", dma((3,))),
    ]
    if mode != "given":
        pieces = 8 if mode == "first" else 2
        scratch += [
            ("gsm_s", pltpu.VMEM(small_shape, BF16)),
            ("own_sem", dma((pieces,))),
            ("send_sem", dma((pieces, Gather.sends(count // 2)))),
            ("recv_sem", dma((pieces, devices))),
            ("store_sem", dma((2,))),
        ]
    names = [entry[0] for entry in inputs + outputs + scratch]
    results = pl.pallas_call(
        functools.partial(forward_kernel, cfg, mode, names),
        out_shape=tuple(entry[1] for entry in outputs),
        in_specs=[entry[2] for entry in inputs],
        out_specs=tuple(entry[2] for entry in outputs),
        scratch_shapes=[entry[1] for entry in scratch],
        compiler_params=pltpu.CompilerParams(
            collective_id={"given": 0, "first": 4, "later": 5}[mode],
            has_side_effects=True,
            vmem_limit_bytes=VMEM_BYTES,
        ),
        name="forward_" + mode,
    )(*[entry[1] for entry in inputs])
    return {entry[0]: result for entry, result in zip(outputs, results)}


def backward_call(cfg, mode, sgrad, stream, weights, saved, later):
    rows, inner, states, taps, rank, count, channels = cfg
    at = Names(states, taps, rank)
    width = stream.shape[1]
    groups = inner // GROUP
    wide = CHUNK * states
    depth = count // 2
    sw, win, wout = weights
    shape = jax.ShapeDtypeStruct
    dma = pltpu.SemaphoreType.DMA
    vmem, any_space = in_vmem(1)[0], in_any(1)[0]
    in_rows, out_rows = win.shape[1], wout.shape[1]
    lead = (1, 1, win.shape[0] // 2, 2) if mode == "given" else (2, 2, depth, 2)
    small_rows = at.rows * channels // 128
    inputs = [
        ("sgrad", sgrad, vmem),
        ("stream", stream, vmem),
        ("sw", sw, vmem),
        ("win", win, any_space),
        ("wout", wout, any_space),
    ]
    for name in ("pad", "act", "sp", "pre", "mixed"):
        inputs.append((name, saved[name], vmem))
    for name in ("gate", "y", "h_hbm"):
        inputs.append((name, saved[name], any_space))
    outputs = [
        ("nsg", shape((rows, width), F32), vmem),
        ("gin", shape(lead + (in_rows, width), BF16), any_space),
        ("gout", shape(lead + (out_rows, inner), BF16), any_space),
    ]
    scratch = [
        ("full_s", pltpu.VMEM((at.rows, inner), F32)),
        ("vec_s", pltpu.VMEM((at.rows - at.vec, inner), F32)),
        ("dtw_s", pltpu.VMEM((at.small, inner), BF16)),
        ("hb", pltpu.VMEM((2, (rows // 2 + 1) * states, GROUP), BF16)),
        ("normed_s", pltpu.VMEM((rows, width), BF16)),
        ("low_s", pltpu.VMEM((rows, width), BF16)),
        ("lowt_s", pltpu.VMEM((width, rows), BF16)),
        ("sg_s", pltpu.VMEM((rows, inner), F32)),
        ("dt_s", pltpu.VMEM((rows, inner), F32)),
        ("dx_s", pltpu.VMEM((rows + HALO, inner), F32)),
        ("stepg_s", pltpu.VMEM((rows + 8, inner), F32)),
        ("pb_s", pltpu.VMEM((rows, 2 * inner), BF16)),
        ("cb_s", pltpu.VMEM((rows, states, 128), F32)),
        ("bd_s", pltpu.VMEM((rows, wide), BF16)),
        ("ab_s", pltpu.VMEM((wide, GROUP), BF16)),
        ("rb_s", pltpu.VMEM((wide, GROUP), BF16)),
        ("pin_s", pltpu.VMEM((rows, wide), F32)),
        ("pout_s", pltpu.VMEM((rows, wide), F32)),
        ("prelow_s", pltpu.VMEM((rows, inner), BF16)),
        ("stage_in", pltpu.VMEM((2, 2, 2, in_rows, width), BF16)),
        ("stage_out", pltpu.VMEM((2, 2, 2, out_rows, inner), BF16)),
        ("win_s", pltpu.VMEM((2, GROUP // in_rows, in_rows, width), BF16)),
        ("wout_s", pltpu.VMEM((2,) + wout.shape[:2] + (GROUP,), BF16)),
        ("gate_s", pltpu.VMEM((2, 2, rows, GROUP), F32)),
        ("halo_s", pltpu.VMEM((8, inner), F32)),
        ("own_sum", pltpu.VMEM((8, inner // 8), F32)),
        ("sum_s", pltpu.VMEM((count, 8, inner // 8), F32)),
        ("own_end", pltpu.VMEM((states, inner), BF16)),
        ("end_s", pltpu.VMEM((count, states, inner), BF16)),
        ("halo_sem", dma((2,))),
        ("sum_send", dma((count,))),
        ("sum_recv", dma((count,))),
        ("end_send", dma((groups, count))),
        ("end_recv", dma((groups, count))),
        ("h_sem", dma((2,))),
        ("in_sem", dma((2,))),
        ("out_sem", dma((2,))),
        ("win_sem", dma((2,))),
        ("wout_sem", dma((2,))),
        ("gate_sem", dma((2, 2))),
    ]
    if mode == "given":
        outputs.append(("gsmall", shape((at.rows, inner), F32), vmem))
    else:
        outputs.append(("sum_out", shape((out_rows, inner), F32), vmem))
        held = [("rout", out_rows // 2, inner, 2, False)]
        pieces = 2
        if mode == "last":
            small_shape = (inner // channels, small_rows, 128)
            outputs.append(("gsmall", shape(small_shape, BF16), vmem))
        else:
            inputs.append(("next_gin", later["gin"], any_space))
            small = later["gsmall"].reshape(lead + (small_rows, 128))
            inputs.append(("next_gsmall", small, any_space))
            outputs.append(("gsmall_hbm", shape(small.shape, BF16), any_space))
            scratch.append(("gsmall_s", pltpu.VMEM(small.shape, BF16)))
            for name in ("sum_in", "sum_next_in"):
                outputs.append((name, shape((in_rows, width), F32), vmem))
            for name in ("sum_small", "sum_next_small"):
                outputs.append((name, shape((small_rows, 128), F32), vmem))
            held.append(("rin", in_rows // 4, width, 4, False))
            held.append(("rsmall", small_rows, 128, 1, False))
            scratch.append(("small_sem", dma((1,))))
            scratch.append(("ready_sem", pltpu.SemaphoreType.REGULAR))
            pieces = 12
        for name, piece, wide_by, cuts, sided in held:
            for k in range(cuts):
                found = Reduce.buffers_of(depth, piece, wide_by, sided)
                for part, buffer in enumerate(found):
                    scratch.append((f"{name}{k}_{part}", buffer))
        scratch += [
            ("own_sem", dma((pieces, 2))),
            ("send_sem", dma((pieces, 4, depth))),
            ("recv_sem", dma((pieces, 4, depth))),
        ]
    names = [entry[0] for entry in inputs + outputs + scratch]
    results = pl.pallas_call(
        functools.partial(backward_kernel, cfg, mode, names),
        out_shape=tuple(entry[1] for entry in outputs),
        in_specs=[entry[2] for entry in inputs],
        out_specs=tuple(entry[2] for entry in outputs),
        scratch_shapes=[entry[1] for entry in scratch],
        compiler_params=pltpu.CompilerParams(
            collective_id={"given": 1, "last": 6, "first": 7}[mode],
            has_side_effects=True,
            vmem_limit_bytes=VMEM_BYTES,
        ),
        name="backward_" + mode,
    )(*[entry[1] for entry in inputs])
    return {entry[0]: result for entry, result in zip(outputs, results)}


def on_device(
    mesh,
    hidden_in,
    cotangent,
    norm_gain,
    in_weight,
    conv_weight,
    conv_bias,
    x_weight,
    dt_weight,
    dt_bias,
    a_log,
    skip_gain,
    out_weight,
):
    layers = norm_gain.shape[0]
    rows, width = hidden_in.shape
    taps, channels = conv_weight.shape[1:]
    states = a_log.shape[2]
    rank = dt_weight.shape[1]
    devices, count = mesh.shape["ctx"] * mesh.shape["seq"], mesh.shape["seq"]
    inner = channels * devices
    gains = norm_gain.shape[1]
    at = Names(states, taps, rank)
    cfg = (rows, inner, states, taps, rank, count, channels)
    depth = count // 2
    by_kernel = (
        mesh.shape["ctx"] == 4
        and depth % 2 == 0
        and layers == 2
        and in_weight.shape[2] % 32 == 0
        and out_weight.shape[2] % 32 == 0
        and 128 % channels == 0
        and at.rows * channels // 128 % 16 == 0
    )

    gain_rows = jnp.pad(norm_gain, ((0, 0), (0, channels - gains)))
    packed = jnp.concatenate(
        [
            x_weight.transpose(0, 2, 1),
            dt_weight,
            a_log.transpose(0, 2, 1),
            conv_weight,
            jnp.stack([conv_bias, dt_bias, skip_gain, gain_rows], 1),
            jnp.zeros((layers, at.rows - at.count, channels), BF16),
        ],
        1,
    )
    all_in, all_out = in_weight.transpose(0, 2, 1), out_weight.transpose(0, 2, 1)
    stream = hidden_in if by_kernel else hidden_in.astype(F32)
    streams, runs, weights = [], [], []
    if by_kernel:
        folds = packed.reshape(layers, 128 // channels, -1, channels)
        all_small = jnp.concatenate([folds[:, k] for k in range(folds.shape[1])], 2)
        operands = [
            ("all_in", all_in),
            ("all_small", all_small),
            ("all_out", all_out),
        ]
        first = forward_call(cfg, "first", stream, operands)
        operands = [
            ("win_hbm", first["win2_all"]),
            ("gsm_hbm", first["gsm2_all"]),
            ("all_out", all_out),
        ]
        second = forward_call(cfg, "later", first["new"], operands)
        runs = [first, second]
        wins = [first["win_all"], first["win2_all"]]
        weights = [
            (run["sw"], win, run["wout_all"]) for run, win in zip(runs, wins)
        ]
        streams = [stream, first["new"]]
        stream = second["new"]
    else:
        for w_in, w_out, w_small in zip(all_in, all_out, packed):
            w_in = lax.all_gather(w_in, ("ctx", "seq"), axis=0, tiled=True)
            w_out = lax.all_gather(w_out, ("ctx", "seq"), axis=0, tiled=True)
            sw = lax.all_gather(w_small, ("ctx", "seq"), axis=1, tiled=True)
            w_in = w_in.reshape(-1, 128, width)
            w_out = w_out.reshape(-1, 32, inner)
            operands = [("win_hbm", w_in), ("sw", sw), ("wout_hbm", w_out)]
            run = forward_call(cfg, "given", stream, operands)
            runs.append(run)
            weights.append((sw, w_in, w_out))
            streams.append(stream)
            stream = run["new"]
    stream_grad = cotangent
    summed = [None] * layers
    if by_kernel:
        last = backward_call(
            cfg, "last", stream_grad, streams[1], weights[1], runs[1], None
        )
        head = backward_call(
            cfg, "first", last["nsg"], streams[0], weights[0], runs[0], last
        )
        stream_grad = head["nsg"]

        def unfold(small):
            small = small.reshape(-1, 128 // channels, channels)
            return small.transpose(1, 0, 2).reshape(at.rows, channels)

        summed = [
            (head["sum_in"], head["sum_out"], unfold(head["sum_small"])),
            (head["sum_next_in"], last["sum_out"], unfold(head["sum_next_small"])),
        ]
    else:
        for layer in reversed(range(layers)):
            run = backward_call(
                cfg,
                "given",
                stream_grad,
                streams[layer],
                weights[layer],
                runs[layer],
                None,
            )
            stream_grad = run["nsg"]
            summed[layer] = [
                lax.psum_scatter(
                    array.astype(F32),
                    ("ctx", "seq"),
                    scatter_dimension=dim,
                    tiled=True,
                )
                for array, dim in (
                    (run["gin"].reshape(-1, width), 0),
                    (run["gout"].reshape(-1, inner), 0),
                    (run["gsmall"], 1),
                )
            ]
    grads = [None] * layers
    for layer in range(layers):
        s_in, s_out, s_small = summed[layer]
        s_x = s_small[: at.small, :channels]
        s_dt = s_small[at.dt : at.dt + rank, :channels]
        s_vec = s_small[at.vec : at.count, :channels]
        grads[layer] = (
            s_vec[at.gain, :gains],
            s_in.T,
            s_vec[at.conv : at.conv + taps],
            s_vec[at.conv_b],
            s_x.T,
            s_dt,
            s_vec[at.dt_b],
            s_vec[:states].T,
            s_vec[at.skip],
            s_out.T,
        )
    stacked = tuple(
        jnp.stack([grads[layer][member] for layer in range(layers)], 0)
        for member in range(10)
    )
    return (stream.astype(BF16), stream_grad) + stacked


def solution(mesh):
    split = ("ctx", "seq")
    tokens, last = P(split, None), P(None, split)
    middle, third = P(None, split, None), P(None, None, split)
    weights = (last, third, third, last, middle, third, last, middle, last, third)
    return jax.shard_map(
        functools.partial(on_device, mesh),
        mesh=mesh,
        in_specs=(tokens, tokens) + weights,
        out_specs=(tokens, tokens) + weights,
        check_vma=False,
    )
```

```python
import collections
import functools
import types

import jax
import jax.numpy as jnp
from jax import lax
from jax.experimental import pallas as pl
from jax.experimental.pallas import tpu as pltpu
from jax.sharding import PartitionSpec as P

EPS = 1e-05
LOG2E = 1.4426950408889634
MESH = pl.DeviceIdType.MESH
F32, BF16 = jnp.float32, jnp.bfloat16
NT = (((1,), (1,)), ((), ()))
TN = (((0,), (0,)), ((), ()))
VMEM_BYTES = 63 * 2**20
CHUNK = 16
GROUP = 512
HALO = 16


def dot(a, b, dims=None):
    if dims is None:
        dims = (((1,), (0,)), ((), ()))
    return lax.dot_general(a, b, dims, preferred_element_type=F32)


def lanes(index, width):
    return pl.ds(pl.multiple_of(index * width, width), width)


def widen(tile, width):
    times = width // tile.shape[1]
    return jnp.concatenate([tile] * times, axis=1) if times > 1 else tile


def softplus(v):
    return jnp.maximum(v, 0.0) + jnp.log1p(jnp.exp(-jnp.abs(v)))


def sigmoid(v):
    return 1.0 / (1.0 + jnp.exp(-v))


def keep_sum(own_sum, i, step):
    total = jnp.sum(step, axis=0, keepdims=True)
    fold = own_sum.shape[1]
    for part in range(GROUP // fold):
        row = i * (GROUP // fold) + part
        own_sum[pl.ds(row, 1), :] = total[:, part * fold : (part + 1) * fold]


def sum_of(sum_s, j, g):
    fold = sum_s.shape[2]
    each = GROUP // fold
    return jnp.concatenate(
        [sum_s[j, pl.ds(g * each + part, 1), :] for part in range(each)], 1
    )


def chunk_mask(rows, states):
    wide = CHUNK * states
    token = lax.rem(lax.broadcasted_iota(jnp.int32, (rows, wide), 0), CHUNK)
    owner = lax.broadcasted_iota(jnp.int32, (rows, wide), 1) // states
    return token == owner


def spread(small_low, first, states):
    wide = CHUNK * states
    row = lax.broadcasted_iota(jnp.int32, (small_low.shape[1], wide), 0)
    col = lax.broadcasted_iota(jnp.int32, (small_low.shape[1], wide), 1)
    pick = (row == first + lax.rem(col, states)).astype(F32).astype(BF16)
    tiled = dot(small_low, pick)
    return jnp.where(chunk_mask(small_low.shape[0], states), tiled, 0.0).astype(BF16)


def gather_back(partial, first, states, width):
    wide = CHUNK * states
    row = lax.broadcasted_iota(jnp.int32, (wide, width), 0)
    col = lax.broadcasted_iota(jnp.int32, (wide, width), 1)
    pick = (col == first + lax.rem(row, states)).astype(F32).astype(BF16)
    kept = jnp.where(chunk_mask(partial.shape[0], states), partial, 0.0)
    return dot(kept.astype(BF16), pick)


class Names:
    def __init__(self, states, taps, rank):
        self.small = rank + 2 * states
        self.dt = self.small
        self.vec = self.small + rank
        self.count = self.vec + states + taps + 4
        self.rows = -(-self.count // 16) * 16
        self.conv = states
        self.conv_b = states + taps
        self.dt_b = states + taps + 1
        self.skip = states + taps + 2
        self.gain = states + taps + 3


def load_small(at, sw_ref, vec_s, dtw_s):
    states, rank = at.conv, at.vec - at.dt
    vec_s[...] = sw_ref[pl.ds(at.vec, at.rows - at.vec), :].astype(F32)
    vec_s[pl.ds(0, states), :] = -jnp.exp(vec_s[pl.ds(0, states), :])
    dtw_s[pl.ds(0, rank), :] = sw_ref[pl.ds(at.dt, rank), :]
    dtw_s[pl.ds(rank, at.small - rank), :] = jnp.zeros(
        (at.small - rank, dtw_s.shape[1]), BF16
    )


def gain_pick(channels):
    gains = channels // 2
    row = lax.broadcasted_iota(jnp.int32, (256, 128), 0)
    col = lax.broadcasted_iota(jnp.int32, (256, 128), 1)
    place = lax.div(col, gains) * channels + lax.rem(col, gains)
    return (row == place).astype(F32).astype(BF16)


def gain_row(at, channels, vec_s):
    pick = gain_pick(channels)
    row = vec_s[pl.ds(at.gain // 8 * 8, 8), :].astype(BF16)
    tiles = [
        dot(row[:, 256 * i : 256 * i + 256], pick) for i in range(row.shape[1] // 256)
    ]
    gain = jnp.concatenate(tiles, 1)
    return gain[at.gain % 8 : at.gain % 8 + 1]


def pack_small(at, layer, raw, sum_s, packed_s):
    x_weight, dt_weight, a_log, conv_weight, vectors, norm_gain = raw
    channels, states, rank = x_weight.shape[1], at.conv, at.vec - at.dt

    def place(count, first):
        row = lax.broadcasted_iota(jnp.int32, (count, 128), 0)
        col = lax.broadcasted_iota(jnp.int32, (count, 128), 1)
        return (col == row + first).astype(F32).astype(BF16)

    beside = place(channels, channels)
    sum_s[...] = dot(x_weight[layer], place(channels, 0), TN)
    sum_s[pl.ds(0, rank), :] += dot(dt_weight[layer], beside)
    sum_s[pl.ds(rank, states), :] += dot(a_log[layer], beside, TN)
    taps = conv_weight.shape[1]
    sum_s[pl.ds(rank + states, taps), :] += dot(conv_weight[layer], beside)
    row = rank + states + taps
    for ref in vectors:
        sum_s[pl.ds(row, 1), :] += dot(ref[...], beside)[layer : layer + 1]
        row += 1
    gains = dot(norm_gain[...], place(norm_gain.shape[1], channels))
    sum_s[pl.ds(row, 1), :] += gains[layer : layer + 1]
    packed_s[layer] = sum_s[...].astype(BF16)


def merge_small(channels, blocks, sw_ref):
    each = 128 // channels
    rows = blocks.shape[1]
    owner = lax.div(lax.broadcasted_iota(jnp.int32, (rows, 128), 1), channels)

    @pl.loop(0, sw_ref.shape[1] // 128)
    def _(j):
        held = [blocks[j * each + part].astype(F32) for part in range(each)]
        for fold in range(each):
            tile = None
            for part in range(each):
                shift = (part - fold) * channels % 128
                moved = pltpu.roll(held[part], shift, 1) if shift else held[part]
                tile = moved if tile is None else jnp.where(owner == part, moved, tile)
            sw_ref[pl.ds(fold * rows, rows), lanes(j, 128)] = tile.astype(BF16)


def split(number, by):
    if isinstance(number, int):
        return divmod(number, by)
    return lax.div(number, by), lax.rem(number, by)


class Folded:
    def __init__(self, ref):
        self.ref, self.shape = ref, ref.shape[3:]

    def __setitem__(self, block, value):
        _, x, z, core = self.ref.shape[:4]
        row = lax.div(block, z * core)
        self.ref[
            lax.div(row, x), lax.rem(row, x), lax.rem(lax.div(block, core), z), lax.rem(block, core)
        ] = value


def split_small(channels, full_ref, blocks):
    each = 128 // channels
    rows = blocks.shape[1]
    owner = lax.div(lax.broadcasted_iota(jnp.int32, (rows, 128), 1), channels)

    @pl.loop(0, full_ref.shape[1] // 128)
    def _(j):
        held = [
            full_ref[pl.ds(fold * rows, rows), lanes(j, 128)] for fold in range(each)
        ]
        for part in range(each):
            tile = None
            for fold in range(each):
                shift = (fold - part) * channels % 128
                moved = pltpu.roll(held[fold], shift, 1) if shift else held[fold]
                tile = moved if tile is None else jnp.where(owner == fold, moved, tile)
            blocks[j * each + part] = tile.astype(BF16)


def places():
    ctx, seq = lax.axis_index("ctx"), lax.axis_index("seq")
    return lax.div(ctx, 2), lax.rem(ctx, 2), lax.div(seq, 2), lax.rem(seq, 2)


def device(y, x, z, core):
    return (2 * y + x, 2 * z + core)


def square_partners(depth):
    y, x, z, core = places()
    partners = [device(y, x, z, 1 - core), device(y, 1 - x, z, core)]
    partners.append(device(1 - y, x, z, core))
    for step in range(1, depth):
        partners.append(device(y, x, lax.rem(z + step, depth), core))
    return partners


def greet_square(depth):
    barrier = pltpu.get_barrier_semaphore()
    partners = square_partners(depth)
    for partner in partners:
        pl.semaphore_signal(barrier, inc=1, device_id=partner, device_id_type=MESH)
    pl.semaphore_wait(barrier, len(partners))


class Gather:
    def __init__(self, depth, pieces, own_sem, send_sem, recv_sem):
        self.depth, self.pieces = depth, pieces
        self.own_sem, self.send_sem, self.recv_sem = own_sem, send_sem, recv_sem
        self.y, self.x, self.z, self.core = places()
        self.used = [0] * len(pieces)
        self.sent = []
        turn = 1 - 2 * lax.div(self.z, max(depth // 2, 1))
        self.line = [
            lax.rem(self.z + turn * step + depth, depth) for step in range(depth)
        ]
        y, x, z, core = self.y, self.x, self.z, self.core
        self.x_side, self.y_side = device(y, 1 - x, z, core), device(1 - y, x, z, core)
        self.sibling = device(y, x, z, 1 - core)

    @staticmethod
    def sends(depth):
        return 3 + depth - 1 + 3 * (depth - 1) + 2 * depth + 2 * depth

    def slot(self, y, x, z, core):
        return ((2 * y + x) * self.depth + z) * 2 + core

    def span(self, item, slot):
        _, whole, first, rows, _ = self.pieces[item]
        return whole.at[slot, pl.ds(first, rows)]

    def send(self, item, slot, to, own=False):
        local, _, first, rows, _ = self.pieces[item]
        copy = pltpu.make_async_remote_copy(
            local.at[pl.ds(first, rows)] if own else self.span(item, slot),
            self.span(item, slot),
            self.send_sem.at[item, self.used[item]],
            self.recv_sem.at[item, slot],
            device_id=to,
            device_id_type=MESH,
        )
        self.used[item] += 1
        copy.start()
        self.sent.append(copy)

    def arrive(self, item, slot):
        pltpu.make_async_remote_copy(
            self.span(item, slot),
            self.span(item, slot),
            self.send_sem.at[item, 0],
            self.recv_sem.at[item, slot],
            device_id=self.sibling,
            device_id_type=MESH,
        ).wait_recv()

    def own_copy(self, item):
        local, _, first, rows, _ = self.pieces[item]
        mine = self.slot(self.y, self.x, self.z, self.core)
        return pltpu.make_async_copy(
            local.at[pl.ds(first, rows)], self.span(item, mine), self.own_sem.at[item]
        )

    def begin(self, item):
        mine = self.slot(self.y, self.x, self.z, self.core)
        self.own_copy(item).start()
        for to in (self.x_side, self.y_side):
            self.send(item, mine, to, own=True)
        for step in range(1, self.depth):
            to = device(self.y, self.x, self.line[step], self.core)
            self.send(item, mine, to, own=True)
        self.send(item, mine, self.sibling, own=True)

    def along(self, item, step):
        slot = self.slot(self.y, self.x, self.line[step], self.core)
        self.arrive(item, slot)
        for to in (self.x_side, self.y_side, self.sibling):
            self.send(item, slot, to)

    def near(self, item, step):
        if self.pieces[item][4]:
            slot = self.slot(self.y, 1 - self.x, self.line[step], self.core)
            to = self.y_side
        else:
            slot = self.slot(1 - self.y, self.x, self.line[step], self.core)
            to = self.x_side
        self.arrive(item, slot)
        self.send(item, slot, to)
        self.send(item, slot, self.sibling)

    def far(self, item, step, other):
        y, x = 1 - self.y, 1 - self.x
        if self.pieces[item][4]:
            x = x if other else self.x
        else:
            y = y if other else self.y
        slot = self.slot(y, x, self.line[step], self.core)
        self.arrive(item, slot)
        self.send(item, slot, self.sibling)

    def settle(self, item):
        self.own_copy(item).wait()
        for step in range(self.depth):
            for y in (self.y, 1 - self.y):
                for x in (self.x, 1 - self.x):
                    self.arrive(item, self.slot(y, x, self.line[step], 1 - self.core))

    def turns(self, items):
        order = [("near", 0)]
        for step in range(1, self.depth):
            order.append(("along", step))
            order.append(("near", step))
            if step >= 2:
                order.append(("far", step - 2, 1))
            order.append(("far", step - 1, 0))
        for step in range(max(self.depth - 2, 0), self.depth):
            if step == self.depth - 1:
                order.append(("far", step, 0))
            order.append(("far", step, 1))
        actions = []
        for name, *rest in order:
            for item in items:
                actions.append(functools.partial(getattr(self, name), item, *rest))
        return actions

    def finish(self):
        for copy in self.sent:
            copy.wait_send()


class Reduce:
    def __init__(self, depth, pieces, buffers, own_sem, send_sem, recv_sem):
        self.depth, self.pieces, self.buffers = depth, pieces, buffers
        self.own_sem, self.send_sem, self.recv_sem = own_sem, send_sem, recv_sem
        y, x, z, core = places()
        self.y, self.x, self.core = y, x, core
        self.line = [lax.rem(z + step + 1, depth) for step in range(depth)]
        self.x_side, self.y_side = device(y, 1 - x, z, core), device(1 - y, x, z, core)
        self.sibling = device(y, x, z, 1 - core)
        self.along = [device(y, x, there, core) for there in self.line]
        self.sent = []

    @staticmethod
    def buffers_of(depth, rows, width, sided=False):
        square, row = ((2,), ()) if sided else ((2, 2), (2,))
        leads = ((2,) + square, (depth,) + square, (depth,) + row, (depth,), (depth - 1,))
        return [pltpu.VMEM(lead + (rows, width), BF16) for lead in leads]

    def part_of(self, item, step, core):
        whole, _, first, rows, _, side = self.pieces[item]
        y = slice(None) if side is None else side
        return whole.at[y, :, self.line[step], core, pl.ds(first, rows)]

    def local(self, item, step):
        return pltpu.make_async_copy(
            self.part_of(item, step, self.core),
            self.buffers[item][0].at[step % 2],
            self.own_sem.at[item, step % 2],
        )

    def hop(self, stage, item, step):
        _, core_in, first_in, second_in, line_in = self.buffers[item]
        crosses_y, side = self.pieces[item][4:]
        y, x = self.y, self.x
        if stage == 0:
            source = self.part_of(item, step, 1 - self.core)
            target, to = core_in.at[step], self.sibling
        elif stage == 1:
            if side is not None:
                source = core_in.at[step, 1 - x]
            elif crosses_y:
                source = core_in.at[step, 1 - y]
            else:
                source = core_in.at[step, :, 1 - x]
            target, to = first_in.at[step], self.y_side if crosses_y else self.x_side
        elif stage == 2:
            if side is not None:
                source = first_in.at[step]
            else:
                source = first_in.at[step, 1 - x if crosses_y else 1 - y]
            target, to = second_in.at[step], self.x_side if crosses_y else self.y_side
        else:
            source, target, to = second_in.at[step], line_in.at[step], self.along[step]
        return pltpu.make_async_remote_copy(
            source,
            target,
            self.send_sem.at[item, stage, step],
            self.recv_sem.at[item, stage, step],
            device_id=to,
            device_id_type=MESH,
        )

    def when(self, stage, item, receives, act):
        side = self.pieces[item][5]
        if side is None or stage < 2:
            act()
        elif stage == 2 and not receives:
            pl.when(self.y != side)(act)
        else:
            pl.when(self.y == side)(act)

    def send(self, stage, item, step):
        copy = self.hop(stage, item, step)
        self.when(stage, item, False, copy.start)
        self.sent.append((stage, item, copy))

    @staticmethod
    def add(target, other, rows):
        @pl.loop(0, rows // 16)
        def _(k):
            here = pl.ds(pl.multiple_of(k * 16, 16), 16)
            target[here] = (
                target[here].astype(F32) + other[here].astype(F32)
            ).astype(BF16)

    def begin(self, item):
        for step in range(self.depth):
            self.send(0, item, step)
            if step < 2:
                self.local(item, step).start()

    def settle(self, stage, item, step):
        self.when(
            stage, item, True, functools.partial(self.receive, stage, item, step)
        )
        if stage < 2 or step < self.depth - 1:
            self.send(stage + 1, item, step)

    def receive(self, stage, item, step):
        own, core_in, first_in, second_in, _ = self.buffers[item]
        rows, crosses_y, side = self.pieces[item][3:]
        self.hop(stage, item, step).wait_recv()
        if stage == 0:
            self.local(item, step).wait()
            for x in (0, 1):
                if side is not None:
                    self.add(core_in.at[step, x], own.at[step % 2, x], rows)
                    continue
                for y in (0, 1):
                    self.add(core_in.at[step, y, x], own.at[step % 2, y, x], rows)
            if step + 2 < self.depth:
                self.local(item, step + 2).start()
        elif stage == 1:
            if side is not None:
                self.add(first_in.at[step], core_in.at[step, self.x], rows)
                return
            for far in (0, 1):
                kept = (
                    core_in.at[step, self.y, far]
                    if crosses_y
                    else core_in.at[step, far, self.x]
                )
                self.add(first_in.at[step, far], kept, rows)
        elif side is not None:
            self.add(second_in.at[step], first_in.at[step], rows)
        else:
            kept = first_in.at[step, self.x if crosses_y else self.y]
            self.add(second_in.at[step], kept, rows)

    def last(self, item):
        self.when(3, item, True, functools.partial(self.total, item))

    def total(self, item):
        _, out, first, rows, _, _ = self.pieces[item]
        second_in, line_in = self.buffers[item][3:]
        for step in range(self.depth - 1):
            self.hop(3, item, step).wait_recv()

        @pl.loop(0, rows // 16)
        def _(k):
            here = pl.ds(pl.multiple_of(k * 16, 16), 16)
            total = second_in[self.depth - 1, here].astype(F32)
            for step in range(self.depth - 1):
                total = total + line_in[step, here].astype(F32)
            out[pl.ds(pl.multiple_of(first + k * 16, 16), 16)] = total

    def turns(self, items):
        actions = []
        for turn in range(self.depth + 2):
            for stage in range(3):
                step = turn - stage
                if 0 <= step < self.depth:
                    for item in items:
                        actions.append(
                            functools.partial(self.settle, stage, item, step)
                        )
        for item in items:
            actions.append(functools.partial(self.last, item))
        return actions

    def finish(self):
        for stage, item, copy in self.sent:
            self.when(stage, item, False, copy.wait_send)
        self.sent = []


def chain(count, me, ctx, own_sum, sum_s, own_end, end_s, sems):
    sum_send, sum_recv, end_send, end_recv = sems

    def sums(j, slot):
        return pltpu.make_async_remote_copy(
            own_sum,
            sum_s.at[slot],
            sum_send.at[j],
            sum_recv.at[slot],
            device_id=(ctx, j),
            device_id_type=MESH,
        )

    def ends(g, j, slot):
        return pltpu.make_async_remote_copy(
            own_end.at[:, pl.ds(g * GROUP, GROUP)],
            end_s.at[slot, :, pl.ds(g * GROUP, GROUP)],
            end_send.at[g, j],
            end_recv.at[g, slot],
            device_id=(ctx, j),
            device_id_type=MESH,
        )

    return sums, ends


def each(first, last, act):
    def body(j, _):
        act(j)
        return 0

    lax.fori_loop(first, last, body, 0)


def forward_kernel(cfg, mode, names, *refs):
    r = types.SimpleNamespace(**dict(zip(names, refs)))
    rows, inner, states, taps, rank, count, channels = cfg
    at = Names(states, taps, rank)
    ctx, me = lax.axis_index("ctx"), lax.axis_index("seq")
    groups, steps, tiles = inner // GROUP, rows // CHUNK, inner // GROUP
    depth = count // 2
    width = r.stream.shape[1]
    barrier = pltpu.get_barrier_semaphore()

    def greet(to):
        pl.semaphore_signal(barrier, inc=1, device_id=to, device_id_type=MESH)

    queue = collections.deque()

    def weave(times):
        for _ in range(min(times, len(queue))):
            queue.popleft()()

    if mode == "given":
        each(0, me, lambda j: greet((ctx, j)))
    else:
        each(0, me, lambda j: greet((ctx, j)))
        each(me + 1, count, lambda j: greet((ctx, j)))
        y, x, z, core = places()
        greet(device(y, 1 - x, z, core))
        greet(device(1 - y, x, z, core))

    if mode != "first":
        half = r.win_hbm.shape[0] // 2
        halves = [
            pltpu.make_async_copy(
                r.win_hbm.at[pl.ds(k * half, half)],
                r.win_s.at[pl.ds(k * half, half)],
                r.load_sem.at[k],
            )
            for k in range(2)
        ]
        if mode == "later":
            small_copy = pltpu.make_async_copy(r.gsm_hbm, r.gsm_s, r.load_sem.at[2])
            small_copy.start()
        for copy in halves:
            copy.start()
    if mode == "given":
        out_copy = pltpu.make_async_copy(r.wout_hbm, r.wout_s, r.load_sem.at[2])
        out_copy.start()

    if mode == "first":
        raw = (
            r.x_weight,
            r.dt_weight,
            r.a_log,
            r.conv_weight,
            (r.conv_bias, r.dt_bias, r.skip_gain),
            r.norm_gain,
        )
        for layer in range(2):
            pack_small(at, layer, raw, r.pack_s, r.packed_s)

    stream = r.stream[...].astype(F32)
    scale = lax.rsqrt(jnp.mean(stream * stream, axis=1, keepdims=True) + EPS)
    stores = []

    if mode == "given":

        @pl.when(me < count - 1)
        def _():
            pl.semaphore_wait(barrier, count - 1 - me)

    else:
        pl.semaphore_wait(barrier, count + 1)
        pieces = []

        def add_piece(local, whole, cuts):
            start = len(pieces)
            total = local.shape[0]
            for k, last_y in enumerate(cuts):
                piece = total // len(cuts)
                pieces.append((local, whole, k * piece, piece, last_y))
            return list(range(start, len(pieces)))

        first_items, next_items = [], []
        if mode == "first":
            first_items = add_piece(r.all_in.at[0], r.win_s, (1, 0))
            first_items += add_piece(r.packed_s.at[0], r.gsm_s, (1,))
        out_items = add_piece(
            r.all_out.at[0 if mode == "first" else 1], r.wout_s, (1, 0)
        )
        if mode == "first":
            next_items = add_piece(r.all_in.at[1], r.win2_all, (1, 0))
            next_items += add_piece(r.packed_s.at[1], r.gsm2_all, (0,))
        gather = Gather(depth, pieces, r.own_sem, r.send_sem, r.recv_sem)

        def begin(items):
            for item in items:
                gather.begin(item)

        def settle(items):
            for item in items:
                gather.settle(item)

        def keep(source, target, slot):
            copy = pltpu.make_async_copy(source, target, r.store_sem.at[slot])
            copy.start()
            stores.append(copy)

        if mode == "first":
            begin(first_items)
            turns = gather.turns(first_items)
            for k, turn in enumerate(turns):
                if k == len(turns) // 2:
                    begin(out_items + next_items)
                turn()
            settle(first_items)
            keep(r.win_s, r.win_all, 1)
            turns = gather.turns(out_items)
            queue.extend(gather.turns(out_items + next_items))
        else:
            begin(out_items)
            queue.extend(gather.turns(out_items))
        queue.append(lambda: settle(out_items))
        queue.append(lambda: keep(r.wout_s, r.wout_all, 0))
        if mode == "first":
            queue.append(lambda: settle(next_items))
        if mode == "later":
            small_copy.wait()
        merge_small(channels, r.gsm_s, r.sw)
    pace = -(-len(queue) // 33)

    load_small(at, r.sw, r.vec_s, r.dtw_s)
    r.normed_s[...] = (stream * scale * gain_row(at, channels, r.vec_s)).astype(BF16)
    per_tile = GROUP // r.win_s.shape[1]

    def win_tile(i):
        return r.win_s[pl.ds(i * per_tile, per_tile)].reshape(GROUP, width)

    if mode != "first":
        halves[0].wait()

    @pl.loop(0, tiles)
    def _(i):
        low = dot(r.normed_s[...], win_tile(i), NT).astype(BF16)
        r.pad[pl.ds(HALO, rows), lanes(i, GROUP)] = low
        r.padf_s[pl.ds(HALO, rows), lanes(i, GROUP)] = low.astype(F32)

    def edge():
        return pltpu.make_async_remote_copy(
            r.pad.at[pl.ds(rows, HALO)],
            r.halo_s,
            r.halo_sem.at[0],
            r.halo_sem.at[1],
            device_id=(ctx, jnp.minimum(me + 1, count - 1)),
            device_id_type=MESH,
        )

    @pl.when(me < count - 1)
    def _():
        edge().start()

    weave(pace)
    if mode != "first":
        halves[1].wait()

    @pl.loop(0, tiles)
    def _(i):
        r.gate[:, lanes(i, GROUP)] = dot(r.normed_s[...], win_tile(i + tiles), NT)

    weave(pace)

    @pl.when(me > 0)
    def _():
        edge().wait_recv()

    @pl.when(me == 0)
    def _():
        r.halo_s[...] = jnp.zeros_like(r.halo_s)

    r.pad[pl.ds(0, HALO), :] = r.halo_s[...]
    r.padf_s[pl.ds(0, HALO), :] = r.halo_s[...].astype(F32)

    @pl.loop(0, tiles)
    def _(i):
        here = lanes(i, GROUP)
        total = r.vec_s[pl.ds(at.conv_b, 1), here]
        for k in range(taps):
            total = (
                total
                + r.vec_s[pl.ds(at.conv + k, 1), here]
                * r.padf_s[pl.ds(HALO - taps + 1 + k, rows), here]
            )
        r.act[:, here] = (total * sigmoid(total)).astype(BF16)

    weave(pace)
    small = dot(r.act[...], r.sw[pl.ds(0, at.small), :], NT)
    r.sp[...] = small
    small_low = small.astype(BF16)

    @pl.loop(0, tiles)
    def _(i):
        here = lanes(i, GROUP)
        before = dot(small_low, r.dtw_s[:, here]) + r.vec_s[pl.ds(at.dt_b, 1), here]
        step = softplus(before)
        r.pre[:, here] = before
        r.dt_s[:, here] = step
        r.dx_s[:, here] = step * r.act[:, here].astype(F32)
        keep_sum(r.own_sum, i, step)

    sums, ends = chain(
        count, me, ctx, r.own_sum, r.sum_s, r.own_end, r.end_s,
        (r.sum_send, r.sum_recv, r.end_send, r.end_recv),
    )
    each(me + 1, count, lambda j: sums(j, me).start())
    saves = []

    def save(name, slot, part=slice(None)):
        copy = pltpu.make_async_copy(
            getattr(r, name).at[:, part],
            getattr(r, name + "_hbm").at[:, part],
            r.save_sem.at[slot],
        )
        copy.start()
        saves.append(copy)

    for slot, name in enumerate(("pad", "gate", "act", "pre")):
        save(name, slot)
    weave(pace)
    for n in range(states):
        r.bb_s[:, n, :] = jnp.broadcast_to(
            small[:, rank + n : rank + n + 1], (rows, 128)
        )
    r.cd_s[...] = spread(small_low, rank + states, states)

    def advance(t, state, rate2, here):
        return (
            jnp.exp2(r.dt_s[pl.ds(t, 1), here] * rate2) * state
            + r.dx_s[pl.ds(t, 1), here] * widen(r.bb_s[t], GROUP)
        )

    for g in range(groups):
        here = pl.ds(g * GROUP, GROUP)
        rate2 = r.vec_s[pl.ds(0, states), here] * LOG2E

        def first_pass(step, state):
            for i in range(CHUNK):
                state = advance(step * CHUNK + i, state, rate2, here)
            return state

        state = jnp.zeros((states, GROUP), F32)
        for part in range(2):
            state = lax.fori_loop(
                steps * part // 2, steps * (part + 1) // 2, first_pass, state
            )
            weave(pace)
        r.own_end[:, here] = state.astype(BF16)
        each(me + 1, count, lambda j: ends(g, j, me).start())

    def h_copy(g):
        here = pl.ds(g * GROUP, GROUP)
        return pltpu.make_async_copy(
            r.hs.at[:, here], r.h_hbm.at[:, here], r.h_sem.at[g]
        )

    for g in range(groups):
        here = pl.ds(g * GROUP, GROUP)
        rate2 = r.vec_s[pl.ds(0, states), here] * LOG2E

        def carry(j, state):
            if g == 0:
                sums(j, j).wait_recv()
            ends(g, j, j).wait_recv()
            return (
                jnp.exp2(rate2 * sum_of(r.sum_s, j, g)) * state
                + r.end_s[j, :, here].astype(F32)
            )

        state = lax.fori_loop(0, me, carry, jnp.zeros((states, GROUP), F32))
        r.hs[pl.ds(0, states), here] = state.astype(BF16)

        def second_pass(step, state):
            base = pl.multiple_of(step * CHUNK * states + states, states)
            for i in range(CHUNK):
                state = advance(step * CHUNK + i, state, rate2, here)
                r.hs[pl.ds(base + i * states, states), here] = state.astype(BF16)
            tokens = pl.ds(pl.multiple_of(step * CHUNK, CHUNK), CHUNK)
            r.y[tokens, here] = dot(
                r.cd_s[tokens, :], r.hs[pl.ds(base, CHUNK * states), here]
            )
            return state

        thirds = 1 if mode == "given" else 5
        for part in range(thirds):
            state = lax.fori_loop(
                steps * part // thirds,
                steps * (part + 1) // thirds,
                second_pass,
                state,
            )
            weave(pace)
        h_copy(g).start()
        y_value = (
            r.y[:, here]
            + r.vec_s[pl.ds(at.skip, 1), here] * r.act[:, here].astype(F32)
        )
        gate = r.gate[:, here]
        r.y[:, here] = y_value
        r.mixed[:, here] = (y_value * gate * sigmoid(gate)).astype(BF16)
        save("y", 4 + 2 * g, here)
        save("mixed", 5 + 2 * g, here)

    if mode == "given":
        out_copy.wait()
    else:
        while queue and not stores_hold_out(mode, stores):
            weave(1)
    out_tile = 256 // r.wout_s.shape[1]
    for i in range(width // 256):
        here = pl.ds(i * 256, 256)
        wout = r.wout_s[pl.ds(i * out_tile, out_tile)].reshape(256, inner)
        r.new[:, here] = (
            r.stream[:, here].astype(F32) + dot(r.mixed[...], wout, NT)
        ).astype(r.new.dtype)

    weave(len(queue))
    if mode != "given":
        gather.finish()

    @pl.when(me < count - 1)
    def _():
        edge().wait_send()

    each(me + 1, count, lambda j: sums(j, me).wait_send())
    for g in range(groups):
        each(me + 1, count, lambda j: ends(g, j, me).wait_send())
        h_copy(g).wait()
    for copy in stores + saves:
        copy.wait()


def stores_hold_out(mode, stores):
    return len(stores) == (2 if mode == "first" else 1)


def backward_kernel(cfg, mode, names, *refs):
    r = types.SimpleNamespace(**dict(zip(names, refs)))
    rows, inner, states, taps, rank, count, channels = cfg
    at = Names(states, taps, rank)
    ctx, me = lax.axis_index("ctx"), lax.axis_index("seq")
    groups, steps, tiles = inner // GROUP, rows // CHUNK, inner // GROUP
    depth = count // 2
    width = r.stream.shape[1]
    barrier = pltpu.get_barrier_semaphore()
    gvec = r.full_s.at[pl.ds(at.vec, at.rows - at.vec)]

    def signal(semaphore, to):
        pl.semaphore_signal(semaphore, inc=1, device_id=to, device_id_type=MESH)

    queue = collections.deque()

    def weave(times):
        for _ in range(min(times, len(queue))):
            queue.popleft()()

    each(me + 1, count, lambda j: signal(barrier, (ctx, j)))
    if mode != "given":
        each(0, me, lambda j: signal(barrier, (ctx, j)))
        y, x, z, core = places()
        signal(barrier, device(y, 1 - x, z, core))
        signal(barrier, device(1 - y, x, z, core))

    def wout_copy(i):
        slot = lax.rem(i, 2)
        return pltpu.make_async_copy(
            r.wout.at[:, :, lanes(i, GROUP)], r.wout_s.at[slot], r.wout_sem.at[slot]
        )

    def gate_copies(i):
        slot = lax.rem(i, 2)
        return [
            pltpu.make_async_copy(
                array.at[:, lanes(i, GROUP)], r.gate_s.at[slot, k], r.gate_sem.at[slot, k]
            )
            for k, array in enumerate((r.gate, r.y))
        ]

    win_rows = r.win_s.shape[1]

    def win_copy(i, slot):
        return pltpu.make_async_copy(
            r.win.at[pl.ds(i * win_rows, win_rows)], r.win_s.at[slot], r.win_sem.at[slot]
        )

    span = rows // 2 * states

    def states_in(k):
        g, half = k // 2, 1 - k % 2
        return pltpu.make_async_copy(
            r.h_hbm.at[pl.ds(half * span, span + states), pl.ds(g * GROUP, GROUP)],
            r.hb.at[k % 2],
            r.h_sem.at[k % 2],
        )

    fetches = {
        name: pltpu.make_async_copy(
            getattr(r, name + "_hbm"), getattr(r, name), r.fetch_sem.at[k]
        )
        for k, name in enumerate(("stream", "pre", "act", "pad"))
    }
    for copy in fetches.values():
        copy.start()
    wout_copy(0).start()
    win_copy(tiles, 0).start()
    for copy in gate_copies(0):
        copy.start()
    load_small(at, r.sw, r.vec_s, r.dtw_s)
    gain = gain_row(at, channels, r.vec_s)
    r.low_s[...] = r.sgrad[...].astype(BF16)
    small_low = r.sp[...].astype(BF16)

    in_items, out_items, own_items = [], [], []
    if mode == "given":

        @pl.when(me > 0)
        def _():
            pl.semaphore_wait(barrier, me)

    else:
        pl.semaphore_wait(barrier, count + 1)
        pieces, buffers = [], []

        def add_piece(whole, out, cuts, held, side=None):
            start = len(pieces)
            total = whole.shape[4]
            for k, first_y in enumerate(cuts):
                piece = total // len(cuts)
                pieces.append((whole, out, k * piece, piece, first_y, side))
                buffers.append(held[k])
            return list(range(start, len(pieces)))

        def held_by(name):
            found = []
            while hasattr(r, f"{name}{len(found)}_0"):
                k = len(found)
                found.append([getattr(r, f"{name}{k}_{part}") for part in range(5)])
            return found

        held_in, held_small, held_out = (
            held_by("rin"),
            held_by("rsmall"),
            held_by("rout"),
        )
        out_items = add_piece(r.gout, r.sum_out, (1, 0), held_out)
        if mode == "first":
            in_items = add_piece(r.next_gin, r.sum_next_in, (1, 0, 1, 0), held_in)
            in_items += add_piece(r.next_gsmall, r.sum_next_small, (1,), held_small)
            own_items = add_piece(r.gin, r.sum_in, (1, 0, 1, 0), held_in)
            own_items += add_piece(r.gsmall_hbm, r.sum_small, (1,), held_small)
        reduce = Reduce(depth, pieces, buffers, r.own_sem, r.send_sem, r.recv_sem)
        for item in in_items:
            reduce.begin(item)

    r.lowt_s[...] = r.sgrad[...].astype(F32).T.astype(BF16)
    out_shape = r.stage_out.shape[1:]
    out_rows = out_shape[0] * out_shape[1] * out_shape[2]
    line = r.gout.shape[2]

    def block_of(whole, i):
        row, z = split(2 * i, line)
        y, x = split(row, 2)
        return whole.at[y, x, pl.ds(z, 2)]

    for k in range(width // out_rows):
        slot = k % 2
        copy = pltpu.make_async_copy(
            r.stage_out.at[slot], block_of(r.gout, k), r.out_sem.at[slot]
        )
        if k >= 2:
            copy.wait()

        @pl.loop(0, tiles)
        def _(i):
            here = lanes(i, GROUP)
            r.stage_out[slot, :, :, :, here] = (
                dot(r.lowt_s[pl.ds(k * out_rows, out_rows), :], r.mixed[:, here])
                .astype(BF16)
                .reshape(out_shape[:-1] + (GROUP,))
            )

        copy.start()
    for slot in range(2):
        pltpu.make_async_copy(
            r.stage_out.at[slot], block_of(r.gout, 0), r.out_sem.at[slot]
        ).wait()
    if mode != "given":
        for item in out_items:
            reduce.begin(item)
        queue.extend(reduce.turns(in_items + out_items))
    pace = -(-len(queue) // (24 if mode == "first" else 26))

    fetches["stream"].wait()
    stream = r.stream[...].astype(F32)
    scale = lax.rsqrt(jnp.mean(stream * stream, axis=1, keepdims=True) + EPS)
    r.normed_s[...] = (stream * scale * gain).astype(BF16)
    fetches["pre"].wait()
    fetches["act"].wait()

    @pl.loop(0, tiles)
    def _(i):
        here = lanes(i, GROUP)
        slot = lax.rem(i, 2)

        @pl.when(i + 1 < tiles)
        def _():
            wout_copy(i + 1).start()
            for copy in gate_copies(i + 1):
                copy.start()

        wout_copy(i).wait()
        for copy in gate_copies(i):
            copy.wait()
        mixed_grad = dot(r.low_s[...], r.wout_s[slot].reshape(width, GROUP))
        gate = r.gate_s[slot, 0]
        sig = sigmoid(gate)
        act = r.act[:, here].astype(F32)
        scan_grad = mixed_grad * gate * sig
        r.sg_s[:, here] = scan_grad
        r.pb_s[:, lanes(i + tiles, GROUP)] = (
            mixed_grad * r.gate_s[slot, 1] * sig * (1.0 + gate * (1.0 - sig))
        ).astype(BF16)
        gvec[pl.ds(at.skip, 1), here] = jnp.sum(scan_grad * act, axis=0, keepdims=True)
        step = softplus(r.pre[:, here])
        r.dt_s[:, here] = step
        r.dx_s[pl.ds(0, rows), here] = step * act
        keep_sum(r.own_sum, i, step)

    sums, ends = chain(
        count, me, ctx, r.own_sum, r.sum_s, r.own_end, r.end_s,
        (r.sum_send, r.sum_recv, r.end_send, r.end_recv),
    )
    each(0, me, lambda j: sums(j, me).start())
    weave(pace)
    in_shape = r.stage_in.shape[1:]

    def in_copy(i, slot):
        return pltpu.make_async_copy(
            r.stage_in.at[slot], block_of(r.gin, i), r.in_sem.at[slot]
        )

    def project(i, turn):
        here = lanes(i, GROUP)
        slot = lax.rem(turn, 2)
        copy = in_copy(i, slot)
        following = lax.rem(i + 1, 2 * tiles)

        @pl.when(turn + 1 < 2 * tiles)
        def _():
            win_copy(following, 1 - slot).start()

        @pl.when(turn >= 2)
        def _():
            copy.wait()

        r.stage_in[slot] = (
            dot(r.pb_s[:, here], r.normed_s[...], TN).astype(BF16).reshape(in_shape)
        )
        copy.start()
        win_copy(i, slot).wait()
        part = dot(r.pb_s[:, here], r.win_s[slot].reshape(GROUP, width))

        @pl.when(turn == 0)
        def _():
            r.nsg[...] = part

        @pl.when(turn > 0)
        def _():
            r.nsg[...] += part

    @pl.loop(0, tiles)
    def _(i):
        project(i + tiles, i)

    weave(pace)
    for n in range(states):
        first = rank + states + n
        r.cb_s[:, n, :] = jnp.broadcast_to(r.sp[:, first : first + 1], (rows, 128))
    r.bd_s[...] = spread(small_low, rank, states)
    ones = jnp.where(chunk_mask(CHUNK, states), 1.0, 0.0).astype(BF16)
    states_in(0).start()

    for g in range(groups):
        here = pl.ds(g * GROUP, GROUP)
        rate2 = r.vec_s[pl.ds(0, states), here] * LOG2E

        def first_pass(k, state):
            step = steps - 1 - k
            for i in reversed(range(CHUNK)):
                t = step * CHUNK + i
                state = jnp.exp2(r.dt_s[pl.ds(t, 1), here] * rate2) * (
                    state + r.sg_s[pl.ds(t, 1), here] * widen(r.cb_s[t], GROUP)
                )
            return state

        r.own_end[:, here] = lax.fori_loop(
            0, steps, first_pass, jnp.zeros((states, GROUP), F32)
        ).astype(BF16)
        each(0, me, lambda j: ends(g, j, me).start())
        weave(pace)

    for g in range(groups):
        here = pl.ds(g * GROUP, GROUP)
        rate = r.vec_s[pl.ds(0, states), here]
        rate2 = rate * LOG2E

        def carry(k, state):
            j = count - 1 - k
            if g == 0:
                sums(j, j).wait_recv()
            ends(g, j, j).wait_recv()
            return (
                jnp.exp2(rate2 * sum_of(r.sum_s, j, g)) * state
                + r.end_s[j, :, here].astype(F32)
            )

        begin = lax.fori_loop(
            0, count - 1 - me, carry, jnp.zeros((states, GROUP), F32)
        )
        both = (begin, jnp.zeros((states, GROUP), F32))
        for part in range(2):
            k = 2 * g + part
            half = 1 - part
            held_states = r.hb.at[k % 2]
            if k + 1 < 2 * groups:
                states_in(k + 1).start()
            states_in(k).wait()

            def second_pass(turn, both):
                state, total = both
                step = steps - 1 - turn
                base = pl.multiple_of(step * CHUNK * states - half * span, states)
                for i in reversed(range(CHUNK)):
                    t = step * CHUNK + i
                    dt = r.dt_s[pl.ds(t, 1), here]
                    adjoint = state + r.sg_s[pl.ds(t, 1), here] * widen(
                        r.cb_s[t], GROUP
                    )
                    state = jnp.exp2(dt * rate2) * adjoint
                    held = held_states[pl.ds(base + i * states, states), :]
                    rated = state * held.astype(F32) * rate
                    total = total + dt * rated
                    r.ab_s[pl.ds(i * states, states), :] = adjoint.astype(BF16)
                    r.rb_s[pl.ds(i * states, states), :] = rated.astype(BF16)
                tokens = pl.ds(pl.multiple_of(step * CHUNK, CHUNK), CHUNK)
                from_in = dot(r.bd_s[tokens, :], r.ab_s[...])
                from_rate = dot(ones, r.rb_s[...])
                scan_grad = r.sg_s[tokens, here]
                into_in = dot(r.dx_s[tokens, here].astype(BF16), r.ab_s[...], NT)
                into_out = dot(
                    scan_grad.astype(BF16),
                    held_states[pl.ds(base + states, CHUNK * states), :],
                    NT,
                )
                if g == 0:
                    r.pin_s[tokens, :] = into_in
                    r.pout_s[tokens, :] = into_out
                else:
                    r.pin_s[tokens, :] += into_in
                    r.pout_s[tokens, :] += into_out
                r.stepg_s[tokens, here] = (
                    r.act[tokens, here].astype(F32) * from_in + from_rate
                )
                r.sg_s[tokens, here] = (
                    r.dt_s[tokens, here] * from_in
                    + r.vec_s[pl.ds(at.skip, 1), here] * scan_grad
                )
                return state, total

            for quarter in range(2):
                low = (2 * part + quarter) * steps // 4
                high = (2 * part + quarter + 1) * steps // 4
                both = lax.fori_loop(low, high, second_pass, both)
                weave(pace)
        gvec[pl.ds(0, states), here] = both[1]

    fetches["pad"].wait()

    @pl.loop(0, tiles)
    def _(i):
        here = lanes(i, GROUP)
        pre_grad = r.stepg_s[pl.ds(0, rows), here] * sigmoid(r.pre[:, here])
        gvec[pl.ds(at.dt_b, 1), here] = jnp.sum(pre_grad, axis=0, keepdims=True)
        r.prelow_s[:, here] = pre_grad.astype(BF16)
        r.dx_s[:, here] = r.pad[:, here].astype(F32)

    small_grad = (
        dot(r.prelow_s[...], r.dtw_s[...], NT)
        + gather_back(r.pin_s[...], rank, states, at.small)
        + gather_back(r.pout_s[...], rank + states, states, at.small)
    ).astype(BF16)

    @pl.loop(0, tiles)
    def _(i):
        here = lanes(i, GROUP)
        r.full_s[pl.ds(at.dt, rank), here] = dot(
            small_low, r.prelow_s[:, here], TN
        )[:rank]
        r.full_s[pl.ds(0, at.small), here] = dot(small_grad, r.act[:, here], TN)
        act_grad = r.sg_s[:, here] + dot(small_grad, r.sw[pl.ds(0, at.small), here])
        total = r.vec_s[pl.ds(at.conv_b, 1), here]
        for k in range(taps):
            total = (
                total
                + r.vec_s[pl.ds(at.conv + k, 1), here]
                * r.dx_s[pl.ds(HALO - taps + 1 + k, rows), here]
            )
        sig = sigmoid(total)
        conv_grad = act_grad * sig * (1.0 + total * (1.0 - sig))
        r.stepg_s[pl.ds(0, rows), here] = conv_grad
        gvec[pl.ds(at.conv_b, 1), here] = jnp.sum(conv_grad, axis=0, keepdims=True)
        for k in range(taps):
            gvec[pl.ds(at.conv + k, 1), here] = jnp.sum(
                conv_grad * r.dx_s[pl.ds(HALO - taps + 1 + k, rows), here],
                axis=0,
                keepdims=True,
            )

    def edge():
        return pltpu.make_async_remote_copy(
            r.stepg_s.at[pl.ds(0, 8)],
            r.halo_s,
            r.halo_sem.at[0],
            r.halo_sem.at[1],
            device_id=(ctx, jnp.maximum(me - 1, 0)),
            device_id_type=MESH,
        )

    @pl.when(me > 0)
    def _():
        edge().start()

    weave(pace)
    @pl.when(me < count - 1)
    def _():
        edge().wait_recv()

    @pl.when(me == count - 1)
    def _():
        r.halo_s[...] = jnp.zeros_like(r.halo_s)

    @pl.when(me > 0)
    def _():
        edge().wait_send()

    r.stepg_s[pl.ds(rows, 8), :] = r.halo_s[...]

    @pl.loop(0, tiles)
    def _(i):
        here = lanes(i, GROUP)
        total = jnp.zeros((rows, GROUP), F32)
        for k in range(taps):
            total = (
                total
                + r.vec_s[pl.ds(at.conv + k, 1), here]
                * r.stepg_s[pl.ds(taps - 1 - k, rows), here]
            )
        r.pb_s[:, here] = total.astype(BF16)
        project(i, i + tiles)

    stream = r.stream[...].astype(F32)
    scale = lax.rsqrt(jnp.mean(stream * stream, axis=1, keepdims=True) + EPS)
    normed_grad = r.nsg[...]
    gain_grad = jnp.sum(normed_grad * stream * scale, axis=0, keepdims=True)
    gain_grad = jnp.broadcast_to(gain_grad, (8, width)).astype(BF16)
    pick = gain_pick(channels)
    for i in range(inner // 256):
        wide = dot(gain_grad[:, 128 * i : 128 * i + 128], pick, NT)
        gvec[pl.ds(at.gain, 1), pl.ds(256 * i, 256)] = wide[:1]
    for k in range(at.count, at.rows):
        r.full_s[pl.ds(k, 1), :] = jnp.zeros((1, inner), F32)
    if mode == "given":
        r.gsmall[...] = r.full_s[...]
    elif mode == "last":
        split_small(channels, r.full_s, r.gsmall)
    else:
        split_small(channels, r.full_s, Folded(r.gsmall_s))
        small_copy = pltpu.make_async_copy(r.gsmall_s, r.gsmall_hbm, r.small_sem.at[0])
        small_copy.start()
    scaled = normed_grad * gain
    inner_sum = jnp.mean(scaled * stream, axis=1, keepdims=True)
    r.nsg[...] = (
        r.sgrad[...].astype(F32) + scale * scaled - stream * (scale * scale * scale) * inner_sum
    )
    for slot in range(2):
        in_copy(0, slot).wait()
    weave(len(queue))
    if mode == "first":
        small_copy.wait()
        reduce.finish()
        for partner in square_partners(depth):
            signal(r.ready_sem, partner)
        pl.semaphore_wait(r.ready_sem, len(square_partners(depth)))
        for item in own_items:
            reduce.begin(item)
        for turn in reduce.turns(own_items):
            turn()
    if mode != "given":
        reduce.finish()
    each(0, me, lambda j: sums(j, me).wait_send())
    for g in range(groups):
        each(0, me, lambda j: ends(g, j, me).wait_send())


def in_vmem(count):
    return [pl.BlockSpec(memory_space=pltpu.VMEM)] * count


def in_any(count):
    return [pl.BlockSpec(memory_space=pl.ANY)] * count


def forward_call(cfg, mode, stream, operands):
    rows, inner, states, taps, rank, count, channels = cfg
    at = Names(states, taps, rank)
    width = stream.shape[1]
    groups = inner // GROUP
    devices = inner // channels
    shape = jax.ShapeDtypeStruct
    dma = pltpu.SemaphoreType.DMA
    vmem, any_space = in_vmem(1)[0], in_any(1)[0]
    inputs = [("stream", stream, vmem)]
    for name, array in operands:
        large = name.startswith(("all_", "win_", "wout_", "gsm_"))
        inputs.append((name, array, any_space if large else vmem))
    outputs = [
        ("new", shape(stream.shape, BF16 if mode == "later" else F32), vmem),
        ("sp", shape((rows, at.small), F32), vmem),
        ("h_hbm", shape(((rows + 1) * states, inner), BF16), any_space),
    ]
    saved = {
        "pad": ((rows + HALO, inner), BF16),
        "gate": ((rows, inner), F32),
        "act": ((rows, inner), BF16),
        "pre": ((rows, inner), F32),
        "y": ((rows, inner), F32),
        "mixed": ((rows, inner), BF16),
    }
    for name, (size, kind) in saved.items():
        outputs.append((name + "_hbm", shape(size, kind), any_space))
    if mode == "given":
        given = dict(operands)
        in_shape, out_shape = given["win_hbm"].shape, given["wout_hbm"].shape
    else:
        in_shape = (devices, 2 * inner // devices, width)
        out_shape = (devices, width // devices, inner)
        small_shape = (devices, at.rows * channels // 128, 128)
        outputs.append(("sw", shape((at.rows, inner), BF16), vmem))
        outputs.append(("wout_all", shape(out_shape, BF16), any_space))
    if mode == "first":
        outputs.append(("win_all", shape(in_shape, BF16), any_space))
        outputs.append(("win2_all", shape(in_shape, BF16), any_space))
        outputs.append(("gsm2_all", shape(small_shape, BF16), any_space))
    scratch = [
        ("win_s", pltpu.VMEM(in_shape, BF16)),
        ("wout_s", pltpu.VMEM(out_shape, BF16)),
        ("vec_s", pltpu.VMEM((at.rows - at.vec, inner), F32)),
        ("dtw_s", pltpu.VMEM((at.small, inner), BF16)),
        ("normed_s", pltpu.VMEM(stream.shape, BF16)),
        ("padf_s", pltpu.VMEM((rows + HALO, inner), F32)),
        ("halo_s", pltpu.VMEM((HALO, inner), BF16)),
        ("dt_s", pltpu.VMEM((rows, inner), F32)),
        ("dx_s", pltpu.VMEM((rows, inner), F32)),
        ("bb_s", pltpu.VMEM((rows, states, 128), F32)),
        ("cd_s", pltpu.VMEM((rows, CHUNK * states), BF16)),
        ("hs", pltpu.VMEM(((rows + 1) * states, inner), BF16)),
        ("own_sum", pltpu.VMEM((8, inner // 8), F32)),
        ("sum_s", pltpu.VMEM((count, 8, inner // 8), F32)),
        ("own_end", pltpu.VMEM((states, inner), BF16)),
        ("end_s", pltpu.VMEM((count, states, inner), BF16)),
        ("halo_sem", dma((2,))),
        ("sum_send", dma((count,))),
        ("sum_recv", dma((count,))),
        ("end_send", dma((groups, count))),
        ("end_recv", dma((groups, count))),
        ("h_sem", dma((groups,))),
        ("load_sem", dma((3,))),
        ("save_sem", dma((4 + 2 * groups,))),
    ]
    for name, (size, kind) in saved.items():
        scratch.append((name, pltpu.VMEM(size, kind)))
    if mode != "given":
        pieces = 8 if mode == "first" else 2
        scratch += [
            ("gsm_s", pltpu.VMEM(small_shape, BF16)),
            ("pack_s", pltpu.VMEM(small_shape[1:], F32)),
            ("packed_s", pltpu.VMEM((2,) + small_shape[1:], BF16)),
            ("own_sem", dma((pieces,))),
            ("send_sem", dma((pieces, Gather.sends(count // 2)))),
            ("recv_sem", dma((pieces, devices))),
            ("store_sem", dma((2,))),
        ]
    names = [entry[0] for entry in inputs + outputs + scratch]
    results = pl.pallas_call(
        functools.partial(forward_kernel, cfg, mode, names),
        out_shape=tuple(entry[1] for entry in outputs),
        in_specs=[entry[2] for entry in inputs],
        out_specs=tuple(entry[2] for entry in outputs),
        scratch_shapes=[entry[1] for entry in scratch],
        compiler_params=pltpu.CompilerParams(
            collective_id={"given": 0, "first": 4, "later": 5}[mode],
            has_side_effects=True,
            vmem_limit_bytes=VMEM_BYTES,
        ),
        name="forward_" + mode,
    )(*[entry[1] for entry in inputs])
    return {
        entry[0].removesuffix("_hbm"): result
        for entry, result in zip(outputs, results)
    }


def backward_call(cfg, mode, sgrad, stream, weights, saved, later):
    rows, inner, states, taps, rank, count, channels = cfg
    at = Names(states, taps, rank)
    width = stream.shape[1]
    groups = inner // GROUP
    wide = CHUNK * states
    depth = count // 2
    sw, win, wout = weights
    shape = jax.ShapeDtypeStruct
    dma = pltpu.SemaphoreType.DMA
    vmem, any_space = in_vmem(1)[0], in_any(1)[0]
    in_rows, out_rows = win.shape[1], wout.shape[1]
    lead = (1, 1, win.shape[0] // 2, 2) if mode == "given" else (2, 2, depth, 2)
    small_rows = at.rows * channels // 128
    inputs = [
        ("sgrad", sgrad, vmem),
        ("sw", sw, vmem),
        ("win", win, any_space),
        ("wout", wout, any_space),
    ]
    for name in ("sp", "mixed"):
        inputs.append((name, saved[name], vmem))
    for name in ("gate", "y"):
        inputs.append((name, saved[name], any_space))
    inputs.append(("h_hbm", saved["h"], any_space))
    fetched = {name: saved[name] for name in ("pre", "act", "pad")}
    fetched["stream"] = stream
    for name, array in fetched.items():
        inputs.append((name + "_hbm", array, any_space))
    outputs = [
        ("nsg", shape((rows, width), F32), vmem),
        ("gin", shape(lead + (in_rows, width), BF16), any_space),
        ("gout", shape(lead + (out_rows, inner), BF16), any_space),
    ]
    scratch = [
        ("full_s", pltpu.VMEM((at.rows, inner), F32)),
        ("vec_s", pltpu.VMEM((at.rows - at.vec, inner), F32)),
        ("dtw_s", pltpu.VMEM((at.small, inner), BF16)),
        ("hb", pltpu.VMEM((2, (rows // 2 + 1) * states, GROUP), BF16)),
        ("normed_s", pltpu.VMEM((rows, width), BF16)),
        ("low_s", pltpu.VMEM((rows, width), BF16)),
        ("lowt_s", pltpu.VMEM((width, rows), BF16)),
        ("sg_s", pltpu.VMEM((rows, inner), F32)),
        ("dt_s", pltpu.VMEM((rows, inner), F32)),
        ("dx_s", pltpu.VMEM((rows + HALO, inner), F32)),
        ("stepg_s", pltpu.VMEM((rows + 8, inner), F32)),
        ("pb_s", pltpu.VMEM((rows, 2 * inner), BF16)),
        ("cb_s", pltpu.VMEM((rows, states, 128), F32)),
        ("bd_s", pltpu.VMEM((rows, wide), BF16)),
        ("ab_s", pltpu.VMEM((wide, GROUP), BF16)),
        ("rb_s", pltpu.VMEM((wide, GROUP), BF16)),
        ("pin_s", pltpu.VMEM((rows, wide), F32)),
        ("pout_s", pltpu.VMEM((rows, wide), F32)),
        ("prelow_s", pltpu.VMEM((rows, inner), BF16)),
        ("stage_in", pltpu.VMEM((2, 2, 2, in_rows, width), BF16)),
        ("stage_out", pltpu.VMEM((2, 2, 2, out_rows, inner), BF16)),
        ("win_s", pltpu.VMEM((2, GROUP // in_rows, in_rows, width), BF16)),
        ("wout_s", pltpu.VMEM((2,) + wout.shape[:2] + (GROUP,), BF16)),
        ("gate_s", pltpu.VMEM((2, 2, rows, GROUP), F32)),
        ("halo_s", pltpu.VMEM((8, inner), F32)),
        ("own_sum", pltpu.VMEM((8, inner // 8), F32)),
        ("sum_s", pltpu.VMEM((count, 8, inner // 8), F32)),
        ("own_end", pltpu.VMEM((states, inner), BF16)),
        ("end_s", pltpu.VMEM((count, states, inner), BF16)),
        ("halo_sem", dma((2,))),
        ("sum_send", dma((count,))),
        ("sum_recv", dma((count,))),
        ("end_send", dma((groups, count))),
        ("end_recv", dma((groups, count))),
        ("h_sem", dma((2,))),
        ("in_sem", dma((2,))),
        ("out_sem", dma((2,))),
        ("win_sem", dma((2,))),
        ("wout_sem", dma((2,))),
        ("gate_sem", dma((2, 2))),
        ("fetch_sem", dma((len(fetched),))),
    ]
    for name, array in fetched.items():
        scratch.append((name, pltpu.VMEM(array.shape, array.dtype)))
    if mode == "given":
        outputs.append(("gsmall", shape((at.rows, inner), F32), vmem))
    else:
        outputs.append(("sum_out", shape((out_rows, inner), F32), vmem))
        held = [("rout", out_rows // 2, inner, 2, False)]
        pieces = 2
        if mode == "last":
            small_shape = (inner // channels, small_rows, 128)
            outputs.append(("gsmall", shape(small_shape, BF16), vmem))
        else:
            inputs.append(("next_gin", later["gin"], any_space))
            small = later["gsmall"].reshape(lead + (small_rows, 128))
            inputs.append(("next_gsmall", small, any_space))
            outputs.append(("gsmall_hbm", shape(small.shape, BF16), any_space))
            scratch.append(("gsmall_s", pltpu.VMEM(small.shape, BF16)))
            for name in ("sum_in", "sum_next_in"):
                outputs.append((name, shape((in_rows, width), F32), vmem))
            for name in ("sum_small", "sum_next_small"):
                outputs.append((name, shape((small_rows, 128), F32), vmem))
            held.append(("rin", in_rows // 4, width, 4, False))
            held.append(("rsmall", small_rows, 128, 1, False))
            scratch.append(("small_sem", dma((1,))))
            scratch.append(("ready_sem", pltpu.SemaphoreType.REGULAR))
            pieces = 12
        for name, piece, wide_by, cuts, sided in held:
            for k in range(cuts):
                found = Reduce.buffers_of(depth, piece, wide_by, sided)
                for part, buffer in enumerate(found):
                    scratch.append((f"{name}{k}_{part}", buffer))
        scratch += [
            ("own_sem", dma((pieces, 2))),
            ("send_sem", dma((pieces, 4, depth))),
            ("recv_sem", dma((pieces, 4, depth))),
        ]
    names = [entry[0] for entry in inputs + outputs + scratch]
    results = pl.pallas_call(
        functools.partial(backward_kernel, cfg, mode, names),
        out_shape=tuple(entry[1] for entry in outputs),
        in_specs=[entry[2] for entry in inputs],
        out_specs=tuple(entry[2] for entry in outputs),
        scratch_shapes=[entry[1] for entry in scratch],
        compiler_params=pltpu.CompilerParams(
            collective_id={"given": 1, "last": 6, "first": 7}[mode],
            has_side_effects=True,
            vmem_limit_bytes=VMEM_BYTES,
        ),
        name="backward_" + mode,
    )(*[entry[1] for entry in inputs])
    return {entry[0]: result for entry, result in zip(outputs, results)}


def on_device(
    mesh,
    hidden_in,
    cotangent,
    norm_gain,
    in_weight,
    conv_weight,
    conv_bias,
    x_weight,
    dt_weight,
    dt_bias,
    a_log,
    skip_gain,
    out_weight,
):
    layers = norm_gain.shape[0]
    rows, width = hidden_in.shape
    taps, channels = conv_weight.shape[1:]
    states = a_log.shape[2]
    rank = dt_weight.shape[1]
    devices, count = mesh.shape["ctx"] * mesh.shape["seq"], mesh.shape["seq"]
    inner = channels * devices
    gains = norm_gain.shape[1]
    at = Names(states, taps, rank)
    cfg = (rows, inner, states, taps, rank, count, channels)
    depth = count // 2
    by_kernel = (
        mesh.shape["ctx"] == 4
        and depth % 2 == 0
        and layers == 2
        and in_weight.shape[2] % 32 == 0
        and out_weight.shape[2] % 32 == 0
        and channels == 64
        and at.rows == 2 * at.small
    )

    all_in, all_out = in_weight.transpose(0, 2, 1), out_weight.transpose(0, 2, 1)
    stream = hidden_in if by_kernel else hidden_in.astype(F32)
    streams, runs, weights = [], [], []
    if by_kernel:
        operands = [
            ("all_in", all_in),
            ("x_weight", x_weight),
            ("dt_weight", dt_weight),
            ("a_log", a_log),
            ("conv_weight", conv_weight),
            ("conv_bias", conv_bias),
            ("dt_bias", dt_bias),
            ("skip_gain", skip_gain),
            ("norm_gain", norm_gain),
            ("all_out", all_out),
        ]
        first = forward_call(cfg, "first", stream, operands)
        operands = [
            ("win_hbm", first["win2_all"]),
            ("gsm_hbm", first["gsm2_all"]),
            ("all_out", all_out),
        ]
        second = forward_call(cfg, "later", first["new"], operands)
        runs = [first, second]
        wins = [first["win_all"], first["win2_all"]]
        weights = [
            (run["sw"], win, run["wout_all"]) for run, win in zip(runs, wins)
        ]
        streams = [stream, first["new"]]
        stream = second["new"]
    else:
        gain_rows = jnp.pad(norm_gain, ((0, 0), (0, channels - gains)))
        packed = jnp.concatenate(
            [
                x_weight.transpose(0, 2, 1),
                dt_weight,
                a_log.transpose(0, 2, 1),
                conv_weight,
                jnp.stack([conv_bias, dt_bias, skip_gain, gain_rows], 1),
                jnp.zeros((layers, at.rows - at.count, channels), BF16),
            ],
            1,
        )
        for w_in, w_out, w_small in zip(all_in, all_out, packed):
            w_in = lax.all_gather(w_in, ("ctx", "seq"), axis=0, tiled=True)
            w_out = lax.all_gather(w_out, ("ctx", "seq"), axis=0, tiled=True)
            sw = lax.all_gather(w_small, ("ctx", "seq"), axis=1, tiled=True)
            w_in = w_in.reshape(-1, 128, width)
            w_out = w_out.reshape(-1, 32, inner)
            operands = [("win_hbm", w_in), ("sw", sw), ("wout_hbm", w_out)]
            run = forward_call(cfg, "given", stream, operands)
            runs.append(run)
            weights.append((sw, w_in, w_out))
            streams.append(stream)
            stream = run["new"]
    stream_grad = cotangent
    summed = [None] * layers
    if by_kernel:
        last = backward_call(
            cfg, "last", stream_grad, streams[1], weights[1], runs[1], None
        )
        head = backward_call(
            cfg, "first", last["nsg"], streams[0], weights[0], runs[0], last
        )
        stream_grad = head["nsg"]

        def unfold(small):
            small = small.reshape(-1, 128 // channels, channels)
            return small.transpose(1, 0, 2).reshape(at.rows, channels)

        summed = [
            (head["sum_in"], head["sum_out"], unfold(head["sum_small"])),
            (head["sum_next_in"], last["sum_out"], unfold(head["sum_next_small"])),
        ]
    else:
        for layer in reversed(range(layers)):
            run = backward_call(
                cfg,
                "given",
                stream_grad,
                streams[layer],
                weights[layer],
                runs[layer],
                None,
            )
            stream_grad = run["nsg"]
            summed[layer] = [
                lax.psum_scatter(
                    array.astype(F32),
                    ("ctx", "seq"),
                    scatter_dimension=dim,
                    tiled=True,
                )
                for array, dim in (
                    (run["gin"].reshape(-1, width), 0),
                    (run["gout"].reshape(-1, inner), 0),
                    (run["gsmall"], 1),
                )
            ]
    grads = [None] * layers
    for layer in range(layers):
        s_in, s_out, s_small = summed[layer]
        s_x = s_small[: at.small, :channels]
        s_dt = s_small[at.dt : at.dt + rank, :channels]
        s_vec = s_small[at.vec : at.count, :channels]
        grads[layer] = (
            s_vec[at.gain, :gains],
            s_in.T,
            s_vec[at.conv : at.conv + taps],
            s_vec[at.conv_b],
            s_x.T,
            s_dt,
            s_vec[at.dt_b],
            s_vec[:states].T,
            s_vec[at.skip],
            s_out.T,
        )
    stacked = tuple(
        jnp.stack([grads[layer][member] for layer in range(layers)], 0)
        for member in range(10)
    )
    return (stream.astype(BF16), stream_grad) + stacked


def solution(mesh):
    split = ("ctx", "seq")
    tokens, last = P(split, None), P(None, split)
    middle, third = P(None, split, None), P(None, None, split)
    weights = (last, third, third, last, middle, third, last, middle, last, third)
    return jax.shard_map(
        functools.partial(on_device, mesh),
        mesh=mesh,
        in_specs=(tokens, tokens) + weights,
        out_specs=(tokens, tokens) + weights,
        check_vma=False,
    )
```

```python
import collections
import functools
import types

import jax
import jax.numpy as jnp
from jax import lax
from jax.experimental import pallas as pl
from jax.experimental.pallas import tpu as pltpu
from jax.sharding import PartitionSpec as P

EPS = 1e-05
LOG2E = 1.4426950408889634
MESH = pl.DeviceIdType.MESH
F32, BF16 = jnp.float32, jnp.bfloat16
NT = (((1,), (1,)), ((), ()))
TN = (((0,), (0,)), ((), ()))
VMEM_BYTES = 63 * 2**20
CHUNK = 16
GROUP = 512
WIDE = 1024
HALO = 16


def dot(a, b, dims=None):
    if dims is None:
        dims = (((1,), (0,)), ((), ()))
    return lax.dot_general(a, b, dims, preferred_element_type=F32)


def lanes(index, width):
    return pl.ds(pl.multiple_of(index * width, width), width)


def widen(tile, width):
    times = width // tile.shape[1]
    return jnp.concatenate([tile] * times, axis=1) if times > 1 else tile


def softplus(v):
    return jnp.maximum(v, 0.0) + jnp.log1p(jnp.exp(-jnp.abs(v)))


def sigmoid(v):
    return 1.0 / (1.0 + jnp.exp(-v))


def keep_sum(own_sum, i, step):
    total = jnp.sum(step, axis=0, keepdims=True)
    fold = own_sum.shape[1]
    for part in range(GROUP // fold):
        row = i * (GROUP // fold) + part
        own_sum[pl.ds(row, 1), :] = total[:, part * fold : (part + 1) * fold]


def sum_of(sum_s, j, g):
    fold = sum_s.shape[2]
    each = GROUP // fold
    return jnp.concatenate(
        [sum_s[j, pl.ds(g * each + part, 1), :] for part in range(each)], 1
    )


def chunk_mask(rows, states):
    wide = CHUNK * states
    token = lax.rem(lax.broadcasted_iota(jnp.int32, (rows, wide), 0), CHUNK)
    owner = lax.broadcasted_iota(jnp.int32, (rows, wide), 1) // states
    return token == owner


def spread(small_low, first, states):
    wide = CHUNK * states
    row = lax.broadcasted_iota(jnp.int32, (small_low.shape[1], wide), 0)
    col = lax.broadcasted_iota(jnp.int32, (small_low.shape[1], wide), 1)
    pick = (row == first + lax.rem(col, states)).astype(F32).astype(BF16)
    tiled = dot(small_low, pick)
    return jnp.where(chunk_mask(small_low.shape[0], states), tiled, 0.0).astype(BF16)


def gather_back(partial, first, states, width):
    wide = CHUNK * states
    row = lax.broadcasted_iota(jnp.int32, (wide, width), 0)
    col = lax.broadcasted_iota(jnp.int32, (wide, width), 1)
    pick = (col == first + lax.rem(row, states)).astype(F32).astype(BF16)
    kept = jnp.where(chunk_mask(partial.shape[0], states), partial, 0.0)
    return dot(kept.astype(BF16), pick)


class Names:
    def __init__(self, states, taps, rank):
        self.small = rank + 2 * states
        self.dt = self.small
        self.vec = self.small + rank
        self.count = self.vec + states + taps + 4
        self.rows = -(-self.count // 16) * 16
        self.conv = states
        self.conv_b = states + taps
        self.dt_b = states + taps + 1
        self.skip = states + taps + 2
        self.gain = states + taps + 3


def load_small(at, sw_ref, vec_s, dtw_s):
    states, rank = at.conv, at.vec - at.dt
    vec_s[...] = sw_ref[pl.ds(at.vec, at.rows - at.vec), :].astype(F32)
    vec_s[pl.ds(0, states), :] = -jnp.exp(vec_s[pl.ds(0, states), :])
    dtw_s[pl.ds(0, rank), :] = sw_ref[pl.ds(at.dt, rank), :]
    dtw_s[pl.ds(rank, at.small - rank), :] = jnp.zeros(
        (at.small - rank, dtw_s.shape[1]), BF16
    )


def gain_pick(channels):
    gains = channels // 2
    row = lax.broadcasted_iota(jnp.int32, (256, 128), 0)
    col = lax.broadcasted_iota(jnp.int32, (256, 128), 1)
    place = lax.div(col, gains) * channels + lax.rem(col, gains)
    return (row == place).astype(F32).astype(BF16)


def gain_row(at, channels, vec_s):
    pick = gain_pick(channels)
    row = vec_s[pl.ds(at.gain // 8 * 8, 8), :].astype(BF16)
    tiles = [
        dot(row[:, 256 * i : 256 * i + 256], pick) for i in range(row.shape[1] // 256)
    ]
    gain = jnp.concatenate(tiles, 1)
    return gain[at.gain % 8 : at.gain % 8 + 1]


def pack_small(at, layer, raw, sum_s, packed_s):
    x_weight, dt_weight, a_log, conv_weight, vectors, norm_gain = raw
    channels, states, rank = x_weight.shape[1], at.conv, at.vec - at.dt

    def place(count, first):
        row = lax.broadcasted_iota(jnp.int32, (count, 128), 0)
        col = lax.broadcasted_iota(jnp.int32, (count, 128), 1)
        return (col == row + first).astype(F32).astype(BF16)

    beside = place(channels, channels)
    sum_s[...] = dot(x_weight[layer], place(channels, 0), TN)
    sum_s[pl.ds(0, rank), :] += dot(dt_weight[layer], beside)
    sum_s[pl.ds(rank, states), :] += dot(a_log[layer], beside, TN)
    taps = conv_weight.shape[1]
    sum_s[pl.ds(rank + states, taps), :] += dot(conv_weight[layer], beside)
    row = rank + states + taps
    for ref in vectors:
        sum_s[pl.ds(row, 1), :] += dot(ref[...], beside)[layer : layer + 1]
        row += 1
    gains = dot(norm_gain[...], place(norm_gain.shape[1], channels))
    sum_s[pl.ds(row, 1), :] += gains[layer : layer + 1]
    packed_s[layer] = sum_s[...].astype(BF16)


def merge_small(channels, blocks, sw_ref):
    each = 128 // channels
    rows = blocks.shape[1]
    owner = lax.div(lax.broadcasted_iota(jnp.int32, (rows, 128), 1), channels)

    @pl.loop(0, sw_ref.shape[1] // 128)
    def _(j):
        held = [blocks[j * each + part].astype(F32) for part in range(each)]
        for fold in range(each):
            tile = None
            for part in range(each):
                shift = (part - fold) * channels % 128
                moved = pltpu.roll(held[part], shift, 1) if shift else held[part]
                tile = moved if tile is None else jnp.where(owner == part, moved, tile)
            sw_ref[pl.ds(fold * rows, rows), lanes(j, 128)] = tile.astype(BF16)


def split(number, by):
    if isinstance(number, int):
        return divmod(number, by)
    return lax.div(number, by), lax.rem(number, by)


class Folded:
    def __init__(self, ref):
        self.ref, self.shape = ref, ref.shape[3:]

    def __setitem__(self, block, value):
        _, x, z, core = self.ref.shape[:4]
        row = lax.div(block, z * core)
        self.ref[
            lax.div(row, x), lax.rem(row, x), lax.rem(lax.div(block, core), z), lax.rem(block, core)
        ] = value


def split_small(channels, full_ref, blocks):
    each = 128 // channels
    rows = blocks.shape[1]
    owner = lax.div(lax.broadcasted_iota(jnp.int32, (rows, 128), 1), channels)

    @pl.loop(0, full_ref.shape[1] // 128)
    def _(j):
        held = [
            full_ref[pl.ds(fold * rows, rows), lanes(j, 128)] for fold in range(each)
        ]
        for part in range(each):
            tile = None
            for fold in range(each):
                shift = (fold - part) * channels % 128
                moved = pltpu.roll(held[fold], shift, 1) if shift else held[fold]
                tile = moved if tile is None else jnp.where(owner == fold, moved, tile)
            blocks[j * each + part] = tile.astype(BF16)


def places():
    ctx, seq = lax.axis_index("ctx"), lax.axis_index("seq")
    return lax.div(ctx, 2), lax.rem(ctx, 2), lax.div(seq, 2), lax.rem(seq, 2)


def device(y, x, z, core):
    return (2 * y + x, 2 * z + core)


def square_partners(depth):
    y, x, z, core = places()
    partners = [device(y, x, z, 1 - core), device(y, 1 - x, z, core)]
    partners.append(device(1 - y, x, z, core))
    for step in range(1, depth):
        partners.append(device(y, x, lax.rem(z + step, depth), core))
    return partners


def greet_square(depth):
    barrier = pltpu.get_barrier_semaphore()
    partners = square_partners(depth)
    for partner in partners:
        pl.semaphore_signal(barrier, inc=1, device_id=partner, device_id_type=MESH)
    pl.semaphore_wait(barrier, len(partners))


class Gather:
    def __init__(self, depth, pieces, own_sem, send_sem, recv_sem):
        self.depth, self.pieces = depth, pieces
        self.own_sem, self.send_sem, self.recv_sem = own_sem, send_sem, recv_sem
        self.y, self.x, self.z, self.core = places()
        self.used = [0] * len(pieces)
        self.sent = []
        turn = 1 - 2 * lax.div(self.z, max(depth // 2, 1))
        self.line = [
            lax.rem(self.z + turn * step + depth, depth) for step in range(depth)
        ]
        y, x, z, core = self.y, self.x, self.z, self.core
        self.x_side, self.y_side = device(y, 1 - x, z, core), device(1 - y, x, z, core)
        self.sibling = device(y, x, z, 1 - core)

    @staticmethod
    def sends(depth):
        return 3 + depth - 1 + 3 * (depth - 1) + 2 * depth + 2 * depth

    def slot(self, y, x, z, core):
        return ((2 * y + x) * self.depth + z) * 2 + core

    def span(self, item, slot):
        _, whole, first, rows, _ = self.pieces[item]
        return whole.at[slot, pl.ds(first, rows)]

    def send(self, item, slot, to, own=False):
        local, _, first, rows, _ = self.pieces[item]
        copy = pltpu.make_async_remote_copy(
            local.at[pl.ds(first, rows)] if own else self.span(item, slot),
            self.span(item, slot),
            self.send_sem.at[item, self.used[item]],
            self.recv_sem.at[item, slot],
            device_id=to,
            device_id_type=MESH,
        )
        self.used[item] += 1
        copy.start()
        self.sent.append(copy)

    def arrive(self, item, slot):
        pltpu.make_async_remote_copy(
            self.span(item, slot),
            self.span(item, slot),
            self.send_sem.at[item, 0],
            self.recv_sem.at[item, slot],
            device_id=self.sibling,
            device_id_type=MESH,
        ).wait_recv()

    def own_copy(self, item):
        local, _, first, rows, _ = self.pieces[item]
        mine = self.slot(self.y, self.x, self.z, self.core)
        return pltpu.make_async_copy(
            local.at[pl.ds(first, rows)], self.span(item, mine), self.own_sem.at[item]
        )

    def begin(self, item):
        mine = self.slot(self.y, self.x, self.z, self.core)
        self.own_copy(item).start()
        for to in (self.x_side, self.y_side):
            self.send(item, mine, to, own=True)
        for step in range(1, self.depth):
            to = device(self.y, self.x, self.line[step], self.core)
            self.send(item, mine, to, own=True)
        self.send(item, mine, self.sibling, own=True)

    def along(self, item, step):
        slot = self.slot(self.y, self.x, self.line[step], self.core)
        self.arrive(item, slot)
        for to in (self.x_side, self.y_side, self.sibling):
            self.send(item, slot, to)

    def near(self, item, step):
        if self.pieces[item][4]:
            slot = self.slot(self.y, 1 - self.x, self.line[step], self.core)
            to = self.y_side
        else:
            slot = self.slot(1 - self.y, self.x, self.line[step], self.core)
            to = self.x_side
        self.arrive(item, slot)
        self.send(item, slot, to)
        self.send(item, slot, self.sibling)

    def far(self, item, step, other):
        y, x = 1 - self.y, 1 - self.x
        if self.pieces[item][4]:
            x = x if other else self.x
        else:
            y = y if other else self.y
        slot = self.slot(y, x, self.line[step], self.core)
        self.arrive(item, slot)
        self.send(item, slot, self.sibling)

    def settle(self, item):
        self.own_copy(item).wait()
        for step in range(self.depth):
            for y in (self.y, 1 - self.y):
                for x in (self.x, 1 - self.x):
                    self.arrive(item, self.slot(y, x, self.line[step], 1 - self.core))

    def turns(self, items):
        order = [("near", 0)]
        for step in range(1, self.depth):
            order.append(("along", step))
            order.append(("near", step))
            if step >= 2:
                order.append(("far", step - 2, 1))
            order.append(("far", step - 1, 0))
        for step in range(max(self.depth - 2, 0), self.depth):
            if step == self.depth - 1:
                order.append(("far", step, 0))
            order.append(("far", step, 1))
        actions = []
        for name, *rest in order:
            for item in items:
                actions.append(functools.partial(getattr(self, name), item, *rest))
        return actions

    def finish(self):
        for copy in self.sent:
            copy.wait_send()


class Reduce:
    def __init__(self, depth, pieces, buffers, own_sem, send_sem, recv_sem):
        self.depth, self.pieces, self.buffers = depth, pieces, buffers
        self.own_sem, self.send_sem, self.recv_sem = own_sem, send_sem, recv_sem
        y, x, z, core = places()
        self.y, self.x, self.core = y, x, core
        self.line = [lax.rem(z + step + 1, depth) for step in range(depth)]
        self.x_side, self.y_side = device(y, 1 - x, z, core), device(1 - y, x, z, core)
        self.sibling = device(y, x, z, 1 - core)
        self.along = [device(y, x, there, core) for there in self.line]
        self.sent = []

    @staticmethod
    def buffers_of(depth, rows, width, sided=False):
        square, row = ((2,), ()) if sided else ((2, 2), (2,))
        leads = ((2,) + square, (depth,) + square, (depth,) + row, (depth,), (depth - 1,))
        return [pltpu.VMEM(lead + (rows, width), BF16) for lead in leads]

    def part_of(self, item, step, core):
        whole, _, first, rows, _, side = self.pieces[item]
        y = slice(None) if side is None else side
        return whole.at[y, :, self.line[step], core, pl.ds(first, rows)]

    def local(self, item, step):
        return pltpu.make_async_copy(
            self.part_of(item, step, self.core),
            self.buffers[item][0].at[step % 2],
            self.own_sem.at[item, step % 2],
        )

    def hop(self, stage, item, step):
        _, core_in, first_in, second_in, line_in = self.buffers[item]
        crosses_y, side = self.pieces[item][4:]
        y, x = self.y, self.x
        if stage == 0:
            source = self.part_of(item, step, 1 - self.core)
            target, to = core_in.at[step], self.sibling
        elif stage == 1:
            if side is not None:
                source = core_in.at[step, 1 - x]
            elif crosses_y:
                source = core_in.at[step, 1 - y]
            else:
                source = core_in.at[step, :, 1 - x]
            target, to = first_in.at[step], self.y_side if crosses_y else self.x_side
        elif stage == 2:
            if side is not None:
                source = first_in.at[step]
            else:
                source = first_in.at[step, 1 - x if crosses_y else 1 - y]
            target, to = second_in.at[step], self.x_side if crosses_y else self.y_side
        else:
            source, target, to = second_in.at[step], line_in.at[step], self.along[step]
        return pltpu.make_async_remote_copy(
            source,
            target,
            self.send_sem.at[item, stage, step],
            self.recv_sem.at[item, stage, step],
            device_id=to,
            device_id_type=MESH,
        )

    def when(self, stage, item, receives, act):
        side = self.pieces[item][5]
        if side is None or stage < 2:
            act()
        elif stage == 2 and not receives:
            pl.when(self.y != side)(act)
        else:
            pl.when(self.y == side)(act)

    def send(self, stage, item, step):
        copy = self.hop(stage, item, step)
        self.when(stage, item, False, copy.start)
        self.sent.append((stage, item, copy))

    @staticmethod
    def add(target, other, rows):
        @pl.loop(0, rows // 16)
        def _(k):
            here = pl.ds(pl.multiple_of(k * 16, 16), 16)
            target[here] = (
                target[here].astype(F32) + other[here].astype(F32)
            ).astype(BF16)

    def begin(self, item):
        for step in range(self.depth):
            self.send(0, item, step)
            if step < 2:
                self.local(item, step).start()

    def settle(self, stage, item, step):
        self.when(
            stage, item, True, functools.partial(self.receive, stage, item, step)
        )
        if stage < 2 or step < self.depth - 1:
            self.send(stage + 1, item, step)

    def receive(self, stage, item, step):
        own, core_in, first_in, second_in, _ = self.buffers[item]
        rows, crosses_y, side = self.pieces[item][3:]
        self.hop(stage, item, step).wait_recv()
        if stage == 0:
            self.local(item, step).wait()
            for x in (0, 1):
                if side is not None:
                    self.add(core_in.at[step, x], own.at[step % 2, x], rows)
                    continue
                for y in (0, 1):
                    self.add(core_in.at[step, y, x], own.at[step % 2, y, x], rows)
            if step + 2 < self.depth:
                self.local(item, step + 2).start()
        elif stage == 1:
            if side is not None:
                self.add(first_in.at[step], core_in.at[step, self.x], rows)
                return
            for far in (0, 1):
                kept = (
                    core_in.at[step, self.y, far]
                    if crosses_y
                    else core_in.at[step, far, self.x]
                )
                self.add(first_in.at[step, far], kept, rows)
        elif side is not None:
            self.add(second_in.at[step], first_in.at[step], rows)
        else:
            kept = first_in.at[step, self.x if crosses_y else self.y]
            self.add(second_in.at[step], kept, rows)

    def last(self, item):
        self.when(3, item, True, functools.partial(self.total, item))

    def total(self, item):
        _, out, first, rows, _, _ = self.pieces[item]
        second_in, line_in = self.buffers[item][3:]
        for step in range(self.depth - 1):
            self.hop(3, item, step).wait_recv()

        @pl.loop(0, rows // 16)
        def _(k):
            here = pl.ds(pl.multiple_of(k * 16, 16), 16)
            total = second_in[self.depth - 1, here].astype(F32)
            for step in range(self.depth - 1):
                total = total + line_in[step, here].astype(F32)
            out[pl.ds(pl.multiple_of(first + k * 16, 16), 16)] = total

    def turns(self, items):
        actions = []
        for turn in range(self.depth + 2):
            for stage in range(3):
                step = turn - stage
                if 0 <= step < self.depth:
                    for item in items:
                        actions.append(
                            functools.partial(self.settle, stage, item, step)
                        )
        for item in items:
            actions.append(functools.partial(self.last, item))
        return actions

    def finish(self):
        for stage, item, copy in self.sent:
            self.when(stage, item, False, copy.wait_send)
        self.sent = []


def chain(count, me, ctx, own_sum, sum_s, own_end, end_s, sems):
    sum_send, sum_recv, end_send, end_recv = sems

    def sums(j, slot):
        return pltpu.make_async_remote_copy(
            own_sum,
            sum_s.at[slot],
            sum_send.at[j],
            sum_recv.at[slot],
            device_id=(ctx, j),
            device_id_type=MESH,
        )

    def ends(g, j, slot):
        return pltpu.make_async_remote_copy(
            own_end.at[:, pl.ds(g * GROUP, GROUP)],
            end_s.at[slot, :, pl.ds(g * GROUP, GROUP)],
            end_send.at[g, j],
            end_recv.at[g, slot],
            device_id=(ctx, j),
            device_id_type=MESH,
        )

    return sums, ends


def each(first, last, act):
    def body(j, _):
        act(j)
        return 0

    lax.fori_loop(first, last, body, 0)


def forward_kernel(cfg, mode, names, *refs):
    r = types.SimpleNamespace(**dict(zip(names, refs)))
    rows, inner, states, taps, rank, count, channels = cfg
    at = Names(states, taps, rank)
    ctx, me = lax.axis_index("ctx"), lax.axis_index("seq")
    groups, steps, tiles = inner // GROUP, rows // CHUNK, inner // GROUP
    depth = count // 2
    width = r.stream.shape[1]
    barrier = pltpu.get_barrier_semaphore()

    def greet(to):
        pl.semaphore_signal(barrier, inc=1, device_id=to, device_id_type=MESH)

    queue = collections.deque()

    owed = [0.0]

    def weave(times):
        owed[0] += times
        while queue and owed[0] >= 1:
            owed[0] -= 1
            queue.popleft()()

    if mode == "given":
        each(0, me, lambda j: greet((ctx, j)))
    else:
        each(0, me, lambda j: greet((ctx, j)))
        each(me + 1, count, lambda j: greet((ctx, j)))
        y, x, z, core = places()
        greet(device(y, 1 - x, z, core))
        greet(device(1 - y, x, z, core))

    if mode != "first":
        half = r.win_hbm.shape[0] // 2
        halves = [
            pltpu.make_async_copy(
                r.win_hbm.at[pl.ds(k * half, half)],
                r.win_s.at[pl.ds(k * half, half)],
                r.load_sem.at[k],
            )
            for k in range(2)
        ]
        if mode == "later":
            small_copy = pltpu.make_async_copy(r.gsm_hbm, r.gsm_s, r.load_sem.at[2])
            small_copy.start()
        for copy in halves:
            copy.start()
    if mode == "given":
        out_copy = pltpu.make_async_copy(r.wout_hbm, r.wout_s, r.load_sem.at[2])
        out_copy.start()

    if mode == "first":
        raw = (
            r.x_weight,
            r.dt_weight,
            r.a_log,
            r.conv_weight,
            (r.conv_bias, r.dt_bias, r.skip_gain),
            r.norm_gain,
        )
        for layer in range(2):
            pack_small(at, layer, raw, r.pack_s, r.packed_s)

    stream = r.stream[...].astype(F32)
    scale = lax.rsqrt(jnp.mean(stream * stream, axis=1, keepdims=True) + EPS)
    stores = []

    if mode == "given":

        @pl.when(me < count - 1)
        def _():
            pl.semaphore_wait(barrier, count - 1 - me)

    else:
        pl.semaphore_wait(barrier, count + 1)
        pieces = []

        def add_piece(local, whole, cuts):
            start = len(pieces)
            total = local.shape[0]
            for k, last_y in enumerate(cuts):
                piece = total // len(cuts)
                pieces.append((local, whole, k * piece, piece, last_y))
            return list(range(start, len(pieces)))

        first_items, next_items = [], []
        if mode == "first":
            first_items = add_piece(r.all_in.at[0], r.win_s, (1, 0))
            first_items += add_piece(r.packed_s.at[0], r.gsm_s, (1,))
        out_items = add_piece(
            r.all_out.at[0 if mode == "first" else 1], r.wout_s, (1, 0)
        )
        if mode == "first":
            next_items = add_piece(r.all_in.at[1], r.win2_all, (1, 0))
            next_items += add_piece(r.packed_s.at[1], r.gsm2_all, (0,))
        gather = Gather(depth, pieces, r.own_sem, r.send_sem, r.recv_sem)

        def begin(items):
            for item in items:
                gather.begin(item)

        def settle(items):
            for item in items:
                gather.settle(item)

        def keep(source, target, slot):
            copy = pltpu.make_async_copy(source, target, r.store_sem.at[slot])
            copy.start()
            stores.append(copy)

        if mode == "first":
            begin(first_items)
            turns = gather.turns(first_items)
            for k, turn in enumerate(turns):
                if k == len(turns) // 2:
                    begin(out_items + next_items)
                turn()
            settle(first_items)
            keep(r.win_s, r.win_all, 1)
            turns = gather.turns(out_items)
            queue.extend(gather.turns(out_items + next_items))
        else:
            begin(out_items)
            queue.extend(gather.turns(out_items))
        queue.append(lambda: settle(out_items))
        queue.append(lambda: keep(r.wout_s, r.wout_all, 0))
        if mode == "first":
            queue.append(lambda: settle(next_items))
        if mode == "later":
            small_copy.wait()
        merge_small(channels, r.gsm_s, r.sw)
    pace = len(queue) / (36 if mode == "first" else 33)

    load_small(at, r.sw, r.vec_s, r.dtw_s)
    r.normed_s[...] = (stream * scale * gain_row(at, channels, r.vec_s)).astype(BF16)
    per_tile = GROUP // r.win_s.shape[1]

    def win_tile(i):
        return r.win_s[pl.ds(i * per_tile, per_tile)].reshape(GROUP, width)

    if mode != "first":
        halves[0].wait()

    @pl.loop(0, tiles)
    def _(i):
        low = dot(r.normed_s[...], win_tile(i), NT).astype(BF16)
        r.pad[pl.ds(HALO, rows), lanes(i, GROUP)] = low
        r.padf_s[pl.ds(HALO, rows), lanes(i, GROUP)] = low.astype(F32)

    def edge():
        return pltpu.make_async_remote_copy(
            r.pad.at[pl.ds(rows, HALO)],
            r.halo_s,
            r.halo_sem.at[0],
            r.halo_sem.at[1],
            device_id=(ctx, jnp.minimum(me + 1, count - 1)),
            device_id_type=MESH,
        )

    @pl.when(me < count - 1)
    def _():
        edge().start()

    weave(pace)
    if mode != "first":
        halves[1].wait()

    @pl.loop(0, tiles)
    def _(i):
        r.gate[:, lanes(i, GROUP)] = dot(r.normed_s[...], win_tile(i + tiles), NT)

    weave(pace)

    @pl.when(me > 0)
    def _():
        edge().wait_recv()

    @pl.when(me == 0)
    def _():
        r.halo_s[...] = jnp.zeros_like(r.halo_s)

    r.pad[pl.ds(0, HALO), :] = r.halo_s[...]
    r.padf_s[pl.ds(0, HALO), :] = r.halo_s[...].astype(F32)

    @pl.loop(0, tiles)
    def _(i):
        here = lanes(i, GROUP)
        total = r.vec_s[pl.ds(at.conv_b, 1), here]
        for k in range(taps):
            total = (
                total
                + r.vec_s[pl.ds(at.conv + k, 1), here]
                * r.padf_s[pl.ds(HALO - taps + 1 + k, rows), here]
            )
        r.act[:, here] = (total * sigmoid(total)).astype(BF16)

    weave(pace)
    small = dot(r.act[...], r.sw[pl.ds(0, at.small), :], NT)
    r.sp[...] = small
    small_low = small.astype(BF16)

    @pl.loop(0, tiles)
    def _(i):
        here = lanes(i, GROUP)
        before = dot(small_low, r.dtw_s[:, here]) + r.vec_s[pl.ds(at.dt_b, 1), here]
        step = softplus(before)
        r.pre[:, here] = before
        r.dt_s[:, here] = step
        r.dx_s[:, here] = step * r.act[:, here].astype(F32)
        keep_sum(r.own_sum, i, step)

    sums, ends = chain(
        count, me, ctx, r.own_sum, r.sum_s, r.own_end, r.end_s,
        (r.sum_send, r.sum_recv, r.end_send, r.end_recv),
    )
    each(me + 1, count, lambda j: sums(j, me).start())
    saves = []

    def save(name, slot, part=slice(None)):
        copy = pltpu.make_async_copy(
            getattr(r, name).at[:, part],
            getattr(r, name + "_hbm").at[:, part],
            r.save_sem.at[slot],
        )
        copy.start()
        saves.append(copy)

    for slot, name in enumerate(("pad", "gate", "act", "pre")):
        save(name, slot)
    weave(pace)
    for n in range(states):
        r.bb_s[:, n, :] = jnp.broadcast_to(
            small[:, rank + n : rank + n + 1], (rows, 128)
        )
    r.cd_s[...] = spread(small_low, rank + states, states)

    def advance(t, state, rate2, here):
        return (
            jnp.exp2(r.dt_s[pl.ds(t, 1), here] * rate2) * state
            + r.dx_s[pl.ds(t, 1), here] * widen(r.bb_s[t], state.shape[1])
        )

    for g in range(groups):
        here = pl.ds(g * GROUP, GROUP)
        rate2 = r.vec_s[pl.ds(0, states), here] * LOG2E

        def first_pass(step, state):
            for i in range(CHUNK):
                state = advance(step * CHUNK + i, state, rate2, here)
            return state

        state = jnp.zeros((states, GROUP), F32)
        for part in range(2):
            state = lax.fori_loop(
                steps * part // 2, steps * (part + 1) // 2, first_pass, state
            )
            weave(pace)
        r.own_end[:, here] = state.astype(BF16)
        each(me + 1, count, lambda j: ends(g, j, me).start())

    def h_copy(g):
        here = pl.ds(g * WIDE, WIDE)
        return pltpu.make_async_copy(
            r.hs.at[:, here], r.h_hbm.at[:, here], r.h_sem.at[g]
        )

    def start_of(g):
        here = pl.ds(g * GROUP, GROUP)
        rate2 = r.vec_s[pl.ds(0, states), here] * LOG2E

        def carry(j, state):
            if g == 0:
                sums(j, j).wait_recv()
            ends(g, j, j).wait_recv()
            return (
                jnp.exp2(rate2 * sum_of(r.sum_s, j, g)) * state
                + r.end_s[j, :, here].astype(F32)
            )

        return lax.fori_loop(0, me, carry, jnp.zeros((states, GROUP), F32))

    for g in range(inner // WIDE):
        here = pl.ds(g * WIDE, WIDE)
        rate2 = r.vec_s[pl.ds(0, states), here] * LOG2E
        each_wide = WIDE // GROUP
        state = jnp.concatenate(
            [start_of(g * each_wide + part) for part in range(each_wide)], 1
        )
        r.hs[pl.ds(0, states), here] = state.astype(BF16)

        def second_pass(step, state):
            base = pl.multiple_of(step * CHUNK * states + states, states)
            for i in range(CHUNK):
                state = advance(step * CHUNK + i, state, rate2, here)
                r.hs[pl.ds(base + i * states, states), here] = state.astype(BF16)
            tokens = pl.ds(pl.multiple_of(step * CHUNK, CHUNK), CHUNK)
            r.y[tokens, here] = dot(
                r.cd_s[tokens, :], r.hs[pl.ds(base, CHUNK * states), here]
            )
            return state

        thirds = 1 if mode == "given" else 8
        for part in range(thirds):
            state = lax.fori_loop(
                steps * part // thirds,
                steps * (part + 1) // thirds,
                second_pass,
                state,
            )
            weave(pace)
        h_copy(g).start()
        y_value = (
            r.y[:, here]
            + r.vec_s[pl.ds(at.skip, 1), here] * r.act[:, here].astype(F32)
        )
        gate = r.gate[:, here]
        r.y[:, here] = y_value
        r.mixed[:, here] = (y_value * gate * sigmoid(gate)).astype(BF16)
        save("y", 4 + 2 * g, here)
        save("mixed", 5 + 2 * g, here)

    if mode == "given":
        out_copy.wait()
    else:
        while queue and not stores_hold_out(mode, stores):
            weave(1)
    out_tile = 256 // r.wout_s.shape[1]
    for i in range(width // 256):
        here = pl.ds(i * 256, 256)
        wout = r.wout_s[pl.ds(i * out_tile, out_tile)].reshape(256, inner)
        r.new[:, here] = (
            r.stream[:, here].astype(F32) + dot(r.mixed[...], wout, NT)
        ).astype(r.new.dtype)

    weave(len(queue))
    if mode != "given":
        gather.finish()

    @pl.when(me < count - 1)
    def _():
        edge().wait_send()

    each(me + 1, count, lambda j: sums(j, me).wait_send())
    for g in range(groups):
        each(me + 1, count, lambda j: ends(g, j, me).wait_send())
    for g in range(inner // WIDE):
        h_copy(g).wait()
    for copy in stores + saves:
        copy.wait()


def stores_hold_out(mode, stores):
    return len(stores) == (2 if mode == "first" else 1)


def backward_kernel(cfg, mode, names, *refs):
    r = types.SimpleNamespace(**dict(zip(names, refs)))
    rows, inner, states, taps, rank, count, channels = cfg
    at = Names(states, taps, rank)
    ctx, me = lax.axis_index("ctx"), lax.axis_index("seq")
    groups, steps, tiles = inner // GROUP, rows // CHUNK, inner // GROUP
    depth = count // 2
    width = r.stream.shape[1]
    barrier = pltpu.get_barrier_semaphore()
    gvec = r.full_s.at[pl.ds(at.vec, at.rows - at.vec)]

    def signal(semaphore, to):
        pl.semaphore_signal(semaphore, inc=1, device_id=to, device_id_type=MESH)

    queue = collections.deque()

    owed = [0.0]

    def weave(times):
        owed[0] += times
        while queue and owed[0] >= 1:
            owed[0] -= 1
            queue.popleft()()

    each(me + 1, count, lambda j: signal(barrier, (ctx, j)))
    if mode != "given":
        each(0, me, lambda j: signal(barrier, (ctx, j)))
        y, x, z, core = places()
        signal(barrier, device(y, 1 - x, z, core))
        signal(barrier, device(1 - y, x, z, core))

    def wout_copy(i):
        slot = lax.rem(i, 2)
        return pltpu.make_async_copy(
            r.wout.at[:, :, lanes(i, GROUP)], r.wout_s.at[slot], r.wout_sem.at[slot]
        )

    def gate_copies(i):
        slot = lax.rem(i, 2)
        return [
            pltpu.make_async_copy(
                array.at[:, lanes(i, GROUP)], r.gate_s.at[slot, k], r.gate_sem.at[slot, k]
            )
            for k, array in enumerate((r.gate, r.y))
        ]

    win_rows = r.win_s.shape[1]

    def win_copy(i, slot):
        return pltpu.make_async_copy(
            r.win.at[pl.ds(i * win_rows, win_rows)], r.win_s.at[slot], r.win_sem.at[slot]
        )

    quarters = 4
    span = rows // quarters * states

    def states_in(k):
        g, quarter = k // quarters, quarters - 1 - k % quarters
        return pltpu.make_async_copy(
            r.h_hbm.at[pl.ds(quarter * span, span + states), pl.ds(g * WIDE, WIDE)],
            r.hb.at[k % 2],
            r.h_sem.at[k % 2],
        )

    fetches = {
        name: pltpu.make_async_copy(
            getattr(r, name + "_hbm"), getattr(r, name), r.fetch_sem.at[k]
        )
        for k, name in enumerate(("stream", "pre", "act", "pad"))
    }
    for copy in fetches.values():
        copy.start()
    wout_copy(0).start()
    win_copy(tiles, 0).start()
    for copy in gate_copies(0):
        copy.start()
    load_small(at, r.sw, r.vec_s, r.dtw_s)
    gain = gain_row(at, channels, r.vec_s)
    r.low_s[...] = r.sgrad[...].astype(BF16)
    small_low = r.sp[...].astype(BF16)

    in_items, out_items, own_items = [], [], []
    if mode == "given":

        @pl.when(me > 0)
        def _():
            pl.semaphore_wait(barrier, me)

    else:
        pl.semaphore_wait(barrier, count + 1)
        pieces, buffers = [], []

        def add_piece(whole, out, cuts, held, side=None):
            start = len(pieces)
            total = whole.shape[4]
            for k, first_y in enumerate(cuts):
                piece = total // len(cuts)
                pieces.append((whole, out, k * piece, piece, first_y, side))
                buffers.append(held[k])
            return list(range(start, len(pieces)))

        def held_by(name):
            found = []
            while hasattr(r, f"{name}{len(found)}_0"):
                k = len(found)
                found.append([getattr(r, f"{name}{k}_{part}") for part in range(5)])
            return found

        held_in, held_small, held_out = (
            held_by("rin"),
            held_by("rsmall"),
            held_by("rout"),
        )
        out_items = add_piece(r.gout, r.sum_out, (1, 0), held_out)
        if mode == "first":
            in_items = add_piece(r.next_gin, r.sum_in.at[1], (1, 0, 1, 0), held_in)
            in_items += add_piece(r.next_gsmall, r.sum_small.at[1], (1,), held_small)
            own_items = add_piece(r.gin, r.sum_in.at[0], (1, 0, 1, 0), held_in)
            own_items += add_piece(r.gsmall_hbm, r.sum_small.at[0], (1,), held_small)
        reduce = Reduce(depth, pieces, buffers, r.own_sem, r.send_sem, r.recv_sem)
        for item in in_items:
            reduce.begin(item)

    r.lowt_s[...] = r.sgrad[...].astype(F32).T.astype(BF16)
    out_shape = r.stage_out.shape[1:]
    out_rows = out_shape[0] * out_shape[1] * out_shape[2]
    line = r.gout.shape[2]

    def block_of(whole, i):
        row, z = split(2 * i, line)
        y, x = split(row, 2)
        return whole.at[y, x, pl.ds(z, 2)]

    for k in range(width // out_rows):
        slot = k % 2
        copy = pltpu.make_async_copy(
            r.stage_out.at[slot], block_of(r.gout, k), r.out_sem.at[slot]
        )
        if k >= 2:
            copy.wait()

        @pl.loop(0, tiles)
        def _(i):
            here = lanes(i, GROUP)
            r.stage_out[slot, :, :, :, here] = (
                dot(r.lowt_s[pl.ds(k * out_rows, out_rows), :], r.mixed[:, here])
                .astype(BF16)
                .reshape(out_shape[:-1] + (GROUP,))
            )

        copy.start()
    for slot in range(2):
        pltpu.make_async_copy(
            r.stage_out.at[slot], block_of(r.gout, 0), r.out_sem.at[slot]
        ).wait()
    if mode != "given":
        for item in out_items:
            reduce.begin(item)
        queue.extend(reduce.turns(in_items + out_items))
    pace = len(queue) / (24 if mode == "first" else 26)

    fetches["stream"].wait()
    stream = r.stream[...].astype(F32)
    scale = lax.rsqrt(jnp.mean(stream * stream, axis=1, keepdims=True) + EPS)
    r.normed_s[...] = (stream * scale * gain).astype(BF16)
    fetches["pre"].wait()
    fetches["act"].wait()

    @pl.loop(0, tiles)
    def _(i):
        here = lanes(i, GROUP)
        slot = lax.rem(i, 2)

        @pl.when(i + 1 < tiles)
        def _():
            wout_copy(i + 1).start()
            for copy in gate_copies(i + 1):
                copy.start()

        wout_copy(i).wait()
        for copy in gate_copies(i):
            copy.wait()
        mixed_grad = dot(r.low_s[...], r.wout_s[slot].reshape(width, GROUP))
        gate = r.gate_s[slot, 0]
        sig = sigmoid(gate)
        act = r.act[:, here].astype(F32)
        scan_grad = mixed_grad * gate * sig
        r.sg_s[:, here] = scan_grad
        r.pb_s[:, lanes(i + tiles, GROUP)] = (
            mixed_grad * r.gate_s[slot, 1] * sig * (1.0 + gate * (1.0 - sig))
        ).astype(BF16)
        gvec[pl.ds(at.skip, 1), here] = jnp.sum(scan_grad * act, axis=0, keepdims=True)
        step = softplus(r.pre[:, here])
        r.dt_s[:, here] = step
        r.dx_s[pl.ds(0, rows), here] = step * act
        keep_sum(r.own_sum, i, step)

    sums, ends = chain(
        count, me, ctx, r.own_sum, r.sum_s, r.own_end, r.end_s,
        (r.sum_send, r.sum_recv, r.end_send, r.end_recv),
    )
    each(0, me, lambda j: sums(j, me).start())
    weave(pace)
    in_shape = r.stage_in.shape[1:]

    def in_copy(i, slot):
        return pltpu.make_async_copy(
            r.stage_in.at[slot], block_of(r.gin, i), r.in_sem.at[slot]
        )

    def project(i, turn):
        here = lanes(i, GROUP)
        slot = lax.rem(turn, 2)
        copy = in_copy(i, slot)
        following = lax.rem(i + 1, 2 * tiles)

        @pl.when(turn + 1 < 2 * tiles)
        def _():
            win_copy(following, 1 - slot).start()

        @pl.when(turn >= 2)
        def _():
            copy.wait()

        r.stage_in[slot] = (
            dot(r.pb_s[:, here], r.normed_s[...], TN).astype(BF16).reshape(in_shape)
        )
        copy.start()
        win_copy(i, slot).wait()
        part = dot(r.pb_s[:, here], r.win_s[slot].reshape(GROUP, width))

        @pl.when(turn == 0)
        def _():
            r.nsg[...] = part

        @pl.when(turn > 0)
        def _():
            r.nsg[...] += part

    @pl.loop(0, tiles)
    def _(i):
        project(i + tiles, i)

    weave(pace)
    for n in range(states):
        first = rank + states + n
        r.cb_s[:, n, :] = jnp.broadcast_to(r.sp[:, first : first + 1], (rows, 128))
    r.bd_s[...] = spread(small_low, rank, states)
    ones = jnp.where(chunk_mask(CHUNK, states), 1.0, 0.0).astype(BF16)
    states_in(0).start()

    for g in range(groups):
        here = pl.ds(g * GROUP, GROUP)
        rate2 = r.vec_s[pl.ds(0, states), here] * LOG2E

        def first_pass(k, state):
            step = steps - 1 - k
            for i in reversed(range(CHUNK)):
                t = step * CHUNK + i
                state = jnp.exp2(r.dt_s[pl.ds(t, 1), here] * rate2) * (
                    state + r.sg_s[pl.ds(t, 1), here] * widen(r.cb_s[t], GROUP)
                )
            return state

        r.own_end[:, here] = lax.fori_loop(
            0, steps, first_pass, jnp.zeros((states, GROUP), F32)
        ).astype(BF16)
        each(0, me, lambda j: ends(g, j, me).start())
        weave(pace)

    def begin_of(g):
        here = pl.ds(g * GROUP, GROUP)
        rate2 = r.vec_s[pl.ds(0, states), here] * LOG2E

        def carry(k, state):
            j = count - 1 - k
            if g == 0:
                sums(j, j).wait_recv()
            ends(g, j, j).wait_recv()
            return (
                jnp.exp2(rate2 * sum_of(r.sum_s, j, g)) * state
                + r.end_s[j, :, here].astype(F32)
            )

        return lax.fori_loop(
            0, count - 1 - me, carry, jnp.zeros((states, GROUP), F32)
        )

    loads = inner // WIDE * quarters
    for g in range(inner // WIDE):
        here = pl.ds(g * WIDE, WIDE)
        rate = r.vec_s[pl.ds(0, states), here]
        rate2 = rate * LOG2E
        each_wide = WIDE // GROUP
        begin = jnp.concatenate(
            [begin_of(g * each_wide + part) for part in range(each_wide)], 1
        )
        both = (begin, jnp.zeros((states, WIDE), F32))
        for part in range(quarters):
            k = quarters * g + part
            quarter = quarters - 1 - part
            held_states = r.hb.at[k % 2]
            if k + 1 < loads:
                states_in(k + 1).start()
            states_in(k).wait()

            def second_pass(turn, both):
                state, total = both
                step = steps - 1 - turn
                base = pl.multiple_of(step * CHUNK * states - quarter * span, states)
                for i in reversed(range(CHUNK)):
                    t = step * CHUNK + i
                    dt = r.dt_s[pl.ds(t, 1), here]
                    adjoint = state + r.sg_s[pl.ds(t, 1), here] * widen(
                        r.cb_s[t], WIDE
                    )
                    state = jnp.exp2(dt * rate2) * adjoint
                    held = held_states[pl.ds(base + i * states, states), :]
                    rated = state * held.astype(F32) * rate
                    total = total + dt * rated
                    r.ab_s[pl.ds(i * states, states), :] = adjoint.astype(BF16)
                    r.rb_s[pl.ds(i * states, states), :] = rated.astype(BF16)
                tokens = pl.ds(pl.multiple_of(step * CHUNK, CHUNK), CHUNK)
                from_in = dot(r.bd_s[tokens, :], r.ab_s[...])
                from_rate = dot(ones, r.rb_s[...])
                scan_grad = r.sg_s[tokens, here]
                into_in = dot(r.dx_s[tokens, here].astype(BF16), r.ab_s[...], NT)
                into_out = dot(
                    scan_grad.astype(BF16),
                    held_states[pl.ds(base + states, CHUNK * states), :],
                    NT,
                )
                if g == 0:
                    r.pin_s[tokens, :] = into_in
                    r.pout_s[tokens, :] = into_out
                else:
                    r.pin_s[tokens, :] += into_in
                    r.pout_s[tokens, :] += into_out
                r.stepg_s[tokens, here] = (
                    r.act[tokens, here].astype(F32) * from_in + from_rate
                )
                r.sg_s[tokens, here] = (
                    r.dt_s[tokens, here] * from_in
                    + r.vec_s[pl.ds(at.skip, 1), here] * scan_grad
                )
                return state, total

            for k in range(2):
                low = (2 * part + k) * steps // (2 * quarters)
                high = (2 * part + k + 1) * steps // (2 * quarters)
                both = lax.fori_loop(low, high, second_pass, both)
                weave(pace)
        gvec[pl.ds(0, states), here] = both[1]

    fetches["pad"].wait()

    @pl.loop(0, tiles)
    def _(i):
        here = lanes(i, GROUP)
        pre_grad = r.stepg_s[pl.ds(0, rows), here] * sigmoid(r.pre[:, here])
        gvec[pl.ds(at.dt_b, 1), here] = jnp.sum(pre_grad, axis=0, keepdims=True)
        r.prelow_s[:, here] = pre_grad.astype(BF16)
        r.dx_s[:, here] = r.pad[:, here].astype(F32)

    small_grad = (
        dot(r.prelow_s[...], r.dtw_s[...], NT)
        + gather_back(r.pin_s[...], rank, states, at.small)
        + gather_back(r.pout_s[...], rank + states, states, at.small)
    ).astype(BF16)

    @pl.loop(0, tiles)
    def _(i):
        here = lanes(i, GROUP)
        r.full_s[pl.ds(at.dt, rank), here] = dot(
            small_low, r.prelow_s[:, here], TN
        )[:rank]
        r.full_s[pl.ds(0, at.small), here] = dot(small_grad, r.act[:, here], TN)
        act_grad = r.sg_s[:, here] + dot(small_grad, r.sw[pl.ds(0, at.small), here])
        total = r.vec_s[pl.ds(at.conv_b, 1), here]
        for k in range(taps):
            total = (
                total
                + r.vec_s[pl.ds(at.conv + k, 1), here]
                * r.dx_s[pl.ds(HALO - taps + 1 + k, rows), here]
            )
        sig = sigmoid(total)
        conv_grad = act_grad * sig * (1.0 + total * (1.0 - sig))
        r.stepg_s[pl.ds(0, rows), here] = conv_grad
        gvec[pl.ds(at.conv_b, 1), here] = jnp.sum(conv_grad, axis=0, keepdims=True)
        for k in range(taps):
            gvec[pl.ds(at.conv + k, 1), here] = jnp.sum(
                conv_grad * r.dx_s[pl.ds(HALO - taps + 1 + k, rows), here],
                axis=0,
                keepdims=True,
            )

    def edge():
        return pltpu.make_async_remote_copy(
            r.stepg_s.at[pl.ds(0, 8)],
            r.halo_s,
            r.halo_sem.at[0],
            r.halo_sem.at[1],
            device_id=(ctx, jnp.maximum(me - 1, 0)),
            device_id_type=MESH,
        )

    @pl.when(me > 0)
    def _():
        edge().start()

    weave(pace)
    @pl.when(me < count - 1)
    def _():
        edge().wait_recv()

    @pl.when(me == count - 1)
    def _():
        r.halo_s[...] = jnp.zeros_like(r.halo_s)

    @pl.when(me > 0)
    def _():
        edge().wait_send()

    r.stepg_s[pl.ds(rows, 8), :] = r.halo_s[...]

    @pl.loop(0, tiles)
    def _(i):
        here = lanes(i, GROUP)
        total = jnp.zeros((rows, GROUP), F32)
        for k in range(taps):
            total = (
                total
                + r.vec_s[pl.ds(at.conv + k, 1), here]
                * r.stepg_s[pl.ds(taps - 1 - k, rows), here]
            )
        r.pb_s[:, here] = total.astype(BF16)
        project(i, i + tiles)

    stream = r.stream[...].astype(F32)
    scale = lax.rsqrt(jnp.mean(stream * stream, axis=1, keepdims=True) + EPS)
    normed_grad = r.nsg[...]
    gain_grad = jnp.sum(normed_grad * stream * scale, axis=0, keepdims=True)
    gain_grad = jnp.broadcast_to(gain_grad, (8, width)).astype(BF16)
    pick = gain_pick(channels)
    for i in range(inner // 256):
        wide = dot(gain_grad[:, 128 * i : 128 * i + 128], pick, NT)
        gvec[pl.ds(at.gain, 1), pl.ds(256 * i, 256)] = wide[:1]
    for k in range(at.count, at.rows):
        r.full_s[pl.ds(k, 1), :] = jnp.zeros((1, inner), F32)
    if mode == "given":
        r.gsmall[...] = r.full_s[...]
    elif mode == "last":
        split_small(channels, r.full_s, r.gsmall)
    else:
        split_small(channels, r.full_s, Folded(r.gsmall_s))
        small_copy = pltpu.make_async_copy(r.gsmall_s, r.gsmall_hbm, r.small_sem.at[0])
        small_copy.start()
    scaled = normed_grad * gain
    inner_sum = jnp.mean(scaled * stream, axis=1, keepdims=True)
    r.nsg[...] = (
        r.sgrad[...].astype(F32) + scale * scaled - stream * (scale * scale * scale) * inner_sum
    )
    for slot in range(2):
        in_copy(0, slot).wait()
    weave(len(queue))
    if mode == "first":
        small_copy.wait()
        reduce.finish()
        for partner in square_partners(depth):
            signal(r.ready_sem, partner)
        pl.semaphore_wait(r.ready_sem, len(square_partners(depth)))
        for item in own_items:
            reduce.begin(item)
        for turn in reduce.turns(own_items):
            turn()
    if mode != "given":
        reduce.finish()
    each(0, me, lambda j: sums(j, me).wait_send())
    for g in range(groups):
        each(0, me, lambda j: ends(g, j, me).wait_send())


def in_vmem(count):
    return [pl.BlockSpec(memory_space=pltpu.VMEM)] * count


def in_any(count):
    return [pl.BlockSpec(memory_space=pl.ANY)] * count


def forward_call(cfg, mode, stream, operands):
    rows, inner, states, taps, rank, count, channels = cfg
    at = Names(states, taps, rank)
    width = stream.shape[1]
    groups = inner // GROUP
    devices = inner // channels
    shape = jax.ShapeDtypeStruct
    dma = pltpu.SemaphoreType.DMA
    vmem, any_space = in_vmem(1)[0], in_any(1)[0]
    inputs = [("stream", stream, vmem)]
    for name, array in operands:
        large = name.startswith(("all_", "win_", "wout_", "gsm_"))
        inputs.append((name, array, any_space if large else vmem))
    outputs = [
        ("new", shape(stream.shape, BF16 if mode == "later" else F32), vmem),
        ("sp", shape((rows, at.small), F32), vmem),
        ("h_hbm", shape(((rows + 1) * states, inner), BF16), any_space),
    ]
    saved = {
        "pad": ((rows + HALO, inner), BF16),
        "gate": ((rows, inner), F32),
        "act": ((rows, inner), BF16),
        "pre": ((rows, inner), F32),
        "y": ((rows, inner), F32),
        "mixed": ((rows, inner), BF16),
    }
    for name, (size, kind) in saved.items():
        outputs.append((name + "_hbm", shape(size, kind), any_space))
    if mode == "given":
        given = dict(operands)
        in_shape, out_shape = given["win_hbm"].shape, given["wout_hbm"].shape
    else:
        in_shape = (devices, 2 * inner // devices, width)
        out_shape = (devices, width // devices, inner)
        small_shape = (devices, at.rows * channels // 128, 128)
        outputs.append(("sw", shape((at.rows, inner), BF16), vmem))
        outputs.append(("wout_all", shape(out_shape, BF16), any_space))
    if mode == "first":
        outputs.append(("win_all", shape(in_shape, BF16), any_space))
        outputs.append(("win2_all", shape(in_shape, BF16), any_space))
        outputs.append(("gsm2_all", shape(small_shape, BF16), any_space))
    scratch = [
        ("win_s", pltpu.VMEM(in_shape, BF16)),
        ("wout_s", pltpu.VMEM(out_shape, BF16)),
        ("vec_s", pltpu.VMEM((at.rows - at.vec, inner), F32)),
        ("dtw_s", pltpu.VMEM((at.small, inner), BF16)),
        ("normed_s", pltpu.VMEM(stream.shape, BF16)),
        ("padf_s", pltpu.VMEM((rows + HALO, inner), F32)),
        ("halo_s", pltpu.VMEM((HALO, inner), BF16)),
        ("dt_s", pltpu.VMEM((rows, inner), F32)),
        ("dx_s", pltpu.VMEM((rows, inner), F32)),
        ("bb_s", pltpu.VMEM((rows, states, 128), F32)),
        ("cd_s", pltpu.VMEM((rows, CHUNK * states), BF16)),
        ("hs", pltpu.VMEM(((rows + 1) * states, inner), BF16)),
        ("own_sum", pltpu.VMEM((8, inner // 8), F32)),
        ("sum_s", pltpu.VMEM((count, 8, inner // 8), F32)),
        ("own_end", pltpu.VMEM((states, inner), BF16)),
        ("end_s", pltpu.VMEM((count, states, inner), BF16)),
        ("halo_sem", dma((2,))),
        ("sum_send", dma((count,))),
        ("sum_recv", dma((count,))),
        ("end_send", dma((groups, count))),
        ("end_recv", dma((groups, count))),
        ("h_sem", dma((groups,))),
        ("load_sem", dma((3,))),
        ("save_sem", dma((4 + 2 * groups,))),
    ]
    for name, (size, kind) in saved.items():
        scratch.append((name, pltpu.VMEM(size, kind)))
    if mode != "given":
        pieces = 8 if mode == "first" else 2
        scratch += [
            ("gsm_s", pltpu.VMEM(small_shape, BF16)),
            ("pack_s", pltpu.VMEM(small_shape[1:], F32)),
            ("packed_s", pltpu.VMEM((2,) + small_shape[1:], BF16)),
            ("own_sem", dma((pieces,))),
            ("send_sem", dma((pieces, Gather.sends(count // 2)))),
            ("recv_sem", dma((pieces, devices))),
            ("store_sem", dma((2,))),
        ]
    names = [entry[0] for entry in inputs + outputs + scratch]
    results = pl.pallas_call(
        functools.partial(forward_kernel, cfg, mode, names),
        out_shape=tuple(entry[1] for entry in outputs),
        in_specs=[entry[2] for entry in inputs],
        out_specs=tuple(entry[2] for entry in outputs),
        scratch_shapes=[entry[1] for entry in scratch],
        compiler_params=pltpu.CompilerParams(
            collective_id={"given": 0, "first": 4, "later": 5}[mode],
            has_side_effects=True,
            vmem_limit_bytes=VMEM_BYTES,
        ),
        name="forward_" + mode,
    )(*[entry[1] for entry in inputs])
    return {
        entry[0].removesuffix("_hbm"): result
        for entry, result in zip(outputs, results)
    }


def backward_call(cfg, mode, sgrad, stream, weights, saved, later):
    rows, inner, states, taps, rank, count, channels = cfg
    at = Names(states, taps, rank)
    width = stream.shape[1]
    groups = inner // GROUP
    wide = CHUNK * states
    depth = count // 2
    sw, win, wout = weights
    shape = jax.ShapeDtypeStruct
    dma = pltpu.SemaphoreType.DMA
    vmem, any_space = in_vmem(1)[0], in_any(1)[0]
    in_rows, out_rows = win.shape[1], wout.shape[1]
    lead = (1, 1, win.shape[0] // 2, 2) if mode == "given" else (2, 2, depth, 2)
    small_rows = at.rows * channels // 128
    inputs = [
        ("sgrad", sgrad, vmem),
        ("sw", sw, vmem),
        ("win", win, any_space),
        ("wout", wout, any_space),
    ]
    for name in ("sp", "mixed"):
        inputs.append((name, saved[name], vmem))
    for name in ("gate", "y"):
        inputs.append((name, saved[name], any_space))
    inputs.append(("h_hbm", saved["h"], any_space))
    fetched = {name: saved[name] for name in ("pre", "act", "pad")}
    fetched["stream"] = stream
    for name, array in fetched.items():
        inputs.append((name + "_hbm", array, any_space))
    outputs = [
        ("nsg", shape((rows, width), F32), vmem),
        ("gin", shape(lead + (in_rows, width), BF16), any_space),
        ("gout", shape(lead + (out_rows, inner), BF16), any_space),
    ]
    scratch = [
        ("full_s", pltpu.VMEM((at.rows, inner), F32)),
        ("vec_s", pltpu.VMEM((at.rows - at.vec, inner), F32)),
        ("dtw_s", pltpu.VMEM((at.small, inner), BF16)),
        ("hb", pltpu.VMEM((2, (rows // 4 + 1) * states, WIDE), BF16)),
        ("normed_s", pltpu.VMEM((rows, width), BF16)),
        ("low_s", pltpu.VMEM((rows, width), BF16)),
        ("lowt_s", pltpu.VMEM((width, rows), BF16)),
        ("sg_s", pltpu.VMEM((rows, inner), F32)),
        ("dt_s", pltpu.VMEM((rows, inner), F32)),
        ("dx_s", pltpu.VMEM((rows + HALO, inner), F32)),
        ("stepg_s", pltpu.VMEM((rows + 8, inner), F32)),
        ("pb_s", pltpu.VMEM((rows, 2 * inner), BF16)),
        ("cb_s", pltpu.VMEM((rows, states, 128), F32)),
        ("bd_s", pltpu.VMEM((rows, wide), BF16)),
        ("ab_s", pltpu.VMEM((wide, WIDE), BF16)),
        ("rb_s", pltpu.VMEM((wide, WIDE), BF16)),
        ("pin_s", pltpu.VMEM((rows, wide), F32)),
        ("pout_s", pltpu.VMEM((rows, wide), F32)),
        ("prelow_s", pltpu.VMEM((rows, inner), BF16)),
        ("stage_in", pltpu.VMEM((2, 2, 2, in_rows, width), BF16)),
        ("stage_out", pltpu.VMEM((2, 2, 2, out_rows, inner), BF16)),
        ("win_s", pltpu.VMEM((2, GROUP // in_rows, in_rows, width), BF16)),
        ("wout_s", pltpu.VMEM((2,) + wout.shape[:2] + (GROUP,), BF16)),
        ("gate_s", pltpu.VMEM((2, 2, rows, GROUP), F32)),
        ("halo_s", pltpu.VMEM((8, inner), F32)),
        ("own_sum", pltpu.VMEM((8, inner // 8), F32)),
        ("sum_s", pltpu.VMEM((count, 8, inner // 8), F32)),
        ("own_end", pltpu.VMEM((states, inner), BF16)),
        ("end_s", pltpu.VMEM((count, states, inner), BF16)),
        ("halo_sem", dma((2,))),
        ("sum_send", dma((count,))),
        ("sum_recv", dma((count,))),
        ("end_send", dma((groups, count))),
        ("end_recv", dma((groups, count))),
        ("h_sem", dma((2,))),
        ("in_sem", dma((2,))),
        ("out_sem", dma((2,))),
        ("win_sem", dma((2,))),
        ("wout_sem", dma((2,))),
        ("gate_sem", dma((2, 2))),
        ("fetch_sem", dma((len(fetched),))),
    ]
    for name, array in fetched.items():
        scratch.append((name, pltpu.VMEM(array.shape, array.dtype)))
    if mode == "given":
        outputs.append(("gsmall", shape((at.rows, inner), F32), vmem))
    else:
        outputs.append(("sum_out", shape((out_rows, inner), F32), vmem))
        held = [("rout", out_rows // 2, inner, 2, False)]
        pieces = 2
        if mode == "last":
            small_shape = (inner // channels, small_rows, 128)
            outputs.append(("gsmall", shape(small_shape, BF16), vmem))
        else:
            inputs.append(("next_gin", later["gin"], any_space))
            small = later["gsmall"].reshape(lead + (small_rows, 128))
            inputs.append(("next_gsmall", small, any_space))
            outputs.append(("gsmall_hbm", shape(small.shape, BF16), any_space))
            scratch.append(("gsmall_s", pltpu.VMEM(small.shape, BF16)))
            outputs.append(("sum_in", shape((2, in_rows, width), F32), vmem))
            outputs.append(("sum_small", shape((2, small_rows, 128), F32), vmem))
            held.append(("rin", in_rows // 4, width, 4, False))
            held.append(("rsmall", small_rows, 128, 1, False))
            scratch.append(("small_sem", dma((1,))))
            scratch.append(("ready_sem", pltpu.SemaphoreType.REGULAR))
            pieces = 12
        for name, piece, wide_by, cuts, sided in held:
            for k in range(cuts):
                found = Reduce.buffers_of(depth, piece, wide_by, sided)
                for part, buffer in enumerate(found):
                    scratch.append((f"{name}{k}_{part}", buffer))
        scratch += [
            ("own_sem", dma((pieces, 2))),
            ("send_sem", dma((pieces, 4, depth))),
            ("recv_sem", dma((pieces, 4, depth))),
        ]
    names = [entry[0] for entry in inputs + outputs + scratch]
    results = pl.pallas_call(
        functools.partial(backward_kernel, cfg, mode, names),
        out_shape=tuple(entry[1] for entry in outputs),
        in_specs=[entry[2] for entry in inputs],
        out_specs=tuple(entry[2] for entry in outputs),
        scratch_shapes=[entry[1] for entry in scratch],
        compiler_params=pltpu.CompilerParams(
            collective_id={"given": 1, "last": 6, "first": 7}[mode],
            has_side_effects=True,
            vmem_limit_bytes=VMEM_BYTES,
        ),
        name="backward_" + mode,
    )(*[entry[1] for entry in inputs])
    return {entry[0]: result for entry, result in zip(outputs, results)}


def on_device(
    mesh,
    hidden_in,
    cotangent,
    norm_gain,
    in_weight,
    conv_weight,
    conv_bias,
    x_weight,
    dt_weight,
    dt_bias,
    a_log,
    skip_gain,
    out_weight,
):
    layers = norm_gain.shape[0]
    rows, width = hidden_in.shape
    taps, channels = conv_weight.shape[1:]
    states = a_log.shape[2]
    rank = dt_weight.shape[1]
    devices, count = mesh.shape["ctx"] * mesh.shape["seq"], mesh.shape["seq"]
    inner = channels * devices
    gains = norm_gain.shape[1]
    at = Names(states, taps, rank)
    cfg = (rows, inner, states, taps, rank, count, channels)
    depth = count // 2
    by_kernel = (
        mesh.shape["ctx"] == 4
        and depth % 2 == 0
        and layers == 2
        and in_weight.shape[2] % 32 == 0
        and out_weight.shape[2] % 32 == 0
        and channels == 64
        and at.rows == 2 * at.small
    )

    all_in, all_out = in_weight.transpose(0, 2, 1), out_weight.transpose(0, 2, 1)
    stream = hidden_in if by_kernel else hidden_in.astype(F32)
    streams, runs, weights = [], [], []
    if by_kernel:
        operands = [
            ("all_in", all_in),
            ("x_weight", x_weight),
            ("dt_weight", dt_weight),
            ("a_log", a_log),
            ("conv_weight", conv_weight),
            ("conv_bias", conv_bias),
            ("dt_bias", dt_bias),
            ("skip_gain", skip_gain),
            ("norm_gain", norm_gain),
            ("all_out", all_out),
        ]
        first = forward_call(cfg, "first", stream, operands)
        operands = [
            ("win_hbm", first["win2_all"]),
            ("gsm_hbm", first["gsm2_all"]),
            ("all_out", all_out),
        ]
        second = forward_call(cfg, "later", first["new"], operands)
        runs = [first, second]
        wins = [first["win_all"], first["win2_all"]]
        weights = [
            (run["sw"], win, run["wout_all"]) for run, win in zip(runs, wins)
        ]
        streams = [stream, first["new"]]
        stream = second["new"]
    else:
        gain_rows = jnp.pad(norm_gain, ((0, 0), (0, channels - gains)))
        packed = jnp.concatenate(
            [
                x_weight.transpose(0, 2, 1),
                dt_weight,
                a_log.transpose(0, 2, 1),
                conv_weight,
                jnp.stack([conv_bias, dt_bias, skip_gain, gain_rows], 1),
                jnp.zeros((layers, at.rows - at.count, channels), BF16),
            ],
            1,
        )
        for w_in, w_out, w_small in zip(all_in, all_out, packed):
            w_in = lax.all_gather(w_in, ("ctx", "seq"), axis=0, tiled=True)
            w_out = lax.all_gather(w_out, ("ctx", "seq"), axis=0, tiled=True)
            sw = lax.all_gather(w_small, ("ctx", "seq"), axis=1, tiled=True)
            w_in = w_in.reshape(-1, 128, width)
            w_out = w_out.reshape(-1, 32, inner)
            operands = [("win_hbm", w_in), ("sw", sw), ("wout_hbm", w_out)]
            run = forward_call(cfg, "given", stream, operands)
            runs.append(run)
            weights.append((sw, w_in, w_out))
            streams.append(stream)
            stream = run["new"]
    stream_grad = cotangent
    summed = [None] * layers
    if by_kernel:
        last = backward_call(
            cfg, "last", stream_grad, streams[1], weights[1], runs[1], None
        )
        head = backward_call(
            cfg, "first", last["nsg"], streams[0], weights[0], runs[0], last
        )
        stream_grad = head["nsg"]

        sum_in = head["sum_in"]
        sum_out = jnp.stack([head["sum_out"], last["sum_out"]], 0)
        sum_small = head["sum_small"].reshape(layers, -1, 128 // channels, channels)
        sum_small = sum_small.transpose(0, 2, 1, 3).reshape(layers, -1, channels)
    else:
        for layer in reversed(range(layers)):
            run = backward_call(
                cfg,
                "given",
                stream_grad,
                streams[layer],
                weights[layer],
                runs[layer],
                None,
            )
            stream_grad = run["nsg"]
            summed[layer] = [
                lax.psum_scatter(
                    array.astype(F32),
                    ("ctx", "seq"),
                    scatter_dimension=dim,
                    tiled=True,
                )
                for array, dim in (
                    (run["gin"].reshape(-1, width), 0),
                    (run["gout"].reshape(-1, inner), 0),
                    (run["gsmall"], 1),
                )
            ]
        sum_in, sum_out, sum_small = [jnp.stack(each, 0) for each in zip(*summed)]
    vectors = sum_small[:, at.vec : at.count]
    grads = (
        vectors[:, at.gain, :gains],
        sum_in.transpose(0, 2, 1),
        vectors[:, at.conv : at.conv + taps],
        vectors[:, at.conv_b],
        sum_small[:, : at.small].transpose(0, 2, 1),
        sum_small[:, at.dt : at.dt + rank],
        vectors[:, at.dt_b],
        vectors[:, :states].transpose(0, 2, 1),
        vectors[:, at.skip],
        sum_out.transpose(0, 2, 1),
    )
    return (stream.astype(BF16), stream_grad) + grads


def solution(mesh):
    split = ("ctx", "seq")
    tokens, last = P(split, None), P(None, split)
    middle, third = P(None, split, None), P(None, None, split)
    weights = (last, third, third, last, middle, third, last, middle, last, third)
    return jax.shard_map(
        functools.partial(on_device, mesh),
        mesh=mesh,
        in_specs=(tokens, tokens) + weights,
        out_specs=(tokens, tokens) + weights,
        check_vma=False,
    )
```

```python
import collections
import functools
import types

import jax
import jax.numpy as jnp
from jax import lax
from jax.experimental import pallas as pl
from jax.experimental.pallas import tpu as pltpu
from jax.sharding import PartitionSpec as P

EPS = 1e-05
LOG2E = 1.4426950408889634
MESH = pl.DeviceIdType.MESH
F32, BF16 = jnp.float32, jnp.bfloat16
NT = (((1,), (1,)), ((), ()))
TN = (((0,), (0,)), ((), ()))
VMEM_BYTES = 63 * 2**20
CHUNK = 16
GROUP = 512
WIDE = 1024
HALO = 16


def dot(a, b, dims=None):
    if dims is None:
        dims = (((1,), (0,)), ((), ()))
    return lax.dot_general(a, b, dims, preferred_element_type=F32)


def lanes(index, width):
    return pl.ds(pl.multiple_of(index * width, width), width)


def widen(tile, width):
    times = width // tile.shape[1]
    return jnp.concatenate([tile] * times, axis=1) if times > 1 else tile


def softplus(v):
    return jnp.maximum(v, 0.0) + jnp.log1p(jnp.exp(-jnp.abs(v)))


def sigmoid(v):
    return 1.0 / (1.0 + jnp.exp(-v))


def keep_sum(own_sum, i, step):
    total = jnp.sum(step, axis=0, keepdims=True)
    fold = own_sum.shape[1]
    for part in range(GROUP // fold):
        row = i * (GROUP // fold) + part
        own_sum[pl.ds(row, 1), :] = total[:, part * fold : (part + 1) * fold]


def sum_of(sum_s, j, g):
    fold = sum_s.shape[2]
    each = GROUP // fold
    return jnp.concatenate(
        [sum_s[j, pl.ds(g * each + part, 1), :] for part in range(each)], 1
    )


def chunk_mask(rows, states):
    wide = CHUNK * states
    token = lax.rem(lax.broadcasted_iota(jnp.int32, (rows, wide), 0), CHUNK)
    owner = lax.broadcasted_iota(jnp.int32, (rows, wide), 1) // states
    return token == owner


def spread(small_low, first, states):
    wide = CHUNK * states
    row = lax.broadcasted_iota(jnp.int32, (small_low.shape[1], wide), 0)
    col = lax.broadcasted_iota(jnp.int32, (small_low.shape[1], wide), 1)
    pick = (row == first + lax.rem(col, states)).astype(F32).astype(BF16)
    tiled = dot(small_low, pick)
    return jnp.where(chunk_mask(small_low.shape[0], states), tiled, 0.0).astype(BF16)


def gather_back(partial, first, states, width):
    wide = CHUNK * states
    row = lax.broadcasted_iota(jnp.int32, (wide, width), 0)
    col = lax.broadcasted_iota(jnp.int32, (wide, width), 1)
    pick = (col == first + lax.rem(row, states)).astype(F32).astype(BF16)
    kept = jnp.where(chunk_mask(partial.shape[0], states), partial, 0.0)
    return dot(kept.astype(BF16), pick)


class Names:
    def __init__(self, states, taps, rank):
        self.small = rank + 2 * states
        self.dt = self.small
        self.vec = self.small + rank
        self.count = self.vec + states + taps + 4
        self.rows = -(-self.count // 16) * 16
        self.conv = states
        self.conv_b = states + taps
        self.dt_b = states + taps + 1
        self.skip = states + taps + 2
        self.gain = states + taps + 3


def load_small(at, sw_ref, vec_s, dtw_s):
    states, rank = at.conv, at.vec - at.dt
    vec_s[...] = sw_ref[pl.ds(at.vec, at.rows - at.vec), :].astype(F32)
    vec_s[pl.ds(0, states), :] = -jnp.exp(vec_s[pl.ds(0, states), :])
    dtw_s[pl.ds(0, rank), :] = sw_ref[pl.ds(at.dt, rank), :]
    dtw_s[pl.ds(rank, at.small - rank), :] = jnp.zeros(
        (at.small - rank, dtw_s.shape[1]), BF16
    )


def gain_pick(channels):
    gains = channels // 2
    row = lax.broadcasted_iota(jnp.int32, (256, 128), 0)
    col = lax.broadcasted_iota(jnp.int32, (256, 128), 1)
    place = lax.div(col, gains) * channels + lax.rem(col, gains)
    return (row == place).astype(F32).astype(BF16)


def gain_row(at, channels, vec_s):
    pick = gain_pick(channels)
    row = vec_s[pl.ds(at.gain // 8 * 8, 8), :].astype(BF16)
    tiles = [
        dot(row[:, 256 * i : 256 * i + 256], pick) for i in range(row.shape[1] // 256)
    ]
    gain = jnp.concatenate(tiles, 1)
    return gain[at.gain % 8 : at.gain % 8 + 1]


def pack_small(at, layer, raw, sum_s, packed_s):
    x_weight, dt_weight, a_log, conv_weight, vectors, norm_gain = raw
    channels, states, rank = x_weight.shape[1], at.conv, at.vec - at.dt

    def place(count, first):
        row = lax.broadcasted_iota(jnp.int32, (count, 128), 0)
        col = lax.broadcasted_iota(jnp.int32, (count, 128), 1)
        return (col == row + first).astype(F32).astype(BF16)

    beside = place(channels, channels)
    sum_s[...] = dot(x_weight[layer], place(channels, 0), TN)
    sum_s[pl.ds(0, rank), :] += dot(dt_weight[layer], beside)
    sum_s[pl.ds(rank, states), :] += dot(a_log[layer], beside, TN)
    taps = conv_weight.shape[1]
    sum_s[pl.ds(rank + states, taps), :] += dot(conv_weight[layer], beside)
    row = rank + states + taps
    for ref in vectors:
        sum_s[pl.ds(row, 1), :] += dot(ref[...], beside)[layer : layer + 1]
        row += 1
    gains = dot(norm_gain[...], place(norm_gain.shape[1], channels))
    sum_s[pl.ds(row, 1), :] += gains[layer : layer + 1]
    packed_s[layer] = sum_s[...].astype(BF16)


def merge_small(channels, blocks, sw_ref):
    each = 128 // channels
    rows = blocks.shape[1]
    owner = lax.div(lax.broadcasted_iota(jnp.int32, (rows, 128), 1), channels)

    @pl.loop(0, sw_ref.shape[1] // 128)
    def _(j):
        held = [blocks[j * each + part].astype(F32) for part in range(each)]
        for fold in range(each):
            tile = None
            for part in range(each):
                shift = (part - fold) * channels % 128
                moved = pltpu.roll(held[part], shift, 1) if shift else held[part]
                tile = moved if tile is None else jnp.where(owner == part, moved, tile)
            sw_ref[pl.ds(fold * rows, rows), lanes(j, 128)] = tile.astype(BF16)


def split(number, by):
    if isinstance(number, int):
        return divmod(number, by)
    return lax.div(number, by), lax.rem(number, by)


class Folded:
    def __init__(self, ref):
        self.ref, self.shape = ref, ref.shape[3:]

    def __setitem__(self, block, value):
        _, x, z, core = self.ref.shape[:4]
        row = lax.div(block, z * core)
        self.ref[
            lax.div(row, x), lax.rem(row, x), lax.rem(lax.div(block, core), z), lax.rem(block, core)
        ] = value


def split_small(channels, full_ref, blocks):
    each = 128 // channels
    rows = blocks.shape[1]
    owner = lax.div(lax.broadcasted_iota(jnp.int32, (rows, 128), 1), channels)

    @pl.loop(0, full_ref.shape[1] // 128)
    def _(j):
        held = [
            full_ref[pl.ds(fold * rows, rows), lanes(j, 128)] for fold in range(each)
        ]
        for part in range(each):
            tile = None
            for fold in range(each):
                shift = (fold - part) * channels % 128
                moved = pltpu.roll(held[fold], shift, 1) if shift else held[fold]
                tile = moved if tile is None else jnp.where(owner == fold, moved, tile)
            blocks[j * each + part] = tile.astype(BF16)


def places():
    ctx, seq = lax.axis_index("ctx"), lax.axis_index("seq")
    return lax.div(ctx, 2), lax.rem(ctx, 2), lax.div(seq, 2), lax.rem(seq, 2)


def device(y, x, z, core):
    return (2 * y + x, 2 * z + core)


def square_partners(depth):
    y, x, z, core = places()
    partners = [device(y, x, z, 1 - core), device(y, 1 - x, z, core)]
    partners.append(device(1 - y, x, z, core))
    for step in range(1, depth):
        partners.append(device(y, x, lax.rem(z + step, depth), core))
    return partners


def greet_square(depth):
    barrier = pltpu.get_barrier_semaphore()
    partners = square_partners(depth)
    for partner in partners:
        pl.semaphore_signal(barrier, inc=1, device_id=partner, device_id_type=MESH)
    pl.semaphore_wait(barrier, len(partners))


class Gather:
    def __init__(self, depth, pieces, own_sem, send_sem, recv_sem):
        self.depth, self.pieces = depth, pieces
        self.own_sem, self.send_sem, self.recv_sem = own_sem, send_sem, recv_sem
        self.y, self.x, self.z, self.core = places()
        self.used = [0] * len(pieces)
        self.sent = []
        turn = 1 - 2 * lax.div(self.z, max(depth // 2, 1))
        self.line = [
            lax.rem(self.z + turn * step + depth, depth) for step in range(depth)
        ]
        y, x, z, core = self.y, self.x, self.z, self.core
        self.x_side, self.y_side = device(y, 1 - x, z, core), device(1 - y, x, z, core)
        self.sibling = device(y, x, z, 1 - core)

    @staticmethod
    def sends(depth):
        return 3 + depth - 1 + 3 * (depth - 1) + 2 * depth + 2 * depth

    def slot(self, y, x, z, core):
        return ((2 * y + x) * self.depth + z) * 2 + core

    def span(self, item, slot):
        _, whole, first, rows, _ = self.pieces[item]
        return whole.at[slot, pl.ds(first, rows)]

    def send(self, item, slot, to, own=False):
        local, _, first, rows, _ = self.pieces[item]
        copy = pltpu.make_async_remote_copy(
            local.at[pl.ds(first, rows)] if own else self.span(item, slot),
            self.span(item, slot),
            self.send_sem.at[item, self.used[item]],
            self.recv_sem.at[item, slot],
            device_id=to,
            device_id_type=MESH,
        )
        self.used[item] += 1
        copy.start()
        self.sent.append(copy)

    def arrive(self, item, slot):
        pltpu.make_async_remote_copy(
            self.span(item, slot),
            self.span(item, slot),
            self.send_sem.at[item, 0],
            self.recv_sem.at[item, slot],
            device_id=self.sibling,
            device_id_type=MESH,
        ).wait_recv()

    def own_copy(self, item):
        local, _, first, rows, _ = self.pieces[item]
        mine = self.slot(self.y, self.x, self.z, self.core)
        return pltpu.make_async_copy(
            local.at[pl.ds(first, rows)], self.span(item, mine), self.own_sem.at[item]
        )

    def begin(self, item):
        mine = self.slot(self.y, self.x, self.z, self.core)
        self.own_copy(item).start()
        for to in (self.x_side, self.y_side):
            self.send(item, mine, to, own=True)
        for step in range(1, self.depth):
            to = device(self.y, self.x, self.line[step], self.core)
            self.send(item, mine, to, own=True)
        self.send(item, mine, self.sibling, own=True)

    def along(self, item, step):
        slot = self.slot(self.y, self.x, self.line[step], self.core)
        self.arrive(item, slot)
        for to in (self.x_side, self.y_side, self.sibling):
            self.send(item, slot, to)

    def near(self, item, step):
        if self.pieces[item][4]:
            slot = self.slot(self.y, 1 - self.x, self.line[step], self.core)
            to = self.y_side
        else:
            slot = self.slot(1 - self.y, self.x, self.line[step], self.core)
            to = self.x_side
        self.arrive(item, slot)
        self.send(item, slot, to)
        self.send(item, slot, self.sibling)

    def far(self, item, step, other):
        y, x = 1 - self.y, 1 - self.x
        if self.pieces[item][4]:
            x = x if other else self.x
        else:
            y = y if other else self.y
        slot = self.slot(y, x, self.line[step], self.core)
        self.arrive(item, slot)
        self.send(item, slot, self.sibling)

    def settle(self, item):
        self.own_copy(item).wait()
        for step in range(self.depth):
            for y in (self.y, 1 - self.y):
                for x in (self.x, 1 - self.x):
                    self.arrive(item, self.slot(y, x, self.line[step], 1 - self.core))

    def turns(self, items):
        order = [("near", 0)]
        for step in range(1, self.depth):
            order.append(("along", step))
            order.append(("near", step))
            if step >= 2:
                order.append(("far", step - 2, 1))
            order.append(("far", step - 1, 0))
        for step in range(max(self.depth - 2, 0), self.depth):
            if step == self.depth - 1:
                order.append(("far", step, 0))
            order.append(("far", step, 1))
        actions = []
        for name, *rest in order:
            for item in items:
                actions.append(functools.partial(getattr(self, name), item, *rest))
        return actions

    def finish(self):
        for copy in self.sent:
            copy.wait_send()


class Reduce:
    def __init__(self, depth, pieces, buffers, own_sem, send_sem, recv_sem):
        self.depth, self.pieces, self.buffers = depth, pieces, buffers
        self.own_sem, self.send_sem, self.recv_sem = own_sem, send_sem, recv_sem
        y, x, z, core = places()
        self.y, self.x, self.core = y, x, core
        self.line = [lax.rem(z + step + 1, depth) for step in range(depth)]
        self.x_side, self.y_side = device(y, 1 - x, z, core), device(1 - y, x, z, core)
        self.sibling = device(y, x, z, 1 - core)
        self.along = [device(y, x, there, core) for there in self.line]
        self.sent = []

    @staticmethod
    def buffers_of(depth, rows, width, sided=False):
        square, row = ((2,), ()) if sided else ((2, 2), (2,))
        leads = ((2,) + square, (depth,) + square, (depth,) + row, (depth,), (depth - 1,))
        return [pltpu.VMEM(lead + (rows, width), BF16) for lead in leads]

    def part_of(self, item, step, core):
        whole, _, first, rows, _, side = self.pieces[item]
        y = slice(None) if side is None else side
        return whole.at[y, :, self.line[step], core, pl.ds(first, rows)]

    def local(self, item, step):
        return pltpu.make_async_copy(
            self.part_of(item, step, self.core),
            self.buffers[item][0].at[step % 2],
            self.own_sem.at[item, step % 2],
        )

    def hop(self, stage, item, step):
        _, core_in, first_in, second_in, line_in = self.buffers[item]
        crosses_y, side = self.pieces[item][4:]
        y, x = self.y, self.x
        if stage == 0:
            source = self.part_of(item, step, 1 - self.core)
            target, to = core_in.at[step], self.sibling
        elif stage == 1:
            if side is not None:
                source = core_in.at[step, 1 - x]
            elif crosses_y:
                source = core_in.at[step, 1 - y]
            else:
                source = core_in.at[step, :, 1 - x]
            target, to = first_in.at[step], self.y_side if crosses_y else self.x_side
        elif stage == 2:
            if side is not None:
                source = first_in.at[step]
            else:
                source = first_in.at[step, 1 - x if crosses_y else 1 - y]
            target, to = second_in.at[step], self.x_side if crosses_y else self.y_side
        else:
            source, target, to = second_in.at[step], line_in.at[step], self.along[step]
        return pltpu.make_async_remote_copy(
            source,
            target,
            self.send_sem.at[item, stage, step],
            self.recv_sem.at[item, stage, step],
            device_id=to,
            device_id_type=MESH,
        )

    def when(self, stage, item, receives, act):
        side = self.pieces[item][5]
        if side is None or stage < 2:
            act()
        elif stage == 2 and not receives:
            pl.when(self.y != side)(act)
        else:
            pl.when(self.y == side)(act)

    def send(self, stage, item, step):
        copy = self.hop(stage, item, step)
        self.when(stage, item, False, copy.start)
        self.sent.append((stage, item, copy))

    @staticmethod
    def add(target, other, rows):
        @pl.loop(0, rows // 16)
        def _(k):
            here = pl.ds(pl.multiple_of(k * 16, 16), 16)
            target[here] = (
                target[here].astype(F32) + other[here].astype(F32)
            ).astype(BF16)

    def begin(self, items):
        for step in range(self.depth):
            for item in items:
                self.send(0, item, step)
                if step < 2:
                    self.local(item, step).start()

    def settle(self, stage, item, step):
        self.when(
            stage, item, True, functools.partial(self.receive, stage, item, step)
        )
        if stage < 2 or step < self.depth - 1:
            self.send(stage + 1, item, step)

    def receive(self, stage, item, step):
        own, core_in, first_in, second_in, _ = self.buffers[item]
        rows, crosses_y, side = self.pieces[item][3:]
        self.hop(stage, item, step).wait_recv()
        if stage == 0:
            self.local(item, step).wait()
            for x in (0, 1):
                if side is not None:
                    self.add(core_in.at[step, x], own.at[step % 2, x], rows)
                    continue
                for y in (0, 1):
                    self.add(core_in.at[step, y, x], own.at[step % 2, y, x], rows)
            if step + 2 < self.depth:
                self.local(item, step + 2).start()
        elif stage == 1:
            if side is not None:
                self.add(first_in.at[step], core_in.at[step, self.x], rows)
                return
            for far in (0, 1):
                kept = (
                    core_in.at[step, self.y, far]
                    if crosses_y
                    else core_in.at[step, far, self.x]
                )
                self.add(first_in.at[step, far], kept, rows)
        elif side is not None:
            self.add(second_in.at[step], first_in.at[step], rows)
        else:
            kept = first_in.at[step, self.x if crosses_y else self.y]
            self.add(second_in.at[step], kept, rows)

    def last(self, item):
        self.when(3, item, True, functools.partial(self.total, item))

    def total(self, item):
        _, out, first, rows, _, _ = self.pieces[item]
        second_in, line_in = self.buffers[item][3:]
        for step in range(self.depth - 1):
            self.hop(3, item, step).wait_recv()

        @pl.loop(0, rows // 16)
        def _(k):
            here = pl.ds(pl.multiple_of(k * 16, 16), 16)
            total = second_in[self.depth - 1, here].astype(F32)
            for step in range(self.depth - 1):
                total = total + line_in[step, here].astype(F32)
            out[pl.ds(pl.multiple_of(first + k * 16, 16), 16)] = total

    def turns(self, items):
        actions = []
        for turn in range(self.depth + 2):
            for stage in range(3):
                step = turn - stage
                if 0 <= step < self.depth:
                    for item in items:
                        actions.append(
                            functools.partial(self.settle, stage, item, step)
                        )
        for item in items:
            actions.append(functools.partial(self.last, item))
        return actions

    def finish(self):
        for stage, item, copy in self.sent:
            self.when(stage, item, False, copy.wait_send)
        self.sent = []


def chain(count, me, ctx, own_sum, sum_s, own_end, end_s, sems):
    sum_send, sum_recv, end_send, end_recv = sems

    def sums(j, slot):
        return pltpu.make_async_remote_copy(
            own_sum,
            sum_s.at[slot],
            sum_send.at[j],
            sum_recv.at[slot],
            device_id=(ctx, j),
            device_id_type=MESH,
        )

    def ends(g, j, slot):
        return pltpu.make_async_remote_copy(
            own_end.at[:, pl.ds(g * GROUP, GROUP)],
            end_s.at[slot, :, pl.ds(g * GROUP, GROUP)],
            end_send.at[g, j],
            end_recv.at[g, slot],
            device_id=(ctx, j),
            device_id_type=MESH,
        )

    return sums, ends


def each(first, last, act):
    def body(j, _):
        act(j)
        return 0

    lax.fori_loop(first, last, body, 0)


def forward_kernel(cfg, mode, names, *refs):
    r = types.SimpleNamespace(**dict(zip(names, refs)))
    rows, inner, states, taps, rank, count, channels = cfg
    at = Names(states, taps, rank)
    ctx, me = lax.axis_index("ctx"), lax.axis_index("seq")
    groups, steps, tiles = inner // GROUP, rows // CHUNK, inner // GROUP
    depth = count // 2
    width = r.stream.shape[1]
    barrier = pltpu.get_barrier_semaphore()

    def greet(to):
        pl.semaphore_signal(barrier, inc=1, device_id=to, device_id_type=MESH)

    queue = collections.deque()

    owed = [0.0]

    def weave(times):
        owed[0] += times
        while queue and owed[0] >= 1:
            owed[0] -= 1
            queue.popleft()()

    if mode == "given":
        each(0, me, lambda j: greet((ctx, j)))
    else:
        each(0, me, lambda j: greet((ctx, j)))
        each(me + 1, count, lambda j: greet((ctx, j)))
        y, x, z, core = places()
        greet(device(y, 1 - x, z, core))
        greet(device(1 - y, x, z, core))

    if mode != "first":
        half = r.win_hbm.shape[0] // 2
        halves = [
            pltpu.make_async_copy(
                r.win_hbm.at[pl.ds(k * half, half)],
                r.win_s.at[pl.ds(k * half, half)],
                r.load_sem.at[k],
            )
            for k in range(2)
        ]
        if mode == "later":
            small_copy = pltpu.make_async_copy(r.gsm_hbm, r.gsm_s, r.load_sem.at[2])
            small_copy.start()
        for copy in halves:
            copy.start()
    if mode == "given":
        out_copy = pltpu.make_async_copy(r.wout_hbm, r.wout_s, r.load_sem.at[2])
        out_copy.start()

    if mode == "first":
        raw = (
            r.x_weight,
            r.dt_weight,
            r.a_log,
            r.conv_weight,
            (r.conv_bias, r.dt_bias, r.skip_gain),
            r.norm_gain,
        )
        for layer in range(2):
            pack_small(at, layer, raw, r.pack_s, r.packed_s)

    stream = r.stream[...].astype(F32)
    scale = lax.rsqrt(jnp.mean(stream * stream, axis=1, keepdims=True) + EPS)
    stores = []

    if mode == "given":

        @pl.when(me < count - 1)
        def _():
            pl.semaphore_wait(barrier, count - 1 - me)

    else:
        pl.semaphore_wait(barrier, count + 1)
        pieces = []

        def add_piece(local, whole, cuts):
            start = len(pieces)
            total = local.shape[0]
            for k, last_y in enumerate(cuts):
                piece = total // len(cuts)
                pieces.append((local, whole, k * piece, piece, last_y))
            return list(range(start, len(pieces)))

        first_items, next_items = [], []
        if mode == "first":
            first_items = add_piece(r.all_in.at[0], r.win_s, (1, 0))
            first_items += add_piece(r.packed_s.at[0], r.gsm_s, (1,))
        out_items = add_piece(
            r.all_out.at[0 if mode == "first" else 1], r.wout_s, (1, 0)
        )
        if mode == "first":
            next_items = add_piece(r.all_in.at[1], r.win2_all, (1, 0))
            next_items += add_piece(r.packed_s.at[1], r.gsm2_all, (0,))
        gather = Gather(depth, pieces, r.own_sem, r.send_sem, r.recv_sem)

        def begin(items):
            for item in items:
                gather.begin(item)

        def settle(items):
            for item in items:
                gather.settle(item)

        def keep(source, target, slot):
            copy = pltpu.make_async_copy(source, target, r.store_sem.at[slot])
            copy.start()
            stores.append(copy)

        if mode == "first":
            begin(first_items)
            turns = gather.turns(first_items)
            for k, turn in enumerate(turns):
                if k == len(turns) // 2:
                    begin(out_items + next_items)
                turn()
            settle(first_items)
            keep(r.win_s, r.win_all, 1)
            turns = gather.turns(out_items)
            queue.extend(gather.turns(out_items + next_items))
        else:
            begin(out_items)
            queue.extend(gather.turns(out_items))
        queue.append(lambda: settle(out_items))
        queue.append(lambda: keep(r.wout_s, r.wout_all, 0))
        if mode == "first":
            queue.append(lambda: settle(next_items))
        if mode == "later":
            small_copy.wait()
        merge_small(channels, r.gsm_s, r.sw)
    pace = len(queue) / (36 if mode == "first" else 33)

    load_small(at, r.sw, r.vec_s, r.dtw_s)
    r.normed_s[...] = (stream * scale * gain_row(at, channels, r.vec_s)).astype(BF16)
    per_tile = GROUP // r.win_s.shape[1]

    def win_tile(i):
        return r.win_s[pl.ds(i * per_tile, per_tile)].reshape(GROUP, width)

    if mode != "first":
        halves[0].wait()

    @pl.loop(0, tiles)
    def _(i):
        low = dot(r.normed_s[...], win_tile(i), NT).astype(BF16)
        r.pad[pl.ds(HALO, rows), lanes(i, GROUP)] = low
        r.padf_s[pl.ds(HALO, rows), lanes(i, GROUP)] = low.astype(F32)

    def edge():
        return pltpu.make_async_remote_copy(
            r.pad.at[pl.ds(rows, HALO)],
            r.halo_s,
            r.halo_sem.at[0],
            r.halo_sem.at[1],
            device_id=(ctx, jnp.minimum(me + 1, count - 1)),
            device_id_type=MESH,
        )

    @pl.when(me < count - 1)
    def _():
        edge().start()

    weave(pace)
    if mode != "first":
        halves[1].wait()

    @pl.loop(0, tiles)
    def _(i):
        r.gate[:, lanes(i, GROUP)] = dot(r.normed_s[...], win_tile(i + tiles), NT)

    weave(pace)

    @pl.when(me > 0)
    def _():
        edge().wait_recv()

    @pl.when(me == 0)
    def _():
        r.halo_s[...] = jnp.zeros_like(r.halo_s)

    r.pad[pl.ds(0, HALO), :] = r.halo_s[...]
    r.padf_s[pl.ds(0, HALO), :] = r.halo_s[...].astype(F32)

    @pl.loop(0, tiles)
    def _(i):
        here = lanes(i, GROUP)
        total = r.vec_s[pl.ds(at.conv_b, 1), here]
        for k in range(taps):
            total = (
                total
                + r.vec_s[pl.ds(at.conv + k, 1), here]
                * r.padf_s[pl.ds(HALO - taps + 1 + k, rows), here]
            )
        r.act[:, here] = (total * sigmoid(total)).astype(BF16)

    weave(pace)
    small = dot(r.act[...], r.sw[pl.ds(0, at.small), :], NT)
    r.sp[...] = small
    small_low = small.astype(BF16)

    @pl.loop(0, tiles)
    def _(i):
        here = lanes(i, GROUP)
        before = dot(small_low, r.dtw_s[:, here]) + r.vec_s[pl.ds(at.dt_b, 1), here]
        step = softplus(before)
        r.pre[:, here] = before
        r.dt_s[:, here] = step
        r.dx_s[:, here] = step * r.act[:, here].astype(F32)
        keep_sum(r.own_sum, i, step)

    sums, ends = chain(
        count, me, ctx, r.own_sum, r.sum_s, r.own_end, r.end_s,
        (r.sum_send, r.sum_recv, r.end_send, r.end_recv),
    )
    each(me + 1, count, lambda j: sums(j, me).start())
    saves = []

    def save(name, slot, part=slice(None)):
        copy = pltpu.make_async_copy(
            getattr(r, name).at[:, part],
            getattr(r, name + "_hbm").at[:, part],
            r.save_sem.at[slot],
        )
        copy.start()
        saves.append(copy)

    for slot, name in enumerate(("pad", "gate", "act", "pre")):
        save(name, slot)
    weave(pace)
    for n in range(states):
        r.bb_s[:, n, :] = jnp.broadcast_to(
            small[:, rank + n : rank + n + 1], (rows, 128)
        )
    r.cd_s[...] = spread(small_low, rank + states, states)

    def advance(t, state, rate2, here):
        return (
            jnp.exp2(r.dt_s[pl.ds(t, 1), here] * rate2) * state
            + r.dx_s[pl.ds(t, 1), here] * widen(r.bb_s[t], state.shape[1])
        )

    for g in range(groups):
        here = pl.ds(g * GROUP, GROUP)
        rate2 = r.vec_s[pl.ds(0, states), here] * LOG2E

        def first_pass(step, state):
            for i in range(CHUNK):
                state = advance(step * CHUNK + i, state, rate2, here)
            return state

        state = jnp.zeros((states, GROUP), F32)
        for part in range(2):
            state = lax.fori_loop(
                steps * part // 2, steps * (part + 1) // 2, first_pass, state
            )
            weave(pace)
        r.own_end[:, here] = state.astype(BF16)
        each(me + 1, count, lambda j: ends(g, j, me).start())

    def h_copy(g):
        here = pl.ds(g * WIDE, WIDE)
        return pltpu.make_async_copy(
            r.hs.at[:, here], r.h_hbm.at[:, here], r.h_sem.at[g]
        )

    def start_of(g):
        here = pl.ds(g * GROUP, GROUP)
        rate2 = r.vec_s[pl.ds(0, states), here] * LOG2E

        def carry(j, state):
            if g == 0:
                sums(j, j).wait_recv()
            ends(g, j, j).wait_recv()
            return (
                jnp.exp2(rate2 * sum_of(r.sum_s, j, g)) * state
                + r.end_s[j, :, here].astype(F32)
            )

        return lax.fori_loop(0, me, carry, jnp.zeros((states, GROUP), F32))

    for g in range(inner // WIDE):
        here = pl.ds(g * WIDE, WIDE)
        rate2 = r.vec_s[pl.ds(0, states), here] * LOG2E
        each_wide = WIDE // GROUP
        state = jnp.concatenate(
            [start_of(g * each_wide + part) for part in range(each_wide)], 1
        )
        r.hs[pl.ds(0, states), here] = state.astype(BF16)

        def second_pass(step, state):
            base = pl.multiple_of(step * CHUNK * states + states, states)
            for i in range(CHUNK):
                state = advance(step * CHUNK + i, state, rate2, here)
                r.hs[pl.ds(base + i * states, states), here] = state.astype(BF16)
            tokens = pl.ds(pl.multiple_of(step * CHUNK, CHUNK), CHUNK)
            r.y[tokens, here] = dot(
                r.cd_s[tokens, :], r.hs[pl.ds(base, CHUNK * states), here]
            )
            return state

        thirds = 1 if mode == "given" else 8
        for part in range(thirds):
            state = lax.fori_loop(
                steps * part // thirds,
                steps * (part + 1) // thirds,
                second_pass,
                state,
            )
            weave(pace)
        h_copy(g).start()
        y_value = (
            r.y[:, here]
            + r.vec_s[pl.ds(at.skip, 1), here] * r.act[:, here].astype(F32)
        )
        gate = r.gate[:, here]
        r.y[:, here] = y_value
        r.mixed[:, here] = (y_value * gate * sigmoid(gate)).astype(BF16)
        save("y", 4 + 2 * g, here)
        save("mixed", 5 + 2 * g, here)

    if mode == "given":
        out_copy.wait()
    else:
        while queue and not stores_hold_out(mode, stores):
            weave(1)
    out_tile = 256 // r.wout_s.shape[1]
    for i in range(width // 256):
        here = pl.ds(i * 256, 256)
        wout = r.wout_s[pl.ds(i * out_tile, out_tile)].reshape(256, inner)
        r.new[:, here] = (
            r.stream[:, here].astype(F32) + dot(r.mixed[...], wout, NT)
        ).astype(r.new.dtype)

    weave(len(queue))
    if mode != "given":
        gather.finish()

    @pl.when(me < count - 1)
    def _():
        edge().wait_send()

    each(me + 1, count, lambda j: sums(j, me).wait_send())
    for g in range(groups):
        each(me + 1, count, lambda j: ends(g, j, me).wait_send())
    for g in range(inner // WIDE):
        h_copy(g).wait()
    for copy in stores + saves:
        copy.wait()


def stores_hold_out(mode, stores):
    return len(stores) == (2 if mode == "first" else 1)


def backward_kernel(cfg, mode, names, *refs):
    r = types.SimpleNamespace(**dict(zip(names, refs)))
    rows, inner, states, taps, rank, count, channels = cfg
    at = Names(states, taps, rank)
    ctx, me = lax.axis_index("ctx"), lax.axis_index("seq")
    groups, steps, tiles = inner // GROUP, rows // CHUNK, inner // GROUP
    depth = count // 2
    width = r.stream.shape[1]
    barrier = pltpu.get_barrier_semaphore()
    gvec = r.full_s.at[pl.ds(at.vec, at.rows - at.vec)]

    def signal(semaphore, to):
        pl.semaphore_signal(semaphore, inc=1, device_id=to, device_id_type=MESH)

    queue = collections.deque()

    owed = [0.0]

    def weave(times):
        owed[0] += times
        while queue and owed[0] >= 1:
            owed[0] -= 1
            queue.popleft()()

    each(me + 1, count, lambda j: signal(barrier, (ctx, j)))
    if mode != "given":
        each(0, me, lambda j: signal(barrier, (ctx, j)))
        y, x, z, core = places()
        signal(barrier, device(y, 1 - x, z, core))
        signal(barrier, device(1 - y, x, z, core))

    def wout_copy(i):
        slot = lax.rem(i, 2)
        return pltpu.make_async_copy(
            r.wout.at[:, :, lanes(i, GROUP)], r.wout_s.at[slot], r.wout_sem.at[slot]
        )

    def gate_copies(i):
        slot = lax.rem(i, 2)
        return [
            pltpu.make_async_copy(
                array.at[:, lanes(i, GROUP)], r.gate_s.at[slot, k], r.gate_sem.at[slot, k]
            )
            for k, array in enumerate((r.gate, r.y))
        ]

    win_rows = r.win_s.shape[1]

    def win_copy(i, slot):
        return pltpu.make_async_copy(
            r.win.at[pl.ds(i * win_rows, win_rows)], r.win_s.at[slot], r.win_sem.at[slot]
        )

    quarters = 4
    span = rows // quarters * states

    def states_in(k):
        g, quarter = k // quarters, quarters - 1 - k % quarters
        return pltpu.make_async_copy(
            r.h_hbm.at[pl.ds(quarter * span, span + states), pl.ds(g * WIDE, WIDE)],
            r.hb.at[k % 2],
            r.h_sem.at[k % 2],
        )

    fetches = {
        name: pltpu.make_async_copy(
            getattr(r, name + "_hbm"), getattr(r, name), r.fetch_sem.at[k]
        )
        for k, name in enumerate(("stream", "pre", "act", "pad"))
    }
    for copy in fetches.values():
        copy.start()
    wout_copy(0).start()
    win_copy(tiles, 0).start()
    for copy in gate_copies(0):
        copy.start()
    load_small(at, r.sw, r.vec_s, r.dtw_s)
    gain = gain_row(at, channels, r.vec_s)
    r.low_s[...] = r.sgrad[...].astype(BF16)
    small_low = r.sp[...].astype(BF16)

    in_items, out_items, own_items = [], [], []
    if mode == "given":

        @pl.when(me > 0)
        def _():
            pl.semaphore_wait(barrier, me)

    else:
        pl.semaphore_wait(barrier, count + 1)
        pieces, buffers = [], []

        def add_piece(whole, out, cuts, held, side=None):
            start = len(pieces)
            total = whole.shape[4]
            for k, first_y in enumerate(cuts):
                piece = total // len(cuts)
                pieces.append((whole, out, k * piece, piece, first_y, side))
                buffers.append(held[k])
            return list(range(start, len(pieces)))

        def held_by(name):
            found = []
            while hasattr(r, f"{name}{len(found)}_0"):
                k = len(found)
                found.append([getattr(r, f"{name}{k}_{part}") for part in range(5)])
            return found

        held_in, held_small, held_out = (
            held_by("rin"),
            held_by("rsmall"),
            held_by("rout"),
        )
        out_items = add_piece(r.gout, r.sum_out, (1, 0), held_out)
        if mode == "first":
            in_items = add_piece(r.next_gin, r.sum_in.at[1], (1, 0, 1, 0), held_in)
            in_items += add_piece(r.next_gsmall, r.sum_small.at[1], (1,), held_small)
            own_items = add_piece(r.gin, r.sum_in.at[0], (1, 0, 1, 0), held_in)
            own_items += add_piece(r.gsmall_hbm, r.sum_small.at[0], (1,), held_small)
        reduce = Reduce(depth, pieces, buffers, r.own_sem, r.send_sem, r.recv_sem)
        reduce.begin(in_items)

    r.lowt_s[...] = r.sgrad[...].astype(F32).T.astype(BF16)
    out_shape = r.stage_out.shape[1:]
    out_rows = out_shape[0] * out_shape[1] * out_shape[2]
    line = r.gout.shape[2]

    def block_of(whole, i):
        row, z = split(2 * i, line)
        y, x = split(row, 2)
        return whole.at[y, x, pl.ds(z, 2)]

    for k in range(width // out_rows):
        slot = k % 2
        copy = pltpu.make_async_copy(
            r.stage_out.at[slot], block_of(r.gout, k), r.out_sem.at[slot]
        )
        if k >= 2:
            copy.wait()

        @pl.loop(0, tiles)
        def _(i):
            here = lanes(i, GROUP)
            r.stage_out[slot, :, :, :, here] = (
                dot(r.lowt_s[pl.ds(k * out_rows, out_rows), :], r.mixed[:, here])
                .astype(BF16)
                .reshape(out_shape[:-1] + (GROUP,))
            )

        copy.start()
    for slot in range(2):
        pltpu.make_async_copy(
            r.stage_out.at[slot], block_of(r.gout, 0), r.out_sem.at[slot]
        ).wait()
    if mode != "given":
        reduce.begin(out_items)
        queue.extend(reduce.turns(in_items + out_items))
    pace = len(queue) / (24 if mode == "first" else 26)

    fetches["stream"].wait()
    stream = r.stream[...].astype(F32)
    scale = lax.rsqrt(jnp.mean(stream * stream, axis=1, keepdims=True) + EPS)
    r.normed_s[...] = (stream * scale * gain).astype(BF16)
    fetches["pre"].wait()
    fetches["act"].wait()

    @pl.loop(0, tiles)
    def _(i):
        here = lanes(i, GROUP)
        slot = lax.rem(i, 2)

        @pl.when(i + 1 < tiles)
        def _():
            wout_copy(i + 1).start()
            for copy in gate_copies(i + 1):
                copy.start()

        wout_copy(i).wait()
        for copy in gate_copies(i):
            copy.wait()
        mixed_grad = dot(r.low_s[...], r.wout_s[slot].reshape(width, GROUP))
        gate = r.gate_s[slot, 0]
        sig = sigmoid(gate)
        act = r.act[:, here].astype(F32)
        scan_grad = mixed_grad * gate * sig
        r.sg_s[:, here] = scan_grad
        r.pb_s[:, lanes(i + tiles, GROUP)] = (
            mixed_grad * r.gate_s[slot, 1] * sig * (1.0 + gate * (1.0 - sig))
        ).astype(BF16)
        gvec[pl.ds(at.skip, 1), here] = jnp.sum(scan_grad * act, axis=0, keepdims=True)
        step = softplus(r.pre[:, here])
        r.dt_s[:, here] = step
        r.dx_s[pl.ds(0, rows), here] = step * act
        keep_sum(r.own_sum, i, step)

    sums, ends = chain(
        count, me, ctx, r.own_sum, r.sum_s, r.own_end, r.end_s,
        (r.sum_send, r.sum_recv, r.end_send, r.end_recv),
    )
    each(0, me, lambda j: sums(j, me).start())
    weave(pace)
    in_shape = r.stage_in.shape[1:]

    def in_copy(i, slot):
        return pltpu.make_async_copy(
            r.stage_in.at[slot], block_of(r.gin, i), r.in_sem.at[slot]
        )

    def project(i, turn):
        here = lanes(i, GROUP)
        slot = lax.rem(turn, 2)
        copy = in_copy(i, slot)
        following = lax.rem(i + 1, 2 * tiles)

        @pl.when(turn + 1 < 2 * tiles)
        def _():
            win_copy(following, 1 - slot).start()

        @pl.when(turn >= 2)
        def _():
            copy.wait()

        r.stage_in[slot] = (
            dot(r.pb_s[:, here], r.normed_s[...], TN).astype(BF16).reshape(in_shape)
        )
        copy.start()
        win_copy(i, slot).wait()
        part = dot(r.pb_s[:, here], r.win_s[slot].reshape(GROUP, width))

        @pl.when(turn == 0)
        def _():
            r.nsg[...] = part

        @pl.when(turn > 0)
        def _():
            r.nsg[...] += part

    @pl.loop(0, tiles)
    def _(i):
        project(i + tiles, i)

    weave(pace)
    for n in range(states):
        first = rank + states + n
        r.cb_s[:, n, :] = jnp.broadcast_to(r.sp[:, first : first + 1], (rows, 128))
    r.bd_s[...] = spread(small_low, rank, states)
    ones = jnp.where(chunk_mask(CHUNK, states), 1.0, 0.0).astype(BF16)
    states_in(0).start()

    for g in range(groups):
        here = pl.ds(g * GROUP, GROUP)
        rate2 = r.vec_s[pl.ds(0, states), here] * LOG2E

        def first_pass(k, state):
            step = steps - 1 - k
            for i in reversed(range(CHUNK)):
                t = step * CHUNK + i
                state = jnp.exp2(r.dt_s[pl.ds(t, 1), here] * rate2) * (
                    state + r.sg_s[pl.ds(t, 1), here] * widen(r.cb_s[t], GROUP)
                )
            return state

        r.own_end[:, here] = lax.fori_loop(
            0, steps, first_pass, jnp.zeros((states, GROUP), F32)
        ).astype(BF16)
        each(0, me, lambda j: ends(g, j, me).start())
        weave(pace)

    def begin_of(g):
        here = pl.ds(g * GROUP, GROUP)
        rate2 = r.vec_s[pl.ds(0, states), here] * LOG2E

        def carry(k, state):
            j = count - 1 - k
            if g == 0:
                sums(j, j).wait_recv()
            ends(g, j, j).wait_recv()
            return (
                jnp.exp2(rate2 * sum_of(r.sum_s, j, g)) * state
                + r.end_s[j, :, here].astype(F32)
            )

        return lax.fori_loop(
            0, count - 1 - me, carry, jnp.zeros((states, GROUP), F32)
        )

    loads = inner // WIDE * quarters
    for g in range(inner // WIDE):
        here = pl.ds(g * WIDE, WIDE)
        rate = r.vec_s[pl.ds(0, states), here]
        rate2 = rate * LOG2E
        each_wide = WIDE // GROUP
        begin = jnp.concatenate(
            [begin_of(g * each_wide + part) for part in range(each_wide)], 1
        )
        both = (begin, jnp.zeros((states, WIDE), F32))
        for part in range(quarters):
            k = quarters * g + part
            quarter = quarters - 1 - part
            held_states = r.hb.at[k % 2]
            if k + 1 < loads:
                states_in(k + 1).start()
            states_in(k).wait()

            def second_pass(turn, both):
                state, total = both
                step = steps - 1 - turn
                base = pl.multiple_of(step * CHUNK * states - quarter * span, states)
                for i in reversed(range(CHUNK)):
                    t = step * CHUNK + i
                    dt = r.dt_s[pl.ds(t, 1), here]
                    adjoint = state + r.sg_s[pl.ds(t, 1), here] * widen(
                        r.cb_s[t], WIDE
                    )
                    state = jnp.exp2(dt * rate2) * adjoint
                    held = held_states[pl.ds(base + i * states, states), :]
                    rated = state * held.astype(F32) * rate
                    total = total + dt * rated
                    r.ab_s[pl.ds(i * states, states), :] = adjoint.astype(BF16)
                    r.rb_s[pl.ds(i * states, states), :] = rated.astype(BF16)
                tokens = pl.ds(pl.multiple_of(step * CHUNK, CHUNK), CHUNK)
                from_in = dot(r.bd_s[tokens, :], r.ab_s[...])
                from_rate = dot(ones, r.rb_s[...])
                scan_grad = r.sg_s[tokens, here]
                into_in = dot(r.dx_s[tokens, here].astype(BF16), r.ab_s[...], NT)
                into_out = dot(
                    scan_grad.astype(BF16),
                    held_states[pl.ds(base + states, CHUNK * states), :],
                    NT,
                )
                if g == 0:
                    r.pin_s[tokens, :] = into_in
                    r.pout_s[tokens, :] = into_out
                else:
                    r.pin_s[tokens, :] += into_in
                    r.pout_s[tokens, :] += into_out
                r.stepg_s[tokens, here] = (
                    r.act[tokens, here].astype(F32) * from_in + from_rate
                )
                r.sg_s[tokens, here] = (
                    r.dt_s[tokens, here] * from_in
                    + r.vec_s[pl.ds(at.skip, 1), here] * scan_grad
                )
                return state, total

            for k in range(2):
                low = (2 * part + k) * steps // (2 * quarters)
                high = (2 * part + k + 1) * steps // (2 * quarters)
                both = lax.fori_loop(low, high, second_pass, both)
                weave(pace)
        gvec[pl.ds(0, states), here] = both[1]

    fetches["pad"].wait()

    @pl.loop(0, tiles)
    def _(i):
        here = lanes(i, GROUP)
        pre_grad = r.stepg_s[pl.ds(0, rows), here] * sigmoid(r.pre[:, here])
        gvec[pl.ds(at.dt_b, 1), here] = jnp.sum(pre_grad, axis=0, keepdims=True)
        r.prelow_s[:, here] = pre_grad.astype(BF16)
        r.dx_s[:, here] = r.pad[:, here].astype(F32)

    small_grad = (
        dot(r.prelow_s[...], r.dtw_s[...], NT)
        + gather_back(r.pin_s[...], rank, states, at.small)
        + gather_back(r.pout_s[...], rank + states, states, at.small)
    ).astype(BF16)

    @pl.loop(0, tiles)
    def _(i):
        here = lanes(i, GROUP)
        r.full_s[pl.ds(at.dt, rank), here] = dot(
            small_low, r.prelow_s[:, here], TN
        )[:rank]
        r.full_s[pl.ds(0, at.small), here] = dot(small_grad, r.act[:, here], TN)
        act_grad = r.sg_s[:, here] + dot(small_grad, r.sw[pl.ds(0, at.small), here])
        total = r.vec_s[pl.ds(at.conv_b, 1), here]
        for k in range(taps):
            total = (
                total
                + r.vec_s[pl.ds(at.conv + k, 1), here]
                * r.dx_s[pl.ds(HALO - taps + 1 + k, rows), here]
            )
        sig = sigmoid(total)
        conv_grad = act_grad * sig * (1.0 + total * (1.0 - sig))
        r.stepg_s[pl.ds(0, rows), here] = conv_grad
        gvec[pl.ds(at.conv_b, 1), here] = jnp.sum(conv_grad, axis=0, keepdims=True)
        for k in range(taps):
            gvec[pl.ds(at.conv + k, 1), here] = jnp.sum(
                conv_grad * r.dx_s[pl.ds(HALO - taps + 1 + k, rows), here],
                axis=0,
                keepdims=True,
            )

    def edge():
        return pltpu.make_async_remote_copy(
            r.stepg_s.at[pl.ds(0, 8)],
            r.halo_s,
            r.halo_sem.at[0],
            r.halo_sem.at[1],
            device_id=(ctx, jnp.maximum(me - 1, 0)),
            device_id_type=MESH,
        )

    @pl.when(me > 0)
    def _():
        edge().start()

    weave(pace)
    @pl.when(me < count - 1)
    def _():
        edge().wait_recv()

    @pl.when(me == count - 1)
    def _():
        r.halo_s[...] = jnp.zeros_like(r.halo_s)

    @pl.when(me > 0)
    def _():
        edge().wait_send()

    r.stepg_s[pl.ds(rows, 8), :] = r.halo_s[...]

    @pl.loop(0, tiles)
    def _(i):
        here = lanes(i, GROUP)
        total = jnp.zeros((rows, GROUP), F32)
        for k in range(taps):
            total = (
                total
                + r.vec_s[pl.ds(at.conv + k, 1), here]
                * r.stepg_s[pl.ds(taps - 1 - k, rows), here]
            )
        r.pb_s[:, here] = total.astype(BF16)
        project(i, i + tiles)

    stream = r.stream[...].astype(F32)
    scale = lax.rsqrt(jnp.mean(stream * stream, axis=1, keepdims=True) + EPS)
    normed_grad = r.nsg[...]
    gain_grad = jnp.sum(normed_grad * stream * scale, axis=0, keepdims=True)
    gain_grad = jnp.broadcast_to(gain_grad, (8, width)).astype(BF16)
    pick = gain_pick(channels)
    for i in range(inner // 256):
        wide = dot(gain_grad[:, 128 * i : 128 * i + 128], pick, NT)
        gvec[pl.ds(at.gain, 1), pl.ds(256 * i, 256)] = wide[:1]
    for k in range(at.count, at.rows):
        r.full_s[pl.ds(k, 1), :] = jnp.zeros((1, inner), F32)
    if mode == "given":
        r.gsmall[...] = r.full_s[...]
    elif mode == "last":
        split_small(channels, r.full_s, r.gsmall)
    else:
        split_small(channels, r.full_s, Folded(r.gsmall_s))
        small_copy = pltpu.make_async_copy(r.gsmall_s, r.gsmall_hbm, r.small_sem.at[0])
        small_copy.start()
    scaled = normed_grad * gain
    inner_sum = jnp.mean(scaled * stream, axis=1, keepdims=True)
    r.nsg[...] = (
        r.sgrad[...].astype(F32) + scale * scaled - stream * (scale * scale * scale) * inner_sum
    )
    for slot in range(2):
        in_copy(0, slot).wait()
    weave(len(queue))
    if mode == "first":
        small_copy.wait()
        reduce.finish()
        for partner in square_partners(depth):
            signal(r.ready_sem, partner)
        pl.semaphore_wait(r.ready_sem, len(square_partners(depth)))
        reduce.begin(own_items)
        for turn in reduce.turns(own_items):
            turn()
    if mode != "given":
        reduce.finish()
    each(0, me, lambda j: sums(j, me).wait_send())
    for g in range(groups):
        each(0, me, lambda j: ends(g, j, me).wait_send())


def in_vmem(count):
    return [pl.BlockSpec(memory_space=pltpu.VMEM)] * count


def in_any(count):
    return [pl.BlockSpec(memory_space=pl.ANY)] * count


def forward_call(cfg, mode, stream, operands):
    rows, inner, states, taps, rank, count, channels = cfg
    at = Names(states, taps, rank)
    width = stream.shape[1]
    groups = inner // GROUP
    devices = inner // channels
    shape = jax.ShapeDtypeStruct
    dma = pltpu.SemaphoreType.DMA
    vmem, any_space = in_vmem(1)[0], in_any(1)[0]
    inputs = [("stream", stream, vmem)]
    for name, array in operands:
        large = name.startswith(("all_", "win_", "wout_", "gsm_"))
        inputs.append((name, array, any_space if large else vmem))
    outputs = [
        ("new", shape(stream.shape, BF16 if mode == "later" else F32), vmem),
        ("sp", shape((rows, at.small), F32), vmem),
        ("h_hbm", shape(((rows + 1) * states, inner), BF16), any_space),
    ]
    saved = {
        "pad": ((rows + HALO, inner), BF16),
        "gate": ((rows, inner), F32),
        "act": ((rows, inner), BF16),
        "pre": ((rows, inner), F32),
        "y": ((rows, inner), F32),
        "mixed": ((rows, inner), BF16),
    }
    for name, (size, kind) in saved.items():
        outputs.append((name + "_hbm", shape(size, kind), any_space))
    if mode == "given":
        given = dict(operands)
        in_shape, out_shape = given["win_hbm"].shape, given["wout_hbm"].shape
    else:
        in_shape = (devices, 2 * inner // devices, width)
        out_shape = (devices, width // devices, inner)
        small_shape = (devices, at.rows * channels // 128, 128)
        outputs.append(("sw", shape((at.rows, inner), BF16), vmem))
        outputs.append(("wout_all", shape(out_shape, BF16), any_space))
    if mode == "first":
        outputs.append(("win_all", shape(in_shape, BF16), any_space))
        outputs.append(("win2_all", shape(in_shape, BF16), any_space))
        outputs.append(("gsm2_all", shape(small_shape, BF16), any_space))
    scratch = [
        ("win_s", pltpu.VMEM(in_shape, BF16)),
        ("wout_s", pltpu.VMEM(out_shape, BF16)),
        ("vec_s", pltpu.VMEM((at.rows - at.vec, inner), F32)),
        ("dtw_s", pltpu.VMEM((at.small, inner), BF16)),
        ("normed_s", pltpu.VMEM(stream.shape, BF16)),
        ("padf_s", pltpu.VMEM((rows + HALO, inner), F32)),
        ("halo_s", pltpu.VMEM((HALO, inner), BF16)),
        ("dt_s", pltpu.VMEM((rows, inner), F32)),
        ("dx_s", pltpu.VMEM((rows, inner), F32)),
        ("bb_s", pltpu.VMEM((rows, states, 128), F32)),
        ("cd_s", pltpu.VMEM((rows, CHUNK * states), BF16)),
        ("hs", pltpu.VMEM(((rows + 1) * states, inner), BF16)),
        ("own_sum", pltpu.VMEM((8, inner // 8), F32)),
        ("sum_s", pltpu.VMEM((count, 8, inner // 8), F32)),
        ("own_end", pltpu.VMEM((states, inner), BF16)),
        ("end_s", pltpu.VMEM((count, states, inner), BF16)),
        ("halo_sem", dma((2,))),
        ("sum_send", dma((count,))),
        ("sum_recv", dma((count,))),
        ("end_send", dma((groups, count))),
        ("end_recv", dma((groups, count))),
        ("h_sem", dma((groups,))),
        ("load_sem", dma((3,))),
        ("save_sem", dma((4 + 2 * groups,))),
    ]
    for name, (size, kind) in saved.items():
        scratch.append((name, pltpu.VMEM(size, kind)))
    if mode != "given":
        pieces = 8 if mode == "first" else 2
        scratch += [
            ("gsm_s", pltpu.VMEM(small_shape, BF16)),
            ("pack_s", pltpu.VMEM(small_shape[1:], F32)),
            ("packed_s", pltpu.VMEM((2,) + small_shape[1:], BF16)),
            ("own_sem", dma((pieces,))),
            ("send_sem", dma((pieces, Gather.sends(count // 2)))),
            ("recv_sem", dma((pieces, devices))),
            ("store_sem", dma((2,))),
        ]
    names = [entry[0] for entry in inputs + outputs + scratch]
    results = pl.pallas_call(
        functools.partial(forward_kernel, cfg, mode, names),
        out_shape=tuple(entry[1] for entry in outputs),
        in_specs=[entry[2] for entry in inputs],
        out_specs=tuple(entry[2] for entry in outputs),
        scratch_shapes=[entry[1] for entry in scratch],
        compiler_params=pltpu.CompilerParams(
            collective_id={"given": 0, "first": 4, "later": 5}[mode],
            has_side_effects=True,
            vmem_limit_bytes=VMEM_BYTES,
        ),
        name="forward_" + mode,
    )(*[entry[1] for entry in inputs])
    return {
        entry[0].removesuffix("_hbm"): result
        for entry, result in zip(outputs, results)
    }


def backward_call(cfg, mode, sgrad, stream, weights, saved, later):
    rows, inner, states, taps, rank, count, channels = cfg
    at = Names(states, taps, rank)
    width = stream.shape[1]
    groups = inner // GROUP
    wide = CHUNK * states
    depth = count // 2
    sw, win, wout = weights
    shape = jax.ShapeDtypeStruct
    dma = pltpu.SemaphoreType.DMA
    vmem, any_space = in_vmem(1)[0], in_any(1)[0]
    in_rows, out_rows = win.shape[1], wout.shape[1]
    lead = (1, 1, win.shape[0] // 2, 2) if mode == "given" else (2, 2, depth, 2)
    small_rows = at.rows * channels // 128
    inputs = [
        ("sgrad", sgrad, vmem),
        ("sw", sw, vmem),
        ("win", win, any_space),
        ("wout", wout, any_space),
    ]
    for name in ("sp", "mixed"):
        inputs.append((name, saved[name], vmem))
    for name in ("gate", "y"):
        inputs.append((name, saved[name], any_space))
    inputs.append(("h_hbm", saved["h"], any_space))
    fetched = {name: saved[name] for name in ("pre", "act", "pad")}
    fetched["stream"] = stream
    for name, array in fetched.items():
        inputs.append((name + "_hbm", array, any_space))
    outputs = [
        ("nsg", shape((rows, width), F32), vmem),
        ("gin", shape(lead + (in_rows, width), BF16), any_space),
        ("gout", shape(lead + (out_rows, inner), BF16), any_space),
    ]
    scratch = [
        ("full_s", pltpu.VMEM((at.rows, inner), F32)),
        ("vec_s", pltpu.VMEM((at.rows - at.vec, inner), F32)),
        ("dtw_s", pltpu.VMEM((at.small, inner), BF16)),
        ("hb", pltpu.VMEM((2, (rows // 4 + 1) * states, WIDE), BF16)),
        ("normed_s", pltpu.VMEM((rows, width), BF16)),
        ("low_s", pltpu.VMEM((rows, width), BF16)),
        ("lowt_s", pltpu.VMEM((width, rows), BF16)),
        ("sg_s", pltpu.VMEM((rows, inner), F32)),
        ("dt_s", pltpu.VMEM((rows, inner), F32)),
        ("dx_s", pltpu.VMEM((rows + HALO, inner), F32)),
        ("stepg_s", pltpu.VMEM((rows + 8, inner), F32)),
        ("pb_s", pltpu.VMEM((rows, 2 * inner), BF16)),
        ("cb_s", pltpu.VMEM((rows, states, 128), F32)),
        ("bd_s", pltpu.VMEM((rows, wide), BF16)),
        ("ab_s", pltpu.VMEM((wide, WIDE), BF16)),
        ("rb_s", pltpu.VMEM((wide, WIDE), BF16)),
        ("pin_s", pltpu.VMEM((rows, wide), F32)),
        ("pout_s", pltpu.VMEM((rows, wide), F32)),
        ("prelow_s", pltpu.VMEM((rows, inner), BF16)),
        ("stage_in", pltpu.VMEM((2, 2, 2, in_rows, width), BF16)),
        ("stage_out", pltpu.VMEM((2, 2, 2, out_rows, inner), BF16)),
        ("win_s", pltpu.VMEM((2, GROUP // in_rows, in_rows, width), BF16)),
        ("wout_s", pltpu.VMEM((2,) + wout.shape[:2] + (GROUP,), BF16)),
        ("gate_s", pltpu.VMEM((2, 2, rows, GROUP), F32)),
        ("halo_s", pltpu.VMEM((8, inner), F32)),
        ("own_sum", pltpu.VMEM((8, inner // 8), F32)),
        ("sum_s", pltpu.VMEM((count, 8, inner // 8), F32)),
        ("own_end", pltpu.VMEM((states, inner), BF16)),
        ("end_s", pltpu.VMEM((count, states, inner), BF16)),
        ("halo_sem", dma((2,))),
        ("sum_send", dma((count,))),
        ("sum_recv", dma((count,))),
        ("end_send", dma((groups, count))),
        ("end_recv", dma((groups, count))),
        ("h_sem", dma((2,))),
        ("in_sem", dma((2,))),
        ("out_sem", dma((2,))),
        ("win_sem", dma((2,))),
        ("wout_sem", dma((2,))),
        ("gate_sem", dma((2, 2))),
        ("fetch_sem", dma((len(fetched),))),
    ]
    for name, array in fetched.items():
        scratch.append((name, pltpu.VMEM(array.shape, array.dtype)))
    if mode == "given":
        outputs.append(("gsmall", shape((at.rows, inner), F32), vmem))
    else:
        outputs.append(("sum_out", shape((out_rows, inner), F32), vmem))
        held = [("rout", out_rows // 2, inner, 2, False)]
        pieces = 2
        if mode == "last":
            small_shape = (inner // channels, small_rows, 128)
            outputs.append(("gsmall", shape(small_shape, BF16), vmem))
        else:
            inputs.append(("next_gin", later["gin"], any_space))
            small = later["gsmall"].reshape(lead + (small_rows, 128))
            inputs.append(("next_gsmall", small, any_space))
            outputs.append(("gsmall_hbm", shape(small.shape, BF16), any_space))
            scratch.append(("gsmall_s", pltpu.VMEM(small.shape, BF16)))
            outputs.append(("sum_in", shape((2, in_rows, width), F32), vmem))
            outputs.append(("sum_small", shape((2, small_rows, 128), F32), vmem))
            held.append(("rin", in_rows // 4, width, 4, False))
            held.append(("rsmall", small_rows, 128, 1, False))
            scratch.append(("small_sem", dma((1,))))
            scratch.append(("ready_sem", pltpu.SemaphoreType.REGULAR))
            pieces = 12
        for name, piece, wide_by, cuts, sided in held:
            for k in range(cuts):
                found = Reduce.buffers_of(depth, piece, wide_by, sided)
                for part, buffer in enumerate(found):
                    scratch.append((f"{name}{k}_{part}", buffer))
        scratch += [
            ("own_sem", dma((pieces, 2))),
            ("send_sem", dma((pieces, 4, depth))),
            ("recv_sem", dma((pieces, 4, depth))),
        ]
    names = [entry[0] for entry in inputs + outputs + scratch]
    results = pl.pallas_call(
        functools.partial(backward_kernel, cfg, mode, names),
        out_shape=tuple(entry[1] for entry in outputs),
        in_specs=[entry[2] for entry in inputs],
        out_specs=tuple(entry[2] for entry in outputs),
        scratch_shapes=[entry[1] for entry in scratch],
        compiler_params=pltpu.CompilerParams(
            collective_id={"given": 1, "last": 6, "first": 7}[mode],
            has_side_effects=True,
            vmem_limit_bytes=VMEM_BYTES,
        ),
        name="backward_" + mode,
    )(*[entry[1] for entry in inputs])
    return {entry[0]: result for entry, result in zip(outputs, results)}


def on_device(
    mesh,
    hidden_in,
    cotangent,
    norm_gain,
    in_weight,
    conv_weight,
    conv_bias,
    x_weight,
    dt_weight,
    dt_bias,
    a_log,
    skip_gain,
    out_weight,
):
    layers = norm_gain.shape[0]
    rows, width = hidden_in.shape
    taps, channels = conv_weight.shape[1:]
    states = a_log.shape[2]
    rank = dt_weight.shape[1]
    devices, count = mesh.shape["ctx"] * mesh.shape["seq"], mesh.shape["seq"]
    inner = channels * devices
    gains = norm_gain.shape[1]
    at = Names(states, taps, rank)
    cfg = (rows, inner, states, taps, rank, count, channels)
    depth = count // 2
    by_kernel = (
        mesh.shape["ctx"] == 4
        and depth % 2 == 0
        and layers == 2
        and in_weight.shape[2] % 32 == 0
        and out_weight.shape[2] % 32 == 0
        and channels == 64
        and at.rows == 2 * at.small
    )

    all_in, all_out = in_weight.transpose(0, 2, 1), out_weight.transpose(0, 2, 1)
    stream = hidden_in if by_kernel else hidden_in.astype(F32)
    streams, runs, weights = [], [], []
    if by_kernel:
        operands = [
            ("all_in", all_in),
            ("x_weight", x_weight),
            ("dt_weight", dt_weight),
            ("a_log", a_log),
            ("conv_weight", conv_weight),
            ("conv_bias", conv_bias),
            ("dt_bias", dt_bias),
            ("skip_gain", skip_gain),
            ("norm_gain", norm_gain),
            ("all_out", all_out),
        ]
        first = forward_call(cfg, "first", stream, operands)
        operands = [
            ("win_hbm", first["win2_all"]),
            ("gsm_hbm", first["gsm2_all"]),
            ("all_out", all_out),
        ]
        second = forward_call(cfg, "later", first["new"], operands)
        runs = [first, second]
        wins = [first["win_all"], first["win2_all"]]
        weights = [
            (run["sw"], win, run["wout_all"]) for run, win in zip(runs, wins)
        ]
        streams = [stream, first["new"]]
        stream = second["new"]
    else:
        gain_rows = jnp.pad(norm_gain, ((0, 0), (0, channels - gains)))
        packed = jnp.concatenate(
            [
                x_weight.transpose(0, 2, 1),
                dt_weight,
                a_log.transpose(0, 2, 1),
                conv_weight,
                jnp.stack([conv_bias, dt_bias, skip_gain, gain_rows], 1),
                jnp.zeros((layers, at.rows - at.count, channels), BF16),
            ],
            1,
        )
        for w_in, w_out, w_small in zip(all_in, all_out, packed):
            w_in = lax.all_gather(w_in, ("ctx", "seq"), axis=0, tiled=True)
            w_out = lax.all_gather(w_out, ("ctx", "seq"), axis=0, tiled=True)
            sw = lax.all_gather(w_small, ("ctx", "seq"), axis=1, tiled=True)
            w_in = w_in.reshape(-1, 128, width)
            w_out = w_out.reshape(-1, 32, inner)
            operands = [("win_hbm", w_in), ("sw", sw), ("wout_hbm", w_out)]
            run = forward_call(cfg, "given", stream, operands)
            runs.append(run)
            weights.append((sw, w_in, w_out))
            streams.append(stream)
            stream = run["new"]
    stream_grad = cotangent
    summed = [None] * layers
    if by_kernel:
        last = backward_call(
            cfg, "last", stream_grad, streams[1], weights[1], runs[1], None
        )
        head = backward_call(
            cfg, "first", last["nsg"], streams[0], weights[0], runs[0], last
        )
        stream_grad = head["nsg"]

        sum_in = head["sum_in"]
        sum_out = jnp.stack([head["sum_out"], last["sum_out"]], 0)
        sum_small = head["sum_small"].reshape(layers, -1, 128 // channels, channels)
        sum_small = sum_small.transpose(0, 2, 1, 3).reshape(layers, -1, channels)
    else:
        for layer in reversed(range(layers)):
            run = backward_call(
                cfg,
                "given",
                stream_grad,
                streams[layer],
                weights[layer],
                runs[layer],
                None,
            )
            stream_grad = run["nsg"]
            summed[layer] = [
                lax.psum_scatter(
                    array.astype(F32),
                    ("ctx", "seq"),
                    scatter_dimension=dim,
                    tiled=True,
                )
                for array, dim in (
                    (run["gin"].reshape(-1, width), 0),
                    (run["gout"].reshape(-1, inner), 0),
                    (run["gsmall"], 1),
                )
            ]
        sum_in, sum_out, sum_small = [jnp.stack(each, 0) for each in zip(*summed)]
    vectors = sum_small[:, at.vec : at.count]
    grads = (
        vectors[:, at.gain, :gains],
        sum_in.transpose(0, 2, 1),
        vectors[:, at.conv : at.conv + taps],
        vectors[:, at.conv_b],
        sum_small[:, : at.small].transpose(0, 2, 1),
        sum_small[:, at.dt : at.dt + rank],
        vectors[:, at.dt_b],
        vectors[:, :states].transpose(0, 2, 1),
        vectors[:, at.skip],
        sum_out.transpose(0, 2, 1),
    )
    return (stream.astype(BF16), stream_grad) + grads


def solution(mesh):
    split = ("ctx", "seq")
    tokens, last = P(split, None), P(None, split)
    middle, third = P(None, split, None), P(None, None, split)
    weights = (last, third, third, last, middle, third, last, middle, last, third)
    return jax.shard_map(
        functools.partial(on_device, mesh),
        mesh=mesh,
        in_specs=(tokens, tokens) + weights,
        out_specs=(tokens, tokens) + weights,
        check_vma=False,
    )
```
